32 devices in a mesh: fsdp: 16 (over z, y, x), tensor: 2 (over core).
Axes of the slice: x: 2, y: 2, z: 4, core: 2. Of those that a mesh axis runs over, the one named last changes fastest.
Arguments:
- layer_input: bfloat16 [16384, 1024], P(('fsdp', 'tensor')), may hold values from -6 to 6
- doc_ids: int32 [16, 1024], P('fsdp'), may hold values from 0 to 3, never falling along the last dimension, each value on 1 to 768 neighbouring positions
- input_gain: float32 [1024], replicated, may hold values from 0.1 to 1.9
- mixer_weight: float32 [1024, 2, 1536], P('fsdp', None, 'tensor'), may hold values from -0.1875 to 0.1875
- state_weight: float32 [1024, 256], P('fsdp'), may hold values from -0.1875 to 0.1875
- step_weight: float32 [1024, 24], P('fsdp', 'tensor'), may hold values from -0.1875 to 0.1875
- conv_weight: float32 [4, 1536], P(None, 'tensor'), may hold values from -3 to 3
- conv_bias: float32 [1536], P('tensor'), may hold values from -3 to 3
- state_conv: float32 [4, 256], replicated, may hold values from -3 to 3
- state_conv_bias: float32 [256], replicated, may hold values from -3 to 3
- step_bias: float32 [24], P('tensor'), may hold values from -5 to -1
- decay_log: float32 [24], P('tensor'), may hold values from -1 to 2
- skip_gain: float32 [24], P('tensor'), may hold values from 0.5 to 1.5
- mixer_gain: float32 [1536], P('tensor'), may hold values from 0.1 to 1.9
- mixer_proj: float32 [1536, 1024], P('tensor', 'fsdp'), may hold values from -0.15625 to 0.15625
- query_weight: float32 [1024, 512], P('fsdp', 'tensor'), may hold values from -0.1875 to 0.1875
- keyval_projection: float32 [1024, 2, 128], P('fsdp'), may hold values from -0.1875 to 0.1875
- attention_proj: float32 [512, 1024], P('tensor', 'fsdp'), may hold values from -1.5 to 1.5
- second_gain: float32 [1024], replicated, may hold values from 0.1 to 1.9
- gate_up: float32 [1024, 2, 2048], P('fsdp', None, 'tensor'), may hold values from -0.1875 to 0.1875
- down_proj: float32 [2048, 1024], P('tensor', 'fsdp'), may hold values from -0.125 to 0.125
- cotangent: bfloat16 [16384, 1024], P(('fsdp', 'tensor')), may hold values from -6 to 6
Outputs:
- layer_output: bfloat16 [16384, 1024], P(('fsdp', 'tensor'))
- input_grad: float32 [16384, 1024], P(('fsdp', 'tensor'))
- grad_input_gain: float32 [1024], replicated
- grad_mixer_weight: float32 [1024, 2, 1536], P('fsdp', None, 'tensor')
- grad_state_weight: float32 [1024, 256], P('fsdp')
- grad_step_weight: float32 [1024, 24], P('fsdp', 'tensor')
- grad_conv_weight: float32 [4, 1536], P(None, 'tensor')
- grad_conv_bias: float32 [1536], P('tensor')
- grad_state_conv: float32 [4, 256], replicated
- grad_state_conv_bias: float32 [256], replicated
- grad_step_bias: float32 [24], P('tensor')
- grad_decay_log: float32 [24], P('tensor')
- grad_skip_gain: float32 [24], P('tensor')
- grad_mixer_gain: float32 [1536], P('tensor')
- grad_mixer_proj: float32 [1536, 1024], P('tensor', 'fsdp')
- grad_query_weight: float32 [1024, 512], P('fsdp', 'tensor')
- grad_keyval_weight: float32 [1024, 2, 128], P('fsdp')
- grad_attention_proj: float32 [512, 1024], P('tensor', 'fsdp')
- grad_second_gain: float32 [1024], replicated
- grad_gate_up: float32 [1024, 2, 2048], P('fsdp', None, 'tensor')
- grad_down_proj: float32 [2048, 1024], P('tensor', 'fsdp')
The draws below stay inside these ranges and needn't reach their ends.
Inputs may be any that keep to these rules, and one draw needn't show every extreme that they name: `doc_ids`: in each row the document numbers start at 0, never fall and step by one; no document has more than 768 tokens, and some document has exactly that many.
All inputs are finite; a program needn't handle non-finite values.
Results may differ from the reference program's by a relative error of at most 0.02.
Values may be sent and summed in bfloat16 or wider, within the bound.
A program may use at most 256 MiB of HBM per device.

```python
import math
import jax
import jax.numpy as jnp
import numpy as np
from jax import lax

MODEL_DIM = 1024
QUERY_HEADS = 8
KEYVAL_HEADS = 2
HEAD_SIZE = 64
MH = 24
NS = 128
CONV = 4
FF = 2048
SEQLEN = 1024
SSD_BLOCK = 128
DOCS = 4
DSSM = 1536
NSEQ = 16
TOKENS = 16384


def levels(rng, dims, split, low, largest):
    def one(axis_at, shards_of):
        heights = jax.random.uniform(jax.random.fold_in(jax.random.fold_in(rng, 6), axis_at), (shards_of,), jnp.float32, low / len(split), largest / len(split))
        return jnp.repeat(jnp.exp(heights), dims[axis_at] // shards_of).reshape((-1,) + (1,) * (len(dims) - axis_at - 1))

    loudness = one(*split[0])
    for cut in split[1:]:
        loudness = loudness * one(*cut)
    return loudness


def split_up(count, total, most, lean):
    weights = [(1 << 20) // math.isqrt(standing ** lean) + 1 for standing in range(2, count + 1)]
    surplus, given = total - most - (count - 1), [1] * (count - 1)
    while surplus > 0:
        free = [i for i in range(count - 1) if given[i] < most]
        mass, budget = sum([weights[i] for i in free]), surplus
        for i in free:
            extra = min(most - given[i], max(1, budget * weights[i] // mass), surplus)
            given[i] = given[i] + extra
            surplus = surplus - extra
    return np.array([most] + given)


def uneven(own_key, number_of, total, most, slope):
    if number_of == 2:
        one = jax.random.randint(own_key, (), max(1, total - most), min(most, total - 1) + 1)
        return jnp.stack([one, total - one])
    tallies = jnp.asarray(split_up(number_of, total, most, slope), jnp.int32)
    couples = (number_of - 1) // 2
    giver, taker = tallies[1:1 + 2 * couples:2], tallies[2:2 + 2 * couples:2]
    margin = jnp.minimum(giver - 1, most - taker)
    moved = jax.random.randint(jax.random.fold_in(own_key, 1), (couples,), 0, 1 << 20) % (margin + 1)
    tallies = tallies.at[1:1 + 2 * couples:2].set(giver - moved).at[2:2 + 2 * couples:2].set(taker + moved)
    return tallies[jax.random.permutation(jax.random.fold_in(own_key, 2), number_of)]


def normal_values(own_key, dims, deviation, reach, cuts=(), held_as=jnp.bfloat16):
    values = jax.random.normal(own_key, dims, jnp.float32) * deviation
    if len(cuts) > 0:
        values = levels(own_key, dims, cuts, -0.22, 0.18) * values
    return jnp.clip(values, min=-reach, max=reach).astype(held_as)


def setup_inputs(seed: int = 0) -> dict:
    splits = jax.random.split(jax.random.key(seed), 23)
    layer_input = normal_values(splits[0], (TOKENS, MODEL_DIM), 1.0, 6.0, ((0, 32),))
    doc_ids = jax.vmap(lambda own: jnp.searchsorted(jnp.cumsum(uneven(own, DOCS, SEQLEN, SEQLEN * 3 // 4, 0)), jnp.arange(SEQLEN), side="right"))(jax.random.split(splits[1], NSEQ)).reshape((NSEQ, SEQLEN)).astype(jnp.int32)
    input_gain = jnp.clip(1.0 + 0.18 * jax.random.normal(splits[2], (MODEL_DIM,), jnp.float32), 0.1, 1.9)
    mixer_weight = normal_values(splits[3], (MODEL_DIM, 2, DSSM), MODEL_DIM ** -0.5, 0.1875, ((0, 16), (2, 2)), jnp.float32)
    state_weight = normal_values(splits[4], (MODEL_DIM, 2 * NS), MODEL_DIM ** -0.5, 0.1875, ((0, 16),), jnp.float32)
    step_weight = normal_values(splits[5], (MODEL_DIM, MH), MODEL_DIM ** -0.5, 0.1875, ((0, 16), (1, 2)), jnp.float32)
    conv_weight = normal_values(splits[6], (CONV, DSSM), 0.5, 3.0, ((1, 2),), jnp.float32)
    conv_bias = normal_values(splits[7], (DSSM,), 0.5, 3.0, ((0, 2),), jnp.float32)
    state_conv = normal_values(splits[8], (CONV, 2 * NS), 0.5, 3.0, (), jnp.float32)
    state_conv_bias = normal_values(splits[9], (2 * NS,), 0.5, 3.0, (), jnp.float32)
    step_bias = jnp.clip(-5.0 + 4.0 * jax.random.uniform(splits[10], (MH,), jnp.float32) ** levels(splits[10], (MH,), ((0, 2),), -0.2, 0.2), -5.0, -1.0)
    decay_log = jnp.clip(-1.0 + 3.0 * jax.random.uniform(splits[11], (MH,), jnp.float32) ** levels(splits[11], (MH,), ((0, 2),), -0.2, 0.2), -1.0, 2.0)
    skip_gain = jnp.clip(0.5 + 1.0 * jax.random.uniform(splits[12], (MH,), jnp.float32) ** levels(splits[12], (MH,), ((0, 2),), -0.2, 0.2), 0.5, 1.5)
    mixer_gain = jnp.clip(1.0 + 0.18 * jax.random.normal(splits[13], (DSSM,), jnp.float32), 0.1, 1.9)
    mixer_proj = normal_values(splits[14], (DSSM, MODEL_DIM), DSSM ** -0.5, 0.15625, ((0, 2), (1, 16)), jnp.float32)
    query_weight = normal_values(splits[15], (MODEL_DIM, QUERY_HEADS * HEAD_SIZE), MODEL_DIM ** -0.5, 0.1875, ((0, 16), (1, 2)), jnp.float32)
    keyval_projection = normal_values(splits[16], (MODEL_DIM, 2, KEYVAL_HEADS * HEAD_SIZE), MODEL_DIM ** -0.5, 0.1875, ((0, 16),), jnp.float32)
    attention_proj = normal_values(splits[17], (QUERY_HEADS * HEAD_SIZE, MODEL_DIM), (HEAD_SIZE // 4) ** -0.5, 1.5, ((0, 2), (1, 16)), jnp.float32)
    second_gain = jnp.clip(1.0 + 0.18 * jax.random.normal(splits[18], (MODEL_DIM,), jnp.float32), 0.1, 1.9)
    gate_up = normal_values(splits[19], (MODEL_DIM, 2, FF), MODEL_DIM ** -0.5, 0.1875, ((0, 16), (2, 2)), jnp.float32)
    down_proj = normal_values(splits[20], (FF, MODEL_DIM), FF ** -0.5, 0.125, ((0, 2), (1, 16)), jnp.float32)
    cotangent = normal_values(splits[21], (TOKENS, MODEL_DIM), 1.0, 6.0, ((0, 32),))
    return {"layer_input": layer_input, "doc_ids": doc_ids, "input_gain": input_gain, "mixer_weight": mixer_weight, "state_weight": state_weight, "step_weight": step_weight, "conv_weight": conv_weight, "conv_bias": conv_bias, "state_conv": state_conv, "state_conv_bias": state_conv_bias, "step_bias": step_bias, "decay_log": decay_log, "skip_gain": skip_gain, "mixer_gain": mixer_gain, "mixer_proj": mixer_proj, "query_weight": query_weight, "keyval_projection": keyval_projection, "attention_proj": attention_proj, "second_gain": second_gain, "gate_up": gate_up, "down_proj": down_proj, "cotangent": cotangent}


EPS = 1e-05
THETA = 100000000000.0
MASKED = -1e+30

@jax.custom_vjp
def reduced_precision(v):
    return lax.optimization_barrier(v.astype(jnp.bfloat16)).astype(jnp.float32)

@jax.custom_vjp
def low_back(v):
    return v

def low_keep(v):
    return (reduced_precision(v), None)

def low_pass(kept, grad):
    return (grad,)

def back_keep(v):
    return (v, None)

def back_low(kept, grad):
    return (reduced_precision(grad),)
reduced_precision.defvjp(low_keep, low_pass)
low_back.defvjp(back_keep, back_low)

def accurate_product(left_side, right_side):
    return jnp.dot(left_side, right_side, precision=lax.Precision.HIGHEST, preferred_element_type=jnp.float32)

def norm_scale(values):
    return lax.rsqrt(lax.optimization_barrier(jnp.mean(values * values, axis=-1, keepdims=True)) + EPS)

def positions(segments):
    length = segments.shape[-1]
    position_table = jnp.arange(length, dtype=jnp.int32)
    change = jnp.concatenate([jnp.ones(segments.shape[:-1] + (1,), jnp.bool_), segments[..., 1:] != segments[..., :-1]], axis=-1)
    starts = jnp.where(change, position_table, jnp.zeros_like(position_table))
    begins = lax.cummax(starts, axis=segments.ndim - 1)
    return (position_table - begins).astype(jnp.float32)

def apply_rotation(values, position_table, direction):
    half_width = values.shape[-1] // 2
    frequencies = jnp.exp(jnp.arange(half_width, dtype=jnp.float32) * (-2.0 * math.log(THETA) / values.shape[-1]))
    angles = position_table[:, None] * frequencies[None, :]
    cosine = jnp.cos(angles)[:, None, :]
    sine_part = direction * jnp.sin(angles)[:, None, :]
    front_half = values[..., :half_width]
    rear_half = values[..., half_width:]
    return jnp.concatenate([front_half * cosine - rear_half * sine_part, rear_half * cosine + front_half * sine_part], axis=-1)

def causal_conv(values, segments, kernel, biases):
    kernel_taps = kernel.shape[0]
    result = values * kernel[kernel_taps - 1] + biases
    for offset in range(1, kernel_taps):
        earlier = jnp.concatenate([jnp.zeros((offset, values.shape[1]), jnp.float32), values[:-offset]], axis=0)
        same_doc = jnp.concatenate([jnp.zeros((offset,), jnp.bool_), segments[offset:] == segments[:-offset]], axis=0)
        result = result + jnp.where(same_doc[:, None], earlier, 0.0) * kernel[kernel_taps - 1 - offset]
    return result

def state_scan(inputs, state_in, state_out, step_sizes, decay_rates, segments, block_len):
    length, head_count, channels = inputs.shape
    states = state_in.shape[1]
    blocks = length // block_len
    highest = lax.Precision.HIGHEST

    def advance(carry, pieces):
        memory, before = carry
        values, keys_in, read_keys, widths, labels = pieces
        log_decay = jnp.cumsum(widths * decay_rates[None, :], axis=0)
        position_table = jnp.arange(block_len, dtype=jnp.int32)
        allowed = (labels[:, None] == labels[None, :]) & (position_table[:, None] >= position_table[None, :])
        log_gaps = jnp.where(allowed[:, :, None], log_decay[:, None, :] - log_decay[None, :, :], 0.0)
        decays = jnp.where(allowed[:, :, None], jnp.exp(log_gaps), 0.0)
        intersection = jnp.dot(read_keys, keys_in.T, precision=highest, preferred_element_type=jnp.float32)
        scaled = widths[:, :, None] * values
        within = jnp.einsum('tsh,shp->thp', intersection[:, :, None] * decays, scaled, precision=highest)
        carried_on = (labels == before).astype(jnp.float32)
        carried = jnp.einsum('tn,hpn->thp', read_keys, memory, precision=highest) * (jnp.exp(log_decay) * carried_on[:, None])[:, :, None]
        tail_decay = jnp.where((labels == labels[-1])[:, None], jnp.exp(log_decay[-1][None, :] - log_decay), 0.0)
        memory = memory * (jnp.exp(log_decay[-1]) * carried_on[-1])[:, None, None] + jnp.einsum('sh,shp,sn->hpn', tail_decay, scaled, keys_in, precision=highest)
        return ((memory, labels[-1]), within + carried)
    initial = (jnp.zeros((head_count, channels, states), jnp.float32), jnp.int32(-1))
    pieces = (inputs.reshape(blocks, block_len, head_count, channels), state_in.reshape(blocks, block_len, states), state_out.reshape(blocks, block_len, states), step_sizes.reshape(blocks, block_len, head_count), segments.reshape(blocks, block_len))
    outputs = lax.scan(jax.checkpoint(advance), initial, pieces)[1]
    return outputs.reshape(length, head_count, channels)

def mamba_mixer(mixed_x, state_proj, step_raw, gate_z, segments, conv_weight, conv_bias, state_conv, state_conv_bias, step_bias, decay_log, skip_gain, block_len):
    total_rows = mixed_x.shape[0]
    head_count = step_raw.shape[1]
    conv_values = jax.nn.silu(causal_conv(mixed_x, segments, conv_weight, conv_bias))
    conv_state = jax.nn.silu(causal_conv(state_proj, segments, state_conv, state_conv_bias))
    half_width = conv_state.shape[1] // 2
    step_sizes = jax.nn.softplus(step_raw + step_bias)
    decay_rates = -jnp.exp(decay_log)
    values = conv_values.reshape(total_rows, head_count, -1)
    scanned = state_scan(values, conv_state[:, :half_width], conv_state[:, half_width:], step_sizes, decay_rates, segments, block_len)
    scanned = scanned + skip_gain[None, :, None] * values
    return scanned.reshape(total_rows, -1) * jax.nn.silu(gate_z)

def sequence_layer(pieces, weights):
    tokens, segments = pieces
    input_gain, mixer_weight, state_weight, step_weight, conv_weight, conv_bias, state_conv, state_conv_bias, step_bias, decay_log, skip_gain, mixer_gain, mixer_proj, query_weight, keyval_projection, attention_proj, second_gain, gate_up, down_proj = weights
    total_rows = tokens.shape[0]
    highest = lax.Precision.HIGHEST
    normalized_input = reduced_precision(tokens * norm_scale(tokens) * input_gain)
    mixer_in = low_back(accurate_product(normalized_input, mixer_weight.reshape(MODEL_DIM, 2 * DSSM)))
    state_proj = accurate_product(normalized_input, state_weight)
    step_raw = low_back(accurate_product(normalized_input, step_weight))
    queries = low_back(accurate_product(normalized_input, query_weight))
    keyval_rows = accurate_product(normalized_input, keyval_projection.reshape(MODEL_DIM, 2 * KEYVAL_HEADS * HEAD_SIZE))
    gated_out = mamba_mixer(mixer_in[:, DSSM:], state_proj, step_raw, mixer_in[:, :DSSM], segments, conv_weight, conv_bias, state_conv, state_conv_bias, step_bias, decay_log, skip_gain, SSD_BLOCK)
    mixed_norm = reduced_precision(gated_out * norm_scale(gated_out) * mixer_gain)
    position_table = positions(segments[None, :])[0]
    query_rot = reduced_precision(apply_rotation(queries.reshape(total_rows, QUERY_HEADS, HEAD_SIZE), position_table, 1.0))
    key_rotated = reduced_precision(apply_rotation(keyval_rows[:, :KEYVAL_HEADS * HEAD_SIZE].reshape(total_rows, KEYVAL_HEADS, HEAD_SIZE), position_table, 1.0))
    value_reduced = reduced_precision(keyval_rows[:, KEYVAL_HEADS * HEAD_SIZE:].reshape(total_rows, KEYVAL_HEADS, HEAD_SIZE))
    key_complete = jnp.repeat(key_rotated, QUERY_HEADS // KEYVAL_HEADS, axis=1)
    value_complete = jnp.repeat(value_reduced, QUERY_HEADS // KEYVAL_HEADS, axis=1)
    scores = low_back(jnp.einsum('qhd,khd->hqk', query_rot, key_complete, precision=highest) * HEAD_SIZE ** (-0.5))
    indices = jnp.arange(total_rows, dtype=jnp.int32)
    allowed = (segments[:, None] == segments[None, :]) & (indices[:, None] >= indices[None, :])
    probabilities = jax.nn.softmax(jnp.where(allowed[None], scores, MASKED), axis=-1)
    attended = jnp.einsum('hqk,khd->qhd', reduced_precision(probabilities), value_complete, precision=highest)
    attended = low_back(reduced_precision(attended)).reshape(total_rows, QUERY_HEADS * HEAD_SIZE)
    branch = low_back(accurate_product(mixed_norm, mixer_proj) + accurate_product(attended, attention_proj))
    middle = tokens + branch
    second = reduced_precision(middle * norm_scale(middle) * second_gain)
    gate_vals = low_back(accurate_product(second, gate_up.reshape(MODEL_DIM, 2 * FF)))
    active = reduced_precision(jax.nn.silu(gate_vals[:, :FF]) * gate_vals[:, FF:])
    return middle + low_back(accurate_product(active, down_proj))

def reference(layer_input, doc_ids, input_gain, mixer_weight, state_weight, step_weight, conv_weight, conv_bias, state_conv, state_conv_bias, step_bias, decay_log, skip_gain, mixer_gain, mixer_proj, query_weight, keyval_projection, attention_proj, second_gain, gate_up, down_proj, cotangent):
    tokens_float = layer_input.astype(jnp.float32)

    def forward(tokens, input_gain, mixer_weight, state_weight, step_weight, conv_weight, conv_bias, state_conv, state_conv_bias, step_bias, decay_log, skip_gain, mixer_gain, mixer_proj, query_weight, keyval_projection, attention_proj, second_gain, gate_up, down_proj):
        weights = (input_gain, reduced_precision(mixer_weight), reduced_precision(state_weight), reduced_precision(step_weight), conv_weight, conv_bias, state_conv, state_conv_bias, step_bias, decay_log, skip_gain, mixer_gain, reduced_precision(mixer_proj), reduced_precision(query_weight), reduced_precision(keyval_projection), reduced_precision(attention_proj), second_gain, reduced_precision(gate_up), reduced_precision(down_proj))

        def one_sequence(pieces):
            return sequence_layer(pieces, weights)
        outputs = lax.map(jax.checkpoint(one_sequence), (tokens.reshape(NSEQ, SEQLEN, MODEL_DIM), doc_ids))
        return outputs.reshape(TOKENS, MODEL_DIM)
    result, pullback = jax.vjp(forward, tokens_float, input_gain, mixer_weight, state_weight, step_weight, conv_weight, conv_bias, state_conv, state_conv_bias, step_bias, decay_log, skip_gain, mixer_gain, mixer_proj, query_weight, keyval_projection, attention_proj, second_gain, gate_up, down_proj)
    gradients = pullback(cotangent.astype(jnp.float32))
    return (result.astype(jnp.bfloat16), gradients[0], gradients[1], gradients[2], gradients[3], gradients[4], gradients[5], gradients[6], gradients[7], gradients[8], gradients[9], gradients[10], gradients[11], gradients[12], gradients[13], gradients[14], gradients[15], gradients[16], gradients[17], gradients[18], gradients[19])
```

```python
import functools
import math

import jax
import jax.numpy as jnp
from jax import lax
from jax.experimental import pallas as pl
from jax.experimental.pallas import tpu as pltpu
from jax.sharding import PartitionSpec as P

QUERY_HEADS = 8
KEYVAL_HEADS = 2
HEAD_SIZE = 64
DSSM = 1536
EPS = 1e-05
THETA = 100000000000.0

LANES = 128
CHUNK = 128
MASKED = -1e30
BF, F32 = jnp.bfloat16, jnp.float32


def left_dot(left_side, right_side):
    return lax.dot_general(left_side, right_side, (((0,), (0,)), ((), ())), preferred_element_type=F32)


def right_dot(left_side, right_side):
    return lax.dot_general(left_side, right_side, (((1,), (1,)), ((), ())), preferred_element_type=F32)


def plain_dot(left_side, right_side):
    return jnp.dot(left_side, right_side, preferred_element_type=F32)


def mm(a, b):
    return jnp.dot(a.astype(BF), b.astype(BF), preferred_element_type=F32)


def mm_nt(a, b):
    return lax.dot_general(a.astype(BF), b.astype(BF), (((1,), (1,)), ((), ())), preferred_element_type=F32)


def mm_tn(a, b):
    return lax.dot_general(a.astype(BF), b.astype(BF), (((0,), (0,)), ((), ())), preferred_element_type=F32)


def exact_mm(a, b):
    return jnp.dot(a, b, precision=lax.Precision.HIGHEST, preferred_element_type=F32)


def sigmoid(v):
    return 1.0 / (1.0 + jnp.exp(-v))


def softplus(v):
    return jnp.maximum(v, 0.0) + jnp.log1p(jnp.exp(-jnp.abs(v)))


def split_lanes(values, axis):
    high = values.astype(BF)
    low = (values - high.astype(F32)).astype(BF)
    return jnp.concatenate([high, low], axis=axis)


def iota2(shape, axis):
    return lax.broadcasted_iota(jnp.int32, shape, axis)


def conv_taps(buffer, feats, taps, bias, rows):
    total = buffer[8 : 8 + rows, :] * taps[3:4, :] + bias
    for k in range(1, 4):
        total = total + buffer[8 - k : 8 - k + rows, :] * feats[:, k : k + 1] * taps[3 - k : 4 - k, :]
    return total


def step_parts(step_ref, heads_ref, feats, rows):
    raw = step_ref[...] + heads_ref[0:1, :]
    step = softplus(raw)
    lower = (iota2((rows, rows), 0) >= iota2((rows, rows), 1)).astype(F32)
    log_decay = exact_mm(lower, step * heads_ref[1:2, :])
    last = log_decay[rows - 1 : rows, :]
    enter = jnp.exp(log_decay) * feats[:, 4:5]
    leave = jnp.exp(last - log_decay) * feats[:, 5:6]
    return raw, step, log_decay, enter, leave


def mamba_fwd_kernel(
    feats_ref, docs_ref, x_ref, bc_ref, step_ref, z_ref, taps_ref, staps_ref, heads_ref, expand_ref,
    gain_ref, scan_ref, low_ref, square_ref, states_ref, xbuf, bcbuf, memory,
):
    rows, width = x_ref.shape
    states = bc_ref.shape[1] // 2

    @pl.when(pl.program_id(0) == 0)
    def _():
        xbuf[0:8, :] = jnp.zeros((8, width), F32)
        bcbuf[0:8, :] = jnp.zeros((8, 2 * states), F32)
        memory[...] = jnp.zeros_like(memory)

    feats = feats_ref[...]
    xbuf[8 : 8 + rows, :] = x_ref[...]
    bcbuf[8 : 8 + rows, :] = bc_ref[...]
    pre = conv_taps(xbuf, feats, taps_ref, taps_ref[4:5, :], rows)
    values = pre * sigmoid(pre)
    pre_bc = conv_taps(bcbuf, feats, staps_ref, staps_ref[4:5, :], rows)
    both = pre_bc * sigmoid(pre_bc)
    xbuf[0:8, :] = xbuf[rows : rows + 8, :]
    bcbuf[0:8, :] = bcbuf[rows : rows + 8, :]
    key_in = both[:, :states].astype(BF)
    key_out = both[:, states:].astype(BF)
    _, step, log_decay, enter, leave = step_parts(step_ref, heads_ref, feats, rows)
    expanded = jnp.dot(
        split_lanes(jnp.concatenate([step, enter, leave], axis=0), 1), expand_ref[...], preferred_element_type=F32
    )
    step_w, enter_w, leave_w = expanded[:rows], expanded[rows : 2 * rows], expanded[2 * rows :]
    scaled = values * step_w
    gram = mm_nt(key_out, key_in)
    allowed = (feats[:, 0:1] == docs_ref[...]) & (iota2((rows, rows), 0) >= iota2((rows, rows), 1))
    bias = jnp.where(allowed, 0.0, MASKED)
    log_rows = log_decay.T
    front = iota2((rows, LANES), 1) < LANES // 2
    held = memory[...]
    states_ref[0] = held.astype(BF)
    carried = mm(key_out, held) * enter_w
    fresh = mm_tn(key_in, leave_w * scaled)
    memory[...] = held * enter_w[rows - 1 : rows, :] + fresh
    squares = jnp.zeros((rows, 1), F32)
    for pair in range(width // LANES):
        lanes = slice(pair * LANES, (pair + 1) * LANES)
        mixes = []
        for h in (2 * pair, 2 * pair + 1):
            decay = jnp.exp(log_decay[:, h : h + 1] - log_rows[h : h + 1, :] + bias)
            mixes.append((gram * decay).astype(BF))
        part = scaled[:, lanes]
        stacked = jnp.concatenate([jnp.where(front, part, 0.0), jnp.where(front, 0.0, part)], axis=0)
        inside = mm(jnp.concatenate(mixes, axis=1), stacked)
        scan = inside + carried[:, lanes] + values[:, lanes] * taps_ref[5:6, lanes]
        scan_ref[:, lanes] = scan
        z = z_ref[:, lanes]
        gated = scan * (z * sigmoid(z))
        low_ref[:, lanes] = (gated * gain_ref[:, lanes]).astype(BF)
        squares = squares + jnp.sum(gated * gated, axis=1, keepdims=True)
    square_ref[...] = squares


def mamba_bwd_kernel(
    feats_ref, docs_col_ref, docs_ref, x_ref, x_before_ref, bc_ref, bc_before_ref, step_ref, z_ref, scan_ref, states_ref, norm_grad_ref,
    taps_ref, staps_ref, heads_ref, expand_ref, reduce_ref, gain_ref,
    dz_ref, grads_ref, sums_ref, ssums_ref, hsums_ref,
    xbuf, bcbuf, dxbuf, dbcbuf, dmemory,
):
    rows, width = x_ref.shape
    states = bc_ref.shape[1] // 2

    @pl.when(pl.program_id(0) == 0)
    def _():
        dxbuf[rows : rows + 8, :] = jnp.zeros((8, width), F32)
        dbcbuf[rows : rows + 8, :] = jnp.zeros((8, 2 * states), F32)
        dmemory[...] = jnp.zeros_like(dmemory)
        sums_ref[...] = jnp.zeros_like(sums_ref)
        ssums_ref[...] = jnp.zeros_like(ssums_ref)
        hsums_ref[...] = jnp.zeros_like(hsums_ref)

    feats = feats_ref[...]
    xbuf[0:8, :] = x_before_ref[...]
    bcbuf[0:8, :] = bc_before_ref[...]
    xbuf[8 : 8 + rows, :] = x_ref[...]
    bcbuf[8 : 8 + rows, :] = bc_ref[...]
    pre = conv_taps(xbuf, feats, taps_ref, taps_ref[4:5, :], rows)
    pre_gate = sigmoid(pre)
    values = pre * pre_gate
    pre_bc = conv_taps(bcbuf, feats, staps_ref, staps_ref[4:5, :], rows)
    bc_gate = sigmoid(pre_bc)
    both = pre_bc * bc_gate
    key_in = both[:, :states].astype(BF)
    key_out = both[:, states:].astype(BF)
    raw, step, log_decay, enter, leave = step_parts(step_ref, heads_ref, feats, rows)
    expanded = jnp.dot(
        split_lanes(jnp.concatenate([step, enter, leave], axis=0), 1), expand_ref[...], preferred_element_type=F32
    )
    step_w, enter_w, leave_w = expanded[:rows], expanded[rows : 2 * rows], expanded[2 * rows :]
    scaled = values * step_w
    z = z_ref[...]
    z_gate = sigmoid(z)
    z_silu = z * z_gate
    scan = scan_ref[...]
    gated = scan * z_silu
    norm_grad = norm_grad_ref[...].astype(F32)
    weighted = norm_grad * feats[:, 9:10]
    gated_grad = weighted * gain_ref[...] - gated * feats[:, 10:11]
    dscan = gated_grad * z_silu
    dz_ref[...] = (gated_grad * scan * (z_gate * (1.0 + z * (1.0 - z_gate)))).astype(BF)
    sums_ref[6:7, :] += jnp.sum(weighted * gated, axis=0, keepdims=True)
    sums_ref[5:6, :] += jnp.sum(dscan * values, axis=0, keepdims=True)
    held = states_ref[0]
    dheld = dmemory[...]
    dheld_low = dheld.astype(BF)
    enter_grad = (dscan * enter_w).astype(BF)
    left = leave_w * scaled
    passed = mm(key_in, dheld_low)
    arrived = mm(key_out, held)
    dkey_out = mm_nt(enter_grad, held)
    dkey_in = mm_nt(left, dheld_low)
    carry = enter_w[rows - 1 : rows, :]
    dmemory[...] = dheld * carry + mm_tn(key_out, enter_grad)
    enter_terms = dscan * enter_w * arrived
    leave_terms = left * passed
    carry_terms = jnp.sum(dheld * held.astype(F32), axis=0, keepdims=True) * carry
    gram = mm_nt(key_in, key_out)
    allowed = (docs_col_ref[...] == docs_ref[...]) & (iota2((rows, rows), 0) <= iota2((rows, rows), 1))
    bias = jnp.where(allowed, 0.0, MASKED)
    log_rows = log_decay.T
    front = iota2((rows, LANES), 1) < LANES // 2
    gram_grad = jnp.zeros((rows, rows), F32)
    lane_of = iota2((rows, LANES), 1)
    row_of = iota2((LANES, rows), 0)
    sent = jnp.zeros((rows, LANES), F32)
    received = jnp.zeros((LANES, rows), F32)
    inside_grads = []
    for pair in range(width // LANES):
        lanes = slice(pair * LANES, (pair + 1) * LANES)
        dy = dscan[:, lanes].astype(BF)
        part = scaled[:, lanes]
        stacked = jnp.concatenate([jnp.where(front, part, 0.0), jnp.where(front, 0.0, part)], axis=0)
        cross = mm_nt(stacked, dy)
        mixes = []
        for j, h in enumerate((2 * pair, 2 * pair + 1)):
            decay = jnp.exp(log_rows[h : h + 1, :] - log_decay[:, h : h + 1] + bias)
            mix = gram * decay
            mixes.append(mix.astype(BF))
            dmix = cross[j * rows : (j + 1) * rows, :]
            gram_grad = gram_grad + dmix * decay
            flow = dmix * mix
            sent = jnp.where(lane_of == h, jnp.sum(flow, axis=1, keepdims=True), sent)
            received = jnp.where(row_of == h, jnp.sum(flow, axis=0, keepdims=True), received)
        grads = mm(jnp.concatenate(mixes, axis=0), dy)
        inside_grads.append(jnp.where(front, grads[:rows], grads[rows:]))
    dscaled = jnp.concatenate(inside_grads, axis=1) + leave_w * passed
    dkey_in = dkey_in + mm(gram_grad, key_out)
    dkey_out = dkey_out + mm_tn(gram_grad, key_in)
    reduced = jnp.dot(
        split_lanes(
            jnp.concatenate([enter_terms, leave_terms, dscaled * values, jnp.broadcast_to(carry_terms, (8, width))], axis=0), 1
        ),
        reduce_ref[...],
        preferred_element_type=F32,
    )
    after = reduced[:rows] + received.T - sent
    upper = (iota2((rows, rows), 0) <= iota2((rows, rows), 1)).astype(F32)
    strict = (iota2((rows, rows), 0) > iota2((rows, rows), 1)).astype(F32)
    decay_grad = exact_mm(upper, after) + exact_mm(strict, reduced[rows : 2 * rows]) + reduced[3 * rows : 3 * rows + 1]
    dstep = decay_grad * heads_ref[1:2, :] + reduced[2 * rows : 3 * rows]
    draw = dstep * sigmoid(raw)
    grads_ref[:, width + 2 * states :] = draw.astype(BF)
    hsums_ref[0:1, :] += jnp.sum(draw, axis=0, keepdims=True)
    hsums_ref[1:2, :] += jnp.sum(decay_grad * step, axis=0, keepdims=True) * heads_ref[1:2, :]
    dvalues = dscaled * step_w + dscan * taps_ref[5:6, :]
    dpre = dvalues * (pre_gate * (1.0 + pre * (1.0 - pre_gate)))
    dboth = jnp.concatenate([dkey_in, dkey_out], axis=1)
    dpre_bc = dboth * (bc_gate * (1.0 + pre_bc * (1.0 - bc_gate)))
    for dpre_now, buffer, dbuffer, taps, totals, lanes in (
        (dpre, xbuf, dxbuf, taps_ref, sums_ref, slice(0, width)),
        (dpre_bc, bcbuf, dbcbuf, staps_ref, ssums_ref, slice(width, width + 2 * states)),
    ):
        dbuffer[0:rows, :] = dpre_now
        grad = dpre_now * taps[3:4, :]
        totals[3:4, :] += jnp.sum(dpre_now * buffer[8 : 8 + rows, :], axis=0, keepdims=True)
        totals[4:5, :] += jnp.sum(dpre_now, axis=0, keepdims=True)
        for k in range(1, 4):
            grad = grad + dbuffer[k : k + rows, :] * feats[:, 5 + k : 6 + k] * taps[3 - k : 4 - k, :]
            totals[3 - k : 4 - k, :] += jnp.sum(
                dpre_now * buffer[8 - k : 8 - k + rows, :] * feats[:, k : k + 1], axis=0, keepdims=True
            )
        grads_ref[:, lanes] = grad.astype(BF)
        dbuffer[rows : rows + 8, :] = dbuffer[0:8, :]


def expand_matrix(width):
    head_of = jnp.arange(width, dtype=jnp.int32) // (LANES // 2)
    one = (jnp.arange(LANES, dtype=jnp.int32)[:, None] == head_of[None, :]).astype(BF)
    return jnp.concatenate([one, one], axis=0)


def token_features(docs, chunk):
    total = docs.shape[0]
    doc = docs.astype(F32)
    back = [jnp.concatenate([jnp.zeros((k,), F32), (docs[k:] == docs[:-k]).astype(F32)]) for k in (1, 2, 3)]
    ahead = [jnp.concatenate([(docs[k:] == docs[:-k]).astype(F32), jnp.zeros((k,), F32)]) for k in (1, 2, 3)]
    blocks = docs.reshape(-1, chunk)
    before = jnp.concatenate([jnp.full((1,), -1, jnp.int32), blocks[:-1, -1]])
    entered = (blocks == before[:, None]).astype(F32).reshape(total)
    leaving = (blocks == blocks[:, -1:]).astype(F32).reshape(total)
    return jnp.stack([doc] + back + [entered, leaving] + ahead, axis=1)


def spec(block, index):
    return pl.BlockSpec(block, index)


def mamba_forward(feats, doc_row, ssm_in, z, taps, staps, heads, gain, width, states2):
    total = z.shape[0]
    rows = CHUNK
    count = total // rows
    block = lambda w, place=0: spec((rows, w), lambda i: (i, place))
    whole = lambda a: spec(a.shape, lambda i: (0,) * a.ndim)
    expand = expand_matrix(width)
    return pl.pallas_call(
        mamba_fwd_kernel,
        grid=(count,),
        in_specs=[
            block(feats.shape[1]), spec((1, rows), lambda i: (0, i)), block(width), block(states2, width // states2),
            block(LANES, (width + states2) // LANES), block(width), whole(taps), whole(staps), whole(heads), whole(expand), whole(gain),
        ],
        out_specs=[block(width), block(width), block(1), spec((1, states2 // 2, width), lambda i: (i, 0, 0))],
        out_shape=[
            jax.ShapeDtypeStruct((total, width), F32),
            jax.ShapeDtypeStruct((total, width), BF),
            jax.ShapeDtypeStruct((total, 1), F32),
            jax.ShapeDtypeStruct((count, states2 // 2, width), BF),
        ],
        scratch_shapes=[
            pltpu.VMEM((rows + 8, width), F32), pltpu.VMEM((rows + 8, states2), F32), pltpu.VMEM((states2 // 2, width), F32),
        ],
        compiler_params=pltpu.CompilerParams(vmem_limit_bytes=32 * 2**20),
        cost_estimate=pl.CostEstimate(flops=20 * 10**9, bytes_accessed=total * width * 20, transcendentals=total * width * 4),
        name="mamba_fwd",
    )(feats, doc_row, ssm_in, ssm_in, ssm_in, z, taps, staps, heads, expand, gain)


def mamba_backward(feats, doc_col, doc_row, ssm_in, z, scan, states, norm_grad, taps, staps, heads, gain, width, states2):
    total = z.shape[0]
    rows = CHUNK
    count = total // rows
    back = lambda i: count - 1 - i
    block = lambda w, place=0: spec((rows, w), lambda i: (back(i), place))
    before = lambda w, place=0: spec((8, w), lambda i: (jnp.maximum(back(i) * (rows // 8) - 1, 0), place))
    whole = lambda a: spec(a.shape, lambda i: (0,) * a.ndim)
    expand = expand_matrix(width)
    reduce = expand[:LANES].T
    reduce = jnp.concatenate([reduce, reduce], axis=0)
    totals = lambda w: spec((8, w), lambda i: (0, 0))
    return pl.pallas_call(
        mamba_bwd_kernel,
        grid=(count,),
        in_specs=[
            block(feats.shape[1]), block(1), spec((1, rows), lambda i: (0, back(i))), block(width), before(width),
            block(states2, width // states2), before(states2, width // states2), block(LANES, (width + states2) // LANES),
            block(width), block(width), spec((1, states2 // 2, width), lambda i: (back(i), 0, 0)), block(width),
            whole(taps), whole(staps), whole(heads), whole(expand), whole(reduce), whole(gain),
        ],
        out_specs=[block(width), block(width + states2 + LANES), totals(width), totals(states2), totals(LANES)],
        out_shape=[
            jax.ShapeDtypeStruct((total, width), BF),
            jax.ShapeDtypeStruct((total, width + states2 + LANES), BF),
            jax.ShapeDtypeStruct((8, width), F32),
            jax.ShapeDtypeStruct((8, states2), F32),
            jax.ShapeDtypeStruct((8, LANES), F32),
        ],
        scratch_shapes=[
            pltpu.VMEM((rows + 8, width), F32), pltpu.VMEM((rows + 8, states2), F32),
            pltpu.VMEM((rows + 8, width), F32), pltpu.VMEM((rows + 8, states2), F32), pltpu.VMEM((states2 // 2, width), F32),
        ],
        compiler_params=pltpu.CompilerParams(vmem_limit_bytes=32 * 2**20),
        cost_estimate=pl.CostEstimate(flops=35 * 10**9, bytes_accessed=total * width * 24, transcendentals=total * width * 5),
        name="mamba_bwd",
    )(feats, doc_col, doc_row, ssm_in, ssm_in, ssm_in, ssm_in, ssm_in, z, scan, states, norm_grad, taps, staps, heads, expand, reduce, gain)


QBLOCK = 256


def swap_halves(values):
    lane = iota2(values.shape, 1) % (LANES // 2)
    return jnp.where(lane < LANES // 4, pltpu.roll(values, LANES - LANES // 4, 1), pltpu.roll(values, LANES // 4, 1))


def stack_heads(part):
    front = iota2(part.shape, 1) < LANES // 2
    zero = jnp.zeros_like(part)
    return jnp.concatenate([jnp.where(front, part, zero), jnp.where(front, zero, part)], axis=0)


def attention_fwd_kernel(groups, docs_col_ref, docs_ref, q_ref, kv_ref, cos_ref, sin_ref, out_ref, lse_ref, qrot_ref, keys_ref, values_ref):
    total = q_ref.shape[0]
    pairs = q_ref.shape[1] // LANES
    block = min(QBLOCK, total)
    cos, sin = cos_ref[...], sin_ref[...]
    front = iota2((total, LANES), 1) < LANES // 2
    for g in range(groups):
        lanes = slice(g * LANES, (g + 1) * LANES)
        raw = kv_ref[:, lanes]
        turned = raw * cos + swap_halves(raw) * sin
        keys_ref[:, lanes] = jnp.where(front, turned, pltpu.roll(turned, LANES // 2, 1)).astype(BF)
        values_ref[:, lanes] = jnp.where(front, pltpu.roll(raw, LANES // 2, 1), raw).astype(BF)
    for p in range(pairs):
        lanes = slice(p * LANES, (p + 1) * LANES)
        raw = q_ref[:, lanes]
        qrot_ref[:, lanes] = ((raw * cos + swap_halves(raw) * sin).astype(BF).astype(F32) * (LANES // 2) ** -0.5).astype(BF)
    front = iota2((block, LANES), 1) < LANES // 2
    lane_of = iota2((block, LANES), 1)
    for start in range(0, total, block):
        rows, end = slice(start, start + block), start + block
        allowed = (docs_col_ref[rows, :] == docs_ref[:, :end]) & (
            iota2((block, end), 0) + start >= iota2((block, end), 1)
        )
        bias = jnp.where(allowed, 0.0, MASKED)
        bias = jnp.concatenate([bias, bias], axis=0)
        sums = jnp.zeros((block, LANES), F32)
        for p in range(pairs):
            lanes = slice(p * LANES, (p + 1) * LANES)
            g = p * groups // pairs
            kv = slice(g * LANES, (g + 1) * LANES)
            scores = mm_nt(stack_heads(qrot_ref[rows, lanes]), keys_ref[:end, kv]) + bias
            top = jnp.max(scores, axis=1, keepdims=True)
            raised = jnp.exp(scores - top)
            whole = jnp.sum(raised, axis=1, keepdims=True)
            mixed = mm(raised, values_ref[:end, kv]) / whole
            out_ref[rows, lanes] = jnp.where(front, mixed[:block], mixed[block:]).astype(BF)
            logs = top + jnp.log(whole)
            sums = jnp.where(lane_of == 2 * p, logs[:block], sums)
            sums = jnp.where(lane_of == 2 * p + 1, logs[block:], sums)
        lse_ref[rows, :] = sums


def attention_bwd_kernel(groups, docs_col_ref, docs_ref, qrot_ref, keys_ref, values_ref, lse_ref, up_ref, cos_ref, sin_ref, grads_ref, dk_acc, dv_acc):
    total = qrot_ref.shape[0]
    pairs = qrot_ref.shape[1] // LANES
    block = min(QBLOCK, total)
    dk_acc[...] = jnp.zeros_like(dk_acc)
    dv_acc[...] = jnp.zeros_like(dv_acc)
    front = iota2((block, LANES), 1) < LANES // 2
    for start in range(0, total, block):
        rows, end = slice(start, start + block), start + block
        allowed = (docs_col_ref[:end, :] == docs_ref[:, rows]) & (
            iota2((end, block), 0) <= iota2((end, block), 1) + start
        )
        bias = jnp.where(allowed, 0.0, MASKED)
        logs = lse_ref[rows, :].T
        cos, sin = cos_ref[rows, :], sin_ref[rows, :]
        for p in range(pairs):
            lanes = slice(p * LANES, (p + 1) * LANES)
            g = p * groups // pairs
            kv = slice(g * LANES, (g + 1) * LANES)
            keys, values = keys_ref[:end, kv], values_ref[:end, kv]
            queries = stack_heads(qrot_ref[rows, lanes])
            ups = stack_heads(up_ref[rows, lanes])
            shift = jnp.concatenate([bias - logs[2 * p : 2 * p + 1], bias - logs[2 * p + 1 : 2 * p + 2]], axis=1)
            probs = jnp.exp(mm_nt(keys, queries) + shift)
            grads = mm_nt(values, ups)
            centre = jnp.sum(probs * grads, axis=0, keepdims=True)
            score_grads = (probs * (grads - centre)).astype(BF)
            dk_acc[:end, kv] += mm(score_grads, queries)
            dv_acc[:end, kv] += mm(probs, ups)
            dq = mm_tn(score_grads, keys)
            dq = jnp.where(front, dq[:block], dq[block:]) * (LANES // 2) ** -0.5
            grads_ref[rows, lanes] = (dq * cos - swap_halves(dq) * sin).astype(BF)
    front = iota2((total, LANES), 1) < LANES // 2
    for g in range(groups):
        kv = slice(g * LANES, (g + 1) * LANES)
        dk, dv = dk_acc[:, kv], dv_acc[:, kv]
        dk = dk + pltpu.roll(dk, LANES // 2, 1)
        dk = dk * cos_ref[...] - swap_halves(dk) * sin_ref[...]
        dv = dv + pltpu.roll(dv, LANES // 2, 1)
        out = slice((pairs + g) * LANES, (pairs + g + 1) * LANES)
        grads_ref[:, out] = jnp.where(front, dk, dv).astype(BF)


def attention_forward(groups, doc_col, doc_row, qkv, cos, sin, query_width):
    total = qkv.shape[0]
    kv_width = qkv.shape[1] - query_width
    whole = lambda a: spec(a.shape, lambda i: (0,) * a.ndim)
    columns = lambda w, place=0: spec((total, w), lambda i: (0, place))
    return pl.pallas_call(
        functools.partial(attention_fwd_kernel, groups),
        grid=(1,),
        in_specs=[whole(doc_col), whole(doc_row), columns(query_width), columns(kv_width, query_width // kv_width), whole(cos), whole(sin)],
        out_specs=[columns(query_width), columns(LANES), columns(query_width), columns(kv_width), columns(kv_width)],
        out_shape=[
            jax.ShapeDtypeStruct((total, query_width), BF), jax.ShapeDtypeStruct((total, LANES), F32),
            jax.ShapeDtypeStruct((total, query_width), BF), jax.ShapeDtypeStruct((total, kv_width), BF),
            jax.ShapeDtypeStruct((total, kv_width), BF),
        ],
        compiler_params=pltpu.CompilerParams(vmem_limit_bytes=32 * 2**20),
        cost_estimate=pl.CostEstimate(flops=12 * 10**9, bytes_accessed=total * query_width * 10, transcendentals=total * total * 2),
        name="attention_fwd",
    )(doc_col, doc_row, qkv, qkv, cos, sin)


def attention_backward(groups, doc_col, doc_row, qrot, keys, values, lse, up, cos, sin):
    total = qrot.shape[0]
    return pl.pallas_call(
        functools.partial(attention_bwd_kernel, groups),
        out_shape=jax.ShapeDtypeStruct((total, qrot.shape[1] + keys.shape[1]), BF),
        scratch_shapes=[pltpu.VMEM(keys.shape, F32), pltpu.VMEM(keys.shape, F32)],
        compiler_params=pltpu.CompilerParams(vmem_limit_bytes=32 * 2**20),
        cost_estimate=pl.CostEstimate(flops=16 * 10**9, bytes_accessed=total * qrot.shape[1] * 10, transcendentals=total * total * 2),
        name="attention_bwd",
    )(doc_col, doc_row, qrot, keys, values, lse, up, cos, sin)


def swap(values, mask):
    count = lax.axis_size("fsdp")
    return lax.ppermute(values, "fsdp", [(i, i ^ mask) for i in range(count)])


def high_bits():
    count = lax.axis_size("fsdp")
    bits = []
    while 4 << len(bits) < count:
        bits.append(4 << len(bits))
    return bits


def block_masks(count):
    quarter = count // 4
    places = jnp.arange(count, dtype=jnp.int32)
    return places // quarter + 4 * (places % quarter)


def gather_rows(shard, order):
    block = shard
    for bit in high_bits():
        block = jnp.concatenate([block, swap(block, bit)], axis=0)
    size = block.shape[0]
    near = swap(block, 2 if order else 1)
    far = swap(jnp.concatenate([block, near], axis=0), 1 if order else 2)
    if order:
        return jnp.concatenate([block, far[:size], near, far[size:]], axis=0)
    return jnp.concatenate([block, near, far], axis=0)


def scatter_rows(grads, order):
    size = grads.shape[0] // 4
    if order:
        sent = jnp.concatenate([grads[size : 2 * size], grads[3 * size :]], axis=0)
        kept = jnp.concatenate([grads[:size], grads[2 * size : 3 * size]], axis=0)
    else:
        sent, kept = grads[2 * size :], grads[: 2 * size]
    total = kept.astype(F32) + swap(sent, 1 if order else 2).astype(F32)
    total = total[:size] + swap(total[size:].astype(BF), 2 if order else 1).astype(F32)
    for bit in reversed(high_bits()):
        half = total.shape[0] // 2
        total = total[:half] + swap(total[half:].astype(BF), bit).astype(F32)
    return total


def sum_everywhere(values, names):
    if "fsdp" in names:
        for bit in [1, 2] + high_bits():
            values = values + swap(values, bit)
    if "tensor" in names:
        values = tensor_sum(values)
    return values


def tensor_swap(values):
    return lax.ppermute(values, "tensor", [(0, 1), (1, 0)])


def tensor_sum(values):
    if lax.axis_size("tensor") == 2:
        return values + tensor_swap(values)
    return lax.psum(values, "tensor")


def tensor_sum_low(values):
    if lax.axis_size("tensor") == 2:
        return values + tensor_swap(values.astype(BF)).astype(F32)
    return lax.psum(values, "tensor")


def tensor_gather(values):
    if lax.axis_size("tensor") == 2:
        other = tensor_swap(values)
        first = lax.axis_index("tensor") == 0
        return jnp.concatenate([jnp.where(first, values, other), jnp.where(first, other, values)], axis=0)
    return lax.all_gather(values, "tensor", axis=0, tiled=True)


def tensor_scatter(values):
    if lax.axis_size("tensor") == 2:
        half = values.shape[0] // 2
        first = lax.axis_index("tensor") == 0
        mine = jnp.where(first, values[:half], values[half:])
        other = jnp.where(first, values[half:], values[:half])
        return mine.astype(F32) + tensor_swap(other.astype(BF)).astype(F32)
    return lax.psum_scatter(values.astype(BF), "tensor", scatter_dimension=0, tiled=True).astype(F32)


def pad_to(values, size, axis=-1):
    pads = [(0, 0)] * values.ndim
    pads[axis] = (0, size - values.shape[axis])
    return jnp.pad(values, pads) if size > values.shape[axis] else values


def norm_scale(values):
    return lax.rsqrt(jnp.mean(values * values, axis=-1, keepdims=True) + EPS)


def rotation_tables(place):
    half = HEAD_SIZE // 2
    rates = jnp.exp(jnp.arange(half, dtype=F32) * (-2.0 * math.log(THETA) / HEAD_SIZE))
    angles = place[:, None] * rates[None, :]
    cos, sin = jnp.cos(angles), jnp.sin(angles)
    return jnp.concatenate([cos] * 4, axis=1), jnp.concatenate([-sin, sin, -sin, sin], axis=1)


def body(
    layer_input, doc_ids, input_gain, mixer_weight, state_weight, step_weight, conv_weight, conv_bias, state_conv,
    state_conv_bias, step_bias, decay_log, skip_gain, mixer_gain, mixer_proj, query_weight, keyval_projection,
    attention_proj, second_gain, gate_up, down_proj, cotangent,
):
    tensor_count = lax.axis_size("tensor")
    tensor_index = lax.axis_index("tensor")
    fsdp_count = lax.axis_size("fsdp")
    fsdp_index = lax.axis_index("fsdp")
    own_rows, hidden = layer_input.shape
    unit = state_weight.shape[0]
    seq_count, seq_length = doc_ids.shape
    total = seq_count * seq_length
    heads = step_bias.shape[0]
    width = conv_weight.shape[1]
    wide = -(-width // LANES) * LANES
    query_width = query_weight.shape[1]
    query_wide = -(-query_width // LANES) * LANES
    per_group = QUERY_HEADS // KEYVAL_HEADS
    query_heads = query_width // HEAD_SIZE
    kv_heads = max(1, query_heads // per_group)
    kv_leading = tensor_index * query_heads // per_group
    states2 = state_weight.shape[1]
    ffn = down_proj.shape[0]

    own_keyval = lax.dynamic_slice_in_dim(keyval_projection, kv_leading * HEAD_SIZE, kv_heads * HEAD_SIZE, 2)
    own_keyval = own_keyval.reshape(unit, 2, kv_heads, HEAD_SIZE).transpose(0, 2, 1, 3).reshape(unit, 2 * kv_heads * HEAD_SIZE)
    kv_wide = 2 * kv_heads * HEAD_SIZE
    low = lambda v: v.astype(BF)
    pack = lambda parts: jnp.concatenate([low(v) for v in parts], axis=1)
    ssm_wide, qkv_wide = wide + states2 + LANES, query_wide + kv_wide
    first = gather_rows(
        pack([
            pad_to(mixer_weight[:, 1, :], wide), state_weight, pad_to(step_weight, LANES),
            pad_to(query_weight, query_wide), own_keyval,
        ]),
        0,
    )
    full_ssm, full_qkv = first[:, :ssm_wide], first[:, ssm_wide:]
    after = gather_rows(
        pack([pad_to(mixer_weight[:, 0, :], wide), pad_to(mixer_proj.T, wide), pad_to(attention_proj.T, query_wide)]), 1
    )
    full_z, full_proj, full_attention = after[:, :wide], after[:, wide : 2 * wide], after[:, 2 * wide :]
    full_gate_up = gather_rows(low(gate_up).reshape(unit, 2 * ffn), 0)
    full_down = gather_rows(low(down_proj).T, 1)

    masks = block_masks(fsdp_count)
    features = jnp.arange(hidden, dtype=jnp.int32)
    source = (masks[features // unit] ^ fsdp_index) * unit + features % unit
    turn = (features[:, None] == source[None, :]).astype(BF)
    turn_back = (source[:, None] == features[None, :]).astype(BF)
    tokens = tensor_gather(low(plain_dot(layer_input, turn))).astype(F32)
    upstream = tensor_gather(low(plain_dot(cotangent, turn)))
    gains = jnp.dot(
        jnp.stack([input_gain, second_gain]), turn.astype(F32), precision=lax.Precision.HIGHEST, preferred_element_type=F32
    )
    first_gain, second_gain_turned = gains[0:1], gains[1:2]

    docs = (doc_ids + jnp.arange(seq_count, dtype=jnp.int32)[:, None] * seq_length).reshape(total)
    place = (jnp.arange(total, dtype=jnp.int32) - jnp.sum((docs[None, :] < docs[:, None]).astype(jnp.int32), axis=1)).astype(F32)
    cos, sin = rotation_tables(place)
    feats = token_features(docs, CHUNK)
    doc_col, doc_row = docs.astype(F32)[:, None], docs.astype(F32)[None, :]
    taps = jnp.concatenate(
        [conv_weight, conv_bias[None], jnp.repeat(skip_gain, width // heads)[None], jnp.zeros((2, width), F32)], axis=0
    )
    taps = pad_to(taps, wide)
    state_taps = jnp.concatenate([state_conv, state_conv_bias[None], jnp.zeros((3, states2), F32)], axis=0)
    head_rows = pad_to(pad_to(jnp.stack([step_bias, -jnp.exp(decay_log)]), 8, 0), LANES)
    gain_row = pad_to(mixer_gain[None], wide)

    first_scale = norm_scale(tokens)
    normed = low(tokens * first_scale * first_gain)
    ssm_in = plain_dot(normed, full_ssm)
    qkv_in = plain_dot(normed, full_qkv)
    gate_z = plain_dot(normed, full_z)
    scan, gated_low, squares, states = mamba_forward(feats, doc_row, ssm_in, gate_z, taps, state_taps, head_rows, gain_row, wide, states2)
    attended, log_sums, query_rot, keys, values = attention_forward(kv_heads, doc_col, doc_row, qkv_in, cos, sin, query_wide)
    squares = tensor_sum(squares.reshape(-1, LANES)).reshape(total, 1)
    gated_scale = lax.rsqrt(squares / DSSM + EPS)
    branch = gated_scale * right_dot(gated_low, full_proj) + right_dot(attended, full_attention)
    middle = tokens + tensor_sum_low(branch)
    second_scale = norm_scale(middle)
    second = low(middle * second_scale * second_gain_turned)
    gate_vals = plain_dot(second, full_gate_up)
    gate_part, up_part = gate_vals[:, :ffn], gate_vals[:, ffn:]
    gate_sigmoid = jax.nn.sigmoid(gate_part)
    active = low(gate_part * gate_sigmoid * up_part)
    ffn_out = tensor_scatter(low(right_dot(active, full_down)))
    own = lambda v: lax.dynamic_slice_in_dim(v, tensor_index * own_rows, own_rows, 0)
    layer_output = low(plain_dot(low(own(middle) + ffn_out), turn_back))

    grad_down = low(left_dot(upstream, active))
    active_grad = plain_dot(upstream, full_down)
    gate_grad = active_grad * up_part * gate_sigmoid * (1.0 + gate_part * (1.0 - gate_sigmoid))
    up_grad = active_grad * gate_part * gate_sigmoid
    gu_grad = jnp.concatenate([low(gate_grad), low(up_grad)], axis=-1)
    grad_gate_up = low(left_dot(second, gu_grad))
    second_grad = tensor_sum_low(right_dot(gu_grad, full_gate_up))
    weighted = second_grad * second_gain_turned
    inner = jnp.mean(weighted * middle, axis=-1, keepdims=True)
    middle_grad = upstream.astype(F32) + second_scale * weighted - middle * second_scale**3 * inner
    second_gain_part = jnp.sum(second_grad * middle * second_scale, axis=0) * (1.0 / tensor_count)
    branch_low = low(middle_grad)

    norm_grad = low(plain_dot(branch_low, full_proj))
    attended_grad = low(plain_dot(branch_low, full_attention))
    inner_sums = tensor_sum(jnp.sum(norm_grad.astype(F32) * gated_low.astype(F32), axis=-1).reshape(-1, LANES)).reshape(total, 1)
    back_feats = jnp.concatenate([feats, gated_scale, gated_scale**3 * (inner_sums / DSSM)], axis=1)
    grad_proj = low(left_dot(low(gated_scale * branch_low), gated_low))
    grad_attention = low(left_dot(branch_low, attended))
    gate_z_grad, ssm_grad, sums, state_sums, head_sums = mamba_backward(
        back_feats, doc_col, doc_row, ssm_in, gate_z, scan, states, norm_grad, taps, state_taps, head_rows, gain_row, wide, states2
    )
    qkv_grad = attention_backward(kv_heads, doc_col, doc_row, query_rot, keys, values, log_sums, attended_grad, cos, sin)
    grad_z = low(left_dot(normed, gate_z_grad))
    grad_ssm = low(left_dot(normed, ssm_grad))
    grad_qkv = low(left_dot(normed, qkv_grad))
    normed_part = right_dot(gate_z_grad, full_z) + right_dot(ssm_grad, full_ssm) + right_dot(qkv_grad, full_qkv)
    input_gain_part = jnp.sum(normed_part * tokens * first_scale, axis=0)
    normed_grad = tensor_scatter(low(normed_part))
    own_tokens, own_scale = own(tokens), own(first_scale)
    weighted = normed_grad * first_gain
    inner = jnp.mean(weighted * own_tokens, axis=-1, keepdims=True)
    input_grad = own(middle_grad) + own_scale * weighted - own_tokens * own_scale**3 * inner
    turned = plain_dot(split_lanes(input_grad, 0), turn_back)
    input_grad = turned[:own_rows] + turned[own_rows:]

    sum_gate_up = scatter_rows(grad_gate_up, 0).reshape(unit, 2, ffn)
    sum_down = scatter_rows(grad_down, 1).T
    sum_out = scatter_rows(jnp.concatenate([grad_proj, grad_attention], axis=1), 0)
    sum_z = scatter_rows(grad_z, 1)[:, :width]
    sum_ssm = scatter_rows(grad_ssm, 0)
    sum_qkv = scatter_rows(grad_qkv, 1)
    keyval_sum = sum_qkv[:, query_wide:].reshape(unit, kv_heads, 2, HEAD_SIZE).transpose(0, 2, 1, 3).reshape(unit, 2, kv_heads * HEAD_SIZE)
    keyval_sum = lax.dynamic_update_slice_in_dim(
        jnp.zeros((unit, 2, KEYVAL_HEADS * HEAD_SIZE), F32), keyval_sum, kv_leading * HEAD_SIZE, 2
    ).reshape(unit, 2 * KEYVAL_HEADS * HEAD_SIZE)
    shared = tensor_sum(jnp.concatenate([sum_ssm[:, wide : wide + states2], keyval_sum], axis=1))

    def turn_row(row):
        blocks = (jnp.arange(fsdp_count, dtype=jnp.int32)[:, None] == (masks ^ fsdp_index)[None, :]).astype(F32)
        return exact_mm(blocks, row.reshape(fsdp_count, unit)).reshape(1, hidden)

    split_sums = sum_everywhere(jnp.concatenate([sums, head_sums], axis=1), ("fsdp",))
    sums, head_sums = split_sums[:, :wide], split_sums[:, wide:]
    state_sums = sum_everywhere(
        jnp.concatenate([state_sums, pad_to(turn_row(second_gain_part).reshape(-1, states2), 8, 0)], axis=0), ("fsdp", "tensor")
    )
    second_gain_sum = state_sums[8 : 8 + hidden // states2].reshape(hidden)
    input_gain_sum = sum_everywhere(turn_row(input_gain_part).reshape(-1, LANES), ("fsdp", "tensor")).reshape(hidden)
    return (
        layer_output,
        input_grad,
        input_gain_sum,
        jnp.stack([sum_z, sum_ssm[:, :width]], axis=1),
        shared[:, :states2],
        sum_ssm[:, wide + states2 : wide + states2 + heads],
        sums[0:4, :width],
        sums[4, :width],
        state_sums[0:4],
        state_sums[4],
        head_sums[0, :heads],
        head_sums[1, :heads],
        jnp.sum(sums[5, :width].reshape(heads, -1), axis=1),
        sums[6, :width],
        sum_out[:, :width].T,
        sum_qkv[:, :query_width],
        shared[:, states2:].reshape(unit, 2, KEYVAL_HEADS * HEAD_SIZE),
        sum_out[:, wide : wide + query_width].T,
        second_gain_sum,
        sum_gate_up,
        sum_down,
    )


def solution(mesh):
    placed = (
        P(("fsdp", "tensor"), None),
        P("fsdp", None),
        P(),
        P("fsdp", None, "tensor"),
        P("fsdp", None),
        P("fsdp", "tensor"),
        P(None, "tensor"),
        P("tensor"),
        P(),
        P(),
        P("tensor"),
        P("tensor"),
        P("tensor"),
        P("tensor"),
        P("tensor", "fsdp"),
        P("fsdp", "tensor"),
        P("fsdp", None, None),
        P("tensor", "fsdp"),
        P(),
        P("fsdp", None, "tensor"),
        P("tensor", "fsdp"),
        P(("fsdp", "tensor"), None),
    )
    return jax.shard_map(
        body,
        mesh=mesh,
        in_specs=placed,
        out_specs=(
            P(("fsdp", "tensor"), None),
            P(("fsdp", "tensor"), None),
            P(),
            P("fsdp", None, "tensor"),
            P("fsdp", None),
            P("fsdp", "tensor"),
            P(None, "tensor"),
            P("tensor"),
            P(),
            P(),
            P("tensor"),
            P("tensor"),
            P("tensor"),
            P("tensor"),
            P("tensor", "fsdp"),
            P("fsdp", "tensor"),
            P("fsdp", None, None),
            P("tensor", "fsdp"),
            P(),
            P("fsdp", None, "tensor"),
            P("tensor", "fsdp"),
        ),
        check_vma=False,
    )
```

```python
import functools
import math

import jax
import jax.numpy as jnp
import ml_dtypes
import numpy as np
from jax import lax
from jax.experimental import pallas as pl
from jax.experimental.pallas import tpu as pltpu
from jax.sharding import PartitionSpec as P

QUERY_HEADS = 8
KEYVAL_HEADS = 2
HEAD_SIZE = 64
DSSM = 1536
EPS = 1e-05
THETA = 100000000000.0

LANES = 128
CHUNK = 128
MASKED = -1e30
BF, F32 = jnp.bfloat16, jnp.float32


def left_dot(left_side, right_side):
    return lax.dot_general(left_side, right_side, (((0,), (0,)), ((), ())), preferred_element_type=F32)


def right_dot(left_side, right_side):
    return lax.dot_general(left_side, right_side, (((1,), (1,)), ((), ())), preferred_element_type=F32)


def plain_dot(left_side, right_side):
    return jnp.dot(left_side, right_side, preferred_element_type=F32)


def mm(a, b):
    return jnp.dot(a.astype(BF), b.astype(BF), preferred_element_type=F32)


def mm_nt(a, b):
    return lax.dot_general(a.astype(BF), b.astype(BF), (((1,), (1,)), ((), ())), preferred_element_type=F32)


def mm_tn(a, b):
    return lax.dot_general(a.astype(BF), b.astype(BF), (((0,), (0,)), ((), ())), preferred_element_type=F32)


def exact_mm(a, b):
    return jnp.dot(a, b, precision=lax.Precision.HIGHEST, preferred_element_type=F32)


def sigmoid(v):
    return 1.0 / (1.0 + jnp.exp(-v))


def softplus(v):
    return jnp.maximum(v, 0.0) + jnp.log1p(jnp.exp(-jnp.abs(v)))


def split_lanes(values, axis):
    high = values.astype(BF)
    low = (values - high.astype(F32)).astype(BF)
    return jnp.concatenate([high, low], axis=axis)


def iota2(shape, axis):
    return lax.broadcasted_iota(jnp.int32, shape, axis)


def conv_taps(buffer, feats, taps, bias, rows):
    total = buffer[8 : 8 + rows, :] * taps[3:4, :] + bias
    for k in range(1, 4):
        total = total + buffer[8 - k : 8 - k + rows, :] * feats[:, k : k + 1] * taps[3 - k : 4 - k, :]
    return total


def step_parts(step_ref, heads_ref, feats, rows):
    raw = step_ref[...] + heads_ref[0:1, :]
    step = softplus(raw)
    lower = (iota2((rows, rows), 0) >= iota2((rows, rows), 1)).astype(F32)
    log_decay = exact_mm(lower, step * heads_ref[1:2, :])
    last = log_decay[rows - 1 : rows, :]
    enter = jnp.exp(log_decay) * feats[:, 4:5]
    leave = jnp.exp(last - log_decay) * feats[:, 5:6]
    return raw, step, log_decay, enter, leave


def mamba_fwd_kernel(
    feats_ref, docs_ref, x_ref, bc_ref, step_ref, z_ref, taps_ref, staps_ref, heads_ref, expand_ref,
    gain_ref, scan_ref, low_ref, square_ref, states_ref, xbuf, bcbuf, memory,
):
    rows, width = x_ref.shape
    states = bc_ref.shape[1] // 2

    @pl.when(pl.program_id(0) == 0)
    def _():
        xbuf[0:8, :] = jnp.zeros((8, width), F32)
        bcbuf[0:8, :] = jnp.zeros((8, 2 * states), F32)
        memory[...] = jnp.zeros_like(memory)

    feats = feats_ref[...]
    xbuf[8 : 8 + rows, :] = x_ref[...]
    bcbuf[8 : 8 + rows, :] = bc_ref[...]
    pre = conv_taps(xbuf, feats, taps_ref, taps_ref[4:5, :], rows)
    values = pre * sigmoid(pre)
    pre_bc = conv_taps(bcbuf, feats, staps_ref, staps_ref[4:5, :], rows)
    both = pre_bc * sigmoid(pre_bc)
    xbuf[0:8, :] = xbuf[rows : rows + 8, :]
    bcbuf[0:8, :] = bcbuf[rows : rows + 8, :]
    key_in = both[:, :states].astype(BF)
    key_out = both[:, states:].astype(BF)
    _, step, log_decay, enter, leave = step_parts(step_ref, heads_ref, feats, rows)
    expanded = jnp.dot(
        split_lanes(jnp.concatenate([step, enter, leave], axis=0), 1), expand_ref[...], preferred_element_type=F32
    )
    step_w, enter_w, leave_w = expanded[:rows], expanded[rows : 2 * rows], expanded[2 * rows :]
    scaled = values * step_w
    gram = mm_nt(key_out, key_in)
    allowed = (feats[:, 0:1] == docs_ref[...]) & (iota2((rows, rows), 0) >= iota2((rows, rows), 1))
    bias = jnp.where(allowed, 0.0, MASKED)
    log_rows = log_decay.T
    front = iota2((rows, LANES), 1) < LANES // 2
    held = memory[...]
    states_ref[0] = held.astype(BF)
    carried = mm(key_out, held) * enter_w
    fresh = mm_tn(key_in, leave_w * scaled)
    memory[...] = held * enter_w[rows - 1 : rows, :] + fresh
    squares = jnp.zeros((rows, 1), F32)
    for pair in range(width // LANES):
        lanes = slice(pair * LANES, (pair + 1) * LANES)
        mixes = []
        for h in (2 * pair, 2 * pair + 1):
            decay = jnp.exp(log_decay[:, h : h + 1] - log_rows[h : h + 1, :] + bias)
            mixes.append((gram * decay).astype(BF))
        part = scaled[:, lanes]
        stacked = jnp.concatenate([jnp.where(front, part, 0.0), jnp.where(front, 0.0, part)], axis=0)
        inside = mm(jnp.concatenate(mixes, axis=1), stacked)
        scan = inside + carried[:, lanes] + values[:, lanes] * taps_ref[5:6, lanes]
        scan_ref[:, lanes] = scan
        z = z_ref[:, lanes]
        gated = scan * (z * sigmoid(z))
        low_ref[:, lanes] = (gated * gain_ref[:, lanes]).astype(BF)
        squares = squares + jnp.sum(gated * gated, axis=1, keepdims=True)
    square_ref[...] = squares


def mamba_bwd_kernel(
    feats_ref, scale_ref, coefficient_ref, docs_ref, x_ref, x_before_ref, bc_ref, bc_before_ref, step_ref, z_ref, scan_ref, states_ref, norm_grad_ref,
    taps_ref, staps_ref, heads_ref, expand_ref, reduce_ref, gain_ref,
    grads_ref, sums_ref, ssums_ref, hsums_ref,
    xbuf, bcbuf, dxbuf, dbcbuf, dmemory,
):
    rows, width = x_ref.shape
    states = bc_ref.shape[1] // 2

    @pl.when(pl.program_id(0) == 0)
    def _():
        dxbuf[rows : rows + 8, :] = jnp.zeros((8, width), F32)
        dbcbuf[rows : rows + 8, :] = jnp.zeros((8, 2 * states), F32)
        dmemory[...] = jnp.zeros_like(dmemory)
        sums_ref[...] = jnp.zeros_like(sums_ref)
        ssums_ref[...] = jnp.zeros_like(ssums_ref)
        hsums_ref[...] = jnp.zeros_like(hsums_ref)

    feats = feats_ref[...]
    xbuf[0:8, :] = x_before_ref[...]
    bcbuf[0:8, :] = bc_before_ref[...]
    xbuf[8 : 8 + rows, :] = x_ref[...]
    bcbuf[8 : 8 + rows, :] = bc_ref[...]
    pre = conv_taps(xbuf, feats, taps_ref, taps_ref[4:5, :], rows)
    pre_gate = sigmoid(pre)
    values = pre * pre_gate
    pre_bc = conv_taps(bcbuf, feats, staps_ref, staps_ref[4:5, :], rows)
    bc_gate = sigmoid(pre_bc)
    both = pre_bc * bc_gate
    key_in = both[:, :states].astype(BF)
    key_out = both[:, states:].astype(BF)
    raw, step, log_decay, enter, leave = step_parts(step_ref, heads_ref, feats, rows)
    expanded = jnp.dot(
        split_lanes(jnp.concatenate([step, enter, leave], axis=0), 1), expand_ref[...], preferred_element_type=F32
    )
    step_w, enter_w, leave_w = expanded[:rows], expanded[rows : 2 * rows], expanded[2 * rows :]
    scaled = values * step_w
    z = z_ref[...]
    z_gate = sigmoid(z)
    z_silu = z * z_gate
    scan = scan_ref[...]
    gated = scan * z_silu
    norm_grad = norm_grad_ref[...].astype(F32)
    weighted = norm_grad * scale_ref[...]
    gated_grad = weighted * gain_ref[...] - gated * coefficient_ref[...]
    dscan = gated_grad * z_silu
    grads_ref[:, 0:width] = (gated_grad * scan * (z_gate * (1.0 + z * (1.0 - z_gate)))).astype(BF)
    sums_ref[6:7, :] += jnp.sum(weighted * gated, axis=0, keepdims=True)
    sums_ref[5:6, :] += jnp.sum(dscan * values, axis=0, keepdims=True)
    held = states_ref[0]
    dheld = dmemory[...]
    dheld_low = dheld.astype(BF)
    enter_grad = (dscan * enter_w).astype(BF)
    left = leave_w * scaled
    passed = mm(key_in, dheld_low)
    arrived = mm(key_out, held)
    dkey_out = mm_nt(enter_grad, held)
    dkey_in = mm_nt(left, dheld_low)
    carry = enter_w[rows - 1 : rows, :]
    dmemory[...] = dheld * carry + mm_tn(key_out, enter_grad)
    enter_terms = dscan * enter_w * arrived
    leave_terms = left * passed
    carry_terms = jnp.sum(dheld * held.astype(F32), axis=0, keepdims=True) * carry
    gram = mm_nt(key_in, key_out)
    allowed = (feats[:, 0:1] == docs_ref[...]) & (iota2((rows, rows), 0) <= iota2((rows, rows), 1))
    bias = jnp.where(allowed, 0.0, MASKED)
    log_rows = log_decay.T
    front = iota2((rows, LANES), 1) < LANES // 2
    gram_grad = jnp.zeros((rows, rows), F32)
    lane_of = iota2((rows, LANES), 1)
    row_of = iota2((LANES, rows), 0)
    sent = jnp.zeros((rows, LANES), F32)
    received = jnp.zeros((LANES, rows), F32)
    inside_grads = []
    for pair in range(width // LANES):
        lanes = slice(pair * LANES, (pair + 1) * LANES)
        dy = dscan[:, lanes].astype(BF)
        part = scaled[:, lanes]
        stacked = jnp.concatenate([jnp.where(front, part, 0.0), jnp.where(front, 0.0, part)], axis=0)
        cross = mm_nt(stacked, dy)
        mixes = []
        for j, h in enumerate((2 * pair, 2 * pair + 1)):
            decay = jnp.exp(log_rows[h : h + 1, :] - log_decay[:, h : h + 1] + bias)
            mix = gram * decay
            mixes.append(mix.astype(BF))
            dmix = cross[j * rows : (j + 1) * rows, :]
            gram_grad = gram_grad + dmix * decay
            flow = dmix * mix
            sent = jnp.where(lane_of == h, jnp.sum(flow, axis=1, keepdims=True), sent)
            received = jnp.where(row_of == h, jnp.sum(flow, axis=0, keepdims=True), received)
        grads = mm(jnp.concatenate(mixes, axis=0), dy)
        inside_grads.append(jnp.where(front, grads[:rows], grads[rows:]))
    dscaled = jnp.concatenate(inside_grads, axis=1) + leave_w * passed
    dkey_in = dkey_in + mm(gram_grad, key_out)
    dkey_out = dkey_out + mm_tn(gram_grad, key_in)
    reduced = jnp.dot(
        split_lanes(
            jnp.concatenate([enter_terms, leave_terms, dscaled * values, jnp.broadcast_to(carry_terms, (8, width))], axis=0), 1
        ),
        reduce_ref[...],
        preferred_element_type=F32,
    )
    after = reduced[:rows] + received.T - sent
    upper = (iota2((rows, rows), 0) <= iota2((rows, rows), 1)).astype(F32)
    strict = (iota2((rows, rows), 0) > iota2((rows, rows), 1)).astype(F32)
    decay_grad = exact_mm(upper, after) + exact_mm(strict, reduced[rows : 2 * rows]) + reduced[3 * rows : 3 * rows + 1]
    dstep = decay_grad * heads_ref[1:2, :] + reduced[2 * rows : 3 * rows]
    draw = dstep * sigmoid(raw)
    grads_ref[:, 2 * width + 2 * states :] = draw.astype(BF)
    hsums_ref[0:1, :] += jnp.sum(draw, axis=0, keepdims=True)
    hsums_ref[1:2, :] += jnp.sum(decay_grad * step, axis=0, keepdims=True) * heads_ref[1:2, :]
    dvalues = dscaled * step_w + dscan * taps_ref[5:6, :]
    dpre = dvalues * (pre_gate * (1.0 + pre * (1.0 - pre_gate)))
    dboth = jnp.concatenate([dkey_in, dkey_out], axis=1)
    dpre_bc = dboth * (bc_gate * (1.0 + pre_bc * (1.0 - bc_gate)))
    for dpre_now, buffer, dbuffer, taps, totals, lanes in (
        (dpre, xbuf, dxbuf, taps_ref, sums_ref, slice(width, 2 * width)),
        (dpre_bc, bcbuf, dbcbuf, staps_ref, ssums_ref, slice(2 * width, 2 * width + 2 * states)),
    ):
        dbuffer[0:rows, :] = dpre_now
        grad = dpre_now * taps[3:4, :]
        totals[3:4, :] += jnp.sum(dpre_now * buffer[8 : 8 + rows, :], axis=0, keepdims=True)
        totals[4:5, :] += jnp.sum(dpre_now, axis=0, keepdims=True)
        for k in range(1, 4):
            grad = grad + dbuffer[k : k + rows, :] * feats[:, 5 + k : 6 + k] * taps[3 - k : 4 - k, :]
            totals[3 - k : 4 - k, :] += jnp.sum(
                dpre_now * buffer[8 - k : 8 - k + rows, :] * feats[:, k : k + 1], axis=0, keepdims=True
            )
        grads_ref[:, lanes] = grad.astype(BF)
        dbuffer[rows : rows + 8, :] = dbuffer[0:8, :]


def expand_matrix(width):
    one = np.arange(LANES)[:, None] == np.arange(width)[None, :] // (LANES // 2)
    return np.concatenate([one, one], axis=0).astype(ml_dtypes.bfloat16)


def spec(block, index):
    return pl.BlockSpec(block, index)


def mamba_forward(feats, doc_row, ssm_in, taps, staps, heads, gain, width, states2):
    total = ssm_in.shape[0]
    rows = CHUNK
    count = total // rows
    block = lambda w, place=0: spec((rows, w), lambda i: (i, place))
    whole = lambda a: spec(a.shape, lambda i: (0,) * a.ndim)
    expand = expand_matrix(width)
    return pl.pallas_call(
        mamba_fwd_kernel,
        grid=(count,),
        in_specs=[
            block(LANES), spec((1, rows), lambda i: (0, i)), block(width, 1), block(states2, 2 * width // states2),
            block(LANES, (2 * width + states2) // LANES), block(width), whole(taps), whole(staps), whole(heads), whole(expand), whole(gain),
        ],
        out_specs=[block(width), block(width), block(1), spec((1, states2 // 2, width), lambda i: (i, 0, 0))],
        out_shape=[
            jax.ShapeDtypeStruct((total, width), F32),
            jax.ShapeDtypeStruct((total, width), BF),
            jax.ShapeDtypeStruct((total, 1), F32),
            jax.ShapeDtypeStruct((count, states2 // 2, width), BF),
        ],
        scratch_shapes=[
            pltpu.VMEM((rows + 8, width), F32), pltpu.VMEM((rows + 8, states2), F32), pltpu.VMEM((states2 // 2, width), F32),
        ],
        compiler_params=pltpu.CompilerParams(vmem_limit_bytes=32 * 2**20),
        cost_estimate=pl.CostEstimate(flops=20 * 10**9, bytes_accessed=total * width * 20, transcendentals=total * width * 4),
        name="mamba_fwd",
    )(feats, doc_row, ssm_in, ssm_in, ssm_in, ssm_in, taps, staps, heads, expand, gain)


def mamba_backward(feats, doc_row, scale, coefficient, ssm_in, scan, states, norm_grad, taps, staps, heads, gain, width, states2):
    total = ssm_in.shape[0]
    rows = CHUNK
    count = total // rows
    back = lambda i: count - 1 - i
    block = lambda w, place=0: spec((rows, w), lambda i: (back(i), place))
    before = lambda w, place=0: spec((8, w), lambda i: (jnp.maximum(back(i) * (rows // 8) - 1, 0), place))
    whole = lambda a: spec(a.shape, lambda i: (0,) * a.ndim)
    expand = expand_matrix(width)
    reduce = np.concatenate([expand[:LANES].T] * 2, axis=0)
    totals = lambda w: spec((8, w), lambda i: (0, 0))
    return pl.pallas_call(
        mamba_bwd_kernel,
        grid=(count,),
        in_specs=[
            block(LANES), block(1), block(1), spec((1, rows), lambda i: (0, back(i))), block(width, 1), before(width, 1),
            block(states2, 2 * width // states2), before(states2, 2 * width // states2), block(LANES, (2 * width + states2) // LANES),
            block(width), block(width), spec((1, states2 // 2, width), lambda i: (back(i), 0, 0)), block(width),
            whole(taps), whole(staps), whole(heads), whole(expand), whole(reduce), whole(gain),
        ],
        out_specs=[block(2 * width + states2 + LANES), totals(width), totals(states2), totals(LANES)],
        out_shape=[
            jax.ShapeDtypeStruct((total, 2 * width + states2 + LANES), BF),
            jax.ShapeDtypeStruct((8, width), F32),
            jax.ShapeDtypeStruct((8, states2), F32),
            jax.ShapeDtypeStruct((8, LANES), F32),
        ],
        scratch_shapes=[
            pltpu.VMEM((rows + 8, width), F32), pltpu.VMEM((rows + 8, states2), F32),
            pltpu.VMEM((rows + 8, width), F32), pltpu.VMEM((rows + 8, states2), F32), pltpu.VMEM((states2 // 2, width), F32),
        ],
        compiler_params=pltpu.CompilerParams(vmem_limit_bytes=32 * 2**20),
        cost_estimate=pl.CostEstimate(flops=35 * 10**9, bytes_accessed=total * width * 24, transcendentals=total * width * 5),
        name="mamba_bwd",
    )(feats, scale, coefficient, doc_row, ssm_in, ssm_in, ssm_in, ssm_in, ssm_in, ssm_in, scan, states, norm_grad, taps, staps, heads, expand, reduce, gain)


QBLOCK = 256


def swap_halves(values):
    lane = iota2(values.shape, 1) % (LANES // 2)
    return jnp.where(lane < LANES // 4, pltpu.roll(values, LANES - LANES // 4, 1), pltpu.roll(values, LANES // 4, 1))


def stack_heads(part):
    front = iota2(part.shape, 1) < LANES // 2
    zero = jnp.zeros_like(part)
    return jnp.concatenate([jnp.where(front, part, zero), jnp.where(front, zero, part)], axis=0)


def attention_fwd_kernel(groups, docs_col_ref, docs_ref, q_ref, kv_ref, cos_ref, sin_ref, out_ref, lse_ref, qrot_ref, keys_ref, values_ref):
    total = q_ref.shape[0]
    pairs = q_ref.shape[1] // LANES
    block = min(QBLOCK, total)
    cos, sin = cos_ref[...], sin_ref[...]
    front = iota2((total, LANES), 1) < LANES // 2
    for g in range(groups):
        lanes = slice(g * LANES, (g + 1) * LANES)
        raw = kv_ref[:, lanes]
        turned = raw * cos + swap_halves(raw) * sin
        keys_ref[:, lanes] = jnp.where(front, turned, pltpu.roll(turned, LANES // 2, 1)).astype(BF)
        values_ref[:, lanes] = jnp.where(front, pltpu.roll(raw, LANES // 2, 1), raw).astype(BF)
    for p in range(pairs):
        lanes = slice(p * LANES, (p + 1) * LANES)
        raw = q_ref[:, lanes]
        qrot_ref[:, lanes] = ((raw * cos + swap_halves(raw) * sin).astype(BF).astype(F32) * (LANES // 2) ** -0.5).astype(BF)
    front = iota2((block, LANES), 1) < LANES // 2
    lane_of = iota2((block, LANES), 1)
    for start in range(0, total, block):
        rows, end = slice(start, start + block), start + block
        allowed = (docs_col_ref[rows, 0:1] == docs_ref[:, :end]) & (
            iota2((block, end), 0) + start >= iota2((block, end), 1)
        )
        bias = jnp.where(allowed, 0.0, MASKED)
        bias = jnp.concatenate([bias, bias], axis=0)
        sums = jnp.zeros((block, LANES), F32)
        for p in range(pairs):
            lanes = slice(p * LANES, (p + 1) * LANES)
            g = p * groups // pairs
            kv = slice(g * LANES, (g + 1) * LANES)
            scores = mm_nt(stack_heads(qrot_ref[rows, lanes]), keys_ref[:end, kv]) + bias
            top = jnp.max(scores, axis=1, keepdims=True)
            raised = jnp.exp(scores - top)
            whole = jnp.sum(raised, axis=1, keepdims=True)
            mixed = mm(raised, values_ref[:end, kv]) / whole
            out_ref[rows, lanes] = jnp.where(front, mixed[:block], mixed[block:]).astype(BF)
            logs = top + jnp.log(whole)
            sums = jnp.where(lane_of == 2 * p, logs[:block], sums)
            sums = jnp.where(lane_of == 2 * p + 1, logs[block:], sums)
        lse_ref[rows, :] = sums


def attention_bwd_kernel(groups, docs_col_ref, docs_ref, qrot_ref, keys_ref, values_ref, lse_ref, up_ref, cos_ref, sin_ref, grads_ref, dk_acc, dv_acc):
    total = qrot_ref.shape[0]
    pairs = qrot_ref.shape[1] // LANES
    block = min(QBLOCK, total)
    dk_acc[...] = jnp.zeros_like(dk_acc)
    dv_acc[...] = jnp.zeros_like(dv_acc)
    front = iota2((block, LANES), 1) < LANES // 2
    for start in range(0, total, block):
        rows, end = slice(start, start + block), start + block
        allowed = (docs_col_ref[:end, 0:1] == docs_ref[:, rows]) & (
            iota2((end, block), 0) <= iota2((end, block), 1) + start
        )
        bias = jnp.where(allowed, 0.0, MASKED)
        logs = lse_ref[rows, :].T
        cos, sin = cos_ref[rows, :], sin_ref[rows, :]
        for p in range(pairs):
            lanes = slice(p * LANES, (p + 1) * LANES)
            g = p * groups // pairs
            kv = slice(g * LANES, (g + 1) * LANES)
            keys, values = keys_ref[:end, kv], values_ref[:end, kv]
            queries = stack_heads(qrot_ref[rows, lanes])
            ups = stack_heads(up_ref[rows, lanes])
            shift = jnp.concatenate([bias - logs[2 * p : 2 * p + 1], bias - logs[2 * p + 1 : 2 * p + 2]], axis=1)
            probs = jnp.exp(mm_nt(keys, queries) + shift)
            grads = mm_nt(values, ups)
            centre = jnp.sum(probs * grads, axis=0, keepdims=True)
            score_grads = (probs * (grads - centre)).astype(BF)
            dk_acc[:end, kv] += mm(score_grads, queries)
            dv_acc[:end, kv] += mm(probs, ups)
            dq = mm_tn(score_grads, keys)
            dq = jnp.where(front, dq[:block], dq[block:]) * (LANES // 2) ** -0.5
            grads_ref[rows, lanes] = (dq * cos - swap_halves(dq) * sin).astype(BF)
    front = iota2((total, LANES), 1) < LANES // 2
    for g in range(groups):
        kv = slice(g * LANES, (g + 1) * LANES)
        dk, dv = dk_acc[:, kv], dv_acc[:, kv]
        dk = dk + pltpu.roll(dk, LANES // 2, 1)
        dk = dk * cos_ref[...] - swap_halves(dk) * sin_ref[...]
        dv = dv + pltpu.roll(dv, LANES // 2, 1)
        out = slice((pairs + g) * LANES, (pairs + g + 1) * LANES)
        grads_ref[:, out] = jnp.where(front, dk, dv).astype(BF)


def attention_forward(groups, doc_col, doc_row, qkv, cos, sin, query_width):
    total = qkv.shape[0]
    kv_width = qkv.shape[1] - query_width
    whole = lambda a: spec(a.shape, lambda i: (0,) * a.ndim)
    columns = lambda w, place=0: spec((total, w), lambda i: (0, place))
    return pl.pallas_call(
        functools.partial(attention_fwd_kernel, groups),
        grid=(1,),
        in_specs=[whole(doc_col), whole(doc_row), columns(query_width), columns(kv_width, query_width // kv_width), whole(cos), whole(sin)],
        out_specs=[columns(query_width), columns(LANES), columns(query_width), columns(kv_width), columns(kv_width)],
        out_shape=[
            jax.ShapeDtypeStruct((total, query_width), BF), jax.ShapeDtypeStruct((total, LANES), F32),
            jax.ShapeDtypeStruct((total, query_width), BF), jax.ShapeDtypeStruct((total, kv_width), BF),
            jax.ShapeDtypeStruct((total, kv_width), BF),
        ],
        compiler_params=pltpu.CompilerParams(vmem_limit_bytes=32 * 2**20),
        cost_estimate=pl.CostEstimate(flops=12 * 10**9, bytes_accessed=total * query_width * 10, transcendentals=total * total * 2),
        name="attention_fwd",
    )(doc_col, doc_row, qkv, qkv, cos, sin)


def attention_backward(groups, doc_col, doc_row, qrot, keys, values, lse, up, cos, sin):
    total = qrot.shape[0]
    return pl.pallas_call(
        functools.partial(attention_bwd_kernel, groups),
        out_shape=jax.ShapeDtypeStruct((total, qrot.shape[1] + keys.shape[1]), BF),
        scratch_shapes=[pltpu.VMEM(keys.shape, F32), pltpu.VMEM(keys.shape, F32)],
        compiler_params=pltpu.CompilerParams(vmem_limit_bytes=32 * 2**20),
        cost_estimate=pl.CostEstimate(flops=16 * 10**9, bytes_accessed=total * qrot.shape[1] * 10, transcendentals=total * total * 2),
        name="attention_bwd",
    )(doc_col, doc_row, qrot, keys, values, lse, up, cos, sin)


def flipped(index, mask):
    bit = 1
    while bit <= mask:
        if mask & bit:
            index = index + bit * (1 - 2 * ((index // bit) % 2))
        bit *= 2
    return index


def greet(partners):
    barrier = pltpu.get_barrier_semaphore()
    for axis, place in partners:
        pl.semaphore_signal(barrier, inc=1, device_id={axis: place}, device_id_type=pl.DeviceIdType.MESH)
    pl.semaphore_wait(barrier, len(partners))


def remote(source, target, send, recv, axis, place):
    return pltpu.make_async_remote_copy(
        src_ref=source, dst_ref=target, send_sem=send, recv_sem=recv,
        device_id={axis: place}, device_id_type=pl.DeviceIdType.MESH,
    )


def gather_kernel(count, shard_ref, full_ref, own_sem, send_sems, recv_sems):
    unit, columns = shard_ref.shape
    levels = count // 4
    me = lax.axis_index("fsdp")
    half = columns // 2 // LANES * LANES
    parts = (slice(0, half), slice(half, columns))
    neighbours = (flipped(me, 1), flipped(me, 2))
    far = [flipped(me, 4 * d) for d in range(1, levels)]
    greet([("fsdp", p) for p in neighbours] + [("fsdp", p) for p in far])

    def rows(owner):
        return pl.ds(pl.multiple_of(owner * unit, unit), unit)

    started = []

    def send(source, owner, lanes, slot, place):
        copy = remote(source, full_ref.at[rows(owner), lanes], send_sems.at[slot], recv_sems.at[slot], "fsdp", place)
        copy.start()
        started.append(copy)
        return copy

    def arrival(owner, lanes, slot):
        piece = full_ref.at[rows(owner), lanes]
        return remote(piece, piece, send_sems.at[slot], recv_sems.at[slot], "fsdp", neighbours[0])

    everything = slice(0, columns)
    own = pltpu.make_async_copy(shard_ref, full_ref.at[rows(me), :], own_sem)
    own.start()
    for d in range(1, levels):
        send(shard_ref, me, everything, d, far[d - 1])
    base = levels
    for axis in range(2):
        send(shard_ref, me, everything, base + axis * levels, neighbours[axis])
    cross = base + 2 * levels

    def pass_on(d):
        for axis in range(2):
            owner = flipped(neighbours[axis], 4 * d)
            arrival(owner, everything, base + axis * levels + d).wait_recv()
            piece = full_ref.at[rows(owner), parts[axis]]
            send(piece, owner, parts[axis], cross + axis * levels + d, neighbours[1 - axis])

    for d in range(1, levels):
        arrival(far[d - 1], everything, d).wait_recv()
        for axis in range(2):
            send(full_ref.at[rows(far[d - 1]), :], far[d - 1], everything, base + axis * levels + d, neighbours[axis])
        pass_on(d - 1)
    pass_on(levels - 1)
    for d in range(levels):
        for axis in range(2):
            owner = flipped(me, 4 * d + 3)
            arrival(owner, parts[axis], cross + axis * levels + d).wait_recv()
    for copy in started:
        copy.wait_send()
    own.wait()


def gather_weights(shard, count, collective_id):
    unit, columns = shard.shape
    slots = 5 * (count // 4)
    return pl.pallas_call(
        functools.partial(gather_kernel, count),
        in_specs=[pl.BlockSpec(memory_space=pl.ANY)],
        out_specs=pl.BlockSpec(memory_space=pl.ANY),
        out_shape=jax.ShapeDtypeStruct((count * unit, columns), shard.dtype),
        scratch_shapes=[pltpu.SemaphoreType.DMA, pltpu.SemaphoreType.DMA((slots,)), pltpu.SemaphoreType.DMA((slots,))],
        compiler_params=pltpu.CompilerParams(collective_id=collective_id, has_side_effects=True),
        cost_estimate=pl.CostEstimate(flops=0, bytes_accessed=2 * count * unit * columns * 2, transcendentals=0),
        name="gather_weights",
    )(shard)


def scatter_kernel(count, tensors, paths, split_rows, *refs):
    number = len(paths)
    grads, small_ref = refs[:number], refs[number]
    outs, small_out = refs[number + 1 : 2 * number + 1], refs[2 * number + 1]
    scratch = refs[2 * number + 2 :]
    cross, along_x, along_y, far_in, staged, far_out = (scratch[k * number : (k + 1) * number] for k in range(6))
    sums, arrived, send_sems, recv_sems, sum_send, sum_recv = scratch[6 * number :]
    levels = count // 4
    unit = grads[0].shape[0] // count
    me = lax.axis_index("fsdp")
    core = lax.axis_index("tensor")
    near = (flipped(me, 1), flipped(me, 2))
    far = [None] + [flipped(me, 4 * d) for d in range(1, levels)]
    bits = [1 << k for k in range((count - 1).bit_length())]
    stages = [("fsdp", flipped(me, bit)) for bit in bits]
    cores = [("tensor", flipped(core, 1 << k)) for k in range((tensors - 1).bit_length())]
    greet([("fsdp", p) for p in near] + [("fsdp", p) for p in far[1:]] + cores)
    stages = stages + cores
    started = []

    def rows(owner):
        return pl.ds(pl.multiple_of(owner * unit, unit), unit)

    def link(source, target, slot, place):
        return remote(source, target, send_sems.at[slot], recv_sems.at[slot], "fsdp", place)

    def send(source, target, slot, place):
        copy = link(source, target, slot, place)
        copy.start()
        started.append(copy)

    def slot(i, kind, d):
        return (i * 4 + kind) * levels + d

    pending = []

    def next_stage():
        done = len(pending)
        if done:
            pending[-1].wait()
            sums[done] = sums[done - 1] + arrived[done - 1]
        if done < len(stages):
            axis, place = stages[done]
            copy = remote(sums.at[done], arrived.at[done], sum_send.at[done], sum_recv.at[done], axis, place)
            copy.start()
            pending.append(copy)

    sums[0] = small_ref[...]
    next_stage()
    order = list(range(levels - 1, -1, -1))
    inbound = lambda path, d: (along_x, along_y)[path]
    for d in order:
        for i, path in enumerate(paths):
            send(grads[i].at[rows(flipped(me, 4 * d + 3)), :], cross[i].at[d], slot(i, 0, d), near[1 - path])
        for i, path in enumerate(paths):
            raw = 1 - path
            target = (along_x, along_y)[raw][i]
            send(grads[i].at[rows(flipped(near[raw], 4 * d)), :], target.at[d], slot(i, 1 + raw, d), near[raw])
    for d in order:
        for i, path in enumerate(paths):
            link(cross[i].at[d], cross[i].at[d], slot(i, 0, d), near[0]).wait_recv()
            staged[i][d] = (grads[i][rows(flipped(near[path], 4 * d)), :].astype(F32) + cross[i][d].astype(F32)).astype(BF)
            target = (along_x, along_y)[path][i]
            send(staged[i].at[d], target.at[d], slot(i, 1 + path, d), near[path])
        if d == order[0] or d == 0:
            next_stage()
    for d in order:
        for i, path in enumerate(paths):
            link(along_x[i].at[d], along_x[i].at[d], slot(i, 1, d), near[0]).wait_recv()
            link(along_y[i].at[d], along_y[i].at[d], slot(i, 2, d), near[0]).wait_recv()
            total = grads[i][rows(flipped(me, 4 * d)), :].astype(F32) + along_x[i][d].astype(F32) + along_y[i][d].astype(F32)
            if d:
                far_out[i][d - 1] = total.astype(BF)
                send(far_out[i].at[d - 1], far_in[i].at[d - 1], slot(i, 3, d), far[d])
            else:
                outs[i][...] = total
        if d == order[0] or d == 0:
            next_stage()
    while len(pending) < len(stages):
        next_stage()
    next_stage()
    for d in order[:-1]:
        for i in range(number):
            link(far_in[i].at[d - 1], far_in[i].at[d - 1], slot(i, 3, d), near[0]).wait_recv()
            outs[i][...] += far_in[i][d - 1].astype(F32)
    small_out[:split_rows, :] = sums[len(bits), :split_rows, :]
    small_out[split_rows:, :] = sums[len(stages), split_rows:, :]
    for copy in started:
        copy.wait_send()


def scatter_grads(grads, paths, small, split_rows, count, tensors, collective_id):
    unit = grads[0].shape[0] // count
    levels = count // 4
    stages = (count - 1).bit_length() + (tensors - 1).bit_length()
    vmem = pl.BlockSpec(memory_space=pltpu.VMEM)
    buffers = []
    for slots in (levels, levels, levels, levels - 1, levels, levels - 1):
        buffers += [pltpu.VMEM((slots, unit, g.shape[1]), BF) for g in grads]
    buffers += [pltpu.VMEM((stages + 1,) + small.shape, F32), pltpu.VMEM((stages,) + small.shape, F32)]
    links = 4 * levels * len(grads)
    buffers += [pltpu.SemaphoreType.DMA((links,))] * 2 + [pltpu.SemaphoreType.DMA((stages,))] * 2
    size = sum(g.shape[1] for g in grads)
    return pl.pallas_call(
        functools.partial(scatter_kernel, count, tensors, tuple(paths), split_rows),
        in_specs=[vmem] * (len(grads) + 1),
        out_specs=[vmem] * (len(grads) + 1),
        out_shape=[jax.ShapeDtypeStruct((unit, g.shape[1]), F32) for g in grads] + [jax.ShapeDtypeStruct(small.shape, F32)],
        scratch_shapes=buffers,
        compiler_params=pltpu.CompilerParams(collective_id=collective_id, has_side_effects=True, vmem_limit_bytes=48 * 2**20),
        cost_estimate=pl.CostEstimate(flops=0, bytes_accessed=2 * count * unit * size * 2, transcendentals=0),
        name="scatter_grads",
    )(*grads, small)


def tensor_swap(values):
    return lax.ppermute(values, "tensor", [(0, 1), (1, 0)])


def tensor_sum(values):
    if lax.axis_size("tensor") == 2:
        return values + tensor_swap(values)
    return lax.psum(values, "tensor")


def tensor_sum_low(values):
    if lax.axis_size("tensor") == 2:
        return values + tensor_swap(values.astype(BF)).astype(F32)
    return lax.psum(values, "tensor")


def tensor_gather(values):
    if lax.axis_size("tensor") == 2:
        other = tensor_swap(values)
        first = lax.axis_index("tensor") == 0
        return jnp.concatenate([jnp.where(first, values, other), jnp.where(first, other, values)], axis=0)
    return lax.all_gather(values, "tensor", axis=0, tiled=True)


def tensor_scatter(values):
    if lax.axis_size("tensor") == 2:
        half = values.shape[0] // 2
        first = lax.axis_index("tensor") == 0
        mine = jnp.where(first, values[:half], values[half:])
        other = jnp.where(first, values[half:], values[:half])
        return mine.astype(F32) + tensor_swap(other.astype(BF)).astype(F32)
    return lax.psum_scatter(values.astype(BF), "tensor", scatter_dimension=0, tiled=True).astype(F32)


def pad_to(values, size, axis=-1):
    pads = [(0, 0)] * values.ndim
    pads[axis] = (0, size - values.shape[axis])
    return jnp.pad(values, pads) if size > values.shape[axis] else values


def norm_scale(values):
    return lax.rsqrt(jnp.mean(values * values, axis=-1, keepdims=True) + EPS)


def pack_kernel(
    mixer_ref, state_ref, step_ref, query_ref, keyval_ref, proj_ref, attention_ref, gate_up_ref, down_ref,
    first_ref, second_ref,
):
    unit = state_ref.shape[0]
    width, wide = mixer_ref.shape[2], -(-mixer_ref.shape[2] // LANES) * LANES
    same = (iota2((unit, unit), 0) == iota2((unit, unit), 1)).astype(BF)
    place = 0

    def put(out_ref, value, size):
        nonlocal place
        value = value.astype(BF)
        if size > value.shape[1]:
            value = jnp.concatenate([value, jnp.zeros((unit, size - value.shape[1]), BF)], axis=1)
        out_ref[:, place : place + size] = value
        place += size

    put(first_ref, mixer_ref[:, 0, :], wide)
    put(first_ref, mixer_ref[:, 1, :], wide)
    put(first_ref, state_ref[...], state_ref.shape[1])
    put(first_ref, step_ref[...], LANES)
    query_wide = -(-query_ref.shape[1] // LANES) * LANES
    put(first_ref, query_ref[...], query_wide)
    put(first_ref, keyval_ref[...], keyval_ref.shape[1])
    put(first_ref, mm_nt(same, proj_ref[...]), wide)
    put(first_ref, mm_nt(same, attention_ref[...]), query_wide)
    place = 0
    put(second_ref, gate_up_ref[:, 0, :], gate_up_ref.shape[2])
    put(second_ref, gate_up_ref[:, 1, :], gate_up_ref.shape[2])
    put(second_ref, mm_nt(same, down_ref[...]), down_ref.shape[0])


def pack_weights(mixer, state, step, query, keyval, proj, attention, gate_up, down):
    unit = state.shape[0]
    lanes = lambda size: -(-size // LANES) * LANES
    first = 3 * lanes(mixer.shape[2]) + state.shape[1] + LANES + 2 * lanes(query.shape[1]) + keyval.shape[1]
    second = 2 * gate_up.shape[2] + down.shape[0]
    return pl.pallas_call(
        pack_kernel,
        out_shape=[jax.ShapeDtypeStruct((unit, first), BF), jax.ShapeDtypeStruct((unit, second), BF)],
        compiler_params=pltpu.CompilerParams(vmem_limit_bytes=32 * 2**20),
        name="pack_weights",
    )(mixer, state, step, query, keyval, proj, attention, gate_up, down)


def table_kernel(
    docs_ref, conv_ref, conv_bias_ref, state_conv_ref, state_bias_ref, step_bias_ref, decay_ref, skip_ref,
    feats_ref, cos_ref, sin_ref, taps_ref, state_taps_ref, heads_ref,
):
    total = docs_ref.shape[1]
    docs = docs_ref[...]
    tall = jnp.broadcast_to(docs, (LANES, total)).T
    spot = iota2((1, total), 1)
    begin = jnp.sum((tall[:, 0:1] < docs).astype(F32), axis=0, keepdims=True)
    rows = [docs]
    eight = jnp.broadcast_to(docs, (8, total))
    for k in (1, 2, 3):
        rows.append(jnp.where(spot >= k, (pltpu.roll(eight, k, 1)[0:1] == docs).astype(F32), 0.0))
    blocks = [docs[:, i : i + CHUNK] for i in range(0, total, CHUNK)]
    before = [jnp.full((1, 1), -1.0, F32)] + [v[:, CHUNK - 1 :] for v in blocks[:-1]]
    rows.append(jnp.concatenate([(v == w).astype(F32) for v, w in zip(blocks, before)], axis=1))
    rows.append(jnp.concatenate([(v == v[:, CHUNK - 1 :]).astype(F32) for v in blocks], axis=1))
    for k in (1, 2, 3):
        rows.append(jnp.where(spot < total - k, (pltpu.roll(eight, total - k, 1)[0:1] == docs).astype(F32), 0.0))
    rows.append(spot.astype(F32) - begin)
    rows.append(jnp.zeros((LANES - len(rows), total), F32))
    feats = jnp.concatenate(rows, axis=0).T
    feats_ref[...] = feats
    lane = iota2((1, LANES), 1)
    rates = jnp.exp((lane % (HEAD_SIZE // 2)).astype(F32) * (-2.0 * math.log(THETA) / HEAD_SIZE))
    angles = feats[:, 9:10] * rates
    cos_ref[...] = jnp.cos(angles)
    sin_ref[...] = jnp.sin(angles) * jnp.where(lane % HEAD_SIZE < HEAD_SIZE // 2, -1.0, 1.0)
    width, heads = conv_ref.shape[1], skip_ref.shape[1]
    taps_ref[...] = jnp.zeros_like(taps_ref)
    taps_ref[0:4, :width] = conv_ref[...]
    taps_ref[4:5, :width] = conv_bias_ref[...]
    spread = (iota2((heads, width), 0) == iota2((heads, width), 1) // (width // heads)).astype(F32)
    taps_ref[5:6, :width] = exact_mm(jnp.broadcast_to(skip_ref[...], (8, heads)), spread)[0:1]
    state_taps_ref[...] = jnp.zeros_like(state_taps_ref)
    state_taps_ref[0:4, :] = state_conv_ref[...]
    state_taps_ref[4:5, :] = state_bias_ref[...]
    heads_ref[...] = jnp.zeros_like(heads_ref)
    heads_ref[0:1, :heads] = step_bias_ref[...]
    heads_ref[1:2, :heads] = -jnp.exp(decay_ref[...])


def make_tables(docs, wide, conv, conv_bias, state_conv, state_bias, step_bias, decay, skip):
    total = docs.shape[1]
    shape = lambda r, c: jax.ShapeDtypeStruct((r, c), F32)
    return pl.pallas_call(
        table_kernel,
        out_shape=[shape(total, LANES), shape(total, LANES), shape(total, LANES), shape(8, wide), shape(8, state_conv.shape[1]), shape(8, LANES)],
        compiler_params=pltpu.CompilerParams(vmem_limit_bytes=32 * 2**20),
        name="make_tables",
    )(docs, conv, conv_bias[None], state_conv, state_bias[None], step_bias[None], decay[None], skip[None])


def body(
    layer_input, doc_ids, input_gain, mixer_weight, state_weight, step_weight, conv_weight, conv_bias, state_conv,
    state_conv_bias, step_bias, decay_log, skip_gain, mixer_gain, mixer_proj, query_weight, keyval_projection,
    attention_proj, second_gain, gate_up, down_proj, cotangent,
):
    tensor_count = lax.axis_size("tensor")
    tensor_index = lax.axis_index("tensor")
    fsdp_count = lax.axis_size("fsdp")
    fsdp_index = lax.axis_index("fsdp")
    own_rows, hidden = layer_input.shape
    unit = state_weight.shape[0]
    seq_count, seq_length = doc_ids.shape
    total = seq_count * seq_length
    heads = step_bias.shape[0]
    width = conv_weight.shape[1]
    wide = -(-width // LANES) * LANES
    query_width = query_weight.shape[1]
    query_wide = -(-query_width // LANES) * LANES
    per_group = QUERY_HEADS // KEYVAL_HEADS
    query_heads = query_width // HEAD_SIZE
    kv_heads = max(1, query_heads // per_group)
    kv_leading = tensor_index * query_heads // per_group
    states2 = state_weight.shape[1]
    ffn = down_proj.shape[0]

    own_keyval = lax.dynamic_slice_in_dim(keyval_projection, kv_leading * HEAD_SIZE, kv_heads * HEAD_SIZE, 2)
    own_keyval = own_keyval.reshape(unit, 2, kv_heads, HEAD_SIZE).transpose(0, 2, 1, 3).reshape(unit, 2 * kv_heads * HEAD_SIZE)
    kv_wide = 2 * kv_heads * HEAD_SIZE
    low = lambda v: v.astype(BF)
    first, rest = pack_weights(
        mixer_weight, state_weight, step_weight, query_weight, own_keyval, mixer_proj, attention_proj, gate_up, down_proj
    )
    rest = lax.all_gather(rest, "fsdp", axis=0, tiled=True)
    first = gather_weights(first, fsdp_count, 0)
    ssm_wide = 2 * wide + states2 + LANES
    cuts = np.cumsum([0, ssm_wide, query_wide + kv_wide, wide, query_wide])
    full_ssm, full_qkv, full_proj, full_attention = (first[:, cuts[i] : cuts[i + 1]] for i in range(4))
    full_gate_up, full_down = rest[:, : 2 * ffn], rest[:, 2 * ffn :]

    tokens = tensor_gather(layer_input).astype(F32)
    upstream = tensor_gather(cotangent)
    docs = (doc_ids + jnp.arange(seq_count, dtype=jnp.int32)[:, None] * seq_length).reshape(1, total)
    doc_row = docs.astype(F32)
    feats, cos, sin, taps, state_taps, head_rows = make_tables(
        doc_row, wide, conv_weight, conv_bias, state_conv, state_conv_bias, step_bias, decay_log, skip_gain
    )
    gain_row = pad_to(mixer_gain[None], wide)

    first_scale = norm_scale(tokens)
    normed = low(tokens * first_scale * input_gain)
    ssm_in = plain_dot(normed, full_ssm)
    qkv_in = plain_dot(normed, full_qkv)
    scan, gated_low, squares, states = mamba_forward(feats, doc_row, ssm_in, taps, state_taps, head_rows, gain_row, wide, states2)
    attended, log_sums, query_rot, keys, values = attention_forward(kv_heads, feats, doc_row, qkv_in, cos, sin, query_wide)
    squares = tensor_sum(squares.reshape(-1, LANES)).reshape(total, 1)
    gated_scale = lax.rsqrt(squares / DSSM + EPS)
    branch = gated_scale * right_dot(gated_low, full_proj) + right_dot(attended, full_attention)
    middle = tokens + tensor_sum_low(branch)
    second_scale = norm_scale(middle)
    second = low(middle * second_scale * second_gain)
    gate_vals = plain_dot(second, full_gate_up)
    gate_part, up_part = gate_vals[:, :ffn], gate_vals[:, ffn:]
    gate_sigmoid = jax.nn.sigmoid(gate_part)
    active = low(gate_part * gate_sigmoid * up_part)
    ffn_out = tensor_scatter(low(right_dot(active, full_down)))
    own = lambda v: lax.dynamic_slice_in_dim(v, tensor_index * own_rows, own_rows, 0)
    layer_output = low(own(middle) + ffn_out)

    grad_down = low(left_dot(upstream, active))
    active_grad = plain_dot(upstream, full_down)
    gate_grad = active_grad * up_part * gate_sigmoid * (1.0 + gate_part * (1.0 - gate_sigmoid))
    up_grad = active_grad * gate_part * gate_sigmoid
    gu_grad = jnp.concatenate([low(gate_grad), low(up_grad)], axis=-1)
    grad_gate_up = low(left_dot(second, gu_grad))
    second_grad = tensor_sum_low(right_dot(gu_grad, full_gate_up))
    weighted = second_grad * second_gain
    inner = jnp.mean(weighted * middle, axis=-1, keepdims=True)
    middle_grad = upstream.astype(F32) + second_scale * weighted - middle * second_scale**3 * inner
    second_gain_part = jnp.sum(second_grad * middle * second_scale, axis=0) * (1.0 / tensor_count)
    branch_low = low(middle_grad)

    norm_grad = low(plain_dot(branch_low, full_proj))
    attended_grad = low(plain_dot(branch_low, full_attention))
    inner_sums = tensor_sum(jnp.sum(norm_grad.astype(F32) * gated_low.astype(F32), axis=-1).reshape(-1, LANES)).reshape(total, 1)
    grad_proj = low(left_dot(low(gated_scale * branch_low), gated_low))
    grad_attention = low(left_dot(branch_low, attended))
    ssm_grad, sums, state_sums, head_sums = mamba_backward(
        feats, doc_row, gated_scale, gated_scale**3 * (inner_sums / DSSM), ssm_in, scan, states, norm_grad, taps, state_taps,
        head_rows, gain_row, wide, states2,
    )
    qkv_grad = attention_backward(kv_heads, feats, doc_row, query_rot, keys, values, log_sums, attended_grad, cos, sin)
    grad_ssm = low(left_dot(normed, ssm_grad))
    grad_qkv = low(left_dot(normed, qkv_grad))
    normed_part = right_dot(ssm_grad, full_ssm) + right_dot(qkv_grad, full_qkv)
    input_gain_part = jnp.sum(normed_part * tokens * first_scale, axis=0)
    normed_grad = tensor_scatter(low(normed_part))
    own_tokens, own_scale = own(tokens), own(first_scale)
    weighted = normed_grad * input_gain
    inner = jnp.mean(weighted * own_tokens, axis=-1, keepdims=True)
    input_grad = own(middle_grad) + own_scale * weighted - own_tokens * own_scale**3 * inner

    rest_sum = lax.psum_scatter(jnp.concatenate([grad_gate_up, grad_down], axis=1), "fsdp", scatter_dimension=0, tiled=True).astype(F32)
    split_small = jnp.concatenate([sums, head_sums], axis=1).reshape(-1, LANES)
    shared_small = jnp.concatenate([state_sums.reshape(-1, LANES), second_gain_part.reshape(-1, LANES), input_gain_part.reshape(-1, LANES)], axis=0)
    split_rows = split_small.shape[0]
    sum_ssm, sum_qkv, sum_proj, sum_attention, small = scatter_grads(
        (grad_ssm, grad_qkv, grad_proj, grad_attention), (0, 1, 1, 1), jnp.concatenate([split_small, shared_small], axis=0),
        split_rows, fsdp_count, tensor_count, 1,
    )
    keyval_sum = sum_qkv[:, query_wide:].reshape(unit, kv_heads, 2, HEAD_SIZE).transpose(0, 2, 1, 3).reshape(unit, 2, kv_heads * HEAD_SIZE)
    keyval_sum = lax.dynamic_update_slice_in_dim(
        jnp.zeros((unit, 2, KEYVAL_HEADS * HEAD_SIZE), F32), keyval_sum, kv_leading * HEAD_SIZE, 2
    ).reshape(unit, 2 * KEYVAL_HEADS * HEAD_SIZE)
    shared = tensor_sum(jnp.concatenate([sum_ssm[:, 2 * wide : 2 * wide + states2], keyval_sum], axis=1))
    split_sums = small[:split_rows].reshape(8, wide + LANES)
    sums, head_sums = split_sums[:, :wide], split_sums[:, wide:]
    gain_rows = hidden // LANES
    state_sums = small[split_rows : small.shape[0] - 2 * gain_rows].reshape(8, states2)
    second_gain_sum, input_gain_sum = small[-2 * gain_rows : -gain_rows].reshape(hidden), small[-gain_rows:].reshape(hidden)
    return (
        layer_output,
        input_grad,
        input_gain_sum,
        jnp.stack([sum_ssm[:, :width], sum_ssm[:, wide : wide + width]], axis=1),
        shared[:, :states2],
        sum_ssm[:, 2 * wide + states2 : 2 * wide + states2 + heads],
        sums[0:4, :width],
        sums[4, :width],
        state_sums[0:4],
        state_sums[4],
        head_sums[0, :heads],
        head_sums[1, :heads],
        jnp.sum(sums[5, :width].reshape(heads, -1), axis=1),
        sums[6, :width],
        sum_proj[:, :width].T,
        sum_qkv[:, :query_width],
        shared[:, states2:].reshape(unit, 2, KEYVAL_HEADS * HEAD_SIZE),
        sum_attention[:, :query_width].T,
        second_gain_sum,
        rest_sum[:, : 2 * ffn].reshape(unit, 2, ffn),
        rest_sum[:, 2 * ffn :].T,
    )


def solution(mesh):
    placed = (
        P(("fsdp", "tensor"), None),
        P("fsdp", None),
        P(),
        P("fsdp", None, "tensor"),
        P("fsdp", None),
        P("fsdp", "tensor"),
        P(None, "tensor"),
        P("tensor"),
        P(),
        P(),
        P("tensor"),
        P("tensor"),
        P("tensor"),
        P("tensor"),
        P("tensor", "fsdp"),
        P("fsdp", "tensor"),
        P("fsdp", None, None),
        P("tensor", "fsdp"),
        P(),
        P("fsdp", None, "tensor"),
        P("tensor", "fsdp"),
        P(("fsdp", "tensor"), None),
    )
    return jax.shard_map(
        body,
        mesh=mesh,
        in_specs=placed,
        out_specs=(
            P(("fsdp", "tensor"), None),
            P(("fsdp", "tensor"), None),
            P(),
            P("fsdp", None, "tensor"),
            P("fsdp", None),
            P("fsdp", "tensor"),
            P(None, "tensor"),
            P("tensor"),
            P(),
            P(),
            P("tensor"),
            P("tensor"),
            P("tensor"),
            P("tensor"),
            P("tensor", "fsdp"),
            P("fsdp", "tensor"),
            P("fsdp", None, None),
            P("tensor", "fsdp"),
            P(),
            P("fsdp", None, "tensor"),
            P("tensor", "fsdp"),
        ),
        check_vma=False,
    )
```

```python
import functools
import math

import jax
import jax.numpy as jnp
import ml_dtypes
import numpy as np
from jax import lax
from jax.experimental import pallas as pl
from jax.experimental.pallas import tpu as pltpu
from jax.sharding import PartitionSpec as P

QUERY_HEADS = 8
KEYVAL_HEADS = 2
HEAD_SIZE = 64
DSSM = 1536
EPS = 1e-05
THETA = 100000000000.0

LANES = 128
CHUNK = 128
FFN_ROWS = 512
MASKED = -1e30
BF, F32 = jnp.bfloat16, jnp.float32


def left_dot(left_side, right_side):
    return lax.dot_general(left_side, right_side, (((0,), (0,)), ((), ())), preferred_element_type=F32)


def right_dot(left_side, right_side):
    return lax.dot_general(left_side, right_side, (((1,), (1,)), ((), ())), preferred_element_type=F32)


def plain_dot(left_side, right_side):
    return jnp.dot(left_side, right_side, preferred_element_type=F32)


def mm(a, b):
    return jnp.dot(a.astype(BF), b.astype(BF), preferred_element_type=F32)


def mm_nt(a, b):
    return lax.dot_general(a.astype(BF), b.astype(BF), (((1,), (1,)), ((), ())), preferred_element_type=F32)


def mm_tn(a, b):
    return lax.dot_general(a.astype(BF), b.astype(BF), (((0,), (0,)), ((), ())), preferred_element_type=F32)


def exact_mm(a, b):
    return jnp.dot(a, b, precision=lax.Precision.HIGHEST, preferred_element_type=F32)


def sigmoid(v):
    return 1.0 / (1.0 + jnp.exp(-v))


def softplus(v):
    return jnp.maximum(v, 0.0) + jnp.log1p(jnp.exp(-jnp.abs(v)))


def split_lanes(values, axis):
    high = values.astype(BF)
    low = (values - high.astype(F32)).astype(BF)
    return jnp.concatenate([high, low], axis=axis)


def iota2(shape, axis):
    return lax.broadcasted_iota(jnp.int32, shape, axis)


def conv_taps(buffer, feats, taps, bias, rows):
    total = buffer[8 : 8 + rows, :] * taps[3:4, :] + bias
    for k in range(1, 4):
        total = total + buffer[8 - k : 8 - k + rows, :] * feats[:, k : k + 1] * taps[3 - k : 4 - k, :]
    return total


def step_parts(step_ref, heads_ref, feats, rows):
    raw = step_ref[...] + heads_ref[0:1, :]
    step = softplus(raw)
    lower = (iota2((rows, rows), 0) >= iota2((rows, rows), 1)).astype(F32)
    log_decay = exact_mm(lower, step * heads_ref[1:2, :])
    last = log_decay[rows - 1 : rows, :]
    enter = jnp.exp(log_decay) * feats[:, 4:5]
    leave = jnp.exp(last - log_decay) * feats[:, 5:6]
    return raw, step, log_decay, enter, leave


def gated_scale(squares):
    return lax.rsqrt(squares / DSSM + EPS)


def as_column(row):
    return jnp.broadcast_to(row, (LANES, row.shape[1])).T[:, 0:1]


def mamba_fwd_kernel(
    feats_ref, docs_ref, x_ref, bc_ref, step_ref, z_ref, taps_ref, staps_ref, heads_ref, expand_ref,
    gain_ref, scan_ref, low_ref, square_ref, states_ref, xbuf, bcbuf, memory,
):
    rows, width = x_ref.shape
    states = bc_ref.shape[1] // 2

    @pl.when(pl.program_id(0) == 0)
    def _():
        xbuf[0:8, :] = jnp.zeros((8, width), F32)
        bcbuf[0:8, :] = jnp.zeros((8, 2 * states), F32)
        memory[...] = jnp.zeros_like(memory)

    feats = feats_ref[...]
    xbuf[8 : 8 + rows, :] = x_ref[...]
    bcbuf[8 : 8 + rows, :] = bc_ref[...]
    pre = conv_taps(xbuf, feats, taps_ref, taps_ref[4:5, :], rows)
    values = pre * sigmoid(pre)
    pre_bc = conv_taps(bcbuf, feats, staps_ref, staps_ref[4:5, :], rows)
    both = pre_bc * sigmoid(pre_bc)
    xbuf[0:8, :] = xbuf[rows : rows + 8, :]
    bcbuf[0:8, :] = bcbuf[rows : rows + 8, :]
    key_in = both[:, :states].astype(BF)
    key_out = both[:, states:].astype(BF)
    _, step, log_decay, enter, leave = step_parts(step_ref, heads_ref, feats, rows)
    expanded = jnp.dot(
        split_lanes(jnp.concatenate([step, enter, leave], axis=0), 1), expand_ref[...], preferred_element_type=F32
    )
    step_w, enter_w, leave_w = expanded[:rows], expanded[rows : 2 * rows], expanded[2 * rows :]
    scaled = values * step_w
    gram = mm_nt(key_out, key_in)
    allowed = (feats[:, 0:1] == docs_ref[...]) & (iota2((rows, rows), 0) >= iota2((rows, rows), 1))
    bias = jnp.where(allowed, 0.0, MASKED)
    log_rows = log_decay.T
    front = iota2((rows, LANES), 1) < LANES // 2
    held = memory[...]
    states_ref[0] = held.astype(BF)
    carried = mm(key_out, held) * enter_w
    fresh = mm_tn(key_in, leave_w * scaled)
    memory[...] = held * enter_w[rows - 1 : rows, :] + fresh
    squares = jnp.zeros((rows, 1), F32)
    for pair in range(width // LANES):
        lanes = slice(pair * LANES, (pair + 1) * LANES)
        mixes = []
        for h in (2 * pair, 2 * pair + 1):
            decay = jnp.exp(log_decay[:, h : h + 1] - log_rows[h : h + 1, :] + bias)
            mixes.append((gram * decay).astype(BF))
        part = scaled[:, lanes]
        stacked = jnp.concatenate([jnp.where(front, part, 0.0), jnp.where(front, 0.0, part)], axis=0)
        inside = mm(jnp.concatenate(mixes, axis=1), stacked)
        scan = inside + carried[:, lanes] + values[:, lanes] * taps_ref[5:6, lanes]
        scan_ref[:, lanes] = scan
        z = z_ref[:, lanes]
        gated = scan * (z * sigmoid(z))
        low_ref[:, lanes] = (gated * gain_ref[:, lanes]).astype(BF)
        squares = squares + jnp.sum(gated * gated, axis=1, keepdims=True)
    square_ref[...] = jnp.broadcast_to(squares, (rows, LANES)).T[0:8, :]


def mamba_bwd_kernel(
    feats_ref, square_ref, square_in_ref, inner_ref, inner_in_ref, docs_ref, x_ref, x_before_ref, bc_ref, bc_before_ref, step_ref, z_ref, scan_ref, states_ref, norm_grad_ref,
    taps_ref, staps_ref, heads_ref, expand_ref, reduce_ref, gain_ref,
    grads_ref, sums_ref, ssums_ref, hsums_ref,
    xbuf, bcbuf, dxbuf, dbcbuf, dmemory,
):
    rows, width = x_ref.shape
    states = bc_ref.shape[1] // 2

    @pl.when(pl.program_id(0) == 0)
    def _():
        dxbuf[rows : rows + 8, :] = jnp.zeros((8, width), F32)
        dbcbuf[rows : rows + 8, :] = jnp.zeros((8, 2 * states), F32)
        dmemory[...] = jnp.zeros_like(dmemory)
        sums_ref[...] = jnp.zeros_like(sums_ref)
        ssums_ref[...] = jnp.zeros_like(ssums_ref)
        hsums_ref[...] = jnp.zeros_like(hsums_ref)

    feats = feats_ref[...]
    xbuf[0:8, :] = x_before_ref[...]
    bcbuf[0:8, :] = bc_before_ref[...]
    xbuf[8 : 8 + rows, :] = x_ref[...]
    bcbuf[8 : 8 + rows, :] = bc_ref[...]
    pre = conv_taps(xbuf, feats, taps_ref, taps_ref[4:5, :], rows)
    pre_gate = sigmoid(pre)
    values = pre * pre_gate
    pre_bc = conv_taps(bcbuf, feats, staps_ref, staps_ref[4:5, :], rows)
    bc_gate = sigmoid(pre_bc)
    both = pre_bc * bc_gate
    key_in = both[:, :states].astype(BF)
    key_out = both[:, states:].astype(BF)
    raw, step, log_decay, enter, leave = step_parts(step_ref, heads_ref, feats, rows)
    expanded = jnp.dot(
        split_lanes(jnp.concatenate([step, enter, leave], axis=0), 1), expand_ref[...], preferred_element_type=F32
    )
    step_w, enter_w, leave_w = expanded[:rows], expanded[rows : 2 * rows], expanded[2 * rows :]
    scaled = values * step_w
    z = z_ref[...]
    z_gate = sigmoid(z)
    z_silu = z * z_gate
    scan = scan_ref[...]
    gated = scan * z_silu
    norm_grad = norm_grad_ref[...].astype(F32)
    row_scale = gated_scale(square_ref[0:1, :] + square_in_ref[0:1, :])
    row_inner = (inner_ref[0:1, :] + inner_in_ref[0:1, :]) * row_scale * row_scale / DSSM
    scale, coefficient = as_column(row_scale), as_column(row_inner)
    weighted = norm_grad * scale
    gated_grad = weighted * gain_ref[...] - gated * coefficient
    dscan = gated_grad * z_silu
    grads_ref[:, 0:width] = (gated_grad * scan * (z_gate * (1.0 + z * (1.0 - z_gate)))).astype(BF)
    sums_ref[6:7, :] += jnp.sum(weighted * gated, axis=0, keepdims=True)
    sums_ref[5:6, :] += jnp.sum(dscan * values, axis=0, keepdims=True)
    held = states_ref[0]
    dheld = dmemory[...]
    dheld_low = dheld.astype(BF)
    enter_grad = (dscan * enter_w).astype(BF)
    left = leave_w * scaled
    passed = mm(key_in, dheld_low)
    arrived = mm(key_out, held)
    dkey_out = mm_nt(enter_grad, held)
    dkey_in = mm_nt(left, dheld_low)
    carry = enter_w[rows - 1 : rows, :]
    dmemory[...] = dheld * carry + mm_tn(key_out, enter_grad)
    enter_terms = dscan * enter_w * arrived
    leave_terms = left * passed
    carry_terms = jnp.sum(dheld * held.astype(F32), axis=0, keepdims=True) * carry
    gram = mm_nt(key_in, key_out)
    allowed = (feats[:, 0:1] == docs_ref[...]) & (iota2((rows, rows), 0) <= iota2((rows, rows), 1))
    bias = jnp.where(allowed, 0.0, MASKED)
    log_rows = log_decay.T
    front = iota2((rows, LANES), 1) < LANES // 2
    gram_grad = jnp.zeros((rows, rows), F32)
    lane_of = iota2((rows, LANES), 1)
    row_of = iota2((LANES, rows), 0)
    sent = jnp.zeros((rows, LANES), F32)
    received = jnp.zeros((LANES, rows), F32)
    inside_grads = []
    for pair in range(width // LANES):
        lanes = slice(pair * LANES, (pair + 1) * LANES)
        dy = dscan[:, lanes].astype(BF)
        part = scaled[:, lanes]
        stacked = jnp.concatenate([jnp.where(front, part, 0.0), jnp.where(front, 0.0, part)], axis=0)
        cross = mm_nt(stacked, dy)
        mixes = []
        for j, h in enumerate((2 * pair, 2 * pair + 1)):
            decay = jnp.exp(log_rows[h : h + 1, :] - log_decay[:, h : h + 1] + bias)
            mix = gram * decay
            mixes.append(mix.astype(BF))
            dmix = cross[j * rows : (j + 1) * rows, :]
            gram_grad = gram_grad + dmix * decay
            flow = dmix * mix
            sent = jnp.where(lane_of == h, jnp.sum(flow, axis=1, keepdims=True), sent)
            received = jnp.where(row_of == h, jnp.sum(flow, axis=0, keepdims=True), received)
        grads = mm(jnp.concatenate(mixes, axis=0), dy)
        inside_grads.append(jnp.where(front, grads[:rows], grads[rows:]))
    dscaled = jnp.concatenate(inside_grads, axis=1) + leave_w * passed
    dkey_in = dkey_in + mm(gram_grad, key_out)
    dkey_out = dkey_out + mm_tn(gram_grad, key_in)
    reduced = jnp.dot(
        split_lanes(
            jnp.concatenate([enter_terms, leave_terms, dscaled * values, jnp.broadcast_to(carry_terms, (8, width))], axis=0), 1
        ),
        reduce_ref[...],
        preferred_element_type=F32,
    )
    after = reduced[:rows] + received.T - sent
    upper = (iota2((rows, rows), 0) <= iota2((rows, rows), 1)).astype(F32)
    strict = (iota2((rows, rows), 0) > iota2((rows, rows), 1)).astype(F32)
    decay_grad = exact_mm(upper, after) + exact_mm(strict, reduced[rows : 2 * rows]) + reduced[3 * rows : 3 * rows + 1]
    dstep = decay_grad * heads_ref[1:2, :] + reduced[2 * rows : 3 * rows]
    draw = dstep * sigmoid(raw)
    grads_ref[:, 2 * width + 2 * states :] = draw.astype(BF)
    hsums_ref[0:1, :] += jnp.sum(draw, axis=0, keepdims=True)
    hsums_ref[1:2, :] += jnp.sum(decay_grad * step, axis=0, keepdims=True) * heads_ref[1:2, :]
    dvalues = dscaled * step_w + dscan * taps_ref[5:6, :]
    dpre = dvalues * (pre_gate * (1.0 + pre * (1.0 - pre_gate)))
    dboth = jnp.concatenate([dkey_in, dkey_out], axis=1)
    dpre_bc = dboth * (bc_gate * (1.0 + pre_bc * (1.0 - bc_gate)))
    for dpre_now, buffer, dbuffer, taps, totals, lanes in (
        (dpre, xbuf, dxbuf, taps_ref, sums_ref, slice(width, 2 * width)),
        (dpre_bc, bcbuf, dbcbuf, staps_ref, ssums_ref, slice(2 * width, 2 * width + 2 * states)),
    ):
        dbuffer[0:rows, :] = dpre_now
        grad = dpre_now * taps[3:4, :]
        totals[3:4, :] += jnp.sum(dpre_now * buffer[8 : 8 + rows, :], axis=0, keepdims=True)
        totals[4:5, :] += jnp.sum(dpre_now, axis=0, keepdims=True)
        for k in range(1, 4):
            grad = grad + dbuffer[k : k + rows, :] * feats[:, 5 + k : 6 + k] * taps[3 - k : 4 - k, :]
            totals[3 - k : 4 - k, :] += jnp.sum(
                dpre_now * buffer[8 - k : 8 - k + rows, :] * feats[:, k : k + 1], axis=0, keepdims=True
            )
        grads_ref[:, lanes] = grad.astype(BF)
        dbuffer[rows : rows + 8, :] = dbuffer[0:8, :]


def expand_matrix(width):
    one = np.arange(LANES)[:, None] == np.arange(width)[None, :] // (LANES // 2)
    return np.concatenate([one, one], axis=0).astype(ml_dtypes.bfloat16)


def spec(block, index):
    return pl.BlockSpec(block, index)


def mamba_forward(feats, doc_row, ssm_in, taps, staps, heads, gain, width, states2):
    total = ssm_in.shape[0]
    rows = CHUNK
    count = total // rows
    block = lambda w, place=0: spec((rows, w), lambda i: (i, place))
    whole = lambda a: spec(a.shape, lambda i: (0,) * a.ndim)
    expand = expand_matrix(width)
    return pl.pallas_call(
        mamba_fwd_kernel,
        grid=(count,),
        in_specs=[
            block(LANES), spec((1, rows), lambda i: (0, i)), block(width, 1), block(states2, 2 * width // states2),
            block(LANES, (2 * width + states2) // LANES), block(width), whole(taps), whole(staps), whole(heads), whole(expand), whole(gain),
        ],
        out_specs=[block(width), block(width), spec((8, LANES), lambda i: (i, 0)), spec((1, states2 // 2, width), lambda i: (i, 0, 0))],
        out_shape=[
            jax.ShapeDtypeStruct((total, width), F32),
            jax.ShapeDtypeStruct((total, width), BF),
            jax.ShapeDtypeStruct((8 * count, LANES), F32),
            jax.ShapeDtypeStruct((count, states2 // 2, width), BF),
        ],
        scratch_shapes=[
            pltpu.VMEM((rows + 8, width), F32), pltpu.VMEM((rows + 8, states2), F32), pltpu.VMEM((states2 // 2, width), F32),
        ],
        compiler_params=pltpu.CompilerParams(vmem_limit_bytes=32 * 2**20),
        cost_estimate=pl.CostEstimate(flops=20 * 10**9, bytes_accessed=total * width * 20, transcendentals=total * width * 4),
        name="mamba_fwd",
    )(feats, doc_row, ssm_in, ssm_in, ssm_in, ssm_in, taps, staps, heads, expand, gain)


def mamba_backward(feats, doc_row, squares, inners, ssm_in, scan, states, norm_grad, taps, staps, heads, gain, width, states2):
    total = ssm_in.shape[0]
    rows = CHUNK
    count = total // rows
    back = lambda i: count - 1 - i
    block = lambda w, place=0: spec((rows, w), lambda i: (back(i), place))
    before = lambda w, place=0: spec((8, w), lambda i: (jnp.maximum(back(i) * (rows // 8) - 1, 0), place))
    whole = lambda a: spec(a.shape, lambda i: (0,) * a.ndim)
    expand = expand_matrix(width)
    reduce = np.concatenate([expand[:LANES].T] * 2, axis=0)
    totals = lambda w: spec((8, w), lambda i: (0, 0))
    strip = spec((8, LANES), lambda i: (back(i), 0))
    return pl.pallas_call(
        mamba_bwd_kernel,
        grid=(count,),
        in_specs=[
            block(LANES), strip, strip, strip, strip, spec((1, rows), lambda i: (0, back(i))), block(width, 1), before(width, 1),
            block(states2, 2 * width // states2), before(states2, 2 * width // states2), block(LANES, (2 * width + states2) // LANES),
            block(width), block(width), spec((1, states2 // 2, width), lambda i: (back(i), 0, 0)), block(width),
            whole(taps), whole(staps), whole(heads), whole(expand), whole(reduce), whole(gain),
        ],
        out_specs=[block(2 * width + states2 + LANES), totals(width), totals(states2), totals(LANES)],
        out_shape=[
            jax.ShapeDtypeStruct((total, 2 * width + states2 + LANES), BF),
            jax.ShapeDtypeStruct((8, width), F32),
            jax.ShapeDtypeStruct((8, states2), F32),
            jax.ShapeDtypeStruct((8, LANES), F32),
        ],
        scratch_shapes=[
            pltpu.VMEM((rows + 8, width), F32), pltpu.VMEM((rows + 8, states2), F32),
            pltpu.VMEM((rows + 8, width), F32), pltpu.VMEM((rows + 8, states2), F32), pltpu.VMEM((states2 // 2, width), F32),
        ],
        compiler_params=pltpu.CompilerParams(vmem_limit_bytes=32 * 2**20),
        cost_estimate=pl.CostEstimate(flops=35 * 10**9, bytes_accessed=total * width * 24, transcendentals=total * width * 5),
        name="mamba_bwd",
    )(feats, *squares, *inners, doc_row, ssm_in, ssm_in, ssm_in, ssm_in, ssm_in, ssm_in, scan, states, norm_grad, taps, staps, heads, expand, reduce, gain)


QBLOCK = 256


def swap_halves(values):
    lane = iota2(values.shape, 1) % (LANES // 2)
    return jnp.where(lane < LANES // 4, pltpu.roll(values, LANES - LANES // 4, 1), pltpu.roll(values, LANES // 4, 1))


def stack_heads(part):
    front = iota2(part.shape, 1) < LANES // 2
    zero = jnp.zeros_like(part)
    return jnp.concatenate([jnp.where(front, part, zero), jnp.where(front, zero, part)], axis=0)


def attention_fwd_kernel(
    groups, docs_col_ref, docs_ref, q_ref, kv_ref, cos_ref, sin_ref, low_ref, square_ref, square_in_ref, out_ref, lse_ref, qrot_ref, keys_ref, values_ref,
):
    total = q_ref.shape[0]
    wide = low_ref.shape[1]
    for i in range(total // LANES):
        piece = slice(i * LANES, (i + 1) * LANES)
        scale = as_column(gated_scale(square_ref[8 * i : 8 * i + 1, :] + square_in_ref[8 * i : 8 * i + 1, :]))
        out_ref[piece, :wide] = (low_ref[piece, :].astype(F32) * scale).astype(BF)
    pairs = q_ref.shape[1] // LANES
    block = min(QBLOCK, total)
    cos, sin = cos_ref[...], sin_ref[...]
    front = iota2((total, LANES), 1) < LANES // 2
    for g in range(groups):
        lanes = slice(g * LANES, (g + 1) * LANES)
        raw = kv_ref[:, lanes]
        turned = raw * cos + swap_halves(raw) * sin
        keys_ref[:, lanes] = jnp.where(front, turned, pltpu.roll(turned, LANES // 2, 1)).astype(BF)
        values_ref[:, lanes] = jnp.where(front, pltpu.roll(raw, LANES // 2, 1), raw).astype(BF)
    for p in range(pairs):
        lanes = slice(p * LANES, (p + 1) * LANES)
        raw = q_ref[:, lanes]
        qrot_ref[:, lanes] = ((raw * cos + swap_halves(raw) * sin).astype(BF).astype(F32) * (LANES // 2) ** -0.5).astype(BF)
    front = iota2((block, LANES), 1) < LANES // 2
    lane_of = iota2((block, LANES), 1)
    for start in range(0, total, block):
        rows, end = slice(start, start + block), start + block
        allowed = (docs_col_ref[rows, 0:1] == docs_ref[:, :end]) & (
            iota2((block, end), 0) + start >= iota2((block, end), 1)
        )
        bias = jnp.where(allowed, 0.0, MASKED)
        bias = jnp.concatenate([bias, bias], axis=0)
        sums = jnp.zeros((block, LANES), F32)
        for p in range(pairs):
            lanes = slice(p * LANES, (p + 1) * LANES)
            g = p * groups // pairs
            kv = slice(g * LANES, (g + 1) * LANES)
            scores = mm_nt(stack_heads(qrot_ref[rows, lanes]), keys_ref[:end, kv]) + bias
            top = jnp.max(scores, axis=1, keepdims=True)
            raised = jnp.exp(scores - top)
            whole = jnp.sum(raised, axis=1, keepdims=True)
            mixed = mm(raised, values_ref[:end, kv]) / whole
            out_ref[rows, wide + p * LANES : wide + (p + 1) * LANES] = jnp.where(front, mixed[:block], mixed[block:]).astype(BF)
            logs = top + jnp.log(whole)
            sums = jnp.where(lane_of == 2 * p, logs[:block], sums)
            sums = jnp.where(lane_of == 2 * p + 1, logs[block:], sums)
        lse_ref[rows, :] = sums


def attention_bwd_kernel(
    groups, docs_col_ref, docs_ref, qrot_ref, keys_ref, values_ref, lse_ref, mix_grad_ref, mix_ref, cos_ref, sin_ref,
    grads_ref, inner_ref, dk_acc, dv_acc,
):
    total = qrot_ref.shape[0]
    wide = mix_ref.shape[1] - qrot_ref.shape[1]
    for i in range(total // LANES):
        piece = slice(i * LANES, (i + 1) * LANES)
        products = mix_grad_ref[piece, :wide].astype(F32) * mix_ref[piece, :wide].astype(F32)
        inner = jnp.sum(products, axis=1, keepdims=True)
        inner_ref[8 * i : 8 * i + 8, :] = jnp.broadcast_to(inner, (LANES, LANES)).T[0:8, :]
    pairs = qrot_ref.shape[1] // LANES
    block = min(QBLOCK, total)
    dk_acc[...] = jnp.zeros_like(dk_acc)
    dv_acc[...] = jnp.zeros_like(dv_acc)
    front = iota2((block, LANES), 1) < LANES // 2
    for start in range(0, total, block):
        rows, end = slice(start, start + block), start + block
        allowed = (docs_col_ref[:end, 0:1] == docs_ref[:, rows]) & (
            iota2((end, block), 0) <= iota2((end, block), 1) + start
        )
        bias = jnp.where(allowed, 0.0, MASKED)
        logs = lse_ref[rows, :].T
        cos, sin = cos_ref[rows, :], sin_ref[rows, :]
        for p in range(pairs):
            lanes = slice(p * LANES, (p + 1) * LANES)
            g = p * groups // pairs
            kv = slice(g * LANES, (g + 1) * LANES)
            keys, values = keys_ref[:end, kv], values_ref[:end, kv]
            queries = stack_heads(qrot_ref[rows, lanes])
            ups = stack_heads(mix_grad_ref[rows, wide + p * LANES : wide + (p + 1) * LANES])
            shift = jnp.concatenate([bias - logs[2 * p : 2 * p + 1], bias - logs[2 * p + 1 : 2 * p + 2]], axis=1)
            probs = jnp.exp(mm_nt(keys, queries) + shift)
            grads = mm_nt(values, ups)
            centre = jnp.sum(probs * grads, axis=0, keepdims=True)
            score_grads = (probs * (grads - centre)).astype(BF)
            dk_acc[:end, kv] += mm(score_grads, queries)
            dv_acc[:end, kv] += mm(probs, ups)
            dq = mm_tn(score_grads, keys)
            dq = jnp.where(front, dq[:block], dq[block:]) * (LANES // 2) ** -0.5
            grads_ref[rows, lanes] = (dq * cos - swap_halves(dq) * sin).astype(BF)
    front = iota2((total, LANES), 1) < LANES // 2
    for g in range(groups):
        kv = slice(g * LANES, (g + 1) * LANES)
        dk, dv = dk_acc[:, kv], dv_acc[:, kv]
        dk = dk + pltpu.roll(dk, LANES // 2, 1)
        dk = dk * cos_ref[...] - swap_halves(dk) * sin_ref[...]
        dv = dv + pltpu.roll(dv, LANES // 2, 1)
        out = slice((pairs + g) * LANES, (pairs + g + 1) * LANES)
        grads_ref[:, out] = jnp.where(front, dk, dv).astype(BF)


def attention_forward(groups, doc_col, doc_row, qkv, cos, sin, query_width, low, squares):
    total = qkv.shape[0]
    kv_width = qkv.shape[1] - query_width
    whole = lambda a: spec(a.shape, lambda i: (0,) * a.ndim)
    columns = lambda w, place=0: spec((total, w), lambda i: (0, place))
    return pl.pallas_call(
        functools.partial(attention_fwd_kernel, groups),
        grid=(1,),
        in_specs=[whole(doc_col), whole(doc_row), columns(query_width), columns(kv_width, query_width // kv_width), whole(cos), whole(sin), whole(low), whole(squares[0]), whole(squares[1])],
        out_specs=[columns(low.shape[1] + query_width), columns(LANES), columns(query_width), columns(kv_width), columns(kv_width)],
        out_shape=[
            jax.ShapeDtypeStruct((total, low.shape[1] + query_width), BF), jax.ShapeDtypeStruct((total, LANES), F32),
            jax.ShapeDtypeStruct((total, query_width), BF), jax.ShapeDtypeStruct((total, kv_width), BF),
            jax.ShapeDtypeStruct((total, kv_width), BF),
        ],
        compiler_params=pltpu.CompilerParams(vmem_limit_bytes=32 * 2**20),
        cost_estimate=pl.CostEstimate(flops=12 * 10**9, bytes_accessed=total * query_width * 10, transcendentals=total * total * 2),
        name="attention_fwd",
    )(doc_col, doc_row, qkv, qkv, cos, sin, low, *squares)


def attention_backward(groups, doc_col, doc_row, qrot, keys, values, lse, mix_grad, mix, cos, sin):
    total = qrot.shape[0]
    return pl.pallas_call(
        functools.partial(attention_bwd_kernel, groups),
        out_shape=[jax.ShapeDtypeStruct((total, qrot.shape[1] + keys.shape[1]), BF), jax.ShapeDtypeStruct((total // 16, LANES), F32)],
        scratch_shapes=[pltpu.VMEM(keys.shape, F32), pltpu.VMEM(keys.shape, F32)],
        compiler_params=pltpu.CompilerParams(vmem_limit_bytes=32 * 2**20),
        cost_estimate=pl.CostEstimate(flops=16 * 10**9, bytes_accessed=total * qrot.shape[1] * 10, transcendentals=total * total * 2),
        name="attention_bwd",
    )(doc_col, doc_row, qrot, keys, values, lse, mix_grad, mix, cos, sin)


def flipped(index, mask):
    bit = 1
    while bit <= mask:
        if mask & bit:
            index = index + bit * (1 - 2 * ((index // bit) % 2))
        bit *= 2
    return index


def greet(partners):
    barrier = pltpu.get_barrier_semaphore()
    for axis, place in partners:
        pl.semaphore_signal(barrier, inc=1, device_id={axis: place}, device_id_type=pl.DeviceIdType.MESH)
    pl.semaphore_wait(barrier, len(partners))


def remote(source, target, send, recv, axis, place):
    return pltpu.make_async_remote_copy(
        src_ref=source, dst_ref=target, send_sem=send, recv_sem=recv,
        device_id={axis: place}, device_id_type=pl.DeviceIdType.MESH,
    )


def gather_kernel(
    count, tensors, shard_ref, tokens_ref, cotangent_ref, gain_ref, full_ref, all_tokens_ref, all_cotangent_ref, normed_ref, scale_ref,
    own_sem, send_sems, recv_sems, core_send, core_recv,
):
    unit, columns = shard_ref.shape
    levels = count // 4
    me = lax.axis_index("fsdp")
    half = columns // 2 // LANES * LANES
    parts = (slice(0, half), slice(half, columns))
    neighbours = (flipped(me, 1), flipped(me, 2))
    far = [flipped(me, 4 * d) for d in range(1, levels)]
    core = lax.axis_index("tensor")
    cores = [flipped(core, k) for k in range(1, tensors)]
    greet([("fsdp", p) for p in neighbours] + [("fsdp", p) for p in far] + [("tensor", p) for p in cores])

    def rows(owner):
        return pl.ds(pl.multiple_of(owner * unit, unit), unit)

    started = []

    def send(source, owner, lanes, slot, place):
        copy = remote(source, full_ref.at[rows(owner), lanes], send_sems.at[slot], recv_sems.at[slot], "fsdp", place)
        copy.start()
        started.append(copy)
        return copy

    def arrival(owner, lanes, slot):
        piece = full_ref.at[rows(owner), lanes]
        return remote(piece, piece, send_sems.at[slot], recv_sems.at[slot], "fsdp", neighbours[0])

    everything = slice(0, columns)
    own = pltpu.make_async_copy(shard_ref, full_ref.at[rows(me), :], own_sem)
    own.start()
    for d in range(1, levels):
        send(shard_ref, me, everything, d, far[d - 1])
    base = levels
    for axis in range(2):
        send(shard_ref, me, everything, base + axis * levels, neighbours[axis])
    cross = base + 2 * levels
    own_rows = tokens_ref.shape[0]
    share = lambda owner: pl.ds(pl.multiple_of(owner * own_rows, own_rows), own_rows)
    exchanges = []
    for k, place in enumerate(cores):
        for j, (source, target) in enumerate(((tokens_ref, all_tokens_ref), (cotangent_ref, all_cotangent_ref))):
            copy = remote(
                source, target.at[share(core), :], core_send.at[2 * k + j], core_recv.at[2 * k + j], "tensor", place
            )
            copy.start()
            exchanges.append(copy)
    all_tokens_ref[share(core), :] = tokens_ref[...]
    all_cotangent_ref[share(core), :] = cotangent_ref[...]
    for copy in exchanges:
        copy.wait()

    def norm(i, carry):
        piece = pl.ds(pl.multiple_of(i * LANES, LANES), LANES)
        values = all_tokens_ref[piece, :].astype(F32)
        scale = lax.rsqrt(jnp.mean(values * values, axis=1, keepdims=True) + EPS)
        scale_ref[piece, :] = scale
        normed_ref[piece, :] = (values * scale * gain_ref[...]).astype(BF)
        return carry

    lax.fori_loop(0, normed_ref.shape[0] // LANES, norm, 0)

    def pass_on(d):
        for axis in range(2):
            owner = flipped(neighbours[axis], 4 * d)
            arrival(owner, everything, base + axis * levels + d).wait_recv()
            piece = full_ref.at[rows(owner), parts[axis]]
            send(piece, owner, parts[axis], cross + axis * levels + d, neighbours[1 - axis])

    for d in range(1, levels):
        arrival(far[d - 1], everything, d).wait_recv()
        for axis in range(2):
            send(full_ref.at[rows(far[d - 1]), :], far[d - 1], everything, base + axis * levels + d, neighbours[axis])
        pass_on(d - 1)
    pass_on(levels - 1)
    for d in range(levels):
        for axis in range(2):
            owner = flipped(me, 4 * d + 3)
            arrival(owner, parts[axis], cross + axis * levels + d).wait_recv()
    for copy in started:
        copy.wait_send()
    own.wait()


def gather_weights(shard, tokens, cotangent, gain, count, tensors, collective_id):
    unit, columns = shard.shape
    own_rows, hidden = tokens.shape
    total = own_rows * tensors
    slots = 5 * (count // 4)
    vmem, anywhere = pl.BlockSpec(memory_space=pltpu.VMEM), pl.BlockSpec(memory_space=pl.ANY)
    low = jax.ShapeDtypeStruct((total, hidden), BF)
    return pl.pallas_call(
        functools.partial(gather_kernel, count, tensors),
        in_specs=[anywhere, vmem, vmem, vmem],
        out_specs=[anywhere, vmem, vmem, vmem, vmem],
        out_shape=[jax.ShapeDtypeStruct((count * unit, columns), shard.dtype), low, low, low, jax.ShapeDtypeStruct((total, 1), F32)],
        scratch_shapes=[
            pltpu.SemaphoreType.DMA, pltpu.SemaphoreType.DMA((slots,)), pltpu.SemaphoreType.DMA((slots,)),
            pltpu.SemaphoreType.DMA((2 * (tensors - 1),)), pltpu.SemaphoreType.DMA((2 * (tensors - 1),)),
        ],
        compiler_params=pltpu.CompilerParams(collective_id=collective_id, has_side_effects=True, vmem_limit_bytes=32 * 2**20),
        cost_estimate=pl.CostEstimate(flops=0, bytes_accessed=2 * count * unit * columns * 2, transcendentals=0),
        name="gather_weights",
    )(shard, tokens, cotangent, gain)


def scatter_kernel(count, tensors, paths, split, state_at, kv_at, kv_heads, *refs):
    number = len(paths)
    grads, small_ref = refs[:number], refs[number]
    outs, small_out, shared_out = refs[number + 1 : 2 * number + 1], refs[2 * number + 1], refs[2 * number + 2]
    scratch = refs[2 * number + 3 :]
    cross, along_x, along_y, far_in, staged, far_out = (scratch[k * number : (k + 1) * number] for k in range(6))
    sums, arrived, shared, shared_in, send_sems, recv_sems, sum_send, sum_recv, core_send, core_recv = scratch[6 * number :]
    levels = count // 4
    unit = grads[0].shape[0] // count
    me = lax.axis_index("fsdp")
    core = lax.axis_index("tensor")
    near = (flipped(me, 1), flipped(me, 2))
    far = [None] + [flipped(me, 4 * d) for d in range(1, levels)]
    bits = [1 << k for k in range((count - 1).bit_length())]
    stages = [("fsdp", flipped(me, bit)) for bit in bits]
    cores = [("tensor", flipped(core, 1 << k)) for k in range((tensors - 1).bit_length())]
    greet([("fsdp", p) for p in near] + [("fsdp", p) for p in far[1:]] + cores)
    stages = stages + cores
    started = []

    def rows(owner):
        return pl.ds(pl.multiple_of(owner * unit, unit), unit)

    def link(source, target, slot, place):
        return remote(source, target, send_sems.at[slot], recv_sems.at[slot], "fsdp", place)

    def send(source, target, slot, place):
        copy = link(source, target, slot, place)
        copy.start()
        started.append(copy)

    def slot(i, kind, d):
        return (i * 4 + kind) * levels + d

    pending = []
    settled = []

    def next_stage():
        done = len(settled)
        if done < len(pending):
            pending[done].wait()
            sums[done + 1] = sums[done] + arrived[done]
            settled.append(done)
        if len(settled) == len(pending) and len(pending) < len(stages):
            done = len(pending)
            axis, place = stages[done]
            copy = remote(sums.at[done], arrived.at[done], sum_send.at[done], sum_recv.at[done], axis, place)
            copy.start()
            pending.append(copy)

    def begin(d):
        for i, path in enumerate(paths):
            send(grads[i].at[rows(flipped(me, 4 * d + 3)), :], cross[i].at[d], slot(i, 0, d), near[1 - path])

    def middle(d):
        for i, path in enumerate(paths):
            link(cross[i].at[d], cross[i].at[d], slot(i, 0, d), near[0]).wait_recv()
            staged[i][d] = (grads[i][rows(flipped(near[path], 4 * d)), :].astype(F32) + cross[i][d].astype(F32)).astype(BF)
            send(staged[i].at[d], (along_x, along_y)[path][i].at[d], slot(i, 1 + path, d), near[path])
            raw = 1 - path
            send(grads[i].at[rows(flipped(near[raw], 4 * d)), :], (along_x, along_y)[raw][i].at[d], slot(i, 1 + raw, d), near[raw])

    def finish(d):
        for i, path in enumerate(paths):
            link(along_x[i].at[d], along_x[i].at[d], slot(i, 1, d), near[0]).wait_recv()
            link(along_y[i].at[d], along_y[i].at[d], slot(i, 2, d), near[0]).wait_recv()
            total = grads[i][rows(flipped(me, 4 * d)), :].astype(F32) + along_x[i][d].astype(F32) + along_y[i][d].astype(F32)
            if d:
                far_out[i][d - 1] = total.astype(BF)
                send(far_out[i].at[d - 1], far_in[i].at[d - 1], slot(i, 3, d), far[d])
            else:
                outs[i][...] = total

    order = list(range(levels - 1, -1, -1))
    sums[0] = small_ref[...]
    begin(order[0])
    next_stage()
    begin(order[1])
    for k in range(1, levels + 2):
        if k <= levels:
            middle(order[k - 1])
        if k + 1 < levels:
            begin(order[k + 1])
        if k >= 2:
            finish(order[k - 2])
        next_stage()
    while len(settled) < len(stages):
        next_stage()
    for d in order[:-1]:
        for i in range(number):
            link(far_in[i].at[d - 1], far_in[i].at[d - 1], slot(i, 3, d), near[0]).wait_recv()
            outs[i][...] += far_in[i][d - 1].astype(F32)
    states2, leading = state_at[1] - state_at[0], core * (shared.shape[2] - state_at[1] + state_at[0]) // (tensors * LANES)
    shared[0, :, :states2] = outs[0][:, state_at[0] : state_at[1]]
    for g in range((shared.shape[2] - states2) // LANES):
        value = jnp.zeros((unit, LANES), F32)
        for j in range(kv_heads):
            value = jnp.where(leading + j == g, outs[1][:, kv_at + j * LANES : kv_at + (j + 1) * LANES], value)
        shared[0, :, states2 + g * LANES : states2 + (g + 1) * LANES] = value
    for k, (axis, place) in enumerate(cores):
        copy = remote(shared.at[k], shared_in.at[k], core_send.at[k], core_recv.at[k], axis, place)
        copy.start()
        copy.wait()
        shared[k + 1] = shared[k] + shared_in[k]
    shared_out[...] = shared[len(cores)]
    small_out[:, :split] = sums[len(bits), :, :split]
    small_out[:, split:] = sums[len(stages), :, split:]
    for copy in started:
        copy.wait_send()


def scatter_grads(grads, paths, small, split, state_at, kv_at, kv_heads, count, tensors, collective_id):
    unit = grads[0].shape[0] // count
    levels = count // 4
    stages = (count - 1).bit_length() + (tensors - 1).bit_length()
    vmem = pl.BlockSpec(memory_space=pltpu.VMEM)
    buffers = []
    for slots in (levels, levels, levels, levels - 1, levels, levels - 1):
        buffers += [pltpu.VMEM((slots, unit, g.shape[1]), BF) for g in grads]
    buffers += [pltpu.VMEM((stages + 1,) + small.shape, F32), pltpu.VMEM((stages,) + small.shape, F32)]
    links = 4 * levels * len(grads)
    steps = (tensors - 1).bit_length()
    shared = state_at[1] - state_at[0] + KEYVAL_HEADS * LANES
    buffers += [pltpu.VMEM((steps + 1, unit, shared), F32), pltpu.VMEM((steps, unit, shared), F32)]
    buffers += [pltpu.SemaphoreType.DMA((links,))] * 2 + [pltpu.SemaphoreType.DMA((stages,))] * 2 + [pltpu.SemaphoreType.DMA((steps,))] * 2
    size = sum(g.shape[1] for g in grads)
    return pl.pallas_call(
        functools.partial(scatter_kernel, count, tensors, tuple(paths), split, state_at, kv_at, kv_heads),
        in_specs=[vmem] * (len(grads) + 1),
        out_specs=[vmem] * (len(grads) + 2),
        out_shape=[jax.ShapeDtypeStruct((unit, g.shape[1]), F32) for g in grads]
        + [jax.ShapeDtypeStruct(small.shape, F32), jax.ShapeDtypeStruct((unit, shared), F32)],
        scratch_shapes=buffers,
        compiler_params=pltpu.CompilerParams(collective_id=collective_id, has_side_effects=True, vmem_limit_bytes=48 * 2**20),
        cost_estimate=pl.CostEstimate(flops=0, bytes_accessed=2 * count * unit * size * 2, transcendentals=0),
        name="scatter_grads",
    )(*grads, small)


def tensor_swap(values):
    return lax.ppermute(values, "tensor", [(0, 1), (1, 0)])


def tensor_pair(values):
    if lax.axis_size("tensor") == 2:
        return values, tensor_swap(values)
    return lax.psum(values.astype(F32), "tensor").astype(values.dtype), jnp.zeros_like(values)


def pad_to(values, size, axis=-1):
    pads = [(0, 0)] * values.ndim
    pads[axis] = (0, size - values.shape[axis])
    return jnp.pad(values, pads) if size > values.shape[axis] else values


def pack_kernel(
    mixer_ref, state_ref, step_ref, query_ref, keyval_ref, proj_ref, attention_ref, gate_up_ref, down_ref,
    first_ref, second_ref,
):
    unit = state_ref.shape[0]
    width, wide = mixer_ref.shape[2], -(-mixer_ref.shape[2] // LANES) * LANES
    same = (iota2((unit, unit), 0) == iota2((unit, unit), 1)).astype(BF)
    place = 0

    def put(out_ref, value, size):
        nonlocal place
        value = value.astype(BF)
        if size > value.shape[1]:
            value = jnp.concatenate([value, jnp.zeros((unit, size - value.shape[1]), BF)], axis=1)
        out_ref[:, place : place + size] = value
        place += size

    put(first_ref, mixer_ref[:, 0, :], wide)
    put(first_ref, mixer_ref[:, 1, :], wide)
    put(first_ref, state_ref[...], state_ref.shape[1])
    put(first_ref, lax.dot_general(same, step_ref[...].astype(BF), (((1,), (1,)), ((), ())), preferred_element_type=F32), LANES)
    query_wide = -(-query_ref.shape[1] // LANES) * LANES
    put(first_ref, query_ref[...], query_wide)
    put(first_ref, keyval_ref[...], keyval_ref.shape[1])
    put(first_ref, proj_ref[...], wide)
    put(first_ref, attention_ref[...], query_wide)
    place = 0
    put(second_ref, gate_up_ref[:, 0, :], gate_up_ref.shape[2])
    put(second_ref, gate_up_ref[:, 1, :], gate_up_ref.shape[2])
    put(second_ref, down_ref[...], down_ref.shape[1])


def pack_weights(mixer, state, step, query, keyval, proj, attention, gate_up, down):
    unit = state.shape[0]
    lanes = lambda size: -(-size // LANES) * LANES
    first = 3 * lanes(mixer.shape[2]) + state.shape[1] + LANES + 2 * lanes(query.shape[1]) + keyval.shape[1]
    second = 2 * gate_up.shape[2] + down.shape[1]
    return pl.pallas_call(
        pack_kernel,
        out_shape=[jax.ShapeDtypeStruct((unit, first), BF), jax.ShapeDtypeStruct((unit, second), BF)],
        compiler_params=pltpu.CompilerParams(vmem_limit_bytes=32 * 2**20),
        name="pack_weights",
    )(mixer, state, step, query, keyval, proj, attention, gate_up, down)


def table_kernel(
    docs_ref, conv_ref, conv_bias_ref, state_conv_ref, state_bias_ref, step_bias_ref, decay_ref, skip_ref,
    feats_ref, cos_ref, sin_ref, taps_ref, state_taps_ref, heads_ref,
):
    total = docs_ref.shape[1]
    docs = docs_ref[...]
    tall = jnp.broadcast_to(docs, (LANES, total)).T
    spot = iota2((1, total), 1)
    begin = jnp.sum((tall[:, 0:1] < docs).astype(F32), axis=0, keepdims=True)
    rows = [docs]
    eight = jnp.broadcast_to(docs, (8, total))
    for k in (1, 2, 3):
        rows.append(jnp.where(spot >= k, (pltpu.roll(eight, k, 1)[0:1] == docs).astype(F32), 0.0))
    blocks = [docs[:, i : i + CHUNK] for i in range(0, total, CHUNK)]
    before = [jnp.full((1, 1), -1.0, F32)] + [v[:, CHUNK - 1 :] for v in blocks[:-1]]
    rows.append(jnp.concatenate([(v == w).astype(F32) for v, w in zip(blocks, before)], axis=1))
    rows.append(jnp.concatenate([(v == v[:, CHUNK - 1 :]).astype(F32) for v in blocks], axis=1))
    for k in (1, 2, 3):
        rows.append(jnp.where(spot < total - k, (pltpu.roll(eight, total - k, 1)[0:1] == docs).astype(F32), 0.0))
    rows.append(spot.astype(F32) - begin)
    rows.append(jnp.zeros((LANES - len(rows), total), F32))
    feats = jnp.concatenate(rows, axis=0).T
    feats_ref[...] = feats
    lane = iota2((1, LANES), 1)
    rates = jnp.exp((lane % (HEAD_SIZE // 2)).astype(F32) * (-2.0 * math.log(THETA) / HEAD_SIZE))
    angles = feats[:, 9:10] * rates
    cos_ref[...] = jnp.cos(angles)
    sin_ref[...] = jnp.sin(angles) * jnp.where(lane % HEAD_SIZE < HEAD_SIZE // 2, -1.0, 1.0)
    width, heads = conv_ref.shape[1], skip_ref.shape[1]
    taps_ref[...] = jnp.zeros_like(taps_ref)
    taps_ref[0:4, :width] = conv_ref[...]
    taps_ref[4:5, :width] = conv_bias_ref[...]
    spread = (iota2((heads, width), 0) == iota2((heads, width), 1) // (width // heads)).astype(F32)
    taps_ref[5:6, :width] = exact_mm(jnp.broadcast_to(skip_ref[...], (8, heads)), spread)[0:1]
    state_taps_ref[...] = jnp.zeros_like(state_taps_ref)
    state_taps_ref[0:4, :] = state_conv_ref[...]
    state_taps_ref[4:5, :] = state_bias_ref[...]
    heads_ref[...] = jnp.zeros_like(heads_ref)
    heads_ref[0:1, :heads] = step_bias_ref[...]
    heads_ref[1:2, :heads] = -jnp.exp(decay_ref[...])


def make_tables(docs, wide, conv, conv_bias, state_conv, state_bias, step_bias, decay, skip):
    total = docs.shape[1]
    shape = lambda r, c: jax.ShapeDtypeStruct((r, c), F32)
    return pl.pallas_call(
        table_kernel,
        out_shape=[shape(total, LANES), shape(total, LANES), shape(total, LANES), shape(8, wide), shape(8, state_conv.shape[1]), shape(8, LANES)],
        compiler_params=pltpu.CompilerParams(vmem_limit_bytes=32 * 2**20),
        name="make_tables",
    )(docs, conv, conv_bias[None], state_conv, state_bias[None], step_bias[None], decay[None], skip[None])


def second_norm_kernel(tokens_ref, part_ref, part_in_ref, gain_ref, middle_ref, second_ref, scale_ref):
    middle = tokens_ref[...].astype(F32) + part_ref[...].astype(F32) + part_in_ref[...].astype(F32)
    scale = lax.rsqrt(jnp.mean(middle * middle, axis=1, keepdims=True) + EPS)
    middle_ref[...] = middle
    scale_ref[...] = scale
    second_ref[...] = (middle * scale * gain_ref[...]).astype(BF)


def by_rows(kernel, name, rows, count, ins, outs, scalars=(), scratch=()):
    number = len(scalars)

    def place(shape, kind):
        if kind == "whole":
            return spec(shape, lambda i, *s: (0,) * len(shape))
        if kind == "own":
            return spec((rows, shape[1]), lambda i, *s: (s[0][0] * count + i, 0))
        return spec((rows, shape[1]), lambda i, *s: (i, 0))

    return pl.pallas_call(
        kernel,
        grid_spec=pltpu.PrefetchScalarGridSpec(
            num_scalar_prefetch=number,
            grid=(count,),
            in_specs=[place(v.shape, kind) for v, kind in ins],
            out_specs=[place((r, c), kind) for r, c, _, kind in outs],
        ),
        out_shape=[jax.ShapeDtypeStruct((r, c), dtype) for r, c, dtype, _ in outs],
        compiler_params=pltpu.CompilerParams(vmem_limit_bytes=40 * 2**20),
        name=name,
    )(*scalars, *(v for v, _ in ins))


def ffn_kernel(second_ref, up_ref, weights_ref, active_ref, grads_ref, out_ref, back_ref):
    ffn = active_ref.shape[1]
    gate_vals = jnp.dot(second_ref[...], weights_ref[:, : 2 * ffn], preferred_element_type=F32)
    active_grad = jnp.dot(up_ref[...], weights_ref[:, 2 * ffn :], preferred_element_type=F32)
    gate, up = gate_vals[:, :ffn], gate_vals[:, ffn:]
    sig = sigmoid(gate)
    silu = gate * sig
    active = (silu * up).astype(BF)
    active_ref[...] = active
    grads_ref[:, :ffn] = (active_grad * up * (sig + silu * (1.0 - sig))).astype(BF)
    grads_ref[:, ffn:] = (active_grad * silu).astype(BF)
    out_ref[...] = mm_nt(active, weights_ref[:, 2 * ffn :]).astype(BF)
    back_ref[...] = mm_nt(grads_ref[...], weights_ref[:, : 2 * ffn]).astype(BF)


def second_back_kernel(grad_ref, grad_in_ref, middle_ref, scale_ref, up_ref, gain_ref, low_ref, gain_grad_ref):
    @pl.when(pl.program_id(0) == 0)
    def _():
        gain_grad_ref[...] = jnp.zeros_like(gain_grad_ref)

    grad = grad_ref[...].astype(F32) + grad_in_ref[...].astype(F32)
    middle, scale = middle_ref[...], scale_ref[...]
    shape = middle * scale
    weighted = grad * gain_ref[...]
    inner = jnp.mean(weighted * shape, axis=1, keepdims=True)
    low_ref[...] = (up_ref[...].astype(F32) + scale * (weighted - shape * inner)).astype(BF)
    gain_grad_ref[0:1, :] += jnp.sum(grad * shape, axis=0, keepdims=True)


def output_kernel(core_ref, middle_ref, part_ref, part_in_ref, out_ref):
    out_ref[...] = (middle_ref[...] + part_ref[...].astype(F32) + part_in_ref[...].astype(F32)).astype(BF)


def input_back_kernel(core_ref, grad_ref, grad_in_ref, middle_grad_ref, tokens_ref, scale_ref, gain_ref, out_ref, gain_grad_ref):
    @pl.when(pl.program_id(0) == 0)
    def _():
        gain_grad_ref[...] = jnp.zeros_like(gain_grad_ref)

    grad = grad_ref[...].astype(F32) + grad_in_ref[...].astype(F32)
    scale = scale_ref[...]
    shape = tokens_ref[...].astype(F32) * scale
    weighted = grad * gain_ref[...]
    inner = jnp.mean(weighted * shape, axis=1, keepdims=True)
    out_ref[...] = middle_grad_ref[...].astype(F32) + scale * (weighted - shape * inner)
    gain_grad_ref[0:1, :] += jnp.sum(grad * shape, axis=0, keepdims=True)


def finish_kernel(
    sizes, ssm_ref, qkv_ref, mix_ref, shared_ref, small_ref, rest_ref,
    mixer_ref, state_ref, step_ref, conv_ref, conv_bias_ref, state_conv_ref, state_bias_ref, step_bias_ref, decay_ref, skip_ref,
    mixer_gain_ref, proj_ref, query_ref, keyval_ref, attention_ref, gate_up_ref, down_ref, second_gain_ref, input_gain_ref,
):
    wide, width, states2, heads, query_width, ffn = sizes
    mixer_ref[:, 0, :] = ssm_ref[:, :width]
    mixer_ref[:, 1, :] = ssm_ref[:, wide : wide + width]
    state_ref[...] = shared_ref[:, :states2]
    step_ref[...] = ssm_ref[:, 2 * wide + states2 : 2 * wide + states2 + heads]
    query_ref[...] = qkv_ref[:, :query_width]
    groups = [shared_ref[:, i : i + LANES] for i in range(states2, shared_ref.shape[1], LANES)]
    keyval_ref[:, 0, :] = jnp.concatenate([v[:, :HEAD_SIZE] for v in groups], axis=1)
    keyval_ref[:, 1, :] = jnp.concatenate([v[:, HEAD_SIZE:] for v in groups], axis=1)
    proj_ref[...] = mix_ref[:, :width]
    attention_ref[...] = mix_ref[:, wide : wide + query_width]
    gate_up_ref[:, 0, :] = rest_ref[:, :ffn].astype(F32)
    gate_up_ref[:, 1, :] = rest_ref[:, ffn : 2 * ffn].astype(F32)
    down_ref[...] = rest_ref[:, 2 * ffn :].astype(F32)
    conv_ref[...] = small_ref[0:4, :width]
    conv_bias_ref[...] = small_ref[4:5, :width]
    mixer_gain_ref[...] = small_ref[6:7, :width]
    place = iota2((width, heads), 0) // (width // heads)
    gather = (place == iota2((width, heads), 1)).astype(F32)
    skip_ref[...] = exact_mm(jnp.broadcast_to(small_ref[5:6, :width], (8, width)), gather)[0:1]
    step_bias_ref[...] = small_ref[0:1, wide : wide + heads]
    decay_ref[...] = small_ref[1:2, wide : wide + heads]
    base = wide + LANES
    state_conv_ref[...] = small_ref[0:4, base : base + states2]
    state_bias_ref[...] = small_ref[4:5, base : base + states2]
    base += states2
    for out_ref in (second_gain_ref, input_gain_ref):
        size = out_ref.shape[1]
        out_ref[...] = jnp.concatenate([small_ref[r : r + 1, base : base + size // 8] for r in range(8)], axis=1)
        base += size // 8


def body(
    layer_input, doc_ids, input_gain, mixer_weight, state_weight, step_weight, conv_weight, conv_bias, state_conv,
    state_conv_bias, step_bias, decay_log, skip_gain, mixer_gain, mixer_proj, query_weight, keyval_projection,
    attention_proj, second_gain, gate_up, down_proj, cotangent,
):
    tensor_count = lax.axis_size("tensor")
    tensor_index = lax.axis_index("tensor")
    fsdp_count = lax.axis_size("fsdp")
    own_rows, hidden = layer_input.shape
    unit = state_weight.shape[0]
    seq_count, seq_length = doc_ids.shape
    total = seq_count * seq_length
    heads = step_bias.shape[0]
    width = conv_weight.shape[1]
    wide = -(-width // LANES) * LANES
    query_width = query_weight.shape[1]
    query_wide = -(-query_width // LANES) * LANES
    query_heads = query_width // HEAD_SIZE
    per_group = QUERY_HEADS // KEYVAL_HEADS
    kv_heads = max(1, query_heads // per_group)
    kv_leading = tensor_index * query_heads // per_group
    states2 = state_weight.shape[1]
    ffn = down_proj.shape[0]
    low = lambda v: v.astype(BF)

    own_keyval = lax.dynamic_slice_in_dim(keyval_projection, kv_leading * HEAD_SIZE, kv_heads * HEAD_SIZE, 2)
    own_keyval = own_keyval.reshape(unit, 2, kv_heads, HEAD_SIZE).transpose(0, 2, 1, 3).reshape(unit, 2 * kv_heads * HEAD_SIZE)
    kv_wide = 2 * kv_heads * HEAD_SIZE
    first, rest = pack_weights(
        mixer_weight, state_weight, step_weight.T, query_weight, own_keyval, mixer_proj.T, attention_proj.T, gate_up, down_proj.T
    )
    rest = lax.all_gather(rest, "fsdp", axis=0, tiled=True)
    first, tokens, upstream, normed, first_scale = gather_weights(
        first, layer_input, cotangent, input_gain[None], fsdp_count, tensor_count, 0
    )
    ssm_wide = 2 * wide + states2 + LANES
    cuts = np.cumsum([0, ssm_wide, query_wide + kv_wide, wide + query_wide])
    full_ssm, full_qkv, full_mix = (first[:, cuts[i] : cuts[i + 1]] for i in range(3))
    docs = (doc_ids + jnp.arange(seq_count, dtype=jnp.int32)[:, None] * seq_length).reshape(1, total)
    doc_row = docs.astype(F32)
    feats, cos, sin, taps, state_taps, head_rows = make_tables(
        doc_row, wide, conv_weight, conv_bias, state_conv, state_conv_bias, step_bias, decay_log, skip_gain
    )
    gain_row = pad_to(mixer_gain[None], wide)
    second_row = second_gain[None]

    ssm_in = plain_dot(normed, full_ssm)
    qkv_in = plain_dot(normed, full_qkv)
    scan, gated_low, squares, states = mamba_forward(feats, doc_row, ssm_in, taps, state_taps, head_rows, gain_row, wide, states2)
    squares = tensor_pair(squares)
    mix, log_sums, query_rot, keys, values = attention_forward(kv_heads, feats, doc_row, qkv_in, cos, sin, query_wide, gated_low, squares)
    branch = tensor_pair(low(right_dot(mix, full_mix)))
    middle, second, second_scale = by_rows(
        second_norm_kernel, "second_norm", CHUNK, total // CHUNK,
        [(tokens, "rows"), (branch[0], "rows"), (branch[1], "rows"), (second_row, "whole")],
        [(total, hidden, F32, "rows"), (total, hidden, BF, "rows"), (total, 1, F32, "rows")],
    )
    active, gu_grad, ffn_out, second_grad = by_rows(
        ffn_kernel, "ffn", min(FFN_ROWS, total), max(total // FFN_ROWS, 1),
        [(second, "rows"), (upstream, "rows"), (rest, "whole")],
        [(total, ffn, BF, "rows"), (total, 2 * ffn, BF, "rows"), (total, hidden, BF, "rows"), (total, hidden, BF, "rows")],
    )
    second_grad, ffn_out = tensor_pair(second_grad), tensor_pair(ffn_out)
    core = jnp.full((1,), tensor_index, jnp.int32)
    own_block = min(CHUNK, own_rows)
    own_count = own_rows // own_block
    (layer_output,) = by_rows(
        output_kernel, "layer_output", own_block, own_count,
        [(middle, "own"), (ffn_out[0], "own"), (ffn_out[1], "own")], [(own_rows, hidden, BF, "rows")], (core,),
    )

    grad_rest = jnp.concatenate([low(left_dot(second, gu_grad)), low(left_dot(upstream, active))], axis=1)
    rest_sum = lax.psum_scatter(grad_rest, "fsdp", scatter_dimension=0, tiled=True)
    branch_low, second_gain_part = by_rows(
        second_back_kernel, "second_back", CHUNK, total // CHUNK,
        [(second_grad[0], "rows"), (second_grad[1], "rows"), (middle, "rows"), (second_scale, "rows"), (upstream, "rows"), (second_row, "whole")],
        [(total, hidden, BF, "rows"), (8, hidden, F32, "whole")],
    )
    mix_grad = low(plain_dot(branch_low, full_mix))
    qkv_grad, inners = attention_backward(kv_heads, feats, doc_row, query_rot, keys, values, log_sums, mix_grad, mix, cos, sin)
    inners = tensor_pair(inners)
    grad_mix = low(left_dot(branch_low, mix))
    grad_qkv = low(left_dot(normed, qkv_grad))
    ssm_grad, sums, state_sums, head_sums = mamba_backward(
        feats, doc_row, squares, inners, ssm_in, scan, states, mix_grad, taps, state_taps, head_rows, gain_row, wide, states2
    )
    normed_grad = tensor_pair(low(right_dot(ssm_grad, full_ssm) + right_dot(qkv_grad, full_qkv)))
    grad_ssm = low(left_dot(normed, ssm_grad))
    input_grad, input_gain_part = by_rows(
        input_back_kernel, "input_back", own_block, own_count,
        [(normed_grad[0], "own"), (normed_grad[1], "own"), (branch_low, "own"), (tokens, "own"), (first_scale, "own"), (input_gain[None], "whole")],
        [(own_rows, hidden, F32, "rows"), (8, hidden, F32, "whole")], (core,),
    )

    fold = lambda row: row[0].reshape(8, hidden // 8)
    split = wide + LANES
    small = jnp.concatenate(
        [sums, head_sums, state_sums, fold(second_gain_part) * (1.0 / tensor_count), fold(input_gain_part)], axis=1
    )
    sum_ssm, sum_qkv, sum_mix, small, shared = scatter_grads(
        (grad_ssm, grad_qkv, grad_mix), (0, 1, 1), small, split, (2 * wide, 2 * wide + states2), query_wide, kv_heads,
        fsdp_count, tensor_count, 1,
    )
    shape = lambda *dims: jax.ShapeDtypeStruct(dims, F32)
    done = pl.pallas_call(
        functools.partial(finish_kernel, (wide, width, states2, heads, query_width, ffn)),
        out_shape=[
            shape(unit, 2, width), shape(unit, states2), shape(unit, heads), shape(4, width), shape(1, width), shape(4, states2),
            shape(1, states2), shape(1, heads), shape(1, heads), shape(1, heads), shape(1, width), shape(unit, width),
            shape(unit, query_width), shape(unit, 2, KEYVAL_HEADS * HEAD_SIZE), shape(unit, query_width), shape(unit, 2, ffn),
            shape(unit, ffn), shape(1, hidden), shape(1, hidden),
        ],
        compiler_params=pltpu.CompilerParams(vmem_limit_bytes=32 * 2**20),
        name="finish",
    )(sum_ssm, sum_qkv, sum_mix, shared, small, rest_sum)
    (
        mixer_sum, state_sum, step_sum, conv_sum, conv_bias_sum, state_conv_sum, state_bias_sum, step_bias_sum, decay_sum, skip_sum,
        mixer_gain_sum, proj_sum, query_sum, keyval_sum, attention_sum, gate_up_sum, down_sum, second_gain_sum, input_gain_sum,
    ) = done
    return (
        layer_output, input_grad, input_gain_sum[0], mixer_sum, state_sum, step_sum, conv_sum, conv_bias_sum[0], state_conv_sum,
        state_bias_sum[0], step_bias_sum[0], decay_sum[0], skip_sum[0], mixer_gain_sum[0], proj_sum.T, query_sum, keyval_sum,
        attention_sum.T, second_gain_sum[0], gate_up_sum, down_sum.T,
    )


def solution(mesh):
    placed = (
        P(("fsdp", "tensor"), None),
        P("fsdp", None),
        P(),
        P("fsdp", None, "tensor"),
        P("fsdp", None),
        P("fsdp", "tensor"),
        P(None, "tensor"),
        P("tensor"),
        P(),
        P(),
        P("tensor"),
        P("tensor"),
        P("tensor"),
        P("tensor"),
        P("tensor", "fsdp"),
        P("fsdp", "tensor"),
        P("fsdp", None, None),
        P("tensor", "fsdp"),
        P(),
        P("fsdp", None, "tensor"),
        P("tensor", "fsdp"),
        P(("fsdp", "tensor"), None),
    )
    return jax.shard_map(
        body,
        mesh=mesh,
        in_specs=placed,
        out_specs=(
            P(("fsdp", "tensor"), None),
            P(("fsdp", "tensor"), None),
            P(),
            P("fsdp", None, "tensor"),
            P("fsdp", None),
            P("fsdp", "tensor"),
            P(None, "tensor"),
            P("tensor"),
            P(),
            P(),
            P("tensor"),
            P("tensor"),
            P("tensor"),
            P("tensor"),
            P("tensor", "fsdp"),
            P("fsdp", "tensor"),
            P("fsdp", None, None),
            P("tensor", "fsdp"),
            P(),
            P("fsdp", None, "tensor"),
            P("tensor", "fsdp"),
        ),
        check_vma=False,
    )
```

```python
import functools
import math

import jax
import jax.numpy as jnp
import ml_dtypes
import numpy as np
from jax import lax
from jax.experimental import pallas as pl
from jax.experimental.pallas import tpu as pltpu
from jax.sharding import PartitionSpec as P

QUERY_HEADS = 8
KEYVAL_HEADS = 2
HEAD_SIZE = 64
DSSM = 1536
EPS = 1e-05
THETA = 100000000000.0

LANES = 128
CHUNK = 128
FFN_ROWS = 512
VMEM_LIMIT = 32 * 2**20
VMEM_WHOLE = 60 * 2**20
MASKED = -1e30
BF, F32 = jnp.bfloat16, jnp.float32


def left_dot(left_side, right_side):
    return lax.dot_general(left_side, right_side, (((0,), (0,)), ((), ())), preferred_element_type=F32)


def right_dot(left_side, right_side):
    return lax.dot_general(left_side, right_side, (((1,), (1,)), ((), ())), preferred_element_type=F32)


def plain_dot(left_side, right_side):
    return jnp.dot(left_side, right_side, preferred_element_type=F32)


def mm(a, b):
    return jnp.dot(a.astype(BF), b.astype(BF), preferred_element_type=F32)


def mm_nt(a, b):
    return lax.dot_general(a.astype(BF), b.astype(BF), (((1,), (1,)), ((), ())), preferred_element_type=F32)


def mm_tn(a, b):
    return lax.dot_general(a.astype(BF), b.astype(BF), (((0,), (0,)), ((), ())), preferred_element_type=F32)


def exact_mm(a, b):
    return jnp.dot(a, b, precision=lax.Precision.HIGHEST, preferred_element_type=F32)


def sigmoid(v):
    return 1.0 / (1.0 + jnp.exp(-v))


def softplus(v):
    return jnp.maximum(v, 0.0) + jnp.log1p(jnp.exp(-jnp.abs(v)))


def split_lanes(values, axis):
    high = values.astype(BF)
    low = (values - high.astype(F32)).astype(BF)
    return jnp.concatenate([high, low], axis=axis)


def iota2(shape, axis):
    return lax.broadcasted_iota(jnp.int32, shape, axis)


def flipped(index, mask):
    bit = 1
    while bit <= mask:
        if mask & bit:
            index = index + bit * (1 - 2 * ((index // bit) % 2))
        bit *= 2
    return index


def greet(partners):
    barrier = pltpu.get_barrier_semaphore()
    for axis, place in partners:
        pl.semaphore_signal(barrier, inc=1, device_id={axis: place}, device_id_type=pl.DeviceIdType.MESH)
    pl.semaphore_wait(barrier, len(partners))


def remote(source, target, send, recv, axis, place):
    return pltpu.make_async_remote_copy(
        src_ref=source, dst_ref=target, send_sem=send, recv_sem=recv,
        device_id={axis: place}, device_id_type=pl.DeviceIdType.MESH,
    )


class TensorSum:
    def __init__(self, tensors, own, arrived, send, recv):
        self.core = lax.axis_index("tensor")
        self.places = [flipped(self.core, 1 << k) for k in range((tensors - 1).bit_length())]
        self.refs = own, arrived, send, recv

    def copy(self, k):
        own, arrived, send, recv = self.refs
        return remote(own.at[k], arrived.at[k], send.at[k], recv.at[k], "tensor", self.places[k])

    def begin(self, value):
        greet([("tensor", place) for place in self.places])
        self.refs[0][0] = value
        self.first = self.copy(0)
        self.first.start()

    def end(self):
        own, arrived, _, _ = self.refs
        for k in range(len(self.places)):
            copy = self.first if k == 0 else self.copy(k)
            if k:
                copy.start()
            copy.wait()
            own[k + 1] = own[k] + arrived[k]
        return own[len(self.places)]


def tensor_sum_scratch(tensors, shape):
    steps = (tensors - 1).bit_length()
    return [
        pltpu.VMEM((steps + 1,) + shape, F32), pltpu.VMEM((steps,) + shape, F32),
        pltpu.SemaphoreType.DMA((steps,)), pltpu.SemaphoreType.DMA((steps,)),
    ]


def conv_taps(buffer, feats, taps, bias, rows):
    total = buffer[8 : 8 + rows, :] * taps[3:4, :] + bias
    for k in range(1, 4):
        total = total + buffer[8 - k : 8 - k + rows, :] * feats[:, k : k + 1] * taps[3 - k : 4 - k, :]
    return total


def step_parts(step_ref, heads_ref, feats, rows):
    raw = step_ref[...] + heads_ref[0:1, :]
    step = softplus(raw)
    lower = (iota2((rows, rows), 0) >= iota2((rows, rows), 1)).astype(F32)
    log_decay = exact_mm(lower, step * heads_ref[1:2, :])
    last = log_decay[rows - 1 : rows, :]
    enter = jnp.exp(log_decay) * feats[:, 4:5]
    leave = jnp.exp(last - log_decay) * feats[:, 5:6]
    return raw, step, log_decay, enter, leave


def gated_scale(squares):
    return lax.rsqrt(squares / DSSM + EPS)


def as_column(row):
    return jnp.broadcast_to(row, (LANES, row.shape[1])).T[:, 0:1]


def mamba_fwd_kernel(
    feats_ref, docs_ref, x_ref, bc_ref, step_ref, z_ref, taps_ref, staps_ref, heads_ref, expand_ref,
    gain_ref, scan_ref, low_ref, square_ref, states_ref, xbuf, bcbuf, memory,
):
    rows, width = x_ref.shape
    states = bc_ref.shape[1] // 2

    @pl.when(pl.program_id(0) == 0)
    def _():
        xbuf[0:8, :] = jnp.zeros((8, width), F32)
        bcbuf[0:8, :] = jnp.zeros((8, 2 * states), F32)
        memory[...] = jnp.zeros_like(memory)

    feats = feats_ref[...]
    xbuf[8 : 8 + rows, :] = x_ref[...]
    bcbuf[8 : 8 + rows, :] = bc_ref[...]
    pre = conv_taps(xbuf, feats, taps_ref, taps_ref[4:5, :], rows)
    values = pre * sigmoid(pre)
    pre_bc = conv_taps(bcbuf, feats, staps_ref, staps_ref[4:5, :], rows)
    both = pre_bc * sigmoid(pre_bc)
    xbuf[0:8, :] = xbuf[rows : rows + 8, :]
    bcbuf[0:8, :] = bcbuf[rows : rows + 8, :]
    key_in = both[:, :states].astype(BF)
    key_out = both[:, states:].astype(BF)
    _, step, log_decay, enter, leave = step_parts(step_ref, heads_ref, feats, rows)
    expanded = jnp.dot(
        split_lanes(jnp.concatenate([step, enter, leave], axis=0), 1), expand_ref[...], preferred_element_type=F32
    )
    step_w, enter_w, leave_w = expanded[:rows], expanded[rows : 2 * rows], expanded[2 * rows :]
    scaled = values * step_w
    gram = mm_nt(key_out, key_in)
    allowed = (feats[:, 0:1] == docs_ref[...]) & (iota2((rows, rows), 0) >= iota2((rows, rows), 1))
    bias = jnp.where(allowed, 0.0, MASKED)
    log_rows = log_decay.T
    front = iota2((rows, LANES), 1) < LANES // 2
    held = memory[...]
    states_ref[0] = held.astype(BF)
    carried = mm(key_out, held) * enter_w
    fresh = mm_tn(key_in, leave_w * scaled)
    memory[...] = held * enter_w[rows - 1 : rows, :] + fresh
    squares = jnp.zeros((rows, 1), F32)
    for pair in range(width // LANES):
        lanes = slice(pair * LANES, (pair + 1) * LANES)
        mixes = []
        for h in (2 * pair, 2 * pair + 1):
            decay = jnp.exp(log_decay[:, h : h + 1] - log_rows[h : h + 1, :] + bias)
            mixes.append((gram * decay).astype(BF))
        part = scaled[:, lanes]
        stacked = jnp.concatenate([jnp.where(front, part, 0.0), jnp.where(front, 0.0, part)], axis=0)
        inside = mm(jnp.concatenate(mixes, axis=1), stacked)
        scan = inside + carried[:, lanes] + values[:, lanes] * taps_ref[5:6, lanes]
        scan_ref[:, lanes] = scan
        z = z_ref[:, lanes]
        gated = scan * (z * sigmoid(z))
        low_ref[:, lanes] = (gated * gain_ref[:, lanes]).astype(BF)
        squares = squares + jnp.sum(gated * gated, axis=1, keepdims=True)
    square_ref[...] = jnp.broadcast_to(squares, (rows, LANES)).T[0:8, :]


def mamba_bwd_kernel(
    tensors, feats_ref, square_ref, inners_ref, docs_ref, x_ref, x_before_ref, bc_ref, bc_before_ref, step_ref, z_ref, scan_ref, states_ref, norm_grad_ref,
    taps_ref, staps_ref, heads_ref, expand_ref, reduce_ref, gain_ref,
    grads_ref, sums_ref, ssums_ref, hsums_ref,
    xbuf, bcbuf, dxbuf, dbcbuf, dmemory, inner_sum, *scratch,
):
    rows, width = x_ref.shape
    states = bc_ref.shape[1] // 2

    @pl.when(pl.program_id(0) == 0)
    def _():
        dxbuf[rows : rows + 8, :] = jnp.zeros((8, width), F32)
        dbcbuf[rows : rows + 8, :] = jnp.zeros((8, 2 * states), F32)
        dmemory[...] = jnp.zeros_like(dmemory)
        sums_ref[...] = jnp.zeros_like(sums_ref)
        ssums_ref[...] = jnp.zeros_like(ssums_ref)
        hsums_ref[...] = jnp.zeros_like(hsums_ref)
        exchange = TensorSum(tensors, *scratch)
        exchange.begin(inners_ref[...])
        inner_sum[...] = exchange.end()

    feats = feats_ref[...]
    xbuf[0:8, :] = x_before_ref[...]
    bcbuf[0:8, :] = bc_before_ref[...]
    xbuf[8 : 8 + rows, :] = x_ref[...]
    bcbuf[8 : 8 + rows, :] = bc_ref[...]
    pre = conv_taps(xbuf, feats, taps_ref, taps_ref[4:5, :], rows)
    pre_gate = sigmoid(pre)
    values = pre * pre_gate
    pre_bc = conv_taps(bcbuf, feats, staps_ref, staps_ref[4:5, :], rows)
    bc_gate = sigmoid(pre_bc)
    both = pre_bc * bc_gate
    key_in = both[:, :states].astype(BF)
    key_out = both[:, states:].astype(BF)
    raw, step, log_decay, enter, leave = step_parts(step_ref, heads_ref, feats, rows)
    expanded = jnp.dot(
        split_lanes(jnp.concatenate([step, enter, leave], axis=0), 1), expand_ref[...], preferred_element_type=F32
    )
    step_w, enter_w, leave_w = expanded[:rows], expanded[rows : 2 * rows], expanded[2 * rows :]
    scaled = values * step_w
    z = z_ref[...]
    z_gate = sigmoid(z)
    z_silu = z * z_gate
    scan = scan_ref[...]
    gated = scan * z_silu
    norm_grad = norm_grad_ref[...].astype(F32)
    row_scale = gated_scale(square_ref[0:1, :])
    block = pl.num_programs(0) - 1 - pl.program_id(0)
    row_inner = inner_sum[pl.ds(pl.multiple_of(block * 8, 8), 8), :][0:1, :] * row_scale * row_scale / DSSM
    scale, coefficient = as_column(row_scale), as_column(row_inner)
    weighted = norm_grad * scale
    gated_grad = weighted * gain_ref[...] - gated * coefficient
    dscan = gated_grad * z_silu
    grads_ref[:, 0:width] = (gated_grad * scan * (z_gate * (1.0 + z * (1.0 - z_gate)))).astype(BF)
    sums_ref[6:7, :] += jnp.sum(weighted * gated, axis=0, keepdims=True)
    sums_ref[5:6, :] += jnp.sum(dscan * values, axis=0, keepdims=True)
    held = states_ref[0]
    dheld = dmemory[...]
    dheld_low = dheld.astype(BF)
    enter_grad = (dscan * enter_w).astype(BF)
    left = leave_w * scaled
    passed = mm(key_in, dheld_low)
    arrived = mm(key_out, held)
    dkey_out = mm_nt(enter_grad, held)
    dkey_in = mm_nt(left, dheld_low)
    carry = enter_w[rows - 1 : rows, :]
    dmemory[...] = dheld * carry + mm_tn(key_out, enter_grad)
    enter_terms = dscan * enter_w * arrived
    leave_terms = left * passed
    carry_terms = jnp.sum(dheld * held.astype(F32), axis=0, keepdims=True) * carry
    gram = mm_nt(key_in, key_out)
    allowed = (feats[:, 0:1] == docs_ref[...]) & (iota2((rows, rows), 0) <= iota2((rows, rows), 1))
    bias = jnp.where(allowed, 0.0, MASKED)
    log_rows = log_decay.T
    front = iota2((rows, LANES), 1) < LANES // 2
    gram_grad = jnp.zeros((rows, rows), F32)
    lane_of = iota2((rows, LANES), 1)
    row_of = iota2((LANES, rows), 0)
    sent = jnp.zeros((rows, LANES), F32)
    received = jnp.zeros((LANES, rows), F32)
    inside_grads = []
    for pair in range(width // LANES):
        lanes = slice(pair * LANES, (pair + 1) * LANES)
        dy = dscan[:, lanes].astype(BF)
        part = scaled[:, lanes]
        stacked = jnp.concatenate([jnp.where(front, part, 0.0), jnp.where(front, 0.0, part)], axis=0)
        cross = mm_nt(stacked, dy)
        mixes = []
        for j, h in enumerate((2 * pair, 2 * pair + 1)):
            decay = jnp.exp(log_rows[h : h + 1, :] - log_decay[:, h : h + 1] + bias)
            mix = gram * decay
            mixes.append(mix.astype(BF))
            dmix = cross[j * rows : (j + 1) * rows, :]
            gram_grad = gram_grad + dmix * decay
            flow = dmix * mix
            sent = jnp.where(lane_of == h, jnp.sum(flow, axis=1, keepdims=True), sent)
            received = jnp.where(row_of == h, jnp.sum(flow, axis=0, keepdims=True), received)
        grads = mm(jnp.concatenate(mixes, axis=0), dy)
        inside_grads.append(jnp.where(front, grads[:rows], grads[rows:]))
    dscaled = jnp.concatenate(inside_grads, axis=1) + leave_w * passed
    dkey_in = dkey_in + mm(gram_grad, key_out)
    dkey_out = dkey_out + mm_tn(gram_grad, key_in)
    reduced = jnp.dot(
        split_lanes(
            jnp.concatenate([enter_terms, leave_terms, dscaled * values, jnp.broadcast_to(carry_terms, (8, width))], axis=0), 1
        ),
        reduce_ref[...],
        preferred_element_type=F32,
    )
    after = reduced[:rows] + received.T - sent
    upper = (iota2((rows, rows), 0) <= iota2((rows, rows), 1)).astype(F32)
    strict = (iota2((rows, rows), 0) > iota2((rows, rows), 1)).astype(F32)
    decay_grad = exact_mm(upper, after) + exact_mm(strict, reduced[rows : 2 * rows]) + reduced[3 * rows : 3 * rows + 1]
    dstep = decay_grad * heads_ref[1:2, :] + reduced[2 * rows : 3 * rows]
    draw = dstep * sigmoid(raw)
    grads_ref[:, 2 * width + 2 * states :] = draw.astype(BF)
    hsums_ref[0:1, :] += jnp.sum(draw, axis=0, keepdims=True)
    hsums_ref[1:2, :] += jnp.sum(decay_grad * step, axis=0, keepdims=True) * heads_ref[1:2, :]
    dvalues = dscaled * step_w + dscan * taps_ref[5:6, :]
    dpre = dvalues * (pre_gate * (1.0 + pre * (1.0 - pre_gate)))
    dboth = jnp.concatenate([dkey_in, dkey_out], axis=1)
    dpre_bc = dboth * (bc_gate * (1.0 + pre_bc * (1.0 - bc_gate)))
    for dpre_now, buffer, dbuffer, taps, totals, lanes in (
        (dpre, xbuf, dxbuf, taps_ref, sums_ref, slice(width, 2 * width)),
        (dpre_bc, bcbuf, dbcbuf, staps_ref, ssums_ref, slice(2 * width, 2 * width + 2 * states)),
    ):
        dbuffer[0:rows, :] = dpre_now
        grad = dpre_now * taps[3:4, :]
        totals[3:4, :] += jnp.sum(dpre_now * buffer[8 : 8 + rows, :], axis=0, keepdims=True)
        totals[4:5, :] += jnp.sum(dpre_now, axis=0, keepdims=True)
        for k in range(1, 4):
            grad = grad + dbuffer[k : k + rows, :] * feats[:, 5 + k : 6 + k] * taps[3 - k : 4 - k, :]
            totals[3 - k : 4 - k, :] += jnp.sum(
                dpre_now * buffer[8 - k : 8 - k + rows, :] * feats[:, k : k + 1], axis=0, keepdims=True
            )
        grads_ref[:, lanes] = grad.astype(BF)
        dbuffer[rows : rows + 8, :] = dbuffer[0:8, :]


def expand_matrix(width):
    one = np.arange(LANES)[:, None] == np.arange(width)[None, :] // (LANES // 2)
    return np.concatenate([one, one], axis=0).astype(ml_dtypes.bfloat16)


def spec(block, index):
    return pl.BlockSpec(block, index)


def mamba_forward(feats, doc_row, ssm_in, taps, staps, heads, gain, width, states2):
    total = ssm_in.shape[0]
    rows = CHUNK
    count = total // rows
    block = lambda w, place=0: spec((rows, w), lambda i: (i, place))
    whole = lambda a: spec(a.shape, lambda i: (0,) * a.ndim)
    expand = expand_matrix(width)
    return pl.pallas_call(
        mamba_fwd_kernel,
        grid=(count,),
        in_specs=[
            block(LANES), spec((1, rows), lambda i: (0, i)), block(width, 1), block(states2, 2 * width // states2),
            block(LANES, (2 * width + states2) // LANES), block(width), whole(taps), whole(staps), whole(heads), whole(expand), whole(gain),
        ],
        out_specs=[block(width), block(width), spec((8, LANES), lambda i: (i, 0)), spec((1, states2 // 2, width), lambda i: (i, 0, 0))],
        out_shape=[
            jax.ShapeDtypeStruct((total, width), F32),
            jax.ShapeDtypeStruct((total, width), BF),
            jax.ShapeDtypeStruct((8 * count, LANES), F32),
            jax.ShapeDtypeStruct((count, states2 // 2, width), BF),
        ],
        scratch_shapes=[
            pltpu.VMEM((rows + 8, width), F32), pltpu.VMEM((rows + 8, states2), F32), pltpu.VMEM((states2 // 2, width), F32),
        ],
        compiler_params=pltpu.CompilerParams(vmem_limit_bytes=VMEM_LIMIT),
        cost_estimate=pl.CostEstimate(flops=20 * 10**9, bytes_accessed=total * width * 20, transcendentals=total * width * 4),
        name="mamba_fwd",
    )(feats, doc_row, ssm_in, ssm_in, ssm_in, ssm_in, taps, staps, heads, expand, gain)


def mamba_backward(tensors, feats, doc_row, squares, inners, ssm_in, scan, states, norm_grad, taps, staps, heads, gain, width, states2, collective_id):
    total = ssm_in.shape[0]
    rows = CHUNK
    count = total // rows
    back = lambda i: count - 1 - i
    block = lambda w, place=0: spec((rows, w), lambda i: (back(i), place))
    before = lambda w, place=0: spec((8, w), lambda i: (jnp.maximum(back(i) * (rows // 8) - 1, 0), place))
    whole = lambda a: spec(a.shape, lambda i: (0,) * a.ndim)
    expand = expand_matrix(width)
    reduce = np.concatenate([expand[:LANES].T] * 2, axis=0)
    totals = lambda w: spec((8, w), lambda i: (0, 0))
    strip = spec((8, LANES), lambda i: (back(i), 0))
    return pl.pallas_call(
        functools.partial(mamba_bwd_kernel, tensors),
        grid=(count,),
        in_specs=[
            block(LANES), strip, whole(inners), spec((1, rows), lambda i: (0, back(i))), block(width, 1), before(width, 1),
            block(states2, 2 * width // states2), before(states2, 2 * width // states2), block(LANES, (2 * width + states2) // LANES),
            block(width), block(width), spec((1, states2 // 2, width), lambda i: (back(i), 0, 0)), block(width),
            whole(taps), whole(staps), whole(heads), whole(expand), whole(reduce), whole(gain),
        ],
        out_specs=[block(2 * width + states2 + LANES), totals(width), totals(states2), totals(LANES)],
        out_shape=[
            jax.ShapeDtypeStruct((total, 2 * width + states2 + LANES), BF),
            jax.ShapeDtypeStruct((8, width), F32),
            jax.ShapeDtypeStruct((8, states2), F32),
            jax.ShapeDtypeStruct((8, LANES), F32),
        ],
        scratch_shapes=[
            pltpu.VMEM((rows + 8, width), F32), pltpu.VMEM((rows + 8, states2), F32),
            pltpu.VMEM((rows + 8, width), F32), pltpu.VMEM((rows + 8, states2), F32), pltpu.VMEM((states2 // 2, width), F32),
            pltpu.VMEM(inners.shape, F32), *tensor_sum_scratch(tensors, inners.shape),
        ],
        compiler_params=pltpu.CompilerParams(vmem_limit_bytes=VMEM_WHOLE, collective_id=collective_id, has_side_effects=True),
        cost_estimate=pl.CostEstimate(flops=35 * 10**9, bytes_accessed=total * width * 24, transcendentals=total * width * 5),
        name="mamba_bwd",
    )(feats, squares, inners, doc_row, ssm_in, ssm_in, ssm_in, ssm_in, ssm_in, ssm_in, scan, states, norm_grad, taps, staps, heads, expand, reduce, gain)


QBLOCK = 256


def swap_halves(values):
    lane = iota2(values.shape, 1) % (LANES // 2)
    return jnp.where(lane < LANES // 4, pltpu.roll(values, LANES - LANES // 4, 1), pltpu.roll(values, LANES // 4, 1))


def stack_heads(part):
    front = iota2(part.shape, 1) < LANES // 2
    zero = jnp.zeros_like(part)
    return jnp.concatenate([jnp.where(front, part, zero), jnp.where(front, zero, part)], axis=0)


def attention_fwd_kernel(
    groups, tensors, docs_col_ref, docs_ref, q_ref, kv_ref, cos_ref, sin_ref, low_ref, square_ref, out_ref, lse_ref, qrot_ref, keys_ref, values_ref, square_out_ref, *scratch,
):
    total = q_ref.shape[0]
    wide = low_ref.shape[1]
    exchange = TensorSum(tensors, *scratch)
    exchange.begin(square_ref[...])
    pairs = q_ref.shape[1] // LANES
    block = min(QBLOCK, total)
    cos, sin = cos_ref[...], sin_ref[...]
    front = iota2((total, LANES), 1) < LANES // 2
    for g in range(groups):
        lanes = slice(g * LANES, (g + 1) * LANES)
        raw = kv_ref[:, lanes]
        turned = raw * cos + swap_halves(raw) * sin
        keys_ref[:, lanes] = jnp.where(front, turned, pltpu.roll(turned, LANES // 2, 1)).astype(BF)
        values_ref[:, lanes] = jnp.where(front, pltpu.roll(raw, LANES // 2, 1), raw).astype(BF)
    for p in range(pairs):
        lanes = slice(p * LANES, (p + 1) * LANES)
        raw = q_ref[:, lanes]
        qrot_ref[:, lanes] = ((raw * cos + swap_halves(raw) * sin).astype(BF).astype(F32) * (LANES // 2) ** -0.5).astype(BF)
    front = iota2((block, LANES), 1) < LANES // 2
    lane_of = iota2((block, LANES), 1)
    for start in range(0, total, block):
        rows, end = slice(start, start + block), start + block
        allowed = (docs_col_ref[rows, 0:1] == docs_ref[:, :end]) & (
            iota2((block, end), 0) + start >= iota2((block, end), 1)
        )
        bias = jnp.where(allowed, 0.0, MASKED)
        bias = jnp.concatenate([bias, bias], axis=0)
        sums = jnp.zeros((block, LANES), F32)
        for p in range(pairs):
            lanes = slice(p * LANES, (p + 1) * LANES)
            g = p * groups // pairs
            kv = slice(g * LANES, (g + 1) * LANES)
            scores = mm_nt(stack_heads(qrot_ref[rows, lanes]), keys_ref[:end, kv]) + bias
            top = jnp.max(scores, axis=1, keepdims=True)
            raised = jnp.exp(scores - top)
            whole = jnp.sum(raised, axis=1, keepdims=True)
            mixed = mm(raised, values_ref[:end, kv]) / whole
            out_ref[rows, wide + p * LANES : wide + (p + 1) * LANES] = jnp.where(front, mixed[:block], mixed[block:]).astype(BF)
            logs = top + jnp.log(whole)
            sums = jnp.where(lane_of == 2 * p, logs[:block], sums)
            sums = jnp.where(lane_of == 2 * p + 1, logs[block:], sums)
        lse_ref[rows, :] = sums
    square_out_ref[...] = exchange.end()
    for i in range(total // LANES):
        piece = slice(i * LANES, (i + 1) * LANES)
        scale = as_column(gated_scale(square_out_ref[8 * i : 8 * i + 1, :]))
        out_ref[piece, :wide] = (low_ref[piece, :].astype(F32) * scale).astype(BF)


def attention_bwd_kernel(
    groups, docs_col_ref, docs_ref, qrot_ref, keys_ref, values_ref, lse_ref, mix_grad_ref, mix_ref, cos_ref, sin_ref,
    grads_ref, inner_ref, dk_acc, dv_acc,
):
    total = qrot_ref.shape[0]
    wide = mix_ref.shape[1] - qrot_ref.shape[1]
    for i in range(total // LANES):
        piece = slice(i * LANES, (i + 1) * LANES)
        products = mix_grad_ref[piece, :wide].astype(F32) * mix_ref[piece, :wide].astype(F32)
        inner = jnp.sum(products, axis=1, keepdims=True)
        inner_ref[8 * i : 8 * i + 8, :] = jnp.broadcast_to(inner, (LANES, LANES)).T[0:8, :]
    pairs = qrot_ref.shape[1] // LANES
    block = min(QBLOCK, total)
    dk_acc[...] = jnp.zeros_like(dk_acc)
    dv_acc[...] = jnp.zeros_like(dv_acc)
    front = iota2((block, LANES), 1) < LANES // 2
    for start in range(0, total, block):
        rows, end = slice(start, start + block), start + block
        allowed = (docs_col_ref[:end, 0:1] == docs_ref[:, rows]) & (
            iota2((end, block), 0) <= iota2((end, block), 1) + start
        )
        bias = jnp.where(allowed, 0.0, MASKED)
        logs = lse_ref[rows, :].T
        cos, sin = cos_ref[rows, :], sin_ref[rows, :]
        for p in range(pairs):
            lanes = slice(p * LANES, (p + 1) * LANES)
            g = p * groups // pairs
            kv = slice(g * LANES, (g + 1) * LANES)
            keys, values = keys_ref[:end, kv], values_ref[:end, kv]
            queries = stack_heads(qrot_ref[rows, lanes])
            ups = stack_heads(mix_grad_ref[rows, wide + p * LANES : wide + (p + 1) * LANES])
            shift = jnp.concatenate([bias - logs[2 * p : 2 * p + 1], bias - logs[2 * p + 1 : 2 * p + 2]], axis=1)
            probs = jnp.exp(mm_nt(keys, queries) + shift)
            grads = mm_nt(values, ups)
            centre = jnp.sum(probs * grads, axis=0, keepdims=True)
            score_grads = (probs * (grads - centre)).astype(BF)
            dk_acc[:end, kv] += mm(score_grads, queries)
            dv_acc[:end, kv] += mm(probs, ups)
            dq = mm_tn(score_grads, keys)
            dq = jnp.where(front, dq[:block], dq[block:]) * (LANES // 2) ** -0.5
            grads_ref[rows, lanes] = (dq * cos - swap_halves(dq) * sin).astype(BF)
    front = iota2((total, LANES), 1) < LANES // 2
    for g in range(groups):
        kv = slice(g * LANES, (g + 1) * LANES)
        dk, dv = dk_acc[:, kv], dv_acc[:, kv]
        dk = dk + pltpu.roll(dk, LANES // 2, 1)
        dk = dk * cos_ref[...] - swap_halves(dk) * sin_ref[...]
        dv = dv + pltpu.roll(dv, LANES // 2, 1)
        out = slice((pairs + g) * LANES, (pairs + g + 1) * LANES)
        grads_ref[:, out] = jnp.where(front, dk, dv).astype(BF)


def attention_forward(groups, tensors, doc_col, doc_row, qkv, cos, sin, query_width, low, squares, collective_id):
    total = qkv.shape[0]
    kv_width = qkv.shape[1] - query_width
    whole = lambda a: spec(a.shape, lambda i: (0,) * a.ndim)
    columns = lambda w, place=0: spec((total, w), lambda i: (0, place))
    return pl.pallas_call(
        functools.partial(attention_fwd_kernel, groups, tensors),
        grid=(1,),
        in_specs=[whole(doc_col), whole(doc_row), columns(query_width), columns(kv_width, query_width // kv_width), whole(cos), whole(sin), whole(low), whole(squares)],
        out_specs=[columns(low.shape[1] + query_width), columns(LANES), columns(query_width), columns(kv_width), columns(kv_width), whole(squares)],
        out_shape=[
            jax.ShapeDtypeStruct((total, low.shape[1] + query_width), BF), jax.ShapeDtypeStruct((total, LANES), F32),
            jax.ShapeDtypeStruct((total, query_width), BF), jax.ShapeDtypeStruct((total, kv_width), BF),
            jax.ShapeDtypeStruct((total, kv_width), BF), jax.ShapeDtypeStruct(squares.shape, F32),
        ],
        scratch_shapes=tensor_sum_scratch(tensors, squares.shape),
        compiler_params=pltpu.CompilerParams(vmem_limit_bytes=VMEM_LIMIT, collective_id=collective_id, has_side_effects=True),
        cost_estimate=pl.CostEstimate(flops=12 * 10**9, bytes_accessed=total * query_width * 10, transcendentals=total * total * 2),
        name="attention_fwd",
    )(doc_col, doc_row, qkv, qkv, cos, sin, low, squares)


def attention_backward(groups, doc_col, doc_row, qrot, keys, values, lse, mix_grad, mix, cos, sin):
    total = qrot.shape[0]
    return pl.pallas_call(
        functools.partial(attention_bwd_kernel, groups),
        out_shape=[jax.ShapeDtypeStruct((total, qrot.shape[1] + keys.shape[1]), BF), jax.ShapeDtypeStruct((total // 16, LANES), F32)],
        scratch_shapes=[pltpu.VMEM(keys.shape, F32), pltpu.VMEM(keys.shape, F32)],
        compiler_params=pltpu.CompilerParams(vmem_limit_bytes=VMEM_LIMIT),
        cost_estimate=pl.CostEstimate(flops=16 * 10**9, bytes_accessed=total * qrot.shape[1] * 10, transcendentals=total * total * 2),
        name="attention_bwd",
    )(doc_col, doc_row, qrot, keys, values, lse, mix_grad, mix, cos, sin)


def gather_kernel(
    count, tensors, shard_ref, tokens_ref, cotangent_ref, gain_ref, full_ref, all_tokens_ref, all_cotangent_ref, normed_ref, scale_ref,
    own_sem, send_sems, recv_sems, core_send, core_recv,
):
    unit, columns = shard_ref.shape
    levels = count // 4
    me = lax.axis_index("fsdp")
    half = columns // 2 // LANES * LANES
    parts = (slice(0, half), slice(half, columns))
    neighbours = (flipped(me, 1), flipped(me, 2))
    far = [flipped(me, 4 * d) for d in range(1, levels)]
    core = lax.axis_index("tensor")
    cores = [flipped(core, k) for k in range(1, tensors)]
    greet([("fsdp", p) for p in neighbours] + [("fsdp", p) for p in far] + [("tensor", p) for p in cores])

    def rows(owner):
        return pl.ds(pl.multiple_of(owner * unit, unit), unit)

    started = []

    def send(source, owner, lanes, slot, place):
        copy = remote(source, full_ref.at[rows(owner), lanes], send_sems.at[slot], recv_sems.at[slot], "fsdp", place)
        copy.start()
        started.append(copy)
        return copy

    def arrival(owner, lanes, slot):
        piece = full_ref.at[rows(owner), lanes]
        return remote(piece, piece, send_sems.at[slot], recv_sems.at[slot], "fsdp", neighbours[0])

    everything = slice(0, columns)
    own = pltpu.make_async_copy(shard_ref, full_ref.at[rows(me), :], own_sem)
    own.start()
    for d in range(1, levels):
        send(shard_ref, me, everything, d, far[d - 1])
    base = levels
    for axis in range(2):
        send(shard_ref, me, everything, base + axis * levels, neighbours[axis])
    cross = base + 2 * levels
    own_rows = tokens_ref.shape[0]
    share = lambda owner: pl.ds(pl.multiple_of(owner * own_rows, own_rows), own_rows)
    exchanges = []
    for k, place in enumerate(cores):
        for j, (source, target) in enumerate(((tokens_ref, all_tokens_ref), (cotangent_ref, all_cotangent_ref))):
            copy = remote(
                source, target.at[share(core), :], core_send.at[2 * k + j], core_recv.at[2 * k + j], "tensor", place
            )
            copy.start()
            exchanges.append(copy)
    all_tokens_ref[share(core), :] = tokens_ref[...]
    all_cotangent_ref[share(core), :] = cotangent_ref[...]
    for copy in exchanges:
        copy.wait()

    def norm(i, carry):
        piece = pl.ds(pl.multiple_of(i * LANES, LANES), LANES)
        values = all_tokens_ref[piece, :].astype(F32)
        scale = lax.rsqrt(jnp.mean(values * values, axis=1, keepdims=True) + EPS)
        scale_ref[piece, :] = scale
        normed_ref[piece, :] = (values * scale * gain_ref[...]).astype(BF)
        return carry

    lax.fori_loop(0, normed_ref.shape[0] // LANES, norm, 0)

    def pass_on(d):
        for axis in range(2):
            owner = flipped(neighbours[axis], 4 * d)
            arrival(owner, everything, base + axis * levels + d).wait_recv()
            piece = full_ref.at[rows(owner), parts[axis]]
            send(piece, owner, parts[axis], cross + axis * levels + d, neighbours[1 - axis])

    for d in range(1, levels):
        arrival(far[d - 1], everything, d).wait_recv()
        for axis in range(2):
            send(full_ref.at[rows(far[d - 1]), :], far[d - 1], everything, base + axis * levels + d, neighbours[axis])
        pass_on(d - 1)
    pass_on(levels - 1)
    for d in range(levels):
        for axis in range(2):
            owner = flipped(me, 4 * d + 3)
            arrival(owner, parts[axis], cross + axis * levels + d).wait_recv()
    for copy in started:
        copy.wait_send()
    own.wait()


def gather_weights(shard, tokens, cotangent, gain, count, tensors, collective_id):
    unit, columns = shard.shape
    own_rows, hidden = tokens.shape
    total = own_rows * tensors
    slots = 5 * (count // 4)
    vmem, anywhere = pl.BlockSpec(memory_space=pltpu.VMEM), pl.BlockSpec(memory_space=pl.ANY)
    low = jax.ShapeDtypeStruct((total, hidden), BF)
    return pl.pallas_call(
        functools.partial(gather_kernel, count, tensors),
        in_specs=[anywhere, vmem, vmem, vmem],
        out_specs=[anywhere, vmem, vmem, vmem, vmem],
        out_shape=[jax.ShapeDtypeStruct((count * unit, columns), shard.dtype), low, low, low, jax.ShapeDtypeStruct((total, 1), F32)],
        scratch_shapes=[
            pltpu.SemaphoreType.DMA, pltpu.SemaphoreType.DMA((slots,)), pltpu.SemaphoreType.DMA((slots,)),
            pltpu.SemaphoreType.DMA((2 * (tensors - 1),)), pltpu.SemaphoreType.DMA((2 * (tensors - 1),)),
        ],
        compiler_params=pltpu.CompilerParams(collective_id=collective_id, has_side_effects=True, vmem_limit_bytes=VMEM_LIMIT),
        cost_estimate=pl.CostEstimate(flops=0, bytes_accessed=2 * count * unit * columns * 2, transcendentals=0),
        name="gather_weights",
    )(shard, tokens, cotangent, gain)


def scatter_kernel(count, tensors, paths, split, state_at, kv_at, kv_heads, *refs):
    number = len(paths)
    grads, small_ref = refs[:number], refs[number]
    outs, small_out, shared_out = refs[number + 1 : 2 * number + 1], refs[2 * number + 1], refs[2 * number + 2]
    scratch = refs[2 * number + 3 :]
    cross, along_x, along_y, far_in, staged, far_out = (scratch[k * number : (k + 1) * number] for k in range(6))
    sums, arrived, shared, shared_in, send_sems, recv_sems, sum_send, sum_recv, core_send, core_recv = scratch[6 * number :]
    levels = count // 4
    unit = grads[0].shape[0] // count
    me = lax.axis_index("fsdp")
    core = lax.axis_index("tensor")
    near = (flipped(me, 1), flipped(me, 2))
    far = [None] + [flipped(me, 4 * d) for d in range(1, levels)]
    bits = [1 << k for k in range((count - 1).bit_length())]
    stages = [("fsdp", flipped(me, bit)) for bit in bits]
    cores = [("tensor", flipped(core, 1 << k)) for k in range((tensors - 1).bit_length())]
    greet([("fsdp", p) for p in near] + [("fsdp", p) for p in far[1:]] + cores)
    stages = stages + cores
    started = []

    def rows(owner):
        return pl.ds(pl.multiple_of(owner * unit, unit), unit)

    def link(source, target, slot, place):
        return remote(source, target, send_sems.at[slot], recv_sems.at[slot], "fsdp", place)

    def send(source, target, slot, place):
        copy = link(source, target, slot, place)
        copy.start()
        started.append(copy)

    def slot(i, kind, d):
        return (i * 4 + kind) * levels + d

    pending = []
    settled = []

    def next_stage():
        done = len(settled)
        if done < len(pending):
            pending[done].wait()
            sums[done + 1] = sums[done] + arrived[done]
            settled.append(done)
        if len(settled) == len(pending) and len(pending) < len(stages):
            done = len(pending)
            axis, place = stages[done]
            copy = remote(sums.at[done], arrived.at[done], sum_send.at[done], sum_recv.at[done], axis, place)
            copy.start()
            pending.append(copy)

    def begin(d):
        for i, path in enumerate(paths):
            send(grads[i].at[rows(flipped(me, 4 * d + 3)), :], cross[i].at[d], slot(i, 0, d), near[1 - path])

    def middle(d):
        for i, path in enumerate(paths):
            link(cross[i].at[d], cross[i].at[d], slot(i, 0, d), near[0]).wait_recv()
            staged[i][d] = (grads[i][rows(flipped(near[path], 4 * d)), :].astype(F32) + cross[i][d].astype(F32)).astype(BF)
            send(staged[i].at[d], (along_x, along_y)[path][i].at[d], slot(i, 1 + path, d), near[path])
            raw = 1 - path
            send(grads[i].at[rows(flipped(near[raw], 4 * d)), :], (along_x, along_y)[raw][i].at[d], slot(i, 1 + raw, d), near[raw])

    def finish(d):
        for i, path in enumerate(paths):
            link(along_x[i].at[d], along_x[i].at[d], slot(i, 1, d), near[0]).wait_recv()
            link(along_y[i].at[d], along_y[i].at[d], slot(i, 2, d), near[0]).wait_recv()
            total = grads[i][rows(flipped(me, 4 * d)), :].astype(F32) + along_x[i][d].astype(F32) + along_y[i][d].astype(F32)
            if d:
                far_out[i][d - 1] = total.astype(BF)
                send(far_out[i].at[d - 1], far_in[i].at[d - 1], slot(i, 3, d), far[d])
            else:
                outs[i][...] = total

    order = list(range(levels - 1, -1, -1))
    sums[0] = small_ref[...]
    begin(order[0])
    next_stage()
    begin(order[1])
    for k in range(1, levels + 2):
        if k <= levels:
            middle(order[k - 1])
        if k + 1 < levels:
            begin(order[k + 1])
        if k >= 2:
            finish(order[k - 2])
        next_stage()
    while len(settled) < len(stages):
        next_stage()
    for d in order[:-1]:
        for i in range(number):
            link(far_in[i].at[d - 1], far_in[i].at[d - 1], slot(i, 3, d), near[0]).wait_recv()
            outs[i][...] += far_in[i][d - 1].astype(F32)
    states2, leading = state_at[1] - state_at[0], core * (shared.shape[2] - state_at[1] + state_at[0]) // (tensors * LANES)
    shared[0, :, :states2] = outs[0][:, state_at[0] : state_at[1]]
    for g in range((shared.shape[2] - states2) // LANES):
        value = jnp.zeros((unit, LANES), F32)
        for j in range(kv_heads):
            value = jnp.where(leading + j == g, outs[1][:, kv_at + j * LANES : kv_at + (j + 1) * LANES], value)
        shared[0, :, states2 + g * LANES : states2 + (g + 1) * LANES] = value
    for k, (axis, place) in enumerate(cores):
        copy = remote(shared.at[k], shared_in.at[k], core_send.at[k], core_recv.at[k], axis, place)
        copy.start()
        copy.wait()
        shared[k + 1] = shared[k] + shared_in[k]
    shared_out[...] = shared[len(cores)]
    small_out[:, :split] = sums[len(bits), :, :split]
    small_out[:, split:] = sums[len(stages), :, split:]
    for copy in started:
        copy.wait_send()


def scatter_grads(grads, paths, small, split, state_at, kv_at, kv_heads, count, tensors, collective_id):
    unit = grads[0].shape[0] // count
    levels = count // 4
    stages = (count - 1).bit_length() + (tensors - 1).bit_length()
    vmem = pl.BlockSpec(memory_space=pltpu.VMEM)
    buffers = []
    for slots in (levels, levels, levels, levels - 1, levels, levels - 1):
        buffers += [pltpu.VMEM((slots, unit, g.shape[1]), BF) for g in grads]
    buffers += [pltpu.VMEM((stages + 1,) + small.shape, F32), pltpu.VMEM((stages,) + small.shape, F32)]
    links = 4 * levels * len(grads)
    steps = (tensors - 1).bit_length()
    shared = state_at[1] - state_at[0] + KEYVAL_HEADS * LANES
    buffers += [pltpu.VMEM((steps + 1, unit, shared), F32), pltpu.VMEM((steps, unit, shared), F32)]
    buffers += [pltpu.SemaphoreType.DMA((links,))] * 2 + [pltpu.SemaphoreType.DMA((stages,))] * 2 + [pltpu.SemaphoreType.DMA((steps,))] * 2
    size = sum(g.shape[1] for g in grads)
    return pl.pallas_call(
        functools.partial(scatter_kernel, count, tensors, tuple(paths), split, state_at, kv_at, kv_heads),
        in_specs=[vmem] * (len(grads) + 1),
        out_specs=[vmem] * (len(grads) + 2),
        out_shape=[jax.ShapeDtypeStruct((unit, g.shape[1]), F32) for g in grads]
        + [jax.ShapeDtypeStruct(small.shape, F32), jax.ShapeDtypeStruct((unit, shared), F32)],
        scratch_shapes=buffers,
        compiler_params=pltpu.CompilerParams(collective_id=collective_id, has_side_effects=True, vmem_limit_bytes=VMEM_WHOLE),
        cost_estimate=pl.CostEstimate(flops=0, bytes_accessed=2 * count * unit * size * 2, transcendentals=0),
        name="scatter_grads",
    )(*grads, small)


def tensor_swap(values):
    return lax.ppermute(values, "tensor", [(0, 1), (1, 0)])


def tensor_pair(values):
    if lax.axis_size("tensor") == 2:
        return values, tensor_swap(values)
    return lax.psum(values.astype(F32), "tensor").astype(values.dtype), jnp.zeros_like(values)


def pad_to(values, size, axis=-1):
    pads = [(0, 0)] * values.ndim
    pads[axis] = (0, size - values.shape[axis])
    return jnp.pad(values, pads) if size > values.shape[axis] else values


def pack_kernel(
    mixer_ref, state_ref, step_ref, query_ref, keyval_ref, proj_ref, attention_ref, gate_up_ref, down_ref,
    first_ref, second_ref,
):
    unit = state_ref.shape[0]
    width, wide = mixer_ref.shape[2], -(-mixer_ref.shape[2] // LANES) * LANES
    same = (iota2((unit, unit), 0) == iota2((unit, unit), 1)).astype(BF)
    place = 0

    def put(out_ref, value, size):
        nonlocal place
        value = value.astype(BF)
        if size > value.shape[1]:
            value = jnp.concatenate([value, jnp.zeros((unit, size - value.shape[1]), BF)], axis=1)
        out_ref[:, place : place + size] = value
        place += size

    put(first_ref, mixer_ref[:, 0, :], wide)
    put(first_ref, mixer_ref[:, 1, :], wide)
    put(first_ref, state_ref[...], state_ref.shape[1])
    put(first_ref, lax.dot_general(same, step_ref[...].astype(BF), (((1,), (1,)), ((), ())), preferred_element_type=F32), LANES)
    query_wide = -(-query_ref.shape[1] // LANES) * LANES
    put(first_ref, query_ref[...], query_wide)
    put(first_ref, keyval_ref[...], keyval_ref.shape[1])
    put(first_ref, proj_ref[...], wide)
    put(first_ref, attention_ref[...], query_wide)
    place = 0
    put(second_ref, gate_up_ref[:, 0, :], gate_up_ref.shape[2])
    put(second_ref, gate_up_ref[:, 1, :], gate_up_ref.shape[2])
    put(second_ref, down_ref[...], down_ref.shape[1])


def pack_weights(mixer, state, step, query, keyval, proj, attention, gate_up, down):
    unit = state.shape[0]
    lanes = lambda size: -(-size // LANES) * LANES
    first = 3 * lanes(mixer.shape[2]) + state.shape[1] + LANES + 2 * lanes(query.shape[1]) + keyval.shape[1]
    second = 2 * gate_up.shape[2] + down.shape[1]
    whole = lambda shape: spec(shape, lambda i: (0,) * len(shape))
    weights = (mixer, state, step, query, keyval, proj, attention, gate_up, down)
    return pl.pallas_call(
        pack_kernel,
        grid=(1,),
        in_specs=[whole(v.shape) for v in weights],
        out_specs=[whole((unit, first)), whole((unit, second))],
        out_shape=[jax.ShapeDtypeStruct((unit, first), BF), jax.ShapeDtypeStruct((unit, second), BF)],
        compiler_params=pltpu.CompilerParams(vmem_limit_bytes=VMEM_WHOLE),
        name="pack_weights",
    )(*weights)


def table_kernel(
    docs_ref, conv_ref, conv_bias_ref, state_conv_ref, state_bias_ref, step_bias_ref, decay_ref, skip_ref,
    feats_ref, cos_ref, sin_ref, taps_ref, state_taps_ref, heads_ref,
):
    total = docs_ref.shape[1]
    docs = docs_ref[...]
    tall = jnp.broadcast_to(docs, (LANES, total)).T
    spot = iota2((1, total), 1)
    begin = jnp.sum((tall[:, 0:1] < docs).astype(F32), axis=0, keepdims=True)
    rows = [docs]
    eight = jnp.broadcast_to(docs, (8, total))
    for k in (1, 2, 3):
        rows.append(jnp.where(spot >= k, (pltpu.roll(eight, k, 1)[0:1] == docs).astype(F32), 0.0))
    blocks = [docs[:, i : i + CHUNK] for i in range(0, total, CHUNK)]
    before = [jnp.full((1, 1), -1.0, F32)] + [v[:, CHUNK - 1 :] for v in blocks[:-1]]
    rows.append(jnp.concatenate([(v == w).astype(F32) for v, w in zip(blocks, before)], axis=1))
    rows.append(jnp.concatenate([(v == v[:, CHUNK - 1 :]).astype(F32) for v in blocks], axis=1))
    for k in (1, 2, 3):
        rows.append(jnp.where(spot < total - k, (pltpu.roll(eight, total - k, 1)[0:1] == docs).astype(F32), 0.0))
    rows.append(spot.astype(F32) - begin)
    rows.append(jnp.zeros((LANES - len(rows), total), F32))
    feats = jnp.concatenate(rows, axis=0).T
    feats_ref[...] = feats
    lane = iota2((1, LANES), 1)
    rates = jnp.exp((lane % (HEAD_SIZE // 2)).astype(F32) * (-2.0 * math.log(THETA) / HEAD_SIZE))
    angles = feats[:, 9:10] * rates
    cos_ref[...] = jnp.cos(angles)
    sin_ref[...] = jnp.sin(angles) * jnp.where(lane % HEAD_SIZE < HEAD_SIZE // 2, -1.0, 1.0)
    width, heads = conv_ref.shape[1], skip_ref.shape[1]
    taps_ref[...] = jnp.zeros_like(taps_ref)
    taps_ref[0:4, :width] = conv_ref[...]
    taps_ref[4:5, :width] = conv_bias_ref[...]
    spread = (iota2((heads, width), 0) == iota2((heads, width), 1) // (width // heads)).astype(F32)
    taps_ref[5:6, :width] = exact_mm(jnp.broadcast_to(skip_ref[...], (8, heads)), spread)[0:1]
    state_taps_ref[...] = jnp.zeros_like(state_taps_ref)
    state_taps_ref[0:4, :] = state_conv_ref[...]
    state_taps_ref[4:5, :] = state_bias_ref[...]
    heads_ref[...] = jnp.zeros_like(heads_ref)
    heads_ref[0:1, :heads] = step_bias_ref[...]
    heads_ref[1:2, :heads] = -jnp.exp(decay_ref[...])


def make_tables(docs, wide, conv, conv_bias, state_conv, state_bias, step_bias, decay, skip):
    total = docs.shape[1]
    shape = lambda r, c: jax.ShapeDtypeStruct((r, c), F32)
    return pl.pallas_call(
        table_kernel,
        out_shape=[shape(total, LANES), shape(total, LANES), shape(total, LANES), shape(8, wide), shape(8, state_conv.shape[1]), shape(8, LANES)],
        compiler_params=pltpu.CompilerParams(vmem_limit_bytes=VMEM_LIMIT),
        name="make_tables",
    )(docs, conv, conv_bias[None], state_conv, state_bias[None], step_bias[None], decay[None], skip[None])


def second_norm_kernel(tokens_ref, part_ref, part_in_ref, gain_ref, middle_ref, second_ref, scale_ref):
    middle = tokens_ref[...].astype(F32) + part_ref[...].astype(F32) + part_in_ref[...].astype(F32)
    scale = lax.rsqrt(jnp.mean(middle * middle, axis=1, keepdims=True) + EPS)
    middle_ref[...] = middle
    scale_ref[...] = scale
    second_ref[...] = (middle * scale * gain_ref[...]).astype(BF)


def by_rows(kernel, name, rows, count, ins, outs, scalars=(), scratch=()):
    number = len(scalars)

    def place(shape, kind):
        if kind == "whole":
            return spec(shape, lambda i, *s: (0,) * len(shape))
        if kind == "own":
            return spec((rows, shape[1]), lambda i, *s: (s[0][0] * count + i, 0))
        return spec((rows, shape[1]), lambda i, *s: (i, 0))

    return pl.pallas_call(
        kernel,
        grid_spec=pltpu.PrefetchScalarGridSpec(
            num_scalar_prefetch=number,
            grid=(count,),
            in_specs=[place(v.shape, kind) for v, kind in ins],
            out_specs=[place((r, c), kind) for r, c, _, kind in outs],
        ),
        out_shape=[jax.ShapeDtypeStruct((r, c), dtype) for r, c, dtype, _ in outs],
        compiler_params=pltpu.CompilerParams(vmem_limit_bytes=VMEM_LIMIT),
        name=name,
    )(*scalars, *(v for v, _ in ins))


def ffn_kernel(second_ref, up_ref, weights_ref, active_ref, grads_ref, out_ref, back_ref):
    ffn = active_ref.shape[1]
    gate_vals = jnp.dot(second_ref[...], weights_ref[:, : 2 * ffn], preferred_element_type=F32)
    active_grad = jnp.dot(up_ref[...], weights_ref[:, 2 * ffn :], preferred_element_type=F32)
    gate, up = gate_vals[:, :ffn], gate_vals[:, ffn:]
    sig = sigmoid(gate)
    silu = gate * sig
    active = (silu * up).astype(BF)
    active_ref[...] = active
    grads_ref[:, :ffn] = (active_grad * up * (sig + silu * (1.0 - sig))).astype(BF)
    grads_ref[:, ffn:] = (active_grad * silu).astype(BF)
    out_ref[...] = mm_nt(active, weights_ref[:, 2 * ffn :]).astype(BF)
    back_ref[...] = mm_nt(grads_ref[...], weights_ref[:, : 2 * ffn]).astype(BF)


def second_back_kernel(grad_ref, grad_in_ref, middle_ref, scale_ref, up_ref, gain_ref, low_ref, gain_grad_ref):
    @pl.when(pl.program_id(0) == 0)
    def _():
        gain_grad_ref[...] = jnp.zeros_like(gain_grad_ref)

    grad = grad_ref[...].astype(F32) + grad_in_ref[...].astype(F32)
    middle, scale = middle_ref[...], scale_ref[...]
    shape = middle * scale
    weighted = grad * gain_ref[...]
    inner = jnp.mean(weighted * shape, axis=1, keepdims=True)
    low_ref[...] = (up_ref[...].astype(F32) + scale * (weighted - shape * inner)).astype(BF)
    gain_grad_ref[0:1, :] += jnp.sum(grad * shape, axis=0, keepdims=True)


def output_kernel(core_ref, middle_ref, part_ref, part_in_ref, out_ref):
    out_ref[...] = (middle_ref[...] + part_ref[...].astype(F32) + part_in_ref[...].astype(F32)).astype(BF)


def input_back_kernel(core_ref, grad_ref, grad_in_ref, middle_grad_ref, tokens_ref, scale_ref, gain_ref, out_ref, gain_grad_ref):
    @pl.when(pl.program_id(0) == 0)
    def _():
        gain_grad_ref[...] = jnp.zeros_like(gain_grad_ref)

    grad = grad_ref[...].astype(F32) + grad_in_ref[...].astype(F32)
    scale = scale_ref[...]
    shape = tokens_ref[...].astype(F32) * scale
    weighted = grad * gain_ref[...]
    inner = jnp.mean(weighted * shape, axis=1, keepdims=True)
    out_ref[...] = middle_grad_ref[...].astype(F32) + scale * (weighted - shape * inner)
    gain_grad_ref[0:1, :] += jnp.sum(grad * shape, axis=0, keepdims=True)


def finish_kernel(
    sizes, ssm_ref, qkv_ref, mix_ref, shared_ref, small_ref, rest_ref,
    mixer_ref, state_ref, step_ref, conv_ref, conv_bias_ref, state_conv_ref, state_bias_ref, step_bias_ref, decay_ref, skip_ref,
    mixer_gain_ref, proj_ref, query_ref, keyval_ref, attention_ref, gate_up_ref, down_ref, second_gain_ref, input_gain_ref,
):
    wide, width, states2, heads, query_width, ffn = sizes
    mixer_ref[:, 0, :] = ssm_ref[:, :width]
    mixer_ref[:, 1, :] = ssm_ref[:, wide : wide + width]
    state_ref[...] = shared_ref[:, :states2]
    step_ref[...] = ssm_ref[:, 2 * wide + states2 : 2 * wide + states2 + heads]
    query_ref[...] = qkv_ref[:, :query_width]
    groups = [shared_ref[:, i : i + LANES] for i in range(states2, shared_ref.shape[1], LANES)]
    keyval_ref[:, 0, :] = jnp.concatenate([v[:, :HEAD_SIZE] for v in groups], axis=1)
    keyval_ref[:, 1, :] = jnp.concatenate([v[:, HEAD_SIZE:] for v in groups], axis=1)
    proj_ref[...] = mix_ref[:, :width]
    attention_ref[...] = mix_ref[:, wide : wide + query_width]
    gate_up_ref[:, 0, :] = rest_ref[:, :ffn].astype(F32)
    gate_up_ref[:, 1, :] = rest_ref[:, ffn : 2 * ffn].astype(F32)
    down_ref[...] = rest_ref[:, 2 * ffn :].astype(F32)
    conv_ref[...] = small_ref[0:4, :width]
    conv_bias_ref[...] = small_ref[4:5, :width]
    mixer_gain_ref[...] = small_ref[6:7, :width]
    place = iota2((width, heads), 0) // (width // heads)
    gather = (place == iota2((width, heads), 1)).astype(F32)
    skip_ref[...] = exact_mm(jnp.broadcast_to(small_ref[5:6, :width], (8, width)), gather)[0:1]
    step_bias_ref[...] = small_ref[0:1, wide : wide + heads]
    decay_ref[...] = small_ref[1:2, wide : wide + heads]
    base = wide + LANES
    state_conv_ref[...] = small_ref[0:4, base : base + states2]
    state_bias_ref[...] = small_ref[4:5, base : base + states2]
    base += states2
    for out_ref in (second_gain_ref, input_gain_ref):
        size = out_ref.shape[1]
        out_ref[...] = jnp.concatenate([small_ref[r : r + 1, base : base + size // 8] for r in range(8)], axis=1)
        base += size // 8


def body(
    layer_input, doc_ids, input_gain, mixer_weight, state_weight, step_weight, conv_weight, conv_bias, state_conv,
    state_conv_bias, step_bias, decay_log, skip_gain, mixer_gain, mixer_proj, query_weight, keyval_projection,
    attention_proj, second_gain, gate_up, down_proj, cotangent,
):
    tensor_count = lax.axis_size("tensor")
    tensor_index = lax.axis_index("tensor")
    fsdp_count = lax.axis_size("fsdp")
    own_rows, hidden = layer_input.shape
    unit = state_weight.shape[0]
    seq_count, seq_length = doc_ids.shape
    total = seq_count * seq_length
    heads = step_bias.shape[0]
    width = conv_weight.shape[1]
    wide = -(-width // LANES) * LANES
    query_width = query_weight.shape[1]
    query_wide = -(-query_width // LANES) * LANES
    query_heads = query_width // HEAD_SIZE
    per_group = QUERY_HEADS // KEYVAL_HEADS
    kv_heads = max(1, query_heads // per_group)
    kv_leading = tensor_index * query_heads // per_group
    states2 = state_weight.shape[1]
    ffn = down_proj.shape[0]
    low = lambda v: v.astype(BF)

    own_keyval = lax.dynamic_slice_in_dim(keyval_projection, kv_leading * HEAD_SIZE, kv_heads * HEAD_SIZE, 2)
    own_keyval = own_keyval.reshape(unit, 2, kv_heads, HEAD_SIZE).transpose(0, 2, 1, 3).reshape(unit, 2 * kv_heads * HEAD_SIZE)
    kv_wide = 2 * kv_heads * HEAD_SIZE
    first, rest = pack_weights(
        mixer_weight, state_weight, step_weight.T, query_weight, own_keyval, mixer_proj.T, attention_proj.T, gate_up, down_proj.T
    )
    rest = lax.all_gather(rest, "fsdp", axis=0, tiled=True)
    first, tokens, upstream, normed, first_scale = gather_weights(
        first, layer_input, cotangent, input_gain[None], fsdp_count, tensor_count, 0
    )
    ssm_wide = 2 * wide + states2 + LANES
    cuts = np.cumsum([0, ssm_wide, query_wide + kv_wide, wide + query_wide])
    full_ssm, full_qkv, full_mix = (first[:, cuts[i] : cuts[i + 1]] for i in range(3))
    docs = (doc_ids + jnp.arange(seq_count, dtype=jnp.int32)[:, None] * seq_length).reshape(1, total)
    doc_row = docs.astype(F32)
    feats, cos, sin, taps, state_taps, head_rows = make_tables(
        doc_row, wide, conv_weight, conv_bias, state_conv, state_conv_bias, step_bias, decay_log, skip_gain
    )
    gain_row = pad_to(mixer_gain[None], wide)
    second_row = second_gain[None]

    ssm_in = plain_dot(normed, full_ssm)
    qkv_in = plain_dot(normed, full_qkv)
    scan, gated_low, squares, states = mamba_forward(feats, doc_row, ssm_in, taps, state_taps, head_rows, gain_row, wide, states2)
    mix, log_sums, query_rot, keys, values, squares = attention_forward(
        kv_heads, tensor_count, feats, doc_row, qkv_in, cos, sin, query_wide, gated_low, squares, 2
    )
    branch = tensor_pair(low(right_dot(mix, full_mix)))
    middle, second, second_scale = by_rows(
        second_norm_kernel, "second_norm", CHUNK, total // CHUNK,
        [(tokens, "rows"), (branch[0], "rows"), (branch[1], "rows"), (second_row, "whole")],
        [(total, hidden, F32, "rows"), (total, hidden, BF, "rows"), (total, 1, F32, "rows")],
    )
    active, gu_grad, ffn_out, second_grad = by_rows(
        ffn_kernel, "ffn", min(FFN_ROWS, total), max(total // FFN_ROWS, 1),
        [(second, "rows"), (upstream, "rows"), (rest, "whole")],
        [(total, ffn, BF, "rows"), (total, 2 * ffn, BF, "rows"), (total, hidden, BF, "rows"), (total, hidden, BF, "rows")],
    )
    second_grad, ffn_out = tensor_pair(second_grad), tensor_pair(ffn_out)
    core = jnp.full((1,), tensor_index, jnp.int32)
    own_block = min(CHUNK, own_rows)
    own_count = own_rows // own_block
    (layer_output,) = by_rows(
        output_kernel, "layer_output", own_block, own_count,
        [(middle, "own"), (ffn_out[0], "own"), (ffn_out[1], "own")], [(own_rows, hidden, BF, "rows")], (core,),
    )

    grad_rest = jnp.concatenate([low(left_dot(second, gu_grad)), low(left_dot(upstream, active))], axis=1)
    rest_sum = lax.psum_scatter(grad_rest, "fsdp", scatter_dimension=0, tiled=True)
    branch_low, second_gain_part = by_rows(
        second_back_kernel, "second_back", CHUNK, total // CHUNK,
        [(second_grad[0], "rows"), (second_grad[1], "rows"), (middle, "rows"), (second_scale, "rows"), (upstream, "rows"), (second_row, "whole")],
        [(total, hidden, BF, "rows"), (8, hidden, F32, "whole")],
    )
    mix_grad = low(plain_dot(branch_low, full_mix))
    qkv_grad, inners = attention_backward(kv_heads, feats, doc_row, query_rot, keys, values, log_sums, mix_grad, mix, cos, sin)
    grad_mix = low(left_dot(branch_low, mix))
    grad_qkv = low(left_dot(normed, qkv_grad))
    ssm_grad, sums, state_sums, head_sums = mamba_backward(
        tensor_count, feats, doc_row, squares, inners, ssm_in, scan, states, mix_grad, taps, state_taps, head_rows, gain_row, wide,
        states2, 3,
    )
    normed_grad = tensor_pair(low(right_dot(ssm_grad, full_ssm) + right_dot(qkv_grad, full_qkv)))
    grad_ssm = low(left_dot(normed, ssm_grad))
    input_grad, input_gain_part = by_rows(
        input_back_kernel, "input_back", own_block, own_count,
        [(normed_grad[0], "own"), (normed_grad[1], "own"), (branch_low, "own"), (tokens, "own"), (first_scale, "own"), (input_gain[None], "whole")],
        [(own_rows, hidden, F32, "rows"), (8, hidden, F32, "whole")], (core,),
    )

    fold = lambda row: row[0].reshape(8, hidden // 8)
    split = wide + LANES
    small = jnp.concatenate(
        [sums, head_sums, state_sums, fold(second_gain_part) * (1.0 / tensor_count), fold(input_gain_part)], axis=1
    )
    sum_ssm, sum_qkv, sum_mix, small, shared = scatter_grads(
        (grad_ssm, grad_qkv, grad_mix), (0, 1, 1), small, split, (2 * wide, 2 * wide + states2), query_wide, kv_heads,
        fsdp_count, tensor_count, 1,
    )
    shape = lambda *dims: jax.ShapeDtypeStruct(dims, F32)
    done = pl.pallas_call(
        functools.partial(finish_kernel, (wide, width, states2, heads, query_width, ffn)),
        out_shape=[
            shape(unit, 2, width), shape(unit, states2), shape(unit, heads), shape(4, width), shape(1, width), shape(4, states2),
            shape(1, states2), shape(1, heads), shape(1, heads), shape(1, heads), shape(1, width), shape(unit, width),
            shape(unit, query_width), shape(unit, 2, KEYVAL_HEADS * HEAD_SIZE), shape(unit, query_width), shape(unit, 2, ffn),
            shape(unit, ffn), shape(1, hidden), shape(1, hidden),
        ],
        compiler_params=pltpu.CompilerParams(vmem_limit_bytes=VMEM_LIMIT),
        name="finish",
    )(sum_ssm, sum_qkv, sum_mix, shared, small, rest_sum)
    (
        mixer_sum, state_sum, step_sum, conv_sum, conv_bias_sum, state_conv_sum, state_bias_sum, step_bias_sum, decay_sum, skip_sum,
        mixer_gain_sum, proj_sum, query_sum, keyval_sum, attention_sum, gate_up_sum, down_sum, second_gain_sum, input_gain_sum,
    ) = done
    return (
        layer_output, input_grad, input_gain_sum[0], mixer_sum, state_sum, step_sum, conv_sum, conv_bias_sum[0], state_conv_sum,
        state_bias_sum[0], step_bias_sum[0], decay_sum[0], skip_sum[0], mixer_gain_sum[0], proj_sum.T, query_sum, keyval_sum,
        attention_sum.T, second_gain_sum[0], gate_up_sum, down_sum.T,
    )


def solution(mesh):
    placed = (
        P(("fsdp", "tensor"), None),
        P("fsdp", None),
        P(),
        P("fsdp", None, "tensor"),
        P("fsdp", None),
        P("fsdp", "tensor"),
        P(None, "tensor"),
        P("tensor"),
        P(),
        P(),
        P("tensor"),
        P("tensor"),
        P("tensor"),
        P("tensor"),
        P("tensor", "fsdp"),
        P("fsdp", "tensor"),
        P("fsdp", None, None),
        P("tensor", "fsdp"),
        P(),
        P("fsdp", None, "tensor"),
        P("tensor", "fsdp"),
        P(("fsdp", "tensor"), None),
    )
    return jax.shard_map(
        body,
        mesh=mesh,
        in_specs=placed,
        out_specs=(
            P(("fsdp", "tensor"), None),
            P(("fsdp", "tensor"), None),
            P(),
            P("fsdp", None, "tensor"),
            P("fsdp", None),
            P("fsdp", "tensor"),
            P(None, "tensor"),
            P("tensor"),
            P(),
            P(),
            P("tensor"),
            P("tensor"),
            P("tensor"),
            P("tensor"),
            P("tensor", "fsdp"),
            P("fsdp", "tensor"),
            P("fsdp", None, None),
            P("tensor", "fsdp"),
            P(),
            P("fsdp", None, "tensor"),
            P("tensor", "fsdp"),
        ),
        check_vma=False,
    )
```

```python
import functools
import math
import types

import jax
import jax.numpy as jnp
import ml_dtypes
import numpy as np
from jax import lax
from jax.experimental import pallas as pl
from jax.experimental.pallas import tpu as pltpu
from jax.sharding import PartitionSpec as P

QUERY_HEADS = 8
KEYVAL_HEADS = 2
HEAD_SIZE = 64
DSSM = 1536
EPS = 1e-05
THETA = 100000000000.0

LANES = 128
CHUNK = 128
FFN_ROWS = 512
QBLOCK = 256
VMEM_LIMIT = 32 * 2**20
VMEM_WHOLE = 60 * 2**20
VMEM_ALL = 63 * 2**20
MASKED = -1e30
BF, F32 = jnp.bfloat16, jnp.float32


def left_dot(left_side, right_side):
    return lax.dot_general(left_side, right_side, (((0,), (0,)), ((), ())), preferred_element_type=F32)


def right_dot(left_side, right_side):
    return lax.dot_general(left_side, right_side, (((1,), (1,)), ((), ())), preferred_element_type=F32)


def plain_dot(left_side, right_side):
    return jnp.dot(left_side, right_side, preferred_element_type=F32)


def mm(a, b):
    return jnp.dot(a.astype(BF), b.astype(BF), preferred_element_type=F32)


def mm_nt(a, b):
    return lax.dot_general(a.astype(BF), b.astype(BF), (((1,), (1,)), ((), ())), preferred_element_type=F32)


def mm_tn(a, b):
    return lax.dot_general(a.astype(BF), b.astype(BF), (((0,), (0,)), ((), ())), preferred_element_type=F32)


def exact_mm(a, b):
    return jnp.dot(a, b, precision=lax.Precision.HIGHEST, preferred_element_type=F32)


def sigmoid(v):
    return 1.0 / (1.0 + jnp.exp(-v))


def softplus(v):
    return jnp.maximum(v, 0.0) + jnp.log1p(jnp.exp(-jnp.abs(v)))


def split_lanes(values, axis):
    high = values.astype(BF)
    low = (values - high.astype(F32)).astype(BF)
    return jnp.concatenate([high, low], axis=axis)


def iota2(shape, axis):
    return lax.broadcasted_iota(jnp.int32, shape, axis)


def flipped(index, mask):
    bit = 1
    while bit <= mask:
        if mask & bit:
            index = index + bit * (1 - 2 * ((index // bit) % 2))
        bit *= 2
    return index


def greet(partners):
    barrier = pltpu.get_barrier_semaphore()
    for axis, place in partners:
        pl.semaphore_signal(barrier, inc=1, device_id={axis: place}, device_id_type=pl.DeviceIdType.MESH)
    pl.semaphore_wait(barrier, len(partners))


def remote(source, target, send, recv, axis, place):
    return pltpu.make_async_remote_copy(
        src_ref=source, dst_ref=target, send_sem=send, recv_sem=recv,
        device_id={axis: place}, device_id_type=pl.DeviceIdType.MESH,
    )


class TensorSum:
    def __init__(self, tensors, own, arrived, send, recv):
        self.core = lax.axis_index("tensor")
        self.places = [flipped(self.core, 1 << k) for k in range((tensors - 1).bit_length())]
        self.refs = own, arrived, send, recv

    def copy(self, k):
        own, arrived, send, recv = self.refs
        return remote(own.at[k], arrived.at[k], send.at[k], recv.at[k], "tensor", self.places[k])

    def begin(self, value, met=False):
        if not met:
            greet([("tensor", place) for place in self.places])
        self.refs[0][0] = value
        self.copy(0).start()

    def end(self):
        own, arrived, _, _ = self.refs
        for k in range(len(self.places)):
            copy = self.copy(k)
            if k:
                copy.start()
            copy.wait()
            own[k + 1] = own[k] + arrived[k]
        return own[len(self.places)]


def tensor_sum_scratch(tensors, shape):
    steps = (tensors - 1).bit_length()
    return [
        pltpu.VMEM((steps + 1,) + shape, F32), pltpu.VMEM((steps,) + shape, F32),
        pltpu.SemaphoreType.DMA((steps,)), pltpu.SemaphoreType.DMA((steps,)),
    ]


def conv_taps(buffer, feats, taps, bias, rows):
    total = buffer[8 : 8 + rows, :] * taps[3:4, :] + bias
    for k in range(1, 4):
        total = total + buffer[8 - k : 8 - k + rows, :] * feats[:, k : k + 1] * taps[3 - k : 4 - k, :]
    return total


def step_parts(step_ref, heads_ref, feats, rows):
    raw = step_ref[...] + heads_ref[0:1, :]
    step = softplus(raw)
    lower = (iota2((rows, rows), 0) >= iota2((rows, rows), 1)).astype(F32)
    log_decay = exact_mm(lower, step * heads_ref[1:2, :])
    last = log_decay[rows - 1 : rows, :]
    enter = jnp.exp(log_decay) * feats[:, 4:5]
    leave = jnp.exp(last - log_decay) * feats[:, 5:6]
    return raw, step, log_decay, enter, leave


def gated_scale(squares):
    return lax.rsqrt(squares / DSSM + EPS)


def as_column(row):
    return jnp.broadcast_to(row, (LANES, row.shape[1])).T[:, 0:1]


def mamba_fwd_kernel(
    feats_ref, docs_ref, x_ref, bc_ref, step_ref, z_ref, taps_ref, staps_ref, heads_ref, expand_ref,
    gain_ref, scan_ref, low_ref, square_ref, states_ref, xbuf, bcbuf, memory,
):
    rows, width = x_ref.shape
    states = bc_ref.shape[1] // 2

    @pl.when(pl.program_id(0) == 0)
    def _():
        xbuf[0:8, :] = jnp.zeros((8, width), F32)
        bcbuf[0:8, :] = jnp.zeros((8, 2 * states), F32)
        memory[...] = jnp.zeros_like(memory)

    feats = feats_ref[...]
    xbuf[8 : 8 + rows, :] = x_ref[...]
    bcbuf[8 : 8 + rows, :] = bc_ref[...]
    pre = conv_taps(xbuf, feats, taps_ref, taps_ref[4:5, :], rows)
    values = pre * sigmoid(pre)
    pre_bc = conv_taps(bcbuf, feats, staps_ref, staps_ref[4:5, :], rows)
    both = pre_bc * sigmoid(pre_bc)
    xbuf[0:8, :] = xbuf[rows : rows + 8, :]
    bcbuf[0:8, :] = bcbuf[rows : rows + 8, :]
    key_in = both[:, :states].astype(BF)
    key_out = both[:, states:].astype(BF)
    _, step, log_decay, enter, leave = step_parts(step_ref, heads_ref, feats, rows)
    expanded = jnp.dot(
        split_lanes(jnp.concatenate([step, enter, leave], axis=0), 1), expand_ref[...], preferred_element_type=F32
    )
    step_w, enter_w, leave_w = expanded[:rows], expanded[rows : 2 * rows], expanded[2 * rows :]
    scaled = values * step_w
    gram = mm_nt(key_out, key_in)
    allowed = (feats[:, 0:1] == docs_ref[...]) & (iota2((rows, rows), 0) >= iota2((rows, rows), 1))
    bias = jnp.where(allowed, 0.0, MASKED)
    log_rows = log_decay.T
    front = iota2((rows, LANES), 1) < LANES // 2
    held = memory[...]
    states_ref[0] = held.astype(BF)
    carried = mm(key_out, held) * enter_w
    fresh = mm_tn(key_in, leave_w * scaled)
    memory[...] = held * enter_w[rows - 1 : rows, :] + fresh
    squares = jnp.zeros((rows, 1), F32)
    for pair in range(width // LANES):
        lanes = slice(pair * LANES, (pair + 1) * LANES)
        mixes = []
        for h in (2 * pair, 2 * pair + 1):
            decay = jnp.exp(log_decay[:, h : h + 1] - log_rows[h : h + 1, :] + bias)
            mixes.append((gram * decay).astype(BF))
        part = scaled[:, lanes]
        stacked = jnp.concatenate([jnp.where(front, part, 0.0), jnp.where(front, 0.0, part)], axis=0)
        inside = mm(jnp.concatenate(mixes, axis=1), stacked)
        scan = inside + carried[:, lanes] + values[:, lanes] * taps_ref[5:6, lanes]
        scan_ref[:, lanes] = scan
        z = z_ref[:, lanes]
        gated = scan * (z * sigmoid(z))
        low_ref[:, lanes] = (gated * gain_ref[:, lanes]).astype(BF)
        squares = squares + jnp.sum(gated * gated, axis=1, keepdims=True)
    square_ref[...] = jnp.broadcast_to(squares, (rows, LANES)).T[0:8, :]


def mamba_bwd_block(
    feats_ref, square_ref, inner_sum, block, docs_ref, x_ref, x_before_ref, bc_ref, bc_before_ref, step_ref, z_ref, scan_ref, states_ref, norm_grad_ref,
    taps_ref, staps_ref, heads_ref, expand_ref, reduce_ref, gain_ref,
    grads_ref, sums_ref, ssums_ref, hsums_ref,
    xbuf, bcbuf, dxbuf, dbcbuf, dmemory,
):
    rows, width = x_ref.shape
    states = bc_ref.shape[1] // 2

    feats = feats_ref[...]
    xbuf[0:8, :] = x_before_ref[...]
    bcbuf[0:8, :] = bc_before_ref[...]
    xbuf[8 : 8 + rows, :] = x_ref[...]
    bcbuf[8 : 8 + rows, :] = bc_ref[...]
    pre = conv_taps(xbuf, feats, taps_ref, taps_ref[4:5, :], rows)
    pre_gate = sigmoid(pre)
    values = pre * pre_gate
    pre_bc = conv_taps(bcbuf, feats, staps_ref, staps_ref[4:5, :], rows)
    bc_gate = sigmoid(pre_bc)
    both = pre_bc * bc_gate
    key_in = both[:, :states].astype(BF)
    key_out = both[:, states:].astype(BF)
    raw, step, log_decay, enter, leave = step_parts(step_ref, heads_ref, feats, rows)
    expanded = jnp.dot(
        split_lanes(jnp.concatenate([step, enter, leave], axis=0), 1), expand_ref[...], preferred_element_type=F32
    )
    step_w, enter_w, leave_w = expanded[:rows], expanded[rows : 2 * rows], expanded[2 * rows :]
    scaled = values * step_w
    z = z_ref[...]
    z_gate = sigmoid(z)
    z_silu = z * z_gate
    scan = scan_ref[...]
    gated = scan * z_silu
    norm_grad = norm_grad_ref[...].astype(F32)
    row_scale = gated_scale(square_ref[0:1, :])
    row_inner = inner_sum[pl.ds(pl.multiple_of(block * 8, 8), 8), :][0:1, :] * row_scale * row_scale / DSSM
    scale, coefficient = as_column(row_scale), as_column(row_inner)
    weighted = norm_grad * scale
    gated_grad = weighted * gain_ref[...] - gated * coefficient
    dscan = gated_grad * z_silu
    grads_ref[:, 0:width] = (gated_grad * scan * (z_gate * (1.0 + z * (1.0 - z_gate)))).astype(BF)
    sums_ref[6:7, :] += jnp.sum(weighted * gated, axis=0, keepdims=True)
    sums_ref[5:6, :] += jnp.sum(dscan * values, axis=0, keepdims=True)
    held = states_ref[0]
    dheld = dmemory[...]
    dheld_low = dheld.astype(BF)
    enter_grad = (dscan * enter_w).astype(BF)
    left = leave_w * scaled
    passed = mm(key_in, dheld_low)
    arrived = mm(key_out, held)
    dkey_out = mm_nt(enter_grad, held)
    dkey_in = mm_nt(left, dheld_low)
    carry = enter_w[rows - 1 : rows, :]
    dmemory[...] = dheld * carry + mm_tn(key_out, enter_grad)
    enter_terms = dscan * enter_w * arrived
    leave_terms = left * passed
    carry_terms = jnp.sum(dheld * held.astype(F32), axis=0, keepdims=True) * carry
    gram = mm_nt(key_in, key_out)
    allowed = (feats[:, 0:1] == docs_ref[...]) & (iota2((rows, rows), 0) <= iota2((rows, rows), 1))
    bias = jnp.where(allowed, 0.0, MASKED)
    log_rows = log_decay.T
    front = iota2((rows, LANES), 1) < LANES // 2
    gram_grad = jnp.zeros((rows, rows), F32)
    lane_of = iota2((rows, LANES), 1)
    row_of = iota2((LANES, rows), 0)
    sent = jnp.zeros((rows, LANES), F32)
    received = jnp.zeros((LANES, rows), F32)
    inside_grads = []
    for pair in range(width // LANES):
        lanes = slice(pair * LANES, (pair + 1) * LANES)
        dy = dscan[:, lanes].astype(BF)
        part = scaled[:, lanes]
        stacked = jnp.concatenate([jnp.where(front, part, 0.0), jnp.where(front, 0.0, part)], axis=0)
        cross = mm_nt(stacked, dy)
        mixes = []
        for j, h in enumerate((2 * pair, 2 * pair + 1)):
            decay = jnp.exp(log_rows[h : h + 1, :] - log_decay[:, h : h + 1] + bias)
            mix = gram * decay
            mixes.append(mix.astype(BF))
            dmix = cross[j * rows : (j + 1) * rows, :]
            gram_grad = gram_grad + dmix * decay
            flow = dmix * mix
            sent = jnp.where(lane_of == h, jnp.sum(flow, axis=1, keepdims=True), sent)
            received = jnp.where(row_of == h, jnp.sum(flow, axis=0, keepdims=True), received)
        grads = mm(jnp.concatenate(mixes, axis=0), dy)
        inside_grads.append(jnp.where(front, grads[:rows], grads[rows:]))
    dscaled = jnp.concatenate(inside_grads, axis=1) + leave_w * passed
    dkey_in = dkey_in + mm(gram_grad, key_out)
    dkey_out = dkey_out + mm_tn(gram_grad, key_in)
    reduced = jnp.dot(
        split_lanes(
            jnp.concatenate([enter_terms, leave_terms, dscaled * values, jnp.broadcast_to(carry_terms, (8, width))], axis=0), 1
        ),
        reduce_ref[...],
        preferred_element_type=F32,
    )
    after = reduced[:rows] + received.T - sent
    upper = (iota2((rows, rows), 0) <= iota2((rows, rows), 1)).astype(F32)
    strict = (iota2((rows, rows), 0) > iota2((rows, rows), 1)).astype(F32)
    decay_grad = exact_mm(upper, after) + exact_mm(strict, reduced[rows : 2 * rows]) + reduced[3 * rows : 3 * rows + 1]
    dstep = decay_grad * heads_ref[1:2, :] + reduced[2 * rows : 3 * rows]
    draw = dstep * sigmoid(raw)
    grads_ref[:, 2 * width + 2 * states :] = draw.astype(BF)
    hsums_ref[0:1, :] += jnp.sum(draw, axis=0, keepdims=True)
    hsums_ref[1:2, :] += jnp.sum(decay_grad * step, axis=0, keepdims=True) * heads_ref[1:2, :]
    dvalues = dscaled * step_w + dscan * taps_ref[5:6, :]
    dpre = dvalues * (pre_gate * (1.0 + pre * (1.0 - pre_gate)))
    dboth = jnp.concatenate([dkey_in, dkey_out], axis=1)
    dpre_bc = dboth * (bc_gate * (1.0 + pre_bc * (1.0 - bc_gate)))
    for dpre_now, buffer, dbuffer, taps, totals, lanes in (
        (dpre, xbuf, dxbuf, taps_ref, sums_ref, slice(width, 2 * width)),
        (dpre_bc, bcbuf, dbcbuf, staps_ref, ssums_ref, slice(2 * width, 2 * width + 2 * states)),
    ):
        dbuffer[0:rows, :] = dpre_now
        grad = dpre_now * taps[3:4, :]
        totals[3:4, :] += jnp.sum(dpre_now * buffer[8 : 8 + rows, :], axis=0, keepdims=True)
        totals[4:5, :] += jnp.sum(dpre_now, axis=0, keepdims=True)
        for k in range(1, 4):
            grad = grad + dbuffer[k : k + rows, :] * feats[:, 5 + k : 6 + k] * taps[3 - k : 4 - k, :]
            totals[3 - k : 4 - k, :] += jnp.sum(
                dpre_now * buffer[8 - k : 8 - k + rows, :] * feats[:, k : k + 1], axis=0, keepdims=True
            )
        grads_ref[:, lanes] = grad.astype(BF)
        dbuffer[rows : rows + 8, :] = dbuffer[0:8, :]


def expand_matrix(width):
    one = np.arange(LANES)[:, None] == np.arange(width)[None, :] // (LANES // 2)
    return np.concatenate([one, one], axis=0).astype(ml_dtypes.bfloat16)


def spec(block, index):
    return pl.BlockSpec(block, index)


def mamba_forward(feats, doc_row, ssm_in, taps, staps, heads, gain, width, states2):
    total = ssm_in.shape[0]
    rows = CHUNK
    count = total // rows
    block = lambda w, place=0: spec((rows, w), lambda i: (i, place))
    whole = lambda a: spec(a.shape, lambda i: (0,) * a.ndim)
    expand = expand_matrix(width)
    return pl.pallas_call(
        mamba_fwd_kernel,
        grid=(count,),
        in_specs=[
            block(LANES), spec((1, rows), lambda i: (0, i)), block(width, 1), block(states2, 2 * width // states2),
            block(LANES, (2 * width + states2) // LANES), block(width), whole(taps), whole(staps), whole(heads), whole(expand), whole(gain),
        ],
        out_specs=[block(width), block(width), spec((8, LANES), lambda i: (i, 0)), spec((1, states2 // 2, width), lambda i: (i, 0, 0))],
        out_shape=[
            jax.ShapeDtypeStruct((total, width), F32),
            jax.ShapeDtypeStruct((total, width), BF),
            jax.ShapeDtypeStruct((8 * count, LANES), F32),
            jax.ShapeDtypeStruct((count, states2 // 2, width), BF),
        ],
        scratch_shapes=[
            pltpu.VMEM((rows + 8, width), F32), pltpu.VMEM((rows + 8, states2), F32), pltpu.VMEM((states2 // 2, width), F32),
        ],
        compiler_params=pltpu.CompilerParams(vmem_limit_bytes=VMEM_LIMIT),
        cost_estimate=pl.CostEstimate(flops=20 * 10**9, bytes_accessed=total * width * 20, transcendentals=total * width * 4),
        name="mamba_fwd",
    )(feats, doc_row, ssm_in, ssm_in, ssm_in, ssm_in, taps, staps, heads, expand, gain)


def swap_halves(values):
    lane = iota2(values.shape, 1) % (LANES // 2)
    return jnp.where(lane < LANES // 4, pltpu.roll(values, LANES - LANES // 4, 1), pltpu.roll(values, LANES // 4, 1))


def stack_heads(part):
    front = iota2(part.shape, 1) < LANES // 2
    zero = jnp.zeros_like(part)
    return jnp.concatenate([jnp.where(front, part, zero), jnp.where(front, zero, part)], axis=0)


def attention_fwd_kernel(
    groups, tensors, docs_col_ref, docs_ref, q_ref, kv_ref, cos_ref, sin_ref, low_ref, square_ref, out_ref, lse_ref, qrot_ref, keys_ref, values_ref, square_out_ref, *scratch,
):
    total = q_ref.shape[0]
    wide = low_ref.shape[1]
    exchange = TensorSum(tensors, *scratch)
    exchange.begin(square_ref[...])
    pairs = q_ref.shape[1] // LANES
    block = min(QBLOCK, total)
    cos, sin = cos_ref[...], sin_ref[...]
    front = iota2((total, LANES), 1) < LANES // 2
    for g in range(groups):
        lanes = slice(g * LANES, (g + 1) * LANES)
        raw = kv_ref[:, lanes]
        turned = raw * cos + swap_halves(raw) * sin
        keys_ref[:, lanes] = jnp.where(front, turned, pltpu.roll(turned, LANES // 2, 1)).astype(BF)
        values_ref[:, lanes] = jnp.where(front, pltpu.roll(raw, LANES // 2, 1), raw).astype(BF)
    for p in range(pairs):
        lanes = slice(p * LANES, (p + 1) * LANES)
        raw = q_ref[:, lanes]
        qrot_ref[:, lanes] = ((raw * cos + swap_halves(raw) * sin).astype(BF).astype(F32) * (LANES // 2) ** -0.5).astype(BF)
    front = iota2((block, LANES), 1) < LANES // 2
    lane_of = iota2((block, LANES), 1)
    for start in range(0, total, block):
        rows, end = slice(start, start + block), start + block
        allowed = (docs_col_ref[rows, 0:1] == docs_ref[:, :end]) & (
            iota2((block, end), 0) + start >= iota2((block, end), 1)
        )
        bias = jnp.where(allowed, 0.0, MASKED)
        bias = jnp.concatenate([bias, bias], axis=0)
        sums = jnp.zeros((block, LANES), F32)
        for p in range(pairs):
            lanes = slice(p * LANES, (p + 1) * LANES)
            g = p * groups // pairs
            kv = slice(g * LANES, (g + 1) * LANES)
            scores = mm_nt(stack_heads(qrot_ref[rows, lanes]), keys_ref[:end, kv]) + bias
            top = jnp.max(scores, axis=1, keepdims=True)
            raised = jnp.exp(scores - top)
            whole = jnp.sum(raised, axis=1, keepdims=True)
            mixed = mm(raised, values_ref[:end, kv]) / whole
            out_ref[rows, wide + p * LANES : wide + (p + 1) * LANES] = jnp.where(front, mixed[:block], mixed[block:]).astype(BF)
            logs = top + jnp.log(whole)
            sums = jnp.where(lane_of == 2 * p, logs[:block], sums)
            sums = jnp.where(lane_of == 2 * p + 1, logs[block:], sums)
        lse_ref[rows, :] = sums
    square_out_ref[...] = exchange.end()
    for i in range(total // LANES):
        piece = slice(i * LANES, (i + 1) * LANES)
        scale = as_column(gated_scale(square_out_ref[8 * i : 8 * i + 1, :]))
        out_ref[piece, :wide] = (low_ref[piece, :].astype(F32) * scale).astype(BF)


def attention_bwd_block(
    start, groups, docs_col_ref, docs_ref, qrot_ref, keys_ref, values_ref, lse_ref, up_ref, cos_ref, sin_ref, grads_ref, dk_acc, dv_acc,
):
    pairs = qrot_ref.shape[1] // LANES
    block = up_ref.shape[0]
    front = iota2((block, LANES), 1) < LANES // 2
    rows, end = slice(start, start + block), start + block
    allowed = (docs_col_ref[:end, 0:1] == docs_ref[:, rows]) & (
        iota2((end, block), 0) <= iota2((end, block), 1) + start
    )
    bias = jnp.where(allowed, 0.0, MASKED)
    logs = lse_ref[...].T
    cos, sin = cos_ref[rows, :], sin_ref[rows, :]
    for p in range(pairs):
        lanes = slice(p * LANES, (p + 1) * LANES)
        g = p * groups // pairs
        kv = slice(g * LANES, (g + 1) * LANES)
        keys, values = keys_ref[:end, kv], values_ref[:end, kv]
        queries = stack_heads(qrot_ref[rows, lanes])
        ups = stack_heads(up_ref[:, lanes])
        shift = jnp.concatenate([bias - logs[2 * p : 2 * p + 1], bias - logs[2 * p + 1 : 2 * p + 2]], axis=1)
        probs = jnp.exp(mm_nt(keys, queries) + shift)
        grads = mm_nt(values, ups)
        centre = jnp.sum(probs * grads, axis=0, keepdims=True)
        score_grads = (probs * (grads - centre)).astype(BF)
        dk_acc[:end, kv] += mm(score_grads, queries)
        dv_acc[:end, kv] += mm(probs, ups)
        dq = mm_tn(score_grads, keys)
        dq = jnp.where(front, dq[:block], dq[block:]) * (LANES // 2) ** -0.5
        grads_ref[rows, lanes] = (dq * cos - swap_halves(dq) * sin).astype(BF)


def attention_bwd_end(groups, pairs, cos_ref, sin_ref, grads_ref, dk_acc, dv_acc):
    total = dk_acc.shape[0]
    front = iota2((total, LANES), 1) < LANES // 2
    for g in range(groups):
        kv = slice(g * LANES, (g + 1) * LANES)
        dk, dv = dk_acc[:, kv], dv_acc[:, kv]
        dk = dk + pltpu.roll(dk, LANES // 2, 1)
        dk = dk * cos_ref[...] - swap_halves(dk) * sin_ref[...]
        dv = dv + pltpu.roll(dv, LANES // 2, 1)
        out = slice((pairs + g) * LANES, (pairs + g + 1) * LANES)
        grads_ref[:, out] = jnp.where(front, dk, dv).astype(BF)


def attention_forward(groups, tensors, doc_col, doc_row, qkv, cos, sin, query_width, low, squares, collective_id):
    total = qkv.shape[0]
    kv_width = qkv.shape[1] - query_width
    whole = lambda a: spec(a.shape, lambda i: (0,) * a.ndim)
    columns = lambda w, place=0: spec((total, w), lambda i: (0, place))
    return pl.pallas_call(
        functools.partial(attention_fwd_kernel, groups, tensors),
        grid=(1,),
        in_specs=[whole(doc_col), whole(doc_row), columns(query_width), columns(kv_width, query_width // kv_width), whole(cos), whole(sin), whole(low), whole(squares)],
        out_specs=[columns(low.shape[1] + query_width), columns(LANES), columns(query_width), columns(kv_width), columns(kv_width), whole(squares)],
        out_shape=[
            jax.ShapeDtypeStruct((total, low.shape[1] + query_width), BF), jax.ShapeDtypeStruct((total, LANES), F32),
            jax.ShapeDtypeStruct((total, query_width), BF), jax.ShapeDtypeStruct((total, kv_width), BF),
            jax.ShapeDtypeStruct((total, kv_width), BF), jax.ShapeDtypeStruct(squares.shape, F32),
        ],
        scratch_shapes=tensor_sum_scratch(tensors, squares.shape),
        compiler_params=pltpu.CompilerParams(vmem_limit_bytes=VMEM_LIMIT, collective_id=collective_id, has_side_effects=True),
        cost_estimate=pl.CostEstimate(flops=12 * 10**9, bytes_accessed=total * query_width * 10, transcendentals=total * total * 2),
        name="attention_fwd",
    )(doc_col, doc_row, qkv, qkv, cos, sin, low, squares)


def gather_kernel(
    count, tensors, shard_ref, tokens_ref, cotangent_ref, gain_ref, full_ref, all_tokens_ref, all_cotangent_ref, normed_ref, scale_ref, turned_ref,
    own_sem, send_sems, recv_sems, core_send, core_recv,
):
    unit, columns = shard_ref.shape
    levels = count // 4
    me = lax.axis_index("fsdp")
    half = columns // 2 // LANES * LANES
    parts = (slice(0, half), slice(half, columns))
    neighbours = (flipped(me, 1), flipped(me, 2))
    far = [flipped(me, 4 * d) for d in range(1, levels)]
    core = lax.axis_index("tensor")
    cores = [flipped(core, k) for k in range(1, tensors)]
    greet([("fsdp", p) for p in neighbours] + [("fsdp", p) for p in far] + [("tensor", p) for p in cores])

    def rows(owner):
        return pl.ds(pl.multiple_of(owner * unit, unit), unit)

    started = []

    def send(source, owner, lanes, slot, place):
        copy = remote(source, full_ref.at[rows(owner), lanes], send_sems.at[slot], recv_sems.at[slot], "fsdp", place)
        copy.start()
        started.append(copy)
        return copy

    def arrival(owner, lanes, slot):
        piece = full_ref.at[rows(owner), lanes]
        return remote(piece, piece, send_sems.at[slot], recv_sems.at[slot], "fsdp", neighbours[0])

    everything = slice(0, columns)
    own = pltpu.make_async_copy(shard_ref, full_ref.at[rows(me), :], own_sem)
    own.start()
    for d in range(1, levels):
        send(shard_ref, me, everything, d, far[d - 1])
    base = levels
    for axis in range(2):
        send(shard_ref, me, everything, base + axis * levels, neighbours[axis])
    cross = base + 2 * levels
    own_rows = tokens_ref.shape[0]
    share = lambda owner: pl.ds(pl.multiple_of(owner * own_rows, own_rows), own_rows)
    exchanges = []
    for k, place in enumerate(cores):
        for j, (source, target) in enumerate(((tokens_ref, all_tokens_ref), (cotangent_ref, all_cotangent_ref))):
            copy = remote(
                source, target.at[share(core), :], core_send.at[2 * k + j], core_recv.at[2 * k + j], "tensor", place
            )
            copy.start()
            exchanges.append(copy)
    all_tokens_ref[share(core), :] = tokens_ref[...]
    all_cotangent_ref[share(core), :] = cotangent_ref[...]
    for copy in exchanges:
        copy.wait()

    def norm(i, carry):
        piece = pl.ds(pl.multiple_of(i * LANES, LANES), LANES)
        values = all_tokens_ref[piece, :].astype(F32)
        scale = lax.rsqrt(jnp.mean(values * values, axis=1, keepdims=True) + EPS)
        scale_ref[piece, :] = scale
        normed = values * scale * gain_ref[...]
        normed_ref[piece, :] = normed.astype(BF)
        turned_ref[:, piece] = normed.T.astype(BF)
        return carry

    lax.fori_loop(0, normed_ref.shape[0] // LANES, norm, 0)

    def pass_on(d):
        for axis in range(2):
            owner = flipped(neighbours[axis], 4 * d)
            arrival(owner, everything, base + axis * levels + d).wait_recv()
            piece = full_ref.at[rows(owner), parts[axis]]
            send(piece, owner, parts[axis], cross + axis * levels + d, neighbours[1 - axis])

    for d in range(1, levels):
        arrival(far[d - 1], everything, d).wait_recv()
        for axis in range(2):
            send(full_ref.at[rows(far[d - 1]), :], far[d - 1], everything, base + axis * levels + d, neighbours[axis])
        pass_on(d - 1)
    pass_on(levels - 1)
    for d in range(levels):
        for axis in range(2):
            owner = flipped(me, 4 * d + 3)
            arrival(owner, parts[axis], cross + axis * levels + d).wait_recv()
    for copy in started:
        copy.wait_send()
    own.wait()


def gather_weights(shard, tokens, cotangent, gain, count, tensors, collective_id):
    unit, columns = shard.shape
    own_rows, hidden = tokens.shape
    total = own_rows * tensors
    slots = 5 * (count // 4)
    vmem, anywhere = pl.BlockSpec(memory_space=pltpu.VMEM), pl.BlockSpec(memory_space=pl.ANY)
    low = jax.ShapeDtypeStruct((total, hidden), BF)
    return pl.pallas_call(
        functools.partial(gather_kernel, count, tensors),
        in_specs=[anywhere, vmem, vmem, vmem],
        out_specs=[anywhere, vmem, vmem, vmem, vmem, vmem],
        out_shape=[jax.ShapeDtypeStruct((count * unit, columns), shard.dtype), low, low, low, jax.ShapeDtypeStruct((total, 1), F32),
            jax.ShapeDtypeStruct((hidden, total), BF),
        ],
        scratch_shapes=[
            pltpu.SemaphoreType.DMA, pltpu.SemaphoreType.DMA((slots,)), pltpu.SemaphoreType.DMA((slots,)),
            pltpu.SemaphoreType.DMA((2 * (tensors - 1),)), pltpu.SemaphoreType.DMA((2 * (tensors - 1),)),
        ],
        compiler_params=pltpu.CompilerParams(collective_id=collective_id, has_side_effects=True, vmem_limit_bytes=VMEM_LIMIT),
        cost_estimate=pl.CostEstimate(flops=0, bytes_accessed=2 * count * unit * columns * 2, transcendentals=0),
        name="gather_weights",
    )(shard, tokens, cotangent, gain)


def backward_kernel(c, *refs):
    r = types.SimpleNamespace(**dict(zip(c.names, refs)))
    now = pl.program_id(0)
    me, core = lax.axis_index("fsdp"), lax.axis_index("tensor")
    levels, unit, blocks, chunks, tiles = c.count // 4, c.unit, c.blocks, c.chunks, c.tiles
    near = (flipped(me, 1), flipped(me, 2))
    far = [None] + [flipped(me, 4 * d) for d in range(1, levels)]
    bits = [1 << k for k in range((c.count - 1).bit_length())]
    cores = [flipped(core, k) for k in range(1, c.tensors)]
    halves = [("tensor", flipped(core, 1 << k)) for k in range((c.tensors - 1).bit_length())]
    stages = [("fsdp", flipped(me, bit)) for bit in bits] + halves
    order = sorted(range(levels), key=lambda d: (d & -d if d else levels, -d))
    pieces = []
    for i, (name, lanes, path, out, out_lanes) in enumerate(c.pieces):
        pieces.append((i, getattr(r, name), lanes, path, getattr(r, out), out_lanes))
    early, late = pieces[: c.early], pieces[c.early :]

    def own_copies():
        copies = []
        for i, grad, lanes, path, _, _ in early:
            parts = getattr(r, "own%d" % i)
            for d in order:
                for k, owner in ((d, flipped(near[path], 4 * d)), (levels + d, flipped(me, 4 * d))):
                    copies.append(pltpu.make_async_copy(grad.at[rows(owner), lanes], parts.at[k], r.own_sems.at[i, k]))
        return copies

    def own_part(i, grad, lanes, owner, k):
        if i < c.early:
            return getattr(r, "own%d" % i)[k].astype(F32)
        return grad[rows(owner), lanes].astype(F32)

    cross, along, inbound = [], [], []
    for i in range(len(pieces)):
        cross.append(getattr(r, "cross%d" % i))
        along.append((getattr(r, "along_x%d" % i), getattr(r, "along_y%d" % i)))
        inbound.append(getattr(r, "inbound%d" % i))

    def rows(owner):
        return pl.ds(pl.multiple_of(owner * unit, unit), unit)

    def link(source, target, i, kind, d, place):
        slot = (i * 4 + kind) * levels + d
        return remote(source, target, r.send_sems.at[slot], r.recv_sems.at[slot], "fsdp", place)

    def begin(group, d):
        for i, grad, lanes, path, _, _ in group:
            link(grad.at[rows(flipped(me, 4 * d + 3)), lanes], cross[i].at[d], i, 0, d, near[1 - path]).start()

    def raw(group, d):
        for i, grad, lanes, path, _, _ in group:
            other = 1 - path
            link(grad.at[rows(flipped(near[other], 4 * d)), lanes], along[i][other].at[d], i, 1 + other, d, near[other]).start()

    def middle(group, d):
        for i, grad, lanes, path, _, _ in group:
            link(cross[i].at[d], cross[i].at[d], i, 0, d, near[0]).wait_recv()
            own = own_part(i, grad, lanes, flipped(near[path], 4 * d), d)
            cross[i][d] = (own + cross[i][d].astype(F32)).astype(BF)
            link(cross[i].at[d], along[i][path].at[d], i, 1 + path, d, near[path]).start()

    def finish(group, d):
        lowest = d & -d if d else levels
        for i, grad, lanes, path, out, out_lanes in group:
            for axis in range(2):
                link(along[i][axis].at[d], along[i][axis].at[d], i, 1 + axis, d, near[0]).wait_recv()
            own = own_part(i, grad, lanes, flipped(me, 4 * d), levels + d)
            total = own + along[i][0][d].astype(F32) + along[i][1][d].astype(F32)
            bit = 1
            while bit < lowest:
                slot = d + bit - 1
                link(inbound[i].at[slot], inbound[i].at[slot], i, 3, d + bit, near[0]).wait_recv()
                total = total + inbound[i][slot].astype(F32)
                bit *= 2
            if d:
                along[i][0][d] = total.astype(BF)
                link(along[i][0].at[d], inbound[i].at[d - 1], i, 3, d, far[lowest]).start()
            else:
                out[:, out_lanes] = total

    weights_copy = pltpu.make_async_copy(r.weights.at[:, 0 : r.held.shape[1]], r.held, r.local_sems.at[0])
    own_rows = r.tokens.shape[0]
    share = lambda owner: pl.ds(pl.multiple_of(owner * own_rows, own_rows), own_rows)
    turned_copy = pltpu.make_async_copy(r.normed_turned, r.turned, r.local_sems.at[2])
    branch_copy = pltpu.make_async_copy(r.branch_low.at[share(core), :], r.branch_own, r.local_sems.at[1])
    inners = TensorSum(c.tensors, r.inner_own, r.inner_in, r.inner_send, r.inner_recv)

    @pl.when(now == 0)
    def _():
        greet([("fsdp", p) for p in near] + [("fsdp", flipped(me, bit)) for bit in bits[2:]] + [("tensor", p) for p in cores])
        for d in order:
            begin(early, d)
        for copy in own_copies():
            copy.start()
        turned_copy.start()
        weights_copy.start()
        branch_copy.start()
        r.dk_acc[...] = jnp.zeros_like(r.dk_acc)
        r.dv_acc[...] = jnp.zeros_like(r.dv_acc)

    block = r.mix_up.shape[0]
    for j in range(blocks):

        @pl.when(now == j)
        def _(j=j):
            for i in range(block // LANES):
                part = slice(i * LANES, (i + 1) * LANES)
                inner = jnp.sum(r.mix_norm[part, :].astype(F32) * r.mix_low[part, :].astype(F32), axis=1, keepdims=True)
                at = 8 * (j * (block // LANES) + i)
                r.inner_rows[at : at + 8, :] = jnp.broadcast_to(inner, (LANES, LANES)).T[0:8, :]
            attention_bwd_block(
                j * block, c.groups, r.feats_all, r.doc_row, r.qrot, r.keys, r.values, r.lse, r.mix_up, r.cos, r.sin, r.qkv_grad,
                r.dk_acc, r.dv_acc,
            )
            if j == blocks - 1:
                inners.begin(r.inner_rows[...], met=True)
                attention_bwd_end(c.groups, r.qrot.shape[1] // LANES, r.cos, r.sin, r.qkv_grad, r.dk_acc, r.dv_acc)

    @pl.when(now == blocks)
    def _():
        r.dxbuf[CHUNK : CHUNK + 8, :] = jnp.zeros((8, r.dxbuf.shape[1]), F32)
        r.dbcbuf[CHUNK : CHUNK + 8, :] = jnp.zeros((8, r.dbcbuf.shape[1]), F32)
        r.dmemory[...] = jnp.zeros_like(r.dmemory)
        r.x_sums[...] = jnp.zeros_like(r.x_sums)
        r.state_sums[...] = jnp.zeros_like(r.state_sums)
        r.head_sums[...] = jnp.zeros_like(r.head_sums)
        r.inner_sum[...] = inners.end()

    @pl.when((now >= blocks) & (now < blocks + chunks))
    def _():
        chunk = chunks - 1 - (now - blocks)
        mamba_bwd_block(
            r.feats, r.square, r.inner_sum, chunk, r.docs, r.x, r.x_before, r.bc, r.bc_before, r.step, r.z, r.scan, r.states,
            r.norm_grad, r.taps, r.staps, r.heads, r.expand, r.reduce, r.gain,
            r.ssm_grad.at[pl.ds(pl.multiple_of(chunk * CHUNK, CHUNK), CHUNK), :], r.x_sums, r.state_sums, r.head_sums,
            r.xbuf, r.bcbuf, r.dxbuf, r.dbcbuf, r.dmemory,
        )

    for k, d in enumerate(order):

        @pl.when(now == blocks + 1 + k)
        def _(d=d):
            if d == order[0]:
                for copy in own_copies():
                    copy.wait()
            middle(early, d)
            raw(early, d)

    base = blocks + chunks

    @pl.when(now == base)
    def _():
        weights_copy.wait()

    ssm_wide = r.ssm_grad.shape[1]

    @pl.when((now >= base) & (now < base + tiles))
    def _():
        part = pl.ds(pl.multiple_of((now - base) * c.tile, c.tile), c.tile)
        r.normed_part[part, :] = (
            mm_nt(r.ssm_grad[part, :], r.held[:, :ssm_wide]) + mm_nt(r.qkv_grad[part, :], r.held[:, ssm_wide:])
        ).astype(BF)

    def normed_copies():
        return [
            remote(r.normed_part.at[share(place), :], r.normed_in.at[k], r.core_send.at[k], r.core_recv.at[k], "tensor", place)
            for k, place in enumerate(cores)
        ]

    for k, d in enumerate(order):

        @pl.when(now == base + tiles + k)
        def _(d=d):
            quad = pl.ds(pl.multiple_of(flipped(me, 4 * d) // 4 * (4 * unit), 4 * unit), 4 * unit)
            if d == order[0]:
                turned_copy.wait()
                for copy in normed_copies():
                    copy.start()
            turned = r.turned[quad, :]
            r.held[quad, :ssm_wide] = jnp.dot(turned, r.ssm_grad[...], preferred_element_type=F32).astype(BF)
            r.held[quad, ssm_wide:] = jnp.dot(turned, r.qkv_grad[...], preferred_element_type=F32).astype(BF)
            begin(late, d)
            raw(late, d)

    for k, step in enumerate((base + 1, base + tiles + 1)):

        @pl.when(now == step)
        def _(d=order[k]):
            finish(early, d)

    settled = []

    def stage_copy(k):
        axis, place = stages[k]
        return remote(r.sums.at[k], r.sums_in.at[k], r.sum_send.at[k], r.sum_recv.at[k], axis, place)

    def next_stage():
        k = len(settled)
        if k < len(stages):
            stage_copy(k).wait()
            r.sums[k + 1] = r.sums[k] + r.sums_in[k]
            settled.append(k)
            if k + 1 < len(stages):
                stage_copy(k + 1).start()

    @pl.when(now == base + tiles + levels)
    def _():
        for copy in normed_copies():
            copy.wait()
        branch_copy.wait()
        r.gain_sum[...] = jnp.zeros_like(r.gain_sum)
        size = min(CHUNK, own_rows)

        def first_norm_back(i, carry):
            part = pl.ds(pl.multiple_of(i * size, size), size)
            whole = pl.ds(pl.multiple_of(core * own_rows + i * size, size), size)
            grad = r.normed_part[whole, :].astype(F32)
            for k in range(len(cores)):
                grad = grad + r.normed_in[k, part, :].astype(F32)
            scale = r.scale[whole, :]
            shape = r.tokens[part, :].astype(F32) * scale
            weighted = grad * r.input_gain[...]
            inner = jnp.mean(weighted * shape, axis=1, keepdims=True)
            r.input_grad[part, :] = r.branch_own[part, :].astype(F32) + scale * (weighted - shape * inner)
            r.gain_sum[0:1, :] += jnp.sum(grad * shape, axis=0, keepdims=True)
            return carry

        lax.fori_loop(0, own_rows // size, first_norm_back, 0)
        at = 0
        for ref in (r.x_sums, r.head_sums, r.state_sums):
            r.sums[0, :, at : at + ref.shape[1]] = ref[...]
            at += ref.shape[1]
        eighth = r.gain_sum.shape[1] // 8
        for ref, factor in ((r.second_part, 1.0 / c.tensors), (r.gain_sum, 1.0)):
            for k in range(8):
                r.sums[0, k : k + 1, at : at + eighth] = ref[0:1, k * eighth : (k + 1) * eighth] * factor
            at += eighth
        stage_copy(0).start()
        for d in order[2:]:
            finish(early, d)
            next_stage()
        for d in order:
            middle(late, d)
        for d in order:
            finish(late, d)
            next_stage()
        while len(settled) < len(stages):
            next_stage()
        r.small_out[:, : c.split] = r.sums[len(bits), :, : c.split]
        r.small_out[:, c.split :] = r.sums[len(stages), :, c.split :]
        states2 = c.state_at[1] - c.state_at[0]
        wide_shared = r.shared.shape[2]
        leading = core * (wide_shared - states2) // (c.tensors * LANES)
        r.shared[0, :, :states2] = r.out_first[:, c.state_at[0] : c.state_at[1]]
        for g in range((wide_shared - states2) // LANES):
            value = jnp.zeros((unit, LANES), F32)
            for j in range(c.groups):
                value = jnp.where(leading + j == g, r.out_first[:, c.kv_at + j * LANES : c.kv_at + (j + 1) * LANES], value)
            r.shared[0, :, states2 + g * LANES : states2 + (g + 1) * LANES] = value
        for k, (axis, place) in enumerate(halves):
            copy = remote(r.shared.at[k], r.shared_in.at[k], r.half_send.at[k], r.half_recv.at[k], axis, place)
            copy.start()
            copy.wait()
            r.shared[k + 1] = r.shared[k] + r.shared_in[k]
        r.shared_out[...] = r.shared[len(halves)]
        for i in range(len(pieces)):
            for d in range(levels):
                for kind in range(4):
                    if kind < 3 or d:
                        link(cross[i].at[d], cross[i].at[d], i, kind, d, near[0]).wait_send()


def backward(
    groups, feats, doc_row, qrot, keys, values, lse, mix_grad, mix, cos, sin, squares, ssm_in, scan, states, taps, staps, heads, gain,
    grad_gate_up, grad_down, grad_mix, normed_turned, first, branch_low, tokens, scale, input_gain, second_part, width, states2,
    count, tensors, collective_id,
):
    total, hidden = branch_low.shape
    own_rows = tokens.shape[0]
    unit = hidden // count
    levels = count // 4
    query_wide, kv_wide = qrot.shape[1], keys.shape[1]
    block, tile = min(QBLOCK, total), min(QBLOCK, total)
    blocks, chunks, tiles = total // block, total // CHUNK, total // tile
    ssm_wide, qkv_wide = 2 * width + states2 + LANES, query_wide + kv_wide
    chunk = lambda s: jnp.clip(chunks - 1 - (s - blocks), 0, chunks - 1)
    query = lambda s: jnp.minimum(s, blocks - 1)
    by_chunk = lambda w, place=0: spec((CHUNK, w), lambda s: (chunk(s), place))
    by_query = lambda w, place=0: spec((block, w), lambda s: (query(s), place))
    before = lambda w, place=0: spec((8, w), lambda s: (jnp.maximum(chunk(s) * (CHUNK // 8) - 1, 0), place))
    whole = lambda a: pl.BlockSpec(a.shape, lambda s: (0,) * a.ndim, pipeline_mode=pl.Buffered(1))
    anywhere = pl.BlockSpec(memory_space=pl.ANY)
    vmem = pl.BlockSpec(memory_space=pltpu.VMEM)
    expand = expand_matrix(width)
    reduce = np.concatenate([expand[:LANES].T] * 2, axis=0)
    state_place, step_place = 2 * width // states2, (2 * width + states2) // LANES
    ins = [
        ("feats_all", feats, whole(feats)), ("doc_row", doc_row, whole(doc_row)), ("qrot", qrot, whole(qrot)), ("keys", keys, whole(keys)),
        ("values", values, whole(values)), ("lse", lse, by_query(LANES)), ("mix_up", mix_grad, by_query(query_wide, width // query_wide)),
        ("mix_norm", mix_grad, by_query(width)), ("mix_low", mix, by_query(width)), ("cos", cos, whole(cos)), ("sin", sin, whole(sin)),
        ("feats", feats, by_chunk(LANES)), ("docs", doc_row, spec((1, CHUNK), lambda s: (0, chunk(s)))),
        ("square", squares, spec((8, LANES), lambda s: (chunk(s), 0))), ("x", ssm_in, by_chunk(width, 1)),
        ("x_before", ssm_in, before(width, 1)), ("bc", ssm_in, by_chunk(states2, state_place)),
        ("bc_before", ssm_in, before(states2, state_place)), ("step", ssm_in, by_chunk(LANES, step_place)),
        ("z", ssm_in, by_chunk(width)), ("scan", scan, by_chunk(width)),
        ("states", states, spec((1, states2 // 2, width), lambda s: (chunk(s), 0, 0))), ("norm_grad", mix_grad, by_chunk(width)),
        ("taps", taps, whole(taps)), ("staps", staps, whole(staps)), ("heads", heads, whole(heads)), ("expand", expand, whole(expand)),
        ("reduce", reduce, whole(reduce)), ("gain", gain, whole(gain)), ("grad_gate_up", grad_gate_up, anywhere),
        ("grad_down", grad_down, anywhere), ("grad_mix", grad_mix, anywhere),
        ("normed_turned", normed_turned, anywhere), ("weights", first, anywhere), ("branch_low", branch_low, anywhere),
        ("tokens", tokens, whole(tokens)), ("scale", scale, whole(scale)), ("input_gain", input_gain, whole(input_gain)),
        ("second_part", second_part, whole(second_part)),
    ]
    small = width + LANES + states2 + 2 * (hidden // 8)
    shared = states2 + KEYVAL_HEADS * LANES
    outs = [
        ("input_grad", (own_rows, hidden)), ("out_gate_up", (unit, grad_gate_up.shape[1])), ("out_down", (unit, grad_down.shape[1])),
        ("out_mix", (unit, grad_mix.shape[1])), ("out_first", (unit, ssm_wide + qkv_wide)), ("small_out", (8, small)),
        ("shared_out", (unit, shared)),
    ]
    cut = -(-(ssm_wide + qkv_wide) // (2 * LANES)) * LANES
    every = lambda a: slice(0, a)
    pieces = [
        ("grad_gate_up", every(grad_gate_up.shape[1]), 0, "out_gate_up", every(grad_gate_up.shape[1])),
        ("grad_down", every(grad_down.shape[1]), 1, "out_down", every(grad_down.shape[1])),
        ("grad_mix", every(grad_mix.shape[1]), 1, "out_mix", every(grad_mix.shape[1])),
        ("held", slice(0, cut), 0, "out_first", slice(0, cut)),
        ("held", slice(cut, ssm_wide + qkv_wide), 1, "out_first", slice(cut, ssm_wide + qkv_wide)),
    ]
    steps, stages = (tensors - 1).bit_length(), (count - 1).bit_length() + (tensors - 1).bit_length()
    inner = (total // 16, LANES)
    f32 = lambda *dims: pltpu.VMEM(dims, F32)
    low = lambda *dims: pltpu.VMEM(dims, BF)
    dma = lambda n: pltpu.SemaphoreType.DMA((n,))
    scratch = [
        ("dk_acc", f32(total, kv_wide)), ("dv_acc", f32(total, kv_wide)), ("qkv_grad", low(total, qkv_wide)), ("inner_rows", f32(*inner)),
        ("inner_sum", f32(*inner)), ("inner_own", f32(steps + 1, *inner)), ("inner_in", f32(steps, *inner)), ("inner_send", dma(steps)),
        ("inner_recv", dma(steps)), ("xbuf", f32(CHUNK + 8, width)), ("bcbuf", f32(CHUNK + 8, states2)), ("dxbuf", f32(CHUNK + 8, width)),
        ("dbcbuf", f32(CHUNK + 8, states2)), ("dmemory", f32(states2 // 2, width)), ("ssm_grad", low(total, ssm_wide)),
        ("x_sums", f32(8, width)), ("state_sums", f32(8, states2)), ("head_sums", f32(8, LANES)),
        ("held", low(hidden, ssm_wide + qkv_wide)), ("branch_own", low(own_rows, hidden)),
        ("normed_part", low(total, hidden)), ("normed_in", low(tensors - 1, own_rows, hidden)), ("gain_sum", f32(8, hidden)),
        ("sums", f32(stages + 1, 8, small)), ("sums_in", f32(stages, 8, small)), ("sum_send", dma(stages)), ("sum_recv", dma(stages)),
        ("shared", f32(steps + 1, unit, shared)), ("shared_in", f32(steps, unit, shared)), ("half_send", dma(steps)),
        ("half_recv", dma(steps)), ("core_send", dma(tensors - 1)), ("core_recv", dma(tensors - 1)), ("local_sems", dma(3)), ("turned", low(hidden, total)),
        ("own_sems", pltpu.SemaphoreType.DMA((3, 2 * levels))),
        ("send_sems", dma(4 * levels * len(pieces))), ("recv_sems", dma(4 * levels * len(pieces))),
    ]
    for i, piece in enumerate(pieces):
        columns = piece[1].stop - piece[1].start
        for name, slots in (("cross", levels), ("along_x", levels), ("along_y", levels), ("inbound", levels - 1)):
            scratch.append((name + str(i), low(slots, unit, columns)))
    for i in range(3):
        scratch.append(("own" + str(i), low(2 * levels, unit, pieces[i][1].stop)))
    names = [v[0] for v in ins] + [v[0] for v in outs] + [v[0] for v in scratch]
    c = types.SimpleNamespace(
        names=names, pieces=pieces, early=3, count=count, tensors=tensors, unit=unit, blocks=blocks, chunks=chunks, tiles=tiles, tile=tile,
        groups=groups, split=width + LANES, state_at=(2 * width, 2 * width + states2), kv_at=ssm_wide + query_wide,
    )
    return pl.pallas_call(
        functools.partial(backward_kernel, c),
        grid=(blocks + chunks + levels + tiles + 1,),
        in_specs=[v[2] for v in ins],
        out_specs=[vmem] * len(outs),
        out_shape=[jax.ShapeDtypeStruct(v[1], F32) for v in outs],
        scratch_shapes=[v[1] for v in scratch],
        compiler_params=pltpu.CompilerParams(collective_id=collective_id, has_side_effects=True, vmem_limit_bytes=VMEM_ALL),
        name="backward",
    )(*(v[1] for v in ins))


def tensor_swap(values):
    return lax.ppermute(values, "tensor", [(0, 1), (1, 0)])


def tensor_pair(values):
    if lax.axis_size("tensor") == 2:
        return values, tensor_swap(values)
    return lax.psum(values.astype(F32), "tensor").astype(values.dtype), jnp.zeros_like(values)


def pad_to(values, size, axis=-1):
    pads = [(0, 0)] * values.ndim
    pads[axis] = (0, size - values.shape[axis])
    return jnp.pad(values, pads) if size > values.shape[axis] else values


def pack_kernel(
    mixer_ref, state_ref, step_ref, query_ref, keyval_ref, proj_ref, attention_ref, gate_up_ref, down_ref,
    first_ref, second_ref,
):
    unit = state_ref.shape[0]
    width, wide = mixer_ref.shape[2], -(-mixer_ref.shape[2] // LANES) * LANES
    same = (iota2((unit, unit), 0) == iota2((unit, unit), 1)).astype(BF)
    place = 0

    def put(out_ref, value, size):
        nonlocal place
        value = value.astype(BF)
        if size > value.shape[1]:
            value = jnp.concatenate([value, jnp.zeros((unit, size - value.shape[1]), BF)], axis=1)
        out_ref[:, place : place + size] = value
        place += size

    put(first_ref, mixer_ref[:, 0, :], wide)
    put(first_ref, mixer_ref[:, 1, :], wide)
    put(first_ref, state_ref[...], state_ref.shape[1])
    put(first_ref, lax.dot_general(same, step_ref[...].astype(BF), (((1,), (1,)), ((), ())), preferred_element_type=F32), LANES)
    query_wide = -(-query_ref.shape[1] // LANES) * LANES
    put(first_ref, query_ref[...], query_wide)
    put(first_ref, keyval_ref[...], keyval_ref.shape[1])
    put(first_ref, proj_ref[...], wide)
    put(first_ref, attention_ref[...], query_wide)
    place = 0
    put(second_ref, gate_up_ref[:, 0, :], gate_up_ref.shape[2])
    put(second_ref, gate_up_ref[:, 1, :], gate_up_ref.shape[2])
    put(second_ref, down_ref[...], down_ref.shape[1])


def pack_weights(mixer, state, step, query, keyval, proj, attention, gate_up, down):
    unit = state.shape[0]
    lanes = lambda size: -(-size // LANES) * LANES
    first = 3 * lanes(mixer.shape[2]) + state.shape[1] + LANES + 2 * lanes(query.shape[1]) + keyval.shape[1]
    second = 2 * gate_up.shape[2] + down.shape[1]
    whole = lambda shape: spec(shape, lambda i: (0,) * len(shape))
    weights = (mixer, state, step, query, keyval, proj, attention, gate_up, down)
    return pl.pallas_call(
        pack_kernel,
        grid=(1,),
        in_specs=[whole(v.shape) for v in weights],
        out_specs=[whole((unit, first)), whole((unit, second))],
        out_shape=[jax.ShapeDtypeStruct((unit, first), BF), jax.ShapeDtypeStruct((unit, second), BF)],
        compiler_params=pltpu.CompilerParams(vmem_limit_bytes=VMEM_WHOLE),
        name="pack_weights",
    )(*weights)


def table_kernel(
    docs_ref, conv_ref, conv_bias_ref, state_conv_ref, state_bias_ref, step_bias_ref, decay_ref, skip_ref,
    feats_ref, cos_ref, sin_ref, taps_ref, state_taps_ref, heads_ref,
):
    total = docs_ref.shape[1]
    docs = docs_ref[...]
    tall = jnp.broadcast_to(docs, (LANES, total)).T
    spot = iota2((1, total), 1)
    begin = jnp.sum((tall[:, 0:1] < docs).astype(F32), axis=0, keepdims=True)
    rows = [docs]
    eight = jnp.broadcast_to(docs, (8, total))
    for k in (1, 2, 3):
        rows.append(jnp.where(spot >= k, (pltpu.roll(eight, k, 1)[0:1] == docs).astype(F32), 0.0))
    blocks = [docs[:, i : i + CHUNK] for i in range(0, total, CHUNK)]
    before = [jnp.full((1, 1), -1.0, F32)] + [v[:, CHUNK - 1 :] for v in blocks[:-1]]
    rows.append(jnp.concatenate([(v == w).astype(F32) for v, w in zip(blocks, before)], axis=1))
    rows.append(jnp.concatenate([(v == v[:, CHUNK - 1 :]).astype(F32) for v in blocks], axis=1))
    for k in (1, 2, 3):
        rows.append(jnp.where(spot < total - k, (pltpu.roll(eight, total - k, 1)[0:1] == docs).astype(F32), 0.0))
    rows.append(spot.astype(F32) - begin)
    rows.append(jnp.zeros((LANES - len(rows), total), F32))
    feats = jnp.concatenate(rows, axis=0).T
    feats_ref[...] = feats
    lane = iota2((1, LANES), 1)
    rates = jnp.exp((lane % (HEAD_SIZE // 2)).astype(F32) * (-2.0 * math.log(THETA) / HEAD_SIZE))
    angles = feats[:, 9:10] * rates
    cos_ref[...] = jnp.cos(angles)
    sin_ref[...] = jnp.sin(angles) * jnp.where(lane % HEAD_SIZE < HEAD_SIZE // 2, -1.0, 1.0)
    width, heads = conv_ref.shape[1], skip_ref.shape[1]
    taps_ref[...] = jnp.zeros_like(taps_ref)
    taps_ref[0:4, :width] = conv_ref[...]
    taps_ref[4:5, :width] = conv_bias_ref[...]
    spread = (iota2((heads, width), 0) == iota2((heads, width), 1) // (width // heads)).astype(F32)
    taps_ref[5:6, :width] = exact_mm(jnp.broadcast_to(skip_ref[...], (8, heads)), spread)[0:1]
    state_taps_ref[...] = jnp.zeros_like(state_taps_ref)
    state_taps_ref[0:4, :] = state_conv_ref[...]
    state_taps_ref[4:5, :] = state_bias_ref[...]
    heads_ref[...] = jnp.zeros_like(heads_ref)
    heads_ref[0:1, :heads] = step_bias_ref[...]
    heads_ref[1:2, :heads] = -jnp.exp(decay_ref[...])


def make_tables(docs, wide, conv, conv_bias, state_conv, state_bias, step_bias, decay, skip):
    total = docs.shape[1]
    shape = lambda r, c: jax.ShapeDtypeStruct((r, c), F32)
    return pl.pallas_call(
        table_kernel,
        out_shape=[shape(total, LANES), shape(total, LANES), shape(total, LANES), shape(8, wide), shape(8, state_conv.shape[1]), shape(8, LANES)],
        compiler_params=pltpu.CompilerParams(vmem_limit_bytes=VMEM_LIMIT),
        name="make_tables",
    )(docs, conv, conv_bias[None], state_conv, state_bias[None], step_bias[None], decay[None], skip[None])


def second_norm_kernel(tokens_ref, part_ref, part_in_ref, gain_ref, middle_ref, second_ref, scale_ref):
    middle = tokens_ref[...].astype(F32) + part_ref[...].astype(F32) + part_in_ref[...].astype(F32)
    scale = lax.rsqrt(jnp.mean(middle * middle, axis=1, keepdims=True) + EPS)
    middle_ref[...] = middle
    scale_ref[...] = scale
    second_ref[...] = (middle * scale * gain_ref[...]).astype(BF)


def by_rows(kernel, name, rows, count, ins, outs, scalars=(), tensors=1):
    number = len(scalars)

    def place(shape, kind):
        if kind == "whole":
            return spec(shape, lambda i, *s: (0,) * len(shape))
        if kind == "own":
            own = shape[0] // rows if shape[0] < rows * count else count // tensors
            if shape[0] < rows * count:
                return spec((rows, shape[1]), lambda i, *s: (jnp.clip(i - s[0][0] * own, 0, own - 1), 0))
            return spec((rows, shape[1]), lambda i, *s: (jnp.clip(i, s[0][0] * own, s[0][0] * own + own - 1), 0))
        return spec((rows, shape[1]), lambda i, *s: (i, 0))

    return pl.pallas_call(
        kernel,
        grid_spec=pltpu.PrefetchScalarGridSpec(
            num_scalar_prefetch=number,
            grid=(count,),
            in_specs=[place(v.shape, kind) for v, kind in ins],
            out_specs=[place((r, c), kind) for r, c, _, kind in outs],
        ),
        out_shape=[jax.ShapeDtypeStruct((r, c), dtype) for r, c, dtype, _ in outs],
        compiler_params=pltpu.CompilerParams(vmem_limit_bytes=VMEM_LIMIT),
        name=name,
    )(*scalars, *(v for v, _ in ins))


def ffn_kernel(second_ref, up_ref, weights_ref, active_ref, grads_ref, out_ref, back_ref):
    ffn = active_ref.shape[1]
    gate_vals = jnp.dot(second_ref[...], weights_ref[:, : 2 * ffn], preferred_element_type=F32)
    active_grad = jnp.dot(up_ref[...], weights_ref[:, 2 * ffn :], preferred_element_type=F32)
    gate, up = gate_vals[:, :ffn], gate_vals[:, ffn:]
    sig = sigmoid(gate)
    silu = gate * sig
    active = (silu * up).astype(BF)
    active_ref[...] = active
    grads_ref[:, :ffn] = (active_grad * up * (sig + silu * (1.0 - sig))).astype(BF)
    grads_ref[:, ffn:] = (active_grad * silu).astype(BF)
    out_ref[...] = mm_nt(active, weights_ref[:, 2 * ffn :]).astype(BF)
    back_ref[...] = mm_nt(grads_ref[...], weights_ref[:, : 2 * ffn]).astype(BF)


def second_back_kernel(
    own_count, core_ref, grad_ref, grad_in_ref, middle_ref, scale_ref, up_ref, gain_ref, part_ref, part_in_ref, low_ref, gain_grad_ref, out_ref
):
    offset = pl.program_id(0) - core_ref[0] * own_count

    @pl.when(pl.program_id(0) == 0)
    def _():
        gain_grad_ref[...] = jnp.zeros_like(gain_grad_ref)

    grad = grad_ref[...].astype(F32) + grad_in_ref[...].astype(F32)
    middle, scale = middle_ref[...], scale_ref[...]
    shape = middle * scale
    weighted = grad * gain_ref[...]
    inner = jnp.mean(weighted * shape, axis=1, keepdims=True)
    low_ref[...] = (up_ref[...].astype(F32) + scale * (weighted - shape * inner)).astype(BF)
    gain_grad_ref[0:1, :] += jnp.sum(grad * shape, axis=0, keepdims=True)

    @pl.when((offset >= 0) & (offset < own_count))
    def _():
        out_ref[...] = (middle + part_ref[...].astype(F32) + part_in_ref[...].astype(F32)).astype(BF)


def finish_kernel(
    sizes, first_ref, mix_ref, shared_ref, small_ref, gate_up_sum_ref, down_sum_ref,
    mixer_ref, state_ref, step_ref, conv_ref, conv_bias_ref, state_conv_ref, state_bias_ref, step_bias_ref, decay_ref, skip_ref,
    mixer_gain_ref, proj_ref, query_ref, keyval_ref, attention_ref, gate_up_ref, down_ref, second_gain_ref, input_gain_ref,
):
    wide, width, states2, heads, query_width, ffn = sizes
    mixer_ref[:, 0, :] = first_ref[:, :width]
    mixer_ref[:, 1, :] = first_ref[:, wide : wide + width]
    state_ref[...] = shared_ref[:, :states2]
    step_ref[...] = first_ref[:, 2 * wide + states2 : 2 * wide + states2 + heads]
    start = 2 * wide + states2 + LANES
    query_ref[...] = first_ref[:, start : start + query_width]
    groups = [shared_ref[:, i : i + LANES] for i in range(states2, shared_ref.shape[1], LANES)]
    keyval_ref[:, 0, :] = jnp.concatenate([v[:, :HEAD_SIZE] for v in groups], axis=1)
    keyval_ref[:, 1, :] = jnp.concatenate([v[:, HEAD_SIZE:] for v in groups], axis=1)
    proj_ref[...] = mix_ref[:, :width]
    attention_ref[...] = mix_ref[:, wide : wide + query_width]
    gate_up_ref[:, 0, :] = gate_up_sum_ref[:, :ffn]
    gate_up_ref[:, 1, :] = gate_up_sum_ref[:, ffn:]
    down_ref[...] = down_sum_ref[...]
    conv_ref[...] = small_ref[0:4, :width]
    conv_bias_ref[...] = small_ref[4:5, :width]
    mixer_gain_ref[...] = small_ref[6:7, :width]
    place = iota2((width, heads), 0) // (width // heads)
    gather = (place == iota2((width, heads), 1)).astype(F32)
    skip_ref[...] = exact_mm(jnp.broadcast_to(small_ref[5:6, :width], (8, width)), gather)[0:1]
    step_bias_ref[...] = small_ref[0:1, wide : wide + heads]
    decay_ref[...] = small_ref[1:2, wide : wide + heads]
    base = wide + LANES
    state_conv_ref[...] = small_ref[0:4, base : base + states2]
    state_bias_ref[...] = small_ref[4:5, base : base + states2]
    base += states2
    for out_ref in (second_gain_ref, input_gain_ref):
        size = out_ref.shape[1]
        out_ref[...] = jnp.concatenate([small_ref[r : r + 1, base : base + size // 8] for r in range(8)], axis=1)
        base += size // 8


def body(
    layer_input, doc_ids, input_gain, mixer_weight, state_weight, step_weight, conv_weight, conv_bias, state_conv,
    state_conv_bias, step_bias, decay_log, skip_gain, mixer_gain, mixer_proj, query_weight, keyval_projection,
    attention_proj, second_gain, gate_up, down_proj, cotangent,
):
    tensor_count = lax.axis_size("tensor")
    tensor_index = lax.axis_index("tensor")
    fsdp_count = lax.axis_size("fsdp")
    own_rows, hidden = layer_input.shape
    unit = state_weight.shape[0]
    seq_count, seq_length = doc_ids.shape
    total = seq_count * seq_length
    heads = step_bias.shape[0]
    width = conv_weight.shape[1]
    wide = -(-width // LANES) * LANES
    query_width = query_weight.shape[1]
    query_wide = -(-query_width // LANES) * LANES
    query_heads = query_width // HEAD_SIZE
    per_group = QUERY_HEADS // KEYVAL_HEADS
    kv_heads = max(1, query_heads // per_group)
    kv_leading = tensor_index * query_heads // per_group
    states2 = state_weight.shape[1]
    ffn = down_proj.shape[0]
    low = lambda v: v.astype(BF)

    own_keyval = lax.dynamic_slice_in_dim(keyval_projection, kv_leading * HEAD_SIZE, kv_heads * HEAD_SIZE, 2)
    own_keyval = own_keyval.reshape(unit, 2, kv_heads, HEAD_SIZE).transpose(0, 2, 1, 3).reshape(unit, 2 * kv_heads * HEAD_SIZE)
    kv_wide = 2 * kv_heads * HEAD_SIZE
    first, rest = pack_weights(
        mixer_weight, state_weight, step_weight.T, query_weight, own_keyval, mixer_proj.T, attention_proj.T, gate_up, down_proj.T
    )
    rest = lax.all_gather(rest, "fsdp", axis=0, tiled=True)
    first, tokens, upstream, normed, first_scale, normed_turned = gather_weights(
        first, layer_input, cotangent, input_gain[None], fsdp_count, tensor_count, 0
    )
    ssm_wide = 2 * wide + states2 + LANES
    cuts = np.cumsum([0, ssm_wide, query_wide + kv_wide, wide + query_wide])
    full_ssm, full_qkv, full_mix = (first[:, cuts[i] : cuts[i + 1]] for i in range(3))
    docs = (doc_ids + jnp.arange(seq_count, dtype=jnp.int32)[:, None] * seq_length).reshape(1, total)
    doc_row = docs.astype(F32)
    feats, cos, sin, taps, state_taps, head_rows = make_tables(
        doc_row, wide, conv_weight, conv_bias, state_conv, state_conv_bias, step_bias, decay_log, skip_gain
    )
    gain_row = pad_to(mixer_gain[None], wide)
    second_row = second_gain[None]

    ssm_in = plain_dot(normed, full_ssm)
    qkv_in = plain_dot(normed, full_qkv)
    scan, gated_low, squares, states = mamba_forward(feats, doc_row, ssm_in, taps, state_taps, head_rows, gain_row, wide, states2)
    mix, log_sums, query_rot, keys, values, squares = attention_forward(
        kv_heads, tensor_count, feats, doc_row, qkv_in, cos, sin, query_wide, gated_low, squares, 2
    )
    branch = tensor_pair(low(right_dot(mix, full_mix)))
    middle, second, second_scale = by_rows(
        second_norm_kernel, "second_norm", CHUNK, total // CHUNK,
        [(tokens, "rows"), (branch[0], "rows"), (branch[1], "rows"), (second_row, "whole")],
        [(total, hidden, F32, "rows"), (total, hidden, BF, "rows"), (total, 1, F32, "rows")],
    )
    active, gu_grad, ffn_out, second_grad = by_rows(
        ffn_kernel, "ffn", min(FFN_ROWS, total), max(total // FFN_ROWS, 1),
        [(second, "rows"), (upstream, "rows"), (rest, "whole")],
        [(total, ffn, BF, "rows"), (total, 2 * ffn, BF, "rows"), (total, hidden, BF, "rows"), (total, hidden, BF, "rows")],
    )
    second_grad, ffn_out = tensor_pair(second_grad), tensor_pair(ffn_out)
    grad_gate_up, grad_down = low(left_dot(second, gu_grad)), low(left_dot(upstream, active))
    core = jnp.full((1,), tensor_index, jnp.int32)
    rows = min(CHUNK, own_rows)
    branch_low, second_gain_part, layer_output = by_rows(
        functools.partial(second_back_kernel, own_rows // rows), "second_back", rows, total // rows,
        [
            (second_grad[0], "rows"), (second_grad[1], "rows"), (middle, "rows"), (second_scale, "rows"), (upstream, "rows"),
            (second_row, "whole"), (ffn_out[0], "own"), (ffn_out[1], "own"),
        ],
        [(total, hidden, BF, "rows"), (8, hidden, F32, "whole"), (own_rows, hidden, BF, "own")], (core,), tensor_count,
    )
    mix_grad = low(plain_dot(branch_low, full_mix))
    grad_mix = low(left_dot(branch_low, mix))
    input_grad, sum_gate_up, sum_down, sum_mix, sum_first, small, shared = backward(
        kv_heads, feats, doc_row, query_rot, keys, values, log_sums, mix_grad, mix, cos, sin, squares, ssm_in, scan, states, taps,
        state_taps, head_rows, gain_row, grad_gate_up, grad_down, grad_mix, normed_turned, first, branch_low, layer_input, first_scale,
        input_gain[None], second_gain_part, wide, states2, fsdp_count, tensor_count, 1,
    )
    shape = lambda *dims: jax.ShapeDtypeStruct(dims, F32)
    parts = (sum_first, sum_mix, shared, small, sum_gate_up, sum_down)
    done = pl.pallas_call(
        functools.partial(finish_kernel, (wide, width, states2, heads, query_width, ffn)),
        grid=(1,),
        in_specs=[spec(v.shape, lambda i: (0,) * 2) for v in parts],
        out_shape=[
            shape(unit, 2, width), shape(unit, states2), shape(unit, heads), shape(4, width), shape(1, width), shape(4, states2),
            shape(1, states2), shape(1, heads), shape(1, heads), shape(1, heads), shape(1, width), shape(unit, width),
            shape(unit, query_width), shape(unit, 2, KEYVAL_HEADS * HEAD_SIZE), shape(unit, query_width), shape(unit, 2, ffn),
            shape(unit, ffn), shape(1, hidden), shape(1, hidden),
        ],
        compiler_params=pltpu.CompilerParams(vmem_limit_bytes=VMEM_WHOLE),
        name="finish",
    )(*parts)
    (
        mixer_sum, state_sum, step_sum, conv_sum, conv_bias_sum, state_conv_sum, state_bias_sum, step_bias_sum, decay_sum, skip_sum,
        mixer_gain_sum, proj_sum, query_sum, keyval_sum, attention_sum, gate_up_sum, down_sum, second_gain_sum, input_gain_sum,
    ) = done
    return (
        layer_output, input_grad, input_gain_sum[0], mixer_sum, state_sum, step_sum, conv_sum, conv_bias_sum[0], state_conv_sum,
        state_bias_sum[0], step_bias_sum[0], decay_sum[0], skip_sum[0], mixer_gain_sum[0], proj_sum.T, query_sum, keyval_sum,
        attention_sum.T, second_gain_sum[0], gate_up_sum, down_sum.T,
    )


def solution(mesh):
    placed = (
        P(("fsdp", "tensor"), None),
        P("fsdp", None),
        P(),
        P("fsdp", None, "tensor"),
        P("fsdp", None),
        P("fsdp", "tensor"),
        P(None, "tensor"),
        P("tensor"),
        P(),
        P(),
        P("tensor"),
        P("tensor"),
        P("tensor"),
        P("tensor"),
        P("tensor", "fsdp"),
        P("fsdp", "tensor"),
        P("fsdp", None, None),
        P("tensor", "fsdp"),
        P(),
        P("fsdp", None, "tensor"),
        P("tensor", "fsdp"),
        P(("fsdp", "tensor"), None),
    )
    return jax.shard_map(
        body,
        mesh=mesh,
        in_specs=placed,
        out_specs=(
            P(("fsdp", "tensor"), None),
            P(("fsdp", "tensor"), None),
            P(),
            P("fsdp", None, "tensor"),
            P("fsdp", None),
            P("fsdp", "tensor"),
            P(None, "tensor"),
            P("tensor"),
            P(),
            P(),
            P("tensor"),
            P("tensor"),
            P("tensor"),
            P("tensor"),
            P("tensor", "fsdp"),
            P("fsdp", "tensor"),
            P("fsdp", None, None),
            P("tensor", "fsdp"),
            P(),
            P("fsdp", None, "tensor"),
            P("tensor", "fsdp"),
        ),
        check_vma=False,
    )
```

```python
import functools
import math
import types

import jax
import jax.numpy as jnp
import ml_dtypes
import numpy as np
from jax import lax
from jax.experimental import pallas as pl
from jax.experimental.pallas import tpu as pltpu
from jax.sharding import PartitionSpec as P

QUERY_HEADS = 8
KEYVAL_HEADS = 2
HEAD_SIZE = 64
DSSM = 1536
EPS = 1e-05
THETA = 100000000000.0

LANES = 128
CHUNK = 128
FFN_ROWS = 512
QBLOCK = 256
VMEM_LIMIT = 32 * 2**20
VMEM_WHOLE = 60 * 2**20
VMEM_ALL = 63 * 2**20
MASKED = -1e30
BF, F32 = jnp.bfloat16, jnp.float32


def left_dot(left_side, right_side):
    return lax.dot_general(left_side, right_side, (((0,), (0,)), ((), ())), preferred_element_type=F32)


def right_dot(left_side, right_side):
    return lax.dot_general(left_side, right_side, (((1,), (1,)), ((), ())), preferred_element_type=F32)


def plain_dot(left_side, right_side):
    return jnp.dot(left_side, right_side, preferred_element_type=F32)


def mm(a, b):
    return jnp.dot(a.astype(BF), b.astype(BF), preferred_element_type=F32)


def mm_nt(a, b):
    return lax.dot_general(a.astype(BF), b.astype(BF), (((1,), (1,)), ((), ())), preferred_element_type=F32)


def mm_tn(a, b):
    return lax.dot_general(a.astype(BF), b.astype(BF), (((0,), (0,)), ((), ())), preferred_element_type=F32)


def exact_mm(a, b):
    return jnp.dot(a, b, precision=lax.Precision.HIGHEST, preferred_element_type=F32)


def sigmoid(v):
    return 1.0 / (1.0 + jnp.exp(-v))


def softplus(v):
    return jnp.maximum(v, 0.0) + jnp.log1p(jnp.exp(-jnp.abs(v)))


def split_lanes(values, axis):
    high = values.astype(BF)
    low = (values - high.astype(F32)).astype(BF)
    return jnp.concatenate([high, low], axis=axis)


def iota2(shape, axis):
    return lax.broadcasted_iota(jnp.int32, shape, axis)


def flipped(index, mask):
    bit = 1
    while bit <= mask:
        if mask & bit:
            index = index + bit * (1 - 2 * ((index // bit) % 2))
        bit *= 2
    return index


def greet(partners):
    barrier = pltpu.get_barrier_semaphore()
    for axis, place in partners:
        pl.semaphore_signal(barrier, inc=1, device_id={axis: place}, device_id_type=pl.DeviceIdType.MESH)
    pl.semaphore_wait(barrier, len(partners))


def remote(source, target, send, recv, axis, place):
    return pltpu.make_async_remote_copy(
        src_ref=source, dst_ref=target, send_sem=send, recv_sem=recv,
        device_id={axis: place}, device_id_type=pl.DeviceIdType.MESH,
    )


class TensorSum:
    def __init__(self, tensors, own, arrived, send, recv):
        self.core = lax.axis_index("tensor")
        self.places = [flipped(self.core, 1 << k) for k in range((tensors - 1).bit_length())]
        self.refs = own, arrived, send, recv

    def copy(self, k):
        own, arrived, send, recv = self.refs
        return remote(own.at[k], arrived.at[k], send.at[k], recv.at[k], "tensor", self.places[k])

    def begin(self, value, met=False):
        if not met:
            greet([("tensor", place) for place in self.places])
        self.refs[0][0] = value
        self.copy(0).start()

    def end(self):
        own, arrived, _, _ = self.refs
        for k in range(len(self.places)):
            copy = self.copy(k)
            if k:
                copy.start()
            copy.wait()
            own[k + 1] = own[k] + arrived[k]
        return own[len(self.places)]


def tensor_sum_scratch(tensors, shape):
    steps = (tensors - 1).bit_length()
    return [
        pltpu.VMEM((steps + 1,) + shape, F32), pltpu.VMEM((steps,) + shape, F32),
        pltpu.SemaphoreType.DMA((steps,)), pltpu.SemaphoreType.DMA((steps,)),
    ]


def conv_taps(buffer, feats, taps, bias, rows):
    total = buffer[8 : 8 + rows, :] * taps[3:4, :] + bias
    for k in range(1, 4):
        total = total + buffer[8 - k : 8 - k + rows, :] * feats[:, k : k + 1] * taps[3 - k : 4 - k, :]
    return total


def step_parts(step_ref, heads_ref, feats, rows):
    raw = step_ref[...] + heads_ref[0:1, :]
    step = softplus(raw)
    lower = (iota2((rows, rows), 0) >= iota2((rows, rows), 1)).astype(F32)
    log_decay = exact_mm(lower, step * heads_ref[1:2, :])
    last = log_decay[rows - 1 : rows, :]
    enter = jnp.exp(log_decay) * feats[:, 4:5]
    leave = jnp.exp(last - log_decay) * feats[:, 5:6]
    return raw, step, log_decay, enter, leave


def gated_scale(squares):
    return lax.rsqrt(squares / DSSM + EPS)


def as_column(row):
    return jnp.broadcast_to(row, (LANES, row.shape[1])).T[:, 0:1]


def mamba_fwd_kernel(
    feats_ref, docs_ref, x_ref, bc_ref, step_ref, z_ref, taps_ref, staps_ref, heads_ref, expand_ref,
    gain_ref, scan_ref, low_ref, square_ref, states_ref, xbuf, bcbuf, memory,
):
    rows, width = x_ref.shape
    states = bc_ref.shape[1] // 2

    @pl.when(pl.program_id(0) == 0)
    def _():
        xbuf[0:8, :] = jnp.zeros((8, width), F32)
        bcbuf[0:8, :] = jnp.zeros((8, 2 * states), F32)
        memory[...] = jnp.zeros_like(memory)

    feats = feats_ref[...]
    xbuf[8 : 8 + rows, :] = x_ref[...]
    bcbuf[8 : 8 + rows, :] = bc_ref[...]
    pre = conv_taps(xbuf, feats, taps_ref, taps_ref[4:5, :], rows)
    values = pre * sigmoid(pre)
    pre_bc = conv_taps(bcbuf, feats, staps_ref, staps_ref[4:5, :], rows)
    both = pre_bc * sigmoid(pre_bc)
    xbuf[0:8, :] = xbuf[rows : rows + 8, :]
    bcbuf[0:8, :] = bcbuf[rows : rows + 8, :]
    key_in = both[:, :states].astype(BF)
    key_out = both[:, states:].astype(BF)
    _, step, log_decay, enter, leave = step_parts(step_ref, heads_ref, feats, rows)
    expanded = jnp.dot(
        split_lanes(jnp.concatenate([step, enter, leave], axis=0), 1), expand_ref[...], preferred_element_type=F32
    )
    step_w, enter_w, leave_w = expanded[:rows], expanded[rows : 2 * rows], expanded[2 * rows :]
    scaled = values * step_w
    gram = mm_nt(key_out, key_in)
    allowed = (feats[:, 0:1] == docs_ref[...]) & (iota2((rows, rows), 0) >= iota2((rows, rows), 1))
    bias = jnp.where(allowed, 0.0, MASKED)
    log_rows = log_decay.T
    front = iota2((rows, LANES), 1) < LANES // 2
    held = memory[...]
    states_ref[0] = held.astype(BF)
    carried = mm(key_out, held) * enter_w
    fresh = mm_tn(key_in, leave_w * scaled)
    memory[...] = held * enter_w[rows - 1 : rows, :] + fresh
    squares = jnp.zeros((rows, 1), F32)
    for pair in range(width // LANES):
        lanes = slice(pair * LANES, (pair + 1) * LANES)
        mixes = []
        for h in (2 * pair, 2 * pair + 1):
            decay = jnp.exp(log_decay[:, h : h + 1] - log_rows[h : h + 1, :] + bias)
            mixes.append((gram * decay).astype(BF))
        part = scaled[:, lanes]
        stacked = jnp.concatenate([jnp.where(front, part, 0.0), jnp.where(front, 0.0, part)], axis=0)
        inside = mm(jnp.concatenate(mixes, axis=1), stacked)
        scan = inside + carried[:, lanes] + values[:, lanes] * taps_ref[5:6, lanes]
        scan_ref[:, lanes] = scan
        z = z_ref[:, lanes]
        gated = scan * (z * sigmoid(z))
        low_ref[:, lanes] = (gated * gain_ref[:, lanes]).astype(BF)
        squares = squares + jnp.sum(gated * gated, axis=1, keepdims=True)
    square_ref[...] = jnp.broadcast_to(squares, (rows, LANES)).T[0:8, :]


def mamba_bwd_block(
    feats_ref, square_ref, inner_sum, block, docs_ref, x_ref, x_before_ref, bc_ref, bc_before_ref, step_ref, z_ref, scan_ref, states_ref, norm_grad_ref,
    taps_ref, staps_ref, heads_ref, expand_ref, reduce_ref, gain_ref,
    grads_ref, sums_ref, ssums_ref, hsums_ref,
    xbuf, bcbuf, dxbuf, dbcbuf, dmemory,
):
    rows, width = x_ref.shape
    states = bc_ref.shape[1] // 2

    feats = feats_ref[...]
    xbuf[0:8, :] = x_before_ref[...]
    bcbuf[0:8, :] = bc_before_ref[...]
    xbuf[8 : 8 + rows, :] = x_ref[...]
    bcbuf[8 : 8 + rows, :] = bc_ref[...]
    pre = conv_taps(xbuf, feats, taps_ref, taps_ref[4:5, :], rows)
    pre_gate = sigmoid(pre)
    values = pre * pre_gate
    pre_bc = conv_taps(bcbuf, feats, staps_ref, staps_ref[4:5, :], rows)
    bc_gate = sigmoid(pre_bc)
    both = pre_bc * bc_gate
    key_in = both[:, :states].astype(BF)
    key_out = both[:, states:].astype(BF)
    raw, step, log_decay, enter, leave = step_parts(step_ref, heads_ref, feats, rows)
    expanded = jnp.dot(
        split_lanes(jnp.concatenate([step, enter, leave], axis=0), 1), expand_ref[...], preferred_element_type=F32
    )
    step_w, enter_w, leave_w = expanded[:rows], expanded[rows : 2 * rows], expanded[2 * rows :]
    scaled = values * step_w
    z = z_ref[...]
    z_gate = sigmoid(z)
    z_silu = z * z_gate
    scan = scan_ref[...]
    gated = scan * z_silu
    norm_grad = norm_grad_ref[...].astype(F32)
    row_scale = gated_scale(square_ref[0:1, :])
    row_inner = inner_sum[pl.ds(pl.multiple_of(block * 8, 8), 8), :][0:1, :] * row_scale * row_scale / DSSM
    scale, coefficient = as_column(row_scale), as_column(row_inner)
    weighted = norm_grad * scale
    gated_grad = weighted * gain_ref[...] - gated * coefficient
    dscan = gated_grad * z_silu
    grads_ref[:, 0:width] = (gated_grad * scan * (z_gate * (1.0 + z * (1.0 - z_gate)))).astype(BF)
    sums_ref[6:7, :] += jnp.sum(weighted * gated, axis=0, keepdims=True)
    sums_ref[5:6, :] += jnp.sum(dscan * values, axis=0, keepdims=True)
    held = states_ref[0]
    dheld = dmemory[...]
    dheld_low = dheld.astype(BF)
    enter_grad = (dscan * enter_w).astype(BF)
    left = leave_w * scaled
    passed = mm(key_in, dheld_low)
    arrived = mm(key_out, held)
    dkey_out = mm_nt(enter_grad, held)
    dkey_in = mm_nt(left, dheld_low)
    carry = enter_w[rows - 1 : rows, :]
    dmemory[...] = dheld * carry + mm_tn(key_out, enter_grad)
    enter_terms = dscan * enter_w * arrived
    leave_terms = left * passed
    carry_terms = jnp.sum(dheld * held.astype(F32), axis=0, keepdims=True) * carry
    gram = mm_nt(key_in, key_out)
    allowed = (feats[:, 0:1] == docs_ref[...]) & (iota2((rows, rows), 0) <= iota2((rows, rows), 1))
    bias = jnp.where(allowed, 0.0, MASKED)
    log_rows = log_decay.T
    front = iota2((rows, LANES), 1) < LANES // 2
    gram_grad = jnp.zeros((rows, rows), F32)
    lane_of = iota2((rows, LANES), 1)
    row_of = iota2((LANES, rows), 0)
    sent = jnp.zeros((rows, LANES), F32)
    received = jnp.zeros((LANES, rows), F32)
    inside_grads = []
    for pair in range(width // LANES):
        lanes = slice(pair * LANES, (pair + 1) * LANES)
        dy = dscan[:, lanes].astype(BF)
        part = scaled[:, lanes]
        stacked = jnp.concatenate([jnp.where(front, part, 0.0), jnp.where(front, 0.0, part)], axis=0)
        cross = mm_nt(stacked, dy)
        mixes = []
        for j, h in enumerate((2 * pair, 2 * pair + 1)):
            decay = jnp.exp(log_rows[h : h + 1, :] - log_decay[:, h : h + 1] + bias)
            mix = gram * decay
            mixes.append(mix.astype(BF))
            dmix = cross[j * rows : (j + 1) * rows, :]
            gram_grad = gram_grad + dmix * decay
            flow = dmix * mix
            sent = jnp.where(lane_of == h, jnp.sum(flow, axis=1, keepdims=True), sent)
            received = jnp.where(row_of == h, jnp.sum(flow, axis=0, keepdims=True), received)
        grads = mm(jnp.concatenate(mixes, axis=0), dy)
        inside_grads.append(jnp.where(front, grads[:rows], grads[rows:]))
    dscaled = jnp.concatenate(inside_grads, axis=1) + leave_w * passed
    dkey_in = dkey_in + mm(gram_grad, key_out)
    dkey_out = dkey_out + mm_tn(gram_grad, key_in)
    reduced = jnp.dot(
        split_lanes(
            jnp.concatenate([enter_terms, leave_terms, dscaled * values, jnp.broadcast_to(carry_terms, (8, width))], axis=0), 1
        ),
        reduce_ref[...],
        preferred_element_type=F32,
    )
    after = reduced[:rows] + received.T - sent
    upper = (iota2((rows, rows), 0) <= iota2((rows, rows), 1)).astype(F32)
    strict = (iota2((rows, rows), 0) > iota2((rows, rows), 1)).astype(F32)
    decay_grad = exact_mm(upper, after) + exact_mm(strict, reduced[rows : 2 * rows]) + reduced[3 * rows : 3 * rows + 1]
    dstep = decay_grad * heads_ref[1:2, :] + reduced[2 * rows : 3 * rows]
    draw = dstep * sigmoid(raw)
    grads_ref[:, 2 * width + 2 * states :] = draw.astype(BF)
    hsums_ref[0:1, :] += jnp.sum(draw, axis=0, keepdims=True)
    hsums_ref[1:2, :] += jnp.sum(decay_grad * step, axis=0, keepdims=True) * heads_ref[1:2, :]
    dvalues = dscaled * step_w + dscan * taps_ref[5:6, :]
    dpre = dvalues * (pre_gate * (1.0 + pre * (1.0 - pre_gate)))
    dboth = jnp.concatenate([dkey_in, dkey_out], axis=1)
    dpre_bc = dboth * (bc_gate * (1.0 + pre_bc * (1.0 - bc_gate)))
    for dpre_now, buffer, dbuffer, taps, totals, lanes in (
        (dpre, xbuf, dxbuf, taps_ref, sums_ref, slice(width, 2 * width)),
        (dpre_bc, bcbuf, dbcbuf, staps_ref, ssums_ref, slice(2 * width, 2 * width + 2 * states)),
    ):
        dbuffer[0:rows, :] = dpre_now
        grad = dpre_now * taps[3:4, :]
        totals[3:4, :] += jnp.sum(dpre_now * buffer[8 : 8 + rows, :], axis=0, keepdims=True)
        totals[4:5, :] += jnp.sum(dpre_now, axis=0, keepdims=True)
        for k in range(1, 4):
            grad = grad + dbuffer[k : k + rows, :] * feats[:, 5 + k : 6 + k] * taps[3 - k : 4 - k, :]
            totals[3 - k : 4 - k, :] += jnp.sum(
                dpre_now * buffer[8 - k : 8 - k + rows, :] * feats[:, k : k + 1], axis=0, keepdims=True
            )
        grads_ref[:, lanes] = grad.astype(BF)
        dbuffer[rows : rows + 8, :] = dbuffer[0:8, :]


def expand_matrix(width):
    one = np.arange(LANES)[:, None] == np.arange(width)[None, :] // (LANES // 2)
    return np.concatenate([one, one], axis=0).astype(ml_dtypes.bfloat16)


def spec(block, index):
    return pl.BlockSpec(block, index)


def mamba_forward(feats, doc_row, ssm_in, taps, staps, heads, gain, width, states2):
    total = ssm_in.shape[0]
    rows = CHUNK
    count = total // rows
    block = lambda w, place=0: spec((rows, w), lambda i: (i, place))
    whole = lambda a: spec(a.shape, lambda i: (0,) * a.ndim)
    expand = expand_matrix(width)
    return pl.pallas_call(
        mamba_fwd_kernel,
        grid=(count,),
        in_specs=[
            block(LANES), spec((1, rows), lambda i: (0, i)), block(width, 1), block(states2, 2 * width // states2),
            block(LANES, (2 * width + states2) // LANES), block(width), whole(taps), whole(staps), whole(heads), whole(expand), whole(gain),
        ],
        out_specs=[block(width), block(width), spec((8, LANES), lambda i: (i, 0)), spec((1, states2 // 2, width), lambda i: (i, 0, 0))],
        out_shape=[
            jax.ShapeDtypeStruct((total, width), F32),
            jax.ShapeDtypeStruct((total, width), BF),
            jax.ShapeDtypeStruct((8 * count, LANES), F32),
            jax.ShapeDtypeStruct((count, states2 // 2, width), BF),
        ],
        scratch_shapes=[
            pltpu.VMEM((rows + 8, width), F32), pltpu.VMEM((rows + 8, states2), F32), pltpu.VMEM((states2 // 2, width), F32),
        ],
        compiler_params=pltpu.CompilerParams(vmem_limit_bytes=VMEM_LIMIT),
        cost_estimate=pl.CostEstimate(flops=20 * 10**9, bytes_accessed=total * width * 20, transcendentals=total * width * 4),
        name="mamba_fwd",
    )(feats, doc_row, ssm_in, ssm_in, ssm_in, ssm_in, taps, staps, heads, expand, gain)


def swap_halves(values):
    lane = iota2(values.shape, 1) % (LANES // 2)
    return jnp.where(lane < LANES // 4, pltpu.roll(values, LANES - LANES // 4, 1), pltpu.roll(values, LANES // 4, 1))


def stack_heads(part):
    front = iota2(part.shape, 1) < LANES // 2
    zero = jnp.zeros_like(part)
    return jnp.concatenate([jnp.where(front, part, zero), jnp.where(front, zero, part)], axis=0)


def attention_fwd_kernel(
    groups, tensors, docs_col_ref, docs_ref, q_ref, kv_ref, cos_ref, sin_ref, low_ref, square_ref, out_ref, lse_ref, qrot_ref, keys_ref, values_ref, square_out_ref, *scratch,
):
    total = q_ref.shape[0]
    wide = low_ref.shape[1]
    exchange = TensorSum(tensors, *scratch)
    exchange.begin(square_ref[...])
    pairs = q_ref.shape[1] // LANES
    block = min(QBLOCK, total)
    cos, sin = cos_ref[...], sin_ref[...]
    front = iota2((total, LANES), 1) < LANES // 2
    for g in range(groups):
        lanes = slice(g * LANES, (g + 1) * LANES)
        raw = kv_ref[:, lanes]
        turned = raw * cos + swap_halves(raw) * sin
        keys_ref[:, lanes] = jnp.where(front, turned, pltpu.roll(turned, LANES // 2, 1)).astype(BF)
        values_ref[:, lanes] = jnp.where(front, pltpu.roll(raw, LANES // 2, 1), raw).astype(BF)
    for p in range(pairs):
        lanes = slice(p * LANES, (p + 1) * LANES)
        raw = q_ref[:, lanes]
        qrot_ref[:, lanes] = ((raw * cos + swap_halves(raw) * sin).astype(BF).astype(F32) * (LANES // 2) ** -0.5).astype(BF)
    front = iota2((block, LANES), 1) < LANES // 2
    lane_of = iota2((block, LANES), 1)
    for start in range(0, total, block):
        rows, end = slice(start, start + block), start + block
        allowed = (docs_col_ref[rows, 0:1] == docs_ref[:, :end]) & (
            iota2((block, end), 0) + start >= iota2((block, end), 1)
        )
        bias = jnp.where(allowed, 0.0, MASKED)
        bias = jnp.concatenate([bias, bias], axis=0)
        sums = jnp.zeros((block, LANES), F32)
        for p in range(pairs):
            lanes = slice(p * LANES, (p + 1) * LANES)
            g = p * groups // pairs
            kv = slice(g * LANES, (g + 1) * LANES)
            scores = mm_nt(stack_heads(qrot_ref[rows, lanes]), keys_ref[:end, kv]) + bias
            top = jnp.max(scores, axis=1, keepdims=True)
            raised = jnp.exp(scores - top)
            whole = jnp.sum(raised, axis=1, keepdims=True)
            mixed = mm(raised, values_ref[:end, kv]) / whole
            out_ref[rows, wide + p * LANES : wide + (p + 1) * LANES] = jnp.where(front, mixed[:block], mixed[block:]).astype(BF)
            logs = top + jnp.log(whole)
            sums = jnp.where(lane_of == 2 * p, logs[:block], sums)
            sums = jnp.where(lane_of == 2 * p + 1, logs[block:], sums)
        lse_ref[rows, :] = sums
    square_out_ref[...] = exchange.end()
    for i in range(total // LANES):
        piece = slice(i * LANES, (i + 1) * LANES)
        scale = as_column(gated_scale(square_out_ref[8 * i : 8 * i + 1, :]))
        out_ref[piece, :wide] = (low_ref[piece, :].astype(F32) * scale).astype(BF)


def attention_bwd_block(
    start, groups, docs_col_ref, docs_ref, qrot_ref, keys_ref, values_ref, lse_ref, up_ref, cos_ref, sin_ref, grads_ref, dk_acc, dv_acc,
):
    pairs = qrot_ref.shape[1] // LANES
    block = up_ref.shape[0]
    front = iota2((block, LANES), 1) < LANES // 2
    rows, end = slice(start, start + block), start + block
    allowed = (docs_col_ref[:end, 0:1] == docs_ref[:, rows]) & (
        iota2((end, block), 0) <= iota2((end, block), 1) + start
    )
    bias = jnp.where(allowed, 0.0, MASKED)
    logs = lse_ref[...].T
    cos, sin = cos_ref[rows, :], sin_ref[rows, :]
    for p in range(pairs):
        lanes = slice(p * LANES, (p + 1) * LANES)
        g = p * groups // pairs
        kv = slice(g * LANES, (g + 1) * LANES)
        keys, values = keys_ref[:end, kv], values_ref[:end, kv]
        queries = stack_heads(qrot_ref[rows, lanes])
        ups = stack_heads(up_ref[:, lanes])
        shift = jnp.concatenate([bias - logs[2 * p : 2 * p + 1], bias - logs[2 * p + 1 : 2 * p + 2]], axis=1)
        probs = jnp.exp(mm_nt(keys, queries) + shift)
        grads = mm_nt(values, ups)
        centre = jnp.sum(probs * grads, axis=0, keepdims=True)
        score_grads = (probs * (grads - centre)).astype(BF)
        dk_acc[:end, kv] += mm(score_grads, queries)
        dv_acc[:end, kv] += mm(probs, ups)
        dq = mm_tn(score_grads, keys)
        dq = jnp.where(front, dq[:block], dq[block:]) * (LANES // 2) ** -0.5
        grads_ref[rows, lanes] = (dq * cos - swap_halves(dq) * sin).astype(BF)


def attention_bwd_end(groups, pairs, cos_ref, sin_ref, grads_ref, dk_acc, dv_acc):
    total = dk_acc.shape[0]
    front = iota2((total, LANES), 1) < LANES // 2
    for g in range(groups):
        kv = slice(g * LANES, (g + 1) * LANES)
        dk, dv = dk_acc[:, kv], dv_acc[:, kv]
        dk = dk + pltpu.roll(dk, LANES // 2, 1)
        dk = dk * cos_ref[...] - swap_halves(dk) * sin_ref[...]
        dv = dv + pltpu.roll(dv, LANES // 2, 1)
        out = slice((pairs + g) * LANES, (pairs + g + 1) * LANES)
        grads_ref[:, out] = jnp.where(front, dk, dv).astype(BF)


def attention_forward(groups, tensors, doc_col, doc_row, qkv, cos, sin, query_width, low, squares, collective_id):
    total = qkv.shape[0]
    kv_width = qkv.shape[1] - query_width
    whole = lambda a: spec(a.shape, lambda i: (0,) * a.ndim)
    columns = lambda w, place=0: spec((total, w), lambda i: (0, place))
    return pl.pallas_call(
        functools.partial(attention_fwd_kernel, groups, tensors),
        grid=(1,),
        in_specs=[whole(doc_col), whole(doc_row), columns(query_width), columns(kv_width, query_width // kv_width), whole(cos), whole(sin), whole(low), whole(squares)],
        out_specs=[columns(low.shape[1] + query_width), columns(LANES), columns(query_width), columns(kv_width), columns(kv_width), whole(squares)],
        out_shape=[
            jax.ShapeDtypeStruct((total, low.shape[1] + query_width), BF), jax.ShapeDtypeStruct((total, LANES), F32),
            jax.ShapeDtypeStruct((total, query_width), BF), jax.ShapeDtypeStruct((total, kv_width), BF),
            jax.ShapeDtypeStruct((total, kv_width), BF), jax.ShapeDtypeStruct(squares.shape, F32),
        ],
        scratch_shapes=tensor_sum_scratch(tensors, squares.shape),
        compiler_params=pltpu.CompilerParams(vmem_limit_bytes=VMEM_LIMIT, collective_id=collective_id, has_side_effects=True),
        cost_estimate=pl.CostEstimate(flops=12 * 10**9, bytes_accessed=total * query_width * 10, transcendentals=total * total * 2),
        name="attention_fwd",
    )(doc_col, doc_row, qkv, qkv, cos, sin, low, squares)


def gather_kernel(
    count, tensors, shard_ref, tokens_ref, cotangent_ref, gain_ref, *refs,
):
    tables, (full_ref, all_tokens_ref, all_cotangent_ref, normed_ref, scale_ref, turned_ref) = refs[:8], refs[8:14]
    table_outs, (own_sem, send_sems, recv_sems, core_send, core_recv) = refs[14:20], refs[20:]
    unit, columns = shard_ref.shape
    levels = count // 4
    me = lax.axis_index("fsdp")
    half = columns // 2 // LANES * LANES
    parts = (slice(0, half), slice(half, columns))
    neighbours = (flipped(me, 1), flipped(me, 2))
    far = [flipped(me, 4 * d) for d in range(1, levels)]
    core = lax.axis_index("tensor")
    cores = [flipped(core, k) for k in range(1, tensors)]
    greet([("fsdp", p) for p in neighbours] + [("fsdp", p) for p in far] + [("tensor", p) for p in cores])

    def rows(owner):
        return pl.ds(pl.multiple_of(owner * unit, unit), unit)

    started = []

    def send(source, owner, lanes, slot, place):
        copy = remote(source, full_ref.at[rows(owner), lanes], send_sems.at[slot], recv_sems.at[slot], "fsdp", place)
        copy.start()
        started.append(copy)
        return copy

    def arrival(owner, lanes, slot):
        piece = full_ref.at[rows(owner), lanes]
        return remote(piece, piece, send_sems.at[slot], recv_sems.at[slot], "fsdp", neighbours[0])

    everything = slice(0, columns)
    own = pltpu.make_async_copy(shard_ref, full_ref.at[rows(me), :], own_sem)
    own.start()
    for d in range(1, levels):
        send(shard_ref, me, everything, d, far[d - 1])
    base = levels
    for axis in range(2):
        send(shard_ref, me, everything, base + axis * levels, neighbours[axis])
    cross = base + 2 * levels
    own_rows = tokens_ref.shape[0]
    share = lambda owner: pl.ds(pl.multiple_of(owner * own_rows, own_rows), own_rows)
    exchanges = []
    for k, place in enumerate(cores):
        for j, (source, target) in enumerate(((tokens_ref, all_tokens_ref), (cotangent_ref, all_cotangent_ref))):
            copy = remote(
                source, target.at[share(core), :], core_send.at[2 * k + j], core_recv.at[2 * k + j], "tensor", place
            )
            copy.start()
            exchanges.append(copy)
    all_tokens_ref[share(core), :] = tokens_ref[...]
    all_cotangent_ref[share(core), :] = cotangent_ref[...]
    for copy in exchanges:
        copy.wait()

    def norm(i, carry):
        piece = pl.ds(pl.multiple_of(i * LANES, LANES), LANES)
        values = all_tokens_ref[piece, :].astype(F32)
        scale = lax.rsqrt(jnp.mean(values * values, axis=1, keepdims=True) + EPS)
        scale_ref[piece, :] = scale
        normed = values * scale * gain_ref[...]
        normed_ref[piece, :] = normed.astype(BF)
        turned_ref[:, piece] = normed.T.astype(BF)
        return carry

    lax.fori_loop(0, normed_ref.shape[0] // LANES, norm, 0)
    table_kernel(*tables, *table_outs)

    def pass_on(d):
        for axis in range(2):
            owner = flipped(neighbours[axis], 4 * d)
            arrival(owner, everything, base + axis * levels + d).wait_recv()
            piece = full_ref.at[rows(owner), parts[axis]]
            send(piece, owner, parts[axis], cross + axis * levels + d, neighbours[1 - axis])

    for d in range(1, levels):
        arrival(far[d - 1], everything, d).wait_recv()
        for axis in range(2):
            send(full_ref.at[rows(far[d - 1]), :], far[d - 1], everything, base + axis * levels + d, neighbours[axis])
        pass_on(d - 1)
    pass_on(levels - 1)
    for d in range(levels):
        for axis in range(2):
            owner = flipped(me, 4 * d + 3)
            arrival(owner, parts[axis], cross + axis * levels + d).wait_recv()
    for copy in started:
        copy.wait_send()
    own.wait()


def gather_weights(shard, tokens, cotangent, gain, tables, wide, count, tensors, collective_id):
    unit, columns = shard.shape
    own_rows, hidden = tokens.shape
    total = own_rows * tensors
    slots = 5 * (count // 4)
    vmem, anywhere = pl.BlockSpec(memory_space=pltpu.VMEM), pl.BlockSpec(memory_space=pl.ANY)
    low = jax.ShapeDtypeStruct((total, hidden), BF)
    shape = lambda r, c: jax.ShapeDtypeStruct((r, c), F32)
    return pl.pallas_call(
        functools.partial(gather_kernel, count, tensors),
        in_specs=[anywhere, vmem, vmem, vmem] + [vmem] * len(tables),
        out_specs=[anywhere] + [vmem] * 11,
        out_shape=[jax.ShapeDtypeStruct((count * unit, columns), shard.dtype), low, low, low, jax.ShapeDtypeStruct((total, 1), F32),
            jax.ShapeDtypeStruct((hidden, total), BF), shape(total, LANES), shape(total, LANES), shape(total, LANES), shape(8, wide),
            shape(8, tables[3].shape[1]), shape(8, LANES),
        ],
        scratch_shapes=[
            pltpu.SemaphoreType.DMA, pltpu.SemaphoreType.DMA((slots,)), pltpu.SemaphoreType.DMA((slots,)),
            pltpu.SemaphoreType.DMA((2 * (tensors - 1),)), pltpu.SemaphoreType.DMA((2 * (tensors - 1),)),
        ],
        compiler_params=pltpu.CompilerParams(collective_id=collective_id, has_side_effects=True, vmem_limit_bytes=VMEM_LIMIT),
        cost_estimate=pl.CostEstimate(flops=0, bytes_accessed=2 * count * unit * columns * 2, transcendentals=0),
        name="gather_weights",
    )(shard, tokens, cotangent, gain, *tables)


def backward_kernel(c, *refs):
    r = types.SimpleNamespace(**dict(zip(c.names, refs)))
    now = pl.program_id(0)
    me, core = lax.axis_index("fsdp"), lax.axis_index("tensor")
    levels, unit, blocks, chunks, tiles = c.count // 4, c.unit, c.blocks, c.chunks, c.tiles
    near = (flipped(me, 1), flipped(me, 2))
    far = [None] + [flipped(me, 4 * d) for d in range(1, levels)]
    bits = [1 << k for k in range((c.count - 1).bit_length())]
    cores = [flipped(core, k) for k in range(1, c.tensors)]
    halves = [("tensor", flipped(core, 1 << k)) for k in range((c.tensors - 1).bit_length())]
    stages = [("fsdp", flipped(me, bit)) for bit in bits] + halves
    order = sorted(range(levels), key=lambda d: (d & -d if d else levels, -d))
    pieces = []
    for i, (name, lanes, path, out, out_lanes) in enumerate(c.pieces):
        pieces.append((i, getattr(r, name), lanes, path, getattr(r, out), out_lanes))
    early, late = pieces[: c.early], pieces[c.early :]

    def own_copies():
        copies = []
        for i, grad, lanes, path, _, _ in early:
            parts = getattr(r, "own%d" % i)
            for d in order:
                for k, owner in ((d, flipped(near[path], 4 * d)), (levels + d, flipped(me, 4 * d))):
                    copies.append(pltpu.make_async_copy(grad.at[rows(owner), lanes], parts.at[k], r.own_sems.at[i, k]))
        return copies

    def own_part(i, grad, lanes, owner, k):
        if i < c.early:
            return getattr(r, "own%d" % i)[k].astype(F32)
        return grad[rows(owner), lanes].astype(F32)

    cross, along, inbound = [], [], []
    for i in range(len(pieces)):
        cross.append(getattr(r, "cross%d" % i))
        along.append((getattr(r, "along_x%d" % i), getattr(r, "along_y%d" % i)))
        inbound.append(getattr(r, "inbound%d" % i))

    def rows(owner):
        return pl.ds(pl.multiple_of(owner * unit, unit), unit)

    def link(source, target, i, kind, d, place):
        slot = (i * 4 + kind) * levels + d
        return remote(source, target, r.send_sems.at[slot], r.recv_sems.at[slot], "fsdp", place)

    def begin(group, d):
        for i, grad, lanes, path, _, _ in group:
            link(grad.at[rows(flipped(me, 4 * d + 3)), lanes], cross[i].at[d], i, 0, d, near[1 - path]).start()

    def raw(group, d):
        for i, grad, lanes, path, _, _ in group:
            other = 1 - path
            link(grad.at[rows(flipped(near[other], 4 * d)), lanes], along[i][other].at[d], i, 1 + other, d, near[other]).start()

    def middle(group, d):
        for i, grad, lanes, path, _, _ in group:
            link(cross[i].at[d], cross[i].at[d], i, 0, d, near[0]).wait_recv()
            own = own_part(i, grad, lanes, flipped(near[path], 4 * d), d)
            cross[i][d] = (own + cross[i][d].astype(F32)).astype(BF)
            link(cross[i].at[d], along[i][path].at[d], i, 1 + path, d, near[path]).start()

    def finish(group, d):
        lowest = d & -d if d else levels
        for i, grad, lanes, path, out, out_lanes in group:
            for axis in range(2):
                link(along[i][axis].at[d], along[i][axis].at[d], i, 1 + axis, d, near[0]).wait_recv()
            own = own_part(i, grad, lanes, flipped(me, 4 * d), levels + d)
            total = own + along[i][0][d].astype(F32) + along[i][1][d].astype(F32)
            bit = 1
            while bit < lowest:
                slot = d + bit - 1
                link(inbound[i].at[slot], inbound[i].at[slot], i, 3, d + bit, near[0]).wait_recv()
                total = total + inbound[i][slot].astype(F32)
                bit *= 2
            if d:
                along[i][0][d] = total.astype(BF)
                link(along[i][0].at[d], inbound[i].at[d - 1], i, 3, d, far[lowest]).start()
            else:
                out[:, out_lanes] = total

    weights_copy = pltpu.make_async_copy(r.weights.at[:, 0 : r.held.shape[1]], r.held, r.local_sems.at[0])
    own_rows = r.tokens.shape[0]
    share = lambda owner: pl.ds(pl.multiple_of(owner * own_rows, own_rows), own_rows)
    turned_copy = pltpu.make_async_copy(r.normed_turned, r.turned, r.local_sems.at[2])
    branch_copy = pltpu.make_async_copy(r.branch_low.at[share(core), :], r.branch_own, r.local_sems.at[1])
    inners = TensorSum(c.tensors, r.inner_own, r.inner_in, r.inner_send, r.inner_recv)

    @pl.when(now == 0)
    def _():
        greet([("fsdp", p) for p in near] + [("fsdp", flipped(me, bit)) for bit in bits[2:]] + [("tensor", p) for p in cores])
        for d in order:
            begin(early, d)
        for copy in own_copies():
            copy.start()
        turned_copy.start()
        weights_copy.start()
        branch_copy.start()
        r.dk_acc[...] = jnp.zeros_like(r.dk_acc)
        r.dv_acc[...] = jnp.zeros_like(r.dv_acc)

    block = r.mix_up.shape[0]
    for j in range(blocks):

        @pl.when(now == j)
        def _(j=j):
            for i in range(block // LANES):
                part = slice(i * LANES, (i + 1) * LANES)
                inner = jnp.sum(r.mix_norm[part, :].astype(F32) * r.mix_low[part, :].astype(F32), axis=1, keepdims=True)
                at = 8 * (j * (block // LANES) + i)
                r.inner_rows[at : at + 8, :] = jnp.broadcast_to(inner, (LANES, LANES)).T[0:8, :]
            attention_bwd_block(
                j * block, c.groups, r.feats_all, r.doc_row, r.qrot, r.keys, r.values, r.lse, r.mix_up, r.cos, r.sin, r.qkv_grad,
                r.dk_acc, r.dv_acc,
            )
            if j == blocks - 1:
                inners.begin(r.inner_rows[...], met=True)
                attention_bwd_end(c.groups, r.qrot.shape[1] // LANES, r.cos, r.sin, r.qkv_grad, r.dk_acc, r.dv_acc)

    @pl.when(now == blocks)
    def _():
        r.dxbuf[CHUNK : CHUNK + 8, :] = jnp.zeros((8, r.dxbuf.shape[1]), F32)
        r.dbcbuf[CHUNK : CHUNK + 8, :] = jnp.zeros((8, r.dbcbuf.shape[1]), F32)
        r.dmemory[...] = jnp.zeros_like(r.dmemory)
        r.x_sums[...] = jnp.zeros_like(r.x_sums)
        r.state_sums[...] = jnp.zeros_like(r.state_sums)
        r.head_sums[...] = jnp.zeros_like(r.head_sums)
        r.inner_sum[...] = inners.end()

    @pl.when((now >= blocks) & (now < blocks + chunks))
    def _():
        chunk = chunks - 1 - (now - blocks)
        mamba_bwd_block(
            r.feats, r.square, r.inner_sum, chunk, r.docs, r.x, r.x_before, r.bc, r.bc_before, r.step, r.z, r.scan, r.states,
            r.norm_grad, r.taps, r.staps, r.heads, r.expand, r.reduce, r.gain,
            r.ssm_grad.at[pl.ds(pl.multiple_of(chunk * CHUNK, CHUNK), CHUNK), :], r.x_sums, r.state_sums, r.head_sums,
            r.xbuf, r.bcbuf, r.dxbuf, r.dbcbuf, r.dmemory,
        )

    for k, d in enumerate(order):

        @pl.when(now == blocks + 1 + k)
        def _(d=d):
            if d == order[0]:
                for copy in own_copies():
                    copy.wait()
            middle(early, d)
            raw(early, d)

    base = blocks + chunks
    ssm_wide = r.ssm_grad.shape[1]
    for k, d in enumerate(order):

        @pl.when(now == base + k)
        def _(d=d):
            quad = pl.ds(pl.multiple_of(flipped(me, 4 * d) // 4 * (4 * unit), 4 * unit), 4 * unit)
            if d == order[0]:
                turned_copy.wait()
            turned = r.turned[quad, :]
            r.grad_first[quad, :ssm_wide] = jnp.dot(turned, r.ssm_grad[...], preferred_element_type=F32).astype(BF)
            r.grad_first[quad, ssm_wide:] = jnp.dot(turned, r.qkv_grad[...], preferred_element_type=F32).astype(BF)
            begin(late, d)
            raw(late, d)

    base = base + levels

    @pl.when(now == base)
    def _():
        weights_copy.wait()

    @pl.when((now >= base) & (now < base + tiles))
    def _():
        part = pl.ds(pl.multiple_of((now - base) * c.tile, c.tile), c.tile)
        r.normed_part[part, :] = (
            mm_nt(r.ssm_grad[part, :], r.held[:, :ssm_wide]) + mm_nt(r.qkv_grad[part, :], r.held[:, ssm_wide:])
        ).astype(BF)

    def normed_copies():
        return [
            remote(r.normed_part.at[share(place), :], r.normed_in.at[k], r.core_send.at[k], r.core_recv.at[k], "tensor", place)
            for k, place in enumerate(cores)
        ]

    for k, step in enumerate((base - levels + 1, base + 1)):

        @pl.when(now == step)
        def _(d=order[k]):
            finish(early, d)

    settled = []

    def stage_copy(k):
        axis, place = stages[k]
        return remote(r.sums.at[k], r.sums_in.at[k], r.sum_send.at[k], r.sum_recv.at[k], axis, place)

    def next_stage():
        k = len(settled)
        if k < len(stages):
            stage_copy(k).wait()
            r.sums[k + 1] = r.sums[k] + r.sums_in[k]
            settled.append(k)
            if k + 1 < len(stages):
                stage_copy(k + 1).start()

    @pl.when(now == base + tiles)
    def _():
        for copy in normed_copies():
            copy.start()
        for copy in normed_copies():
            copy.wait()
        branch_copy.wait()
        r.gain_sum[...] = jnp.zeros_like(r.gain_sum)
        size = min(CHUNK, own_rows)

        def first_norm_back(i, carry):
            part = pl.ds(pl.multiple_of(i * size, size), size)
            whole = pl.ds(pl.multiple_of(core * own_rows + i * size, size), size)
            grad = r.normed_part[whole, :].astype(F32)
            for k in range(len(cores)):
                grad = grad + r.normed_in[k, part, :].astype(F32)
            scale = r.scale[whole, :]
            shape = r.tokens[part, :].astype(F32) * scale
            weighted = grad * r.input_gain[...]
            inner = jnp.mean(weighted * shape, axis=1, keepdims=True)
            r.input_grad[part, :] = r.branch_own[part, :].astype(F32) + scale * (weighted - shape * inner)
            r.gain_sum[0:1, :] += jnp.sum(grad * shape, axis=0, keepdims=True)
            return carry

        lax.fori_loop(0, own_rows // size, first_norm_back, 0)
        at = 0
        for ref in (r.x_sums, r.head_sums, r.state_sums):
            r.sums[0, :, at : at + ref.shape[1]] = ref[...]
            at += ref.shape[1]
        eighth = r.gain_sum.shape[1] // 8
        for ref, factor in ((r.second_part, 1.0 / c.tensors), (r.gain_sum, 1.0)):
            for k in range(8):
                r.sums[0, k : k + 1, at : at + eighth] = ref[0:1, k * eighth : (k + 1) * eighth] * factor
            at += eighth
        stage_copy(0).start()
        for d in order[2:]:
            finish(early, d)
            next_stage()
        for d in order:
            middle(late, d)
        for d in order:
            finish(late, d)
            next_stage()
        while len(settled) < len(stages):
            next_stage()
        r.small_out[:, : c.split] = r.sums[len(bits), :, : c.split]
        r.small_out[:, c.split :] = r.sums[len(stages), :, c.split :]
        states2 = c.state_at[1] - c.state_at[0]
        wide_shared = r.shared.shape[2]
        leading = core * (wide_shared - states2) // (c.tensors * LANES)
        r.shared[0, :, :states2] = r.out_first[:, c.state_at[0] : c.state_at[1]]
        for g in range((wide_shared - states2) // LANES):
            value = jnp.zeros((unit, LANES), F32)
            for j in range(c.groups):
                value = jnp.where(leading + j == g, r.out_first[:, c.kv_at + j * LANES : c.kv_at + (j + 1) * LANES], value)
            r.shared[0, :, states2 + g * LANES : states2 + (g + 1) * LANES] = value
        for k, (axis, place) in enumerate(halves):
            copy = remote(r.shared.at[k], r.shared_in.at[k], r.half_send.at[k], r.half_recv.at[k], axis, place)
            copy.start()
            copy.wait()
            r.shared[k + 1] = r.shared[k] + r.shared_in[k]
        r.shared_out[...] = r.shared[len(halves)]
        for i in range(len(pieces)):
            for d in range(levels):
                for kind in range(4):
                    if kind < 3 or d:
                        link(cross[i].at[d], cross[i].at[d], i, kind, d, near[0]).wait_send()


def backward(
    groups, feats, doc_row, qrot, keys, values, lse, mix_grad, mix, cos, sin, squares, ssm_in, scan, states, taps, staps, heads, gain,
    grad_gate_up, grad_down, grad_mix, normed_turned, first, branch_low, tokens, scale, input_gain, second_part, width, states2,
    count, tensors, collective_id,
):
    total, hidden = branch_low.shape
    own_rows = tokens.shape[0]
    unit = hidden // count
    levels = count // 4
    query_wide, kv_wide = qrot.shape[1], keys.shape[1]
    block, tile = min(QBLOCK, total), min(QBLOCK, total)
    blocks, chunks, tiles = total // block, total // CHUNK, total // tile
    ssm_wide, qkv_wide = 2 * width + states2 + LANES, query_wide + kv_wide
    chunk = lambda s: jnp.clip(chunks - 1 - (s - blocks), 0, chunks - 1)
    query = lambda s: jnp.minimum(s, blocks - 1)
    by_chunk = lambda w, place=0: spec((CHUNK, w), lambda s: (chunk(s), place))
    by_query = lambda w, place=0: spec((block, w), lambda s: (query(s), place))
    before = lambda w, place=0: spec((8, w), lambda s: (jnp.maximum(chunk(s) * (CHUNK // 8) - 1, 0), place))
    whole = lambda a: pl.BlockSpec(a.shape, lambda s: (0,) * a.ndim, pipeline_mode=pl.Buffered(1))
    anywhere = pl.BlockSpec(memory_space=pl.ANY)
    vmem = pl.BlockSpec(memory_space=pltpu.VMEM)
    expand = expand_matrix(width)
    reduce = np.concatenate([expand[:LANES].T] * 2, axis=0)
    state_place, step_place = 2 * width // states2, (2 * width + states2) // LANES
    ins = dict(
        feats_all=(feats, whole(feats)), doc_row=(doc_row, whole(doc_row)), qrot=(qrot, whole(qrot)), keys=(keys, whole(keys)),
        values=(values, whole(values)), lse=(lse, by_query(LANES)), mix_up=(mix_grad, by_query(query_wide, width // query_wide)),
        mix_norm=(mix_grad, by_query(width)), mix_low=(mix, by_query(width)), cos=(cos, whole(cos)), sin=(sin, whole(sin)),
        feats=(feats, by_chunk(LANES)), docs=(doc_row, spec((1, CHUNK), lambda s: (0, chunk(s)))),
        square=(squares, spec((8, LANES), lambda s: (chunk(s), 0))), x=(ssm_in, by_chunk(width, 1)),
        x_before=(ssm_in, before(width, 1)), bc=(ssm_in, by_chunk(states2, state_place)),
        bc_before=(ssm_in, before(states2, state_place)), step=(ssm_in, by_chunk(LANES, step_place)),
        z=(ssm_in, by_chunk(width)), scan=(scan, by_chunk(width)),
        states=(states, spec((1, states2 // 2, width), lambda s: (chunk(s), 0, 0))), norm_grad=(mix_grad, by_chunk(width)),
        taps=(taps, whole(taps)), staps=(staps, whole(staps)), heads=(heads, whole(heads)), expand=(expand, whole(expand)),
        reduce=(reduce, whole(reduce)), gain=(gain, whole(gain)), grad_gate_up=(grad_gate_up, anywhere),
        grad_down=(grad_down, anywhere), grad_mix=(grad_mix, anywhere),
        normed_turned=(normed_turned, anywhere), weights=(first, anywhere), branch_low=(branch_low, anywhere),
        tokens=(tokens, whole(tokens)), scale=(scale, whole(scale)), input_gain=(input_gain, whole(input_gain)),
        second_part=(second_part, whole(second_part)),
    )
    small = width + LANES + states2 + 2 * (hidden // 8)
    shared = states2 + KEYVAL_HEADS * LANES
    outs = dict(
        input_grad=(own_rows, hidden), out_gate_up=(unit, grad_gate_up.shape[1]), out_down=(unit, grad_down.shape[1]),
        out_mix=(unit, grad_mix.shape[1]), out_first=(unit, ssm_wide + qkv_wide), small_out=(8, small),
        shared_out=(unit, shared),
    )
    cut = -(-(ssm_wide + qkv_wide) // (2 * LANES)) * LANES
    every = lambda a: slice(0, a)
    pieces = [
        ("grad_gate_up", every(grad_gate_up.shape[1]), 0, "out_gate_up", every(grad_gate_up.shape[1])),
        ("grad_down", every(grad_down.shape[1]), 1, "out_down", every(grad_down.shape[1])),
        ("grad_mix", every(grad_mix.shape[1]), 1, "out_mix", every(grad_mix.shape[1])),
        ("grad_first", slice(0, cut), 0, "out_first", slice(0, cut)),
        ("grad_first", slice(cut, ssm_wide + qkv_wide), 1, "out_first", slice(cut, ssm_wide + qkv_wide)),
    ]
    steps, stages = (tensors - 1).bit_length(), (count - 1).bit_length() + (tensors - 1).bit_length()
    inner = (total // 16, LANES)
    f32 = lambda *dims: pltpu.VMEM(dims, F32)
    low = lambda *dims: pltpu.VMEM(dims, BF)
    dma = lambda n: pltpu.SemaphoreType.DMA((n,))
    scratch = dict(
        dk_acc=f32(total, kv_wide), dv_acc=f32(total, kv_wide), qkv_grad=low(total, qkv_wide), inner_rows=f32(*inner),
        inner_sum=f32(*inner), inner_own=f32(steps + 1, *inner), inner_in=f32(steps, *inner), inner_send=dma(steps),
        inner_recv=dma(steps), xbuf=f32(CHUNK + 8, width), bcbuf=f32(CHUNK + 8, states2), dxbuf=f32(CHUNK + 8, width),
        dbcbuf=f32(CHUNK + 8, states2), dmemory=f32(states2 // 2, width), ssm_grad=low(total, ssm_wide),
        x_sums=f32(8, width), state_sums=f32(8, states2), head_sums=f32(8, LANES),
        held=low(hidden, ssm_wide + qkv_wide), grad_first=low(hidden, ssm_wide + qkv_wide), branch_own=low(own_rows, hidden),
        normed_part=low(total, hidden), normed_in=low(tensors - 1, own_rows, hidden), gain_sum=f32(8, hidden),
        sums=f32(stages + 1, 8, small), sums_in=f32(stages, 8, small), sum_send=dma(stages), sum_recv=dma(stages),
        shared=f32(steps + 1, unit, shared), shared_in=f32(steps, unit, shared), half_send=dma(steps),
        half_recv=dma(steps), core_send=dma(tensors - 1), core_recv=dma(tensors - 1), local_sems=dma(3), turned=low(hidden, total),
        own_sems=pltpu.SemaphoreType.DMA((3, 2 * levels)),
        send_sems=dma(4 * levels * len(pieces)), recv_sems=dma(4 * levels * len(pieces)),
    )
    for i, piece in enumerate(pieces):
        columns = piece[1].stop - piece[1].start
        scratch.update({
            "cross%d" % i: low(levels, unit, columns), "along_x%d" % i: low(levels, unit, columns),
            "along_y%d" % i: low(levels, unit, columns), "inbound%d" % i: low(levels - 1, unit, columns),
        })
    for i in range(3):
        scratch["own%d" % i] = low(2 * levels, unit, pieces[i][1].stop)
    names = list(ins) + list(outs) + list(scratch)
    c = types.SimpleNamespace(
        names=names, pieces=pieces, early=3, count=count, tensors=tensors, unit=unit, blocks=blocks, chunks=chunks, tiles=tiles, tile=tile,
        groups=groups, split=width + LANES, state_at=(2 * width, 2 * width + states2), kv_at=ssm_wide + query_wide,
    )
    return pl.pallas_call(
        functools.partial(backward_kernel, c),
        grid=(blocks + chunks + levels + tiles + 1,),
        in_specs=[v[1] for v in ins.values()],
        out_specs=[vmem] * len(outs),
        out_shape=[jax.ShapeDtypeStruct(v, F32) for v in outs.values()],
        scratch_shapes=list(scratch.values()),
        compiler_params=pltpu.CompilerParams(collective_id=collective_id, has_side_effects=True, vmem_limit_bytes=VMEM_ALL),
        name="backward",
    )(*(v[0] for v in ins.values()))


def tensor_swap(values):
    return lax.ppermute(values, "tensor", [(0, 1), (1, 0)])


def tensor_pair(values):
    if lax.axis_size("tensor") == 2:
        return values, tensor_swap(values)
    return lax.psum(values.astype(F32), "tensor").astype(values.dtype), jnp.zeros_like(values)


def pad_to(values, size, axis=-1):
    pads = [(0, 0)] * values.ndim
    pads[axis] = (0, size - values.shape[axis])
    return jnp.pad(values, pads) if size > values.shape[axis] else values


def pack_kernel(
    mixer_ref, state_ref, step_ref, query_ref, keyval_ref, proj_ref, attention_ref, gate_up_ref, down_ref,
    first_ref, second_ref,
):
    unit = state_ref.shape[0]
    width, wide = mixer_ref.shape[2], -(-mixer_ref.shape[2] // LANES) * LANES
    same = (iota2((unit, unit), 0) == iota2((unit, unit), 1)).astype(BF)
    place = 0

    def put(out_ref, value, size):
        nonlocal place
        value = value.astype(BF)
        if size > value.shape[1]:
            value = jnp.concatenate([value, jnp.zeros((unit, size - value.shape[1]), BF)], axis=1)
        out_ref[:, place : place + size] = value
        place += size

    put(first_ref, mixer_ref[:, 0, :], wide)
    put(first_ref, mixer_ref[:, 1, :], wide)
    put(first_ref, state_ref[...], state_ref.shape[1])
    put(first_ref, lax.dot_general(same, step_ref[...].astype(BF), (((1,), (1,)), ((), ())), preferred_element_type=F32), LANES)
    query_wide = -(-query_ref.shape[1] // LANES) * LANES
    put(first_ref, query_ref[...], query_wide)
    put(first_ref, keyval_ref[...], keyval_ref.shape[1])
    put(first_ref, proj_ref[...], wide)
    put(first_ref, attention_ref[...], query_wide)
    place = 0
    put(second_ref, gate_up_ref[:, 0, :], gate_up_ref.shape[2])
    put(second_ref, gate_up_ref[:, 1, :], gate_up_ref.shape[2])
    put(second_ref, down_ref[...], down_ref.shape[1])


def pack_weights(mixer, state, step, query, keyval, proj, attention, gate_up, down):
    unit = state.shape[0]
    lanes = lambda size: -(-size // LANES) * LANES
    first = 3 * lanes(mixer.shape[2]) + state.shape[1] + LANES + 2 * lanes(query.shape[1]) + keyval.shape[1]
    second = 2 * gate_up.shape[2] + down.shape[1]
    whole = lambda shape: spec(shape, lambda i: (0,) * len(shape))
    weights = (mixer, state, step, query, keyval, proj, attention, gate_up, down)
    return pl.pallas_call(
        pack_kernel,
        grid=(1,),
        in_specs=[whole(v.shape) for v in weights],
        out_specs=[whole((unit, first)), whole((unit, second))],
        out_shape=[jax.ShapeDtypeStruct((unit, first), BF), jax.ShapeDtypeStruct((unit, second), BF)],
        compiler_params=pltpu.CompilerParams(vmem_limit_bytes=VMEM_WHOLE),
        name="pack_weights",
    )(*weights)


def table_kernel(
    docs_ref, conv_ref, conv_bias_ref, state_conv_ref, state_bias_ref, step_bias_ref, decay_ref, skip_ref,
    feats_ref, cos_ref, sin_ref, taps_ref, state_taps_ref, heads_ref,
):
    total = docs_ref.shape[1]
    docs = docs_ref[...]
    tall = jnp.broadcast_to(docs, (LANES, total)).T
    spot = iota2((1, total), 1)
    begin = jnp.sum((tall[:, 0:1] < docs).astype(F32), axis=0, keepdims=True)
    rows = [docs]
    eight = jnp.broadcast_to(docs, (8, total))
    for k in (1, 2, 3):
        rows.append(jnp.where(spot >= k, (pltpu.roll(eight, k, 1)[0:1] == docs).astype(F32), 0.0))
    blocks = [docs[:, i : i + CHUNK] for i in range(0, total, CHUNK)]
    before = [jnp.full((1, 1), -1.0, F32)] + [v[:, CHUNK - 1 :] for v in blocks[:-1]]
    rows.append(jnp.concatenate([(v == w).astype(F32) for v, w in zip(blocks, before)], axis=1))
    rows.append(jnp.concatenate([(v == v[:, CHUNK - 1 :]).astype(F32) for v in blocks], axis=1))
    for k in (1, 2, 3):
        rows.append(jnp.where(spot < total - k, (pltpu.roll(eight, total - k, 1)[0:1] == docs).astype(F32), 0.0))
    rows.append(spot.astype(F32) - begin)
    rows.append(jnp.zeros((LANES - len(rows), total), F32))
    feats = jnp.concatenate(rows, axis=0).T
    feats_ref[...] = feats
    lane = iota2((1, LANES), 1)
    rates = jnp.exp((lane % (HEAD_SIZE // 2)).astype(F32) * (-2.0 * math.log(THETA) / HEAD_SIZE))
    angles = feats[:, 9:10] * rates
    cos_ref[...] = jnp.cos(angles)
    sin_ref[...] = jnp.sin(angles) * jnp.where(lane % HEAD_SIZE < HEAD_SIZE // 2, -1.0, 1.0)
    width, heads = conv_ref.shape[1], skip_ref.shape[1]
    taps_ref[...] = jnp.zeros_like(taps_ref)
    taps_ref[0:4, :width] = conv_ref[...]
    taps_ref[4:5, :width] = conv_bias_ref[...]
    spread = (iota2((heads, width), 0) == iota2((heads, width), 1) // (width // heads)).astype(F32)
    taps_ref[5:6, :width] = exact_mm(jnp.broadcast_to(skip_ref[...], (8, heads)), spread)[0:1]
    state_taps_ref[...] = jnp.zeros_like(state_taps_ref)
    state_taps_ref[0:4, :] = state_conv_ref[...]
    state_taps_ref[4:5, :] = state_bias_ref[...]
    heads_ref[...] = jnp.zeros_like(heads_ref)
    heads_ref[0:1, :heads] = step_bias_ref[...]
    heads_ref[1:2, :heads] = -jnp.exp(decay_ref[...])


def second_norm_kernel(tokens_ref, part_ref, part_in_ref, gain_ref, middle_ref, second_ref, scale_ref):
    middle = tokens_ref[...].astype(F32) + part_ref[...].astype(F32) + part_in_ref[...].astype(F32)
    scale = lax.rsqrt(jnp.mean(middle * middle, axis=1, keepdims=True) + EPS)
    middle_ref[...] = middle
    scale_ref[...] = scale
    second_ref[...] = (middle * scale * gain_ref[...]).astype(BF)


def by_rows(kernel, name, rows, count, ins, outs, scalars=(), tensors=1, limit=VMEM_LIMIT):
    number = len(scalars)

    def place(shape, kind):
        if kind == "whole":
            return spec(shape, lambda i, *s: (0,) * len(shape))
        if kind == "own":
            own = shape[0] // rows if shape[0] < rows * count else count // tensors
            if shape[0] < rows * count:
                return spec((rows, shape[1]), lambda i, *s: (jnp.clip(i - s[0][0] * own, 0, own - 1), 0))
            return spec((rows, shape[1]), lambda i, *s: (jnp.clip(i, s[0][0] * own, s[0][0] * own + own - 1), 0))
        return spec((rows, shape[1]), lambda i, *s: (i, 0))

    return pl.pallas_call(
        kernel,
        grid_spec=pltpu.PrefetchScalarGridSpec(
            num_scalar_prefetch=number,
            grid=(count,),
            in_specs=[place(v.shape, kind) for v, kind in ins],
            out_specs=[place((r, c), kind) for r, c, _, kind in outs],
        ),
        out_shape=[jax.ShapeDtypeStruct((r, c), dtype) for r, c, dtype, _ in outs],
        compiler_params=pltpu.CompilerParams(vmem_limit_bytes=limit),
        name=name,
    )(*scalars, *(v for v, _ in ins))


def ffn_kernel(second_ref, up_ref, weights_ref, active_ref, grads_ref, out_ref, back_ref):
    ffn = active_ref.shape[1]
    gate_vals = jnp.dot(second_ref[...], weights_ref[:, : 2 * ffn], preferred_element_type=F32)
    active_grad = jnp.dot(up_ref[...], weights_ref[:, 2 * ffn :], preferred_element_type=F32)
    gate, up = gate_vals[:, :ffn], gate_vals[:, ffn:]
    sig = sigmoid(gate)
    silu = gate * sig
    active = (silu * up).astype(BF)
    active_ref[...] = active
    grads_ref[:, :ffn] = (active_grad * up * (sig + silu * (1.0 - sig))).astype(BF)
    grads_ref[:, ffn:] = (active_grad * silu).astype(BF)
    out_ref[...] = mm_nt(active, weights_ref[:, 2 * ffn :]).astype(BF)
    back_ref[...] = mm_nt(grads_ref[...], weights_ref[:, : 2 * ffn]).astype(BF)


def second_back_kernel(
    own_count, core_ref, grad_ref, grad_in_ref, middle_ref, scale_ref, up_ref, gain_ref, part_ref, part_in_ref, low_ref, gain_grad_ref, out_ref
):
    offset = pl.program_id(0) - core_ref[0] * own_count

    @pl.when(pl.program_id(0) == 0)
    def _():
        gain_grad_ref[...] = jnp.zeros_like(gain_grad_ref)

    grad = grad_ref[...].astype(F32) + grad_in_ref[...].astype(F32)
    middle, scale = middle_ref[...], scale_ref[...]
    shape = middle * scale
    weighted = grad * gain_ref[...]
    inner = jnp.mean(weighted * shape, axis=1, keepdims=True)
    low_ref[...] = (up_ref[...].astype(F32) + scale * (weighted - shape * inner)).astype(BF)
    gain_grad_ref[0:1, :] += jnp.sum(grad * shape, axis=0, keepdims=True)

    @pl.when((offset >= 0) & (offset < own_count))
    def _():
        out_ref[...] = (middle + part_ref[...].astype(F32) + part_in_ref[...].astype(F32)).astype(BF)


def finish_kernel(
    sizes, first_ref, mix_ref, shared_ref, small_ref, gate_up_sum_ref, down_sum_ref, input_grad_ref,
    mixer_ref, state_ref, step_ref, conv_ref, conv_bias_ref, state_conv_ref, state_bias_ref, step_bias_ref, decay_ref, skip_ref,
    mixer_gain_ref, proj_ref, query_ref, keyval_ref, attention_ref, gate_up_ref, down_ref, second_gain_ref, input_gain_ref, input_back_ref,
):
    wide, width, states2, heads, query_width, ffn = sizes
    input_back_ref[...] = input_grad_ref[...]
    mixer_ref[:, 0, :] = first_ref[:, :width]
    mixer_ref[:, 1, :] = first_ref[:, wide : wide + width]
    state_ref[...] = shared_ref[:, :states2]
    start = 2 * wide + states2
    step_ref[...] = first_ref[:, start : start + LANES].T[:heads, :]
    start = 2 * wide + states2 + LANES
    query_ref[...] = first_ref[:, start : start + query_width]
    groups = [shared_ref[:, i : i + LANES] for i in range(states2, shared_ref.shape[1], LANES)]
    keyval_ref[:, 0, :] = jnp.concatenate([v[:, :HEAD_SIZE] for v in groups], axis=1)
    keyval_ref[:, 1, :] = jnp.concatenate([v[:, HEAD_SIZE:] for v in groups], axis=1)
    proj_ref[...] = mix_ref[:, :width]
    attention_ref[...] = mix_ref[:, wide : wide + query_width]
    gate_up_ref[:, 0, :] = gate_up_sum_ref[:, :ffn]
    gate_up_ref[:, 1, :] = gate_up_sum_ref[:, ffn:]
    down_ref[...] = down_sum_ref[...]
    conv_ref[...] = small_ref[0:4, :width]
    conv_bias_ref[...] = small_ref[4:5, :width]
    mixer_gain_ref[...] = small_ref[6:7, :width]
    place = iota2((width, heads), 0) // (width // heads)
    gather = (place == iota2((width, heads), 1)).astype(F32)
    skip_ref[...] = exact_mm(jnp.broadcast_to(small_ref[5:6, :width], (8, width)), gather)[0:1]
    step_bias_ref[...] = small_ref[0:1, wide : wide + heads]
    decay_ref[...] = small_ref[1:2, wide : wide + heads]
    base = wide + LANES
    state_conv_ref[...] = small_ref[0:4, base : base + states2]
    state_bias_ref[...] = small_ref[4:5, base : base + states2]
    base += states2
    for out_ref in (second_gain_ref, input_gain_ref):
        out_ref[...] = small_ref[:, base : base + out_ref.shape[1]]
        base += out_ref.shape[1]


def body(
    layer_input, doc_ids, input_gain, mixer_weight, state_weight, step_weight, conv_weight, conv_bias, state_conv,
    state_conv_bias, step_bias, decay_log, skip_gain, mixer_gain, mixer_proj, query_weight, keyval_projection,
    attention_proj, second_gain, gate_up, down_proj, cotangent,
):
    tensor_count = lax.axis_size("tensor")
    tensor_index = lax.axis_index("tensor")
    fsdp_count = lax.axis_size("fsdp")
    own_rows, hidden = layer_input.shape
    unit = state_weight.shape[0]
    seq_count, seq_length = doc_ids.shape
    total = seq_count * seq_length
    heads = step_bias.shape[0]
    width = conv_weight.shape[1]
    wide = -(-width // LANES) * LANES
    query_width = query_weight.shape[1]
    query_wide = -(-query_width // LANES) * LANES
    query_heads = query_width // HEAD_SIZE
    per_group = QUERY_HEADS // KEYVAL_HEADS
    kv_heads = max(1, query_heads // per_group)
    kv_leading = tensor_index * query_heads // per_group
    states2 = state_weight.shape[1]
    ffn = down_proj.shape[0]
    low = lambda v: v.astype(BF)

    own_keyval = lax.dynamic_slice_in_dim(keyval_projection, kv_leading * HEAD_SIZE, kv_heads * HEAD_SIZE, 2)
    own_keyval = own_keyval.reshape(unit, 2, kv_heads, HEAD_SIZE).transpose(0, 2, 1, 3).reshape(unit, 2 * kv_heads * HEAD_SIZE)
    kv_wide = 2 * kv_heads * HEAD_SIZE
    first, rest = pack_weights(
        mixer_weight, state_weight, step_weight.T, query_weight, own_keyval, mixer_proj.T, attention_proj.T, gate_up, down_proj.T
    )
    rest = lax.all_gather(rest, "fsdp", axis=0, tiled=True)
    docs = (doc_ids + jnp.arange(seq_count, dtype=jnp.int32)[:, None] * seq_length).reshape(1, total)
    doc_row = docs.astype(F32)
    tables = (
        doc_row, conv_weight, conv_bias[None], state_conv, state_conv_bias[None], step_bias[None], decay_log[None], skip_gain[None]
    )
    first, tokens, upstream, normed, first_scale, normed_turned, feats, cos, sin, taps, state_taps, head_rows = gather_weights(
        first, layer_input, cotangent, input_gain[None], tables, wide, fsdp_count, tensor_count, 0
    )
    ssm_wide = 2 * wide + states2 + LANES
    cuts = np.cumsum([0, ssm_wide, query_wide + kv_wide, wide + query_wide])
    full_ssm, full_qkv, full_mix = (first[:, cuts[i] : cuts[i + 1]] for i in range(3))
    gain_row = pad_to(mixer_gain[None], wide)
    second_row = second_gain[None]

    ssm_in = plain_dot(normed, full_ssm)
    qkv_in = plain_dot(normed, full_qkv)
    scan, gated_low, squares, states = mamba_forward(feats, doc_row, ssm_in, taps, state_taps, head_rows, gain_row, wide, states2)
    mix, log_sums, query_rot, keys, values, squares = attention_forward(
        kv_heads, tensor_count, feats, doc_row, qkv_in, cos, sin, query_wide, gated_low, squares, 2
    )
    branch = tensor_pair(low(right_dot(mix, full_mix)))
    middle, second, second_scale = by_rows(
        second_norm_kernel, "second_norm", CHUNK, total // CHUNK,
        [(tokens, "rows"), (branch[0], "rows"), (branch[1], "rows"), (second_row, "whole")],
        [(total, hidden, F32, "rows"), (total, hidden, BF, "rows"), (total, 1, F32, "rows")],
    )
    active, gu_grad, ffn_out, second_grad = by_rows(
        ffn_kernel, "ffn", min(FFN_ROWS, total), max(total // FFN_ROWS, 1),
        [(second, "rows"), (upstream, "rows"), (rest, "whole")],
        [(total, ffn, BF, "rows"), (total, 2 * ffn, BF, "rows"), (total, hidden, BF, "rows"), (total, hidden, BF, "rows")],
        limit=VMEM_WHOLE,
    )
    second_grad, ffn_out = tensor_pair(second_grad), tensor_pair(ffn_out)
    grad_gate_up, grad_down = low(left_dot(second, gu_grad)), low(left_dot(upstream, active))
    core = jnp.full((1,), tensor_index, jnp.int32)
    rows = min(CHUNK, own_rows)
    branch_low, second_gain_part, layer_output = by_rows(
        functools.partial(second_back_kernel, own_rows // rows), "second_back", rows, total // rows,
        [
            (second_grad[0], "rows"), (second_grad[1], "rows"), (middle, "rows"), (second_scale, "rows"), (upstream, "rows"),
            (second_row, "whole"), (ffn_out[0], "own"), (ffn_out[1], "own"),
        ],
        [(total, hidden, BF, "rows"), (8, hidden, F32, "whole"), (own_rows, hidden, BF, "own")], (core,), tensor_count,
    )
    mix_grad = low(plain_dot(branch_low, full_mix))
    grad_mix = low(left_dot(branch_low, mix))
    input_back, sum_gate_up, sum_down, sum_mix, sum_first, small, shared = backward(
        kv_heads, feats, doc_row, query_rot, keys, values, log_sums, mix_grad, mix, cos, sin, squares, ssm_in, scan, states, taps,
        state_taps, head_rows, gain_row, grad_gate_up, grad_down, grad_mix, normed_turned, first, branch_low, layer_input, first_scale,
        input_gain[None], second_gain_part, wide, states2, fsdp_count, tensor_count, 1,
    )
    shape = lambda *dims: jax.ShapeDtypeStruct(dims, F32)
    parts = (sum_first, sum_mix, shared, small, sum_gate_up, sum_down, input_back)
    done = pl.pallas_call(
        functools.partial(finish_kernel, (wide, width, states2, heads, query_width, ffn)),
        grid=(1,),
        in_specs=[spec(v.shape, lambda i: (0,) * 2) for v in parts],
        out_shape=[
            shape(unit, 2, width), shape(unit, states2), shape(heads, unit), shape(4, width), shape(1, width), shape(4, states2),
            shape(1, states2), shape(1, heads), shape(1, heads), shape(1, heads), shape(1, width), shape(unit, width),
            shape(unit, query_width), shape(unit, 2, KEYVAL_HEADS * HEAD_SIZE), shape(unit, query_width), shape(unit, 2, ffn),
            shape(unit, ffn), shape(8, hidden // 8), shape(8, hidden // 8), shape(own_rows, hidden),
        ],
        compiler_params=pltpu.CompilerParams(vmem_limit_bytes=VMEM_WHOLE),
        name="finish",
    )(*parts)
    (
        mixer_sum, state_sum, step_sum, conv_sum, conv_bias_sum, state_conv_sum, state_bias_sum, step_bias_sum, decay_sum, skip_sum,
        mixer_gain_sum, proj_sum, query_sum, keyval_sum, attention_sum, gate_up_sum, down_sum, second_gain_sum, input_gain_sum, input_grad,
    ) = done
    return (
        layer_output, input_grad, input_gain_sum.reshape(hidden), mixer_sum, state_sum, step_sum.T, conv_sum, conv_bias_sum[0], state_conv_sum,
        state_bias_sum[0], step_bias_sum[0], decay_sum[0], skip_sum[0], mixer_gain_sum[0], proj_sum.T, query_sum, keyval_sum,
        attention_sum.T, second_gain_sum.reshape(hidden), gate_up_sum, down_sum.T,
    )


def solution(mesh):
    placed = (
        P(("fsdp", "tensor"), None),
        P("fsdp", None),
        P(),
        P("fsdp", None, "tensor"),
        P("fsdp", None),
        P("fsdp", "tensor"),
        P(None, "tensor"),
        P("tensor"),
        P(),
        P(),
        P("tensor"),
        P("tensor"),
        P("tensor"),
        P("tensor"),
        P("tensor", "fsdp"),
        P("fsdp", "tensor"),
        P("fsdp", None, None),
        P("tensor", "fsdp"),
        P(),
        P("fsdp", None, "tensor"),
        P("tensor", "fsdp"),
        P(("fsdp", "tensor"), None),
    )
    return jax.shard_map(
        body,
        mesh=mesh,
        in_specs=placed,
        out_specs=(
            P(("fsdp", "tensor"), None),
            P(("fsdp", "tensor"), None),
            P(),
            P("fsdp", None, "tensor"),
            P("fsdp", None),
            P("fsdp", "tensor"),
            P(None, "tensor"),
            P("tensor"),
            P(),
            P(),
            P("tensor"),
            P("tensor"),
            P("tensor"),
            P("tensor"),
            P("tensor", "fsdp"),
            P("fsdp", "tensor"),
            P("fsdp", None, None),
            P("tensor", "fsdp"),
            P(),
            P("fsdp", None, "tensor"),
            P("tensor", "fsdp"),
        ),
        check_vma=False,
    )
```

```python
import functools
import math
import types

import jax
import jax.numpy as jnp
import ml_dtypes
import numpy as np
from jax import lax
from jax.experimental import pallas as pl
from jax.experimental.pallas import tpu as pltpu
from jax.sharding import PartitionSpec as P

QUERY_HEADS = 8
KEYVAL_HEADS = 2
HEAD_SIZE = 64
DSSM = 1536
EPS = 1e-05
THETA = 100000000000.0

LANES = 128
CHUNK = 128
FFN_ROWS = 256
QBLOCK = 256
VMEM_LIMIT = 32 * 2**20
VMEM_WHOLE = 60 * 2**20
VMEM_ALL = 63 * 2**20
MASKED = -1e30
BF, F32 = jnp.bfloat16, jnp.float32


def left_dot(left_side, right_side):
    return lax.dot_general(left_side, right_side, (((0,), (0,)), ((), ())), preferred_element_type=F32)


def right_dot(left_side, right_side):
    return lax.dot_general(left_side, right_side, (((1,), (1,)), ((), ())), preferred_element_type=F32)


def plain_dot(left_side, right_side):
    return jnp.dot(left_side, right_side, preferred_element_type=F32)


def mm(a, b):
    return jnp.dot(a.astype(BF), b.astype(BF), preferred_element_type=F32)


def mm_nt(a, b):
    return lax.dot_general(a.astype(BF), b.astype(BF), (((1,), (1,)), ((), ())), preferred_element_type=F32)


def mm_tn(a, b):
    return lax.dot_general(a.astype(BF), b.astype(BF), (((0,), (0,)), ((), ())), preferred_element_type=F32)


def exact_mm(a, b):
    return jnp.dot(a, b, precision=lax.Precision.HIGHEST, preferred_element_type=F32)


def sigmoid(v):
    return 1.0 / (1.0 + jnp.exp(-v))


def softplus(v):
    return jnp.maximum(v, 0.0) + jnp.log1p(jnp.exp(-jnp.abs(v)))


def split_lanes(values, axis):
    high = values.astype(BF)
    low = (values - high.astype(F32)).astype(BF)
    return jnp.concatenate([high, low], axis=axis)


def iota2(shape, axis):
    return lax.broadcasted_iota(jnp.int32, shape, axis)


def flipped(index, mask):
    bit = 1
    while bit <= mask:
        if mask & bit:
            index = index + bit * (1 - 2 * ((index // bit) % 2))
        bit *= 2
    return index


def greet(partners):
    barrier = pltpu.get_barrier_semaphore()
    for axis, place in partners:
        pl.semaphore_signal(barrier, inc=1, device_id={axis: place}, device_id_type=pl.DeviceIdType.MESH)
    pl.semaphore_wait(barrier, len(partners))


def remote(source, target, send, recv, axis, place):
    return pltpu.make_async_remote_copy(
        src_ref=source, dst_ref=target, send_sem=send, recv_sem=recv,
        device_id={axis: place}, device_id_type=pl.DeviceIdType.MESH,
    )


class TensorSum:
    def __init__(self, tensors, own, arrived, send, recv):
        self.core = lax.axis_index("tensor")
        self.places = [flipped(self.core, 1 << k) for k in range((tensors - 1).bit_length())]
        self.refs = own, arrived, send, recv

    def copy(self, k):
        own, arrived, send, recv = self.refs
        return remote(own.at[k], arrived.at[k], send.at[k], recv.at[k], "tensor", self.places[k])

    def begin(self, value, met=False):
        if not met:
            greet([("tensor", place) for place in self.places])
        self.refs[0][0] = value
        self.copy(0).start()

    def end(self):
        own, arrived, _, _ = self.refs
        for k in range(len(self.places)):
            copy = self.copy(k)
            if k:
                copy.start()
            copy.wait()
            own[k + 1] = own[k] + arrived[k]
        return own[len(self.places)]


def tensor_sum_scratch(tensors, shape):
    steps = (tensors - 1).bit_length()
    return [
        pltpu.VMEM((steps + 1,) + shape, F32), pltpu.VMEM((steps,) + shape, F32),
        pltpu.SemaphoreType.DMA((steps,)), pltpu.SemaphoreType.DMA((steps,)),
    ]


def conv_taps(buffer, feats, taps, bias, rows):
    total = buffer[8 : 8 + rows, :] * taps[3:4, :] + bias
    for k in range(1, 4):
        total = total + buffer[8 - k : 8 - k + rows, :] * feats[:, k : k + 1] * taps[3 - k : 4 - k, :]
    return total


def step_parts(step_ref, heads_ref, feats, rows):
    raw = step_ref[...] + heads_ref[0:1, :]
    step = softplus(raw)
    lower = (iota2((rows, rows), 0) >= iota2((rows, rows), 1)).astype(F32)
    log_decay = exact_mm(lower, step * heads_ref[1:2, :])
    last = log_decay[rows - 1 : rows, :]
    enter = jnp.exp(log_decay) * feats[:, 4:5]
    leave = jnp.exp(last - log_decay) * feats[:, 5:6]
    return raw, step, log_decay, enter, leave


def gated_scale(squares):
    return lax.rsqrt(squares / DSSM + EPS)


def as_column(row):
    return jnp.broadcast_to(row, (LANES, row.shape[1])).T[:, 0:1]


def mamba_fwd_kernel(
    feats_ref, docs_ref, x_ref, bc_ref, step_ref, z_ref, taps_ref, staps_ref, heads_ref, expand_ref,
    gain_ref, scan_ref, low_ref, square_ref, states_ref, xbuf, bcbuf, memory,
):
    rows, width = x_ref.shape
    states = bc_ref.shape[1] // 2

    @pl.when(pl.program_id(0) == 0)
    def _():
        xbuf[0:8, :] = jnp.zeros((8, width), F32)
        bcbuf[0:8, :] = jnp.zeros((8, 2 * states), F32)
        memory[...] = jnp.zeros_like(memory)

    feats = feats_ref[...]
    xbuf[8 : 8 + rows, :] = x_ref[...]
    bcbuf[8 : 8 + rows, :] = bc_ref[...]
    pre = conv_taps(xbuf, feats, taps_ref, taps_ref[4:5, :], rows)
    values = pre * sigmoid(pre)
    pre_bc = conv_taps(bcbuf, feats, staps_ref, staps_ref[4:5, :], rows)
    both = pre_bc * sigmoid(pre_bc)
    xbuf[0:8, :] = xbuf[rows : rows + 8, :]
    bcbuf[0:8, :] = bcbuf[rows : rows + 8, :]
    key_in = both[:, :states].astype(BF)
    key_out = both[:, states:].astype(BF)
    _, step, log_decay, enter, leave = step_parts(step_ref, heads_ref, feats, rows)
    expanded = jnp.dot(
        split_lanes(jnp.concatenate([step, enter, leave], axis=0), 1), expand_ref[...], preferred_element_type=F32
    )
    step_w, enter_w, leave_w = expanded[:rows], expanded[rows : 2 * rows], expanded[2 * rows :]
    scaled = values * step_w
    gram = mm_nt(key_out, key_in)
    allowed = (feats[:, 0:1] == docs_ref[...]) & (iota2((rows, rows), 0) >= iota2((rows, rows), 1))
    bias = jnp.where(allowed, 0.0, MASKED)
    log_rows = log_decay.T
    front = iota2((rows, LANES), 1) < LANES // 2
    held = memory[...]
    states_ref[0] = held.astype(BF)
    carried = mm(key_out, held) * enter_w
    fresh = mm_tn(key_in, leave_w * scaled)
    memory[...] = held * enter_w[rows - 1 : rows, :] + fresh
    squares = jnp.zeros((rows, 1), F32)
    for pair in range(width // LANES):
        lanes = slice(pair * LANES, (pair + 1) * LANES)
        mixes = []
        for h in (2 * pair, 2 * pair + 1):
            decay = jnp.exp(log_decay[:, h : h + 1] - log_rows[h : h + 1, :] + bias)
            mixes.append((gram * decay).astype(BF))
        part = scaled[:, lanes]
        stacked = jnp.concatenate([jnp.where(front, part, 0.0), jnp.where(front, 0.0, part)], axis=0)
        inside = mm(jnp.concatenate(mixes, axis=1), stacked)
        scan = inside + carried[:, lanes] + values[:, lanes] * taps_ref[5:6, lanes]
        scan_ref[:, lanes] = scan
        z = z_ref[:, lanes]
        gated = scan * (z * sigmoid(z))
        low_ref[:, lanes] = (gated * gain_ref[:, lanes]).astype(BF)
        squares = squares + jnp.sum(gated * gated, axis=1, keepdims=True)
    square_ref[...] = jnp.broadcast_to(squares, (rows, LANES)).T[0:8, :]


def mamba_bwd_block(
    feats_ref, square_ref, inner_sum, block, docs_ref, x_ref, x_before_ref, bc_ref, bc_before_ref, step_ref, z_ref, scan_ref, states_ref, norm_grad_ref,
    taps_ref, staps_ref, heads_ref, expand_ref, reduce_ref, gain_ref,
    grads_ref, sums_ref, ssums_ref, hsums_ref,
    xbuf, bcbuf, dxbuf, dbcbuf, dmemory,
):
    rows, width = x_ref.shape
    states = bc_ref.shape[1] // 2

    feats = feats_ref[...]
    xbuf[0:8, :] = x_before_ref[...]
    bcbuf[0:8, :] = bc_before_ref[...]
    xbuf[8 : 8 + rows, :] = x_ref[...]
    bcbuf[8 : 8 + rows, :] = bc_ref[...]
    pre = conv_taps(xbuf, feats, taps_ref, taps_ref[4:5, :], rows)
    pre_gate = sigmoid(pre)
    values = pre * pre_gate
    pre_bc = conv_taps(bcbuf, feats, staps_ref, staps_ref[4:5, :], rows)
    bc_gate = sigmoid(pre_bc)
    both = pre_bc * bc_gate
    key_in = both[:, :states].astype(BF)
    key_out = both[:, states:].astype(BF)
    raw, step, log_decay, enter, leave = step_parts(step_ref, heads_ref, feats, rows)
    expanded = jnp.dot(
        split_lanes(jnp.concatenate([step, enter, leave], axis=0), 1), expand_ref[...], preferred_element_type=F32
    )
    step_w, enter_w, leave_w = expanded[:rows], expanded[rows : 2 * rows], expanded[2 * rows :]
    scaled = values * step_w
    z = z_ref[...]
    z_gate = sigmoid(z)
    z_silu = z * z_gate
    scan = scan_ref[...]
    gated = scan * z_silu
    norm_grad = norm_grad_ref[...].astype(F32)
    row_scale = gated_scale(square_ref[0:1, :])
    row_inner = inner_sum[pl.ds(pl.multiple_of(block * 8, 8), 8), :][0:1, :] * row_scale * row_scale / DSSM
    scale, coefficient = as_column(row_scale), as_column(row_inner)
    weighted = norm_grad * scale
    gated_grad = weighted * gain_ref[...] - gated * coefficient
    dscan = gated_grad * z_silu
    grads_ref[:, 0:width] = (gated_grad * scan * (z_gate * (1.0 + z * (1.0 - z_gate)))).astype(BF)
    sums_ref[6:7, :] += jnp.sum(weighted * gated, axis=0, keepdims=True)
    sums_ref[5:6, :] += jnp.sum(dscan * values, axis=0, keepdims=True)
    held = states_ref[0]
    dheld = dmemory[...]
    dheld_low = dheld.astype(BF)
    enter_grad = (dscan * enter_w).astype(BF)
    left = leave_w * scaled
    passed = mm(key_in, dheld_low)
    arrived = mm(key_out, held)
    dkey_out = mm_nt(enter_grad, held)
    dkey_in = mm_nt(left, dheld_low)
    carry = enter_w[rows - 1 : rows, :]
    dmemory[...] = dheld * carry + mm_tn(key_out, enter_grad)
    enter_terms = dscan * enter_w * arrived
    leave_terms = left * passed
    carry_terms = jnp.sum(dheld * held.astype(F32), axis=0, keepdims=True) * carry
    gram = mm_nt(key_in, key_out)
    allowed = (feats[:, 0:1] == docs_ref[...]) & (iota2((rows, rows), 0) <= iota2((rows, rows), 1))
    bias = jnp.where(allowed, 0.0, MASKED)
    log_rows = log_decay.T
    front = iota2((rows, LANES), 1) < LANES // 2
    gram_grad = jnp.zeros((rows, rows), F32)
    lane_of = iota2((rows, LANES), 1)
    row_of = iota2((LANES, rows), 0)
    sent = jnp.zeros((rows, LANES), F32)
    received = jnp.zeros((LANES, rows), F32)
    inside_grads = []
    for pair in range(width // LANES):
        lanes = slice(pair * LANES, (pair + 1) * LANES)
        dy = dscan[:, lanes].astype(BF)
        part = scaled[:, lanes]
        stacked = jnp.concatenate([jnp.where(front, part, 0.0), jnp.where(front, 0.0, part)], axis=0)
        cross = mm_nt(stacked, dy)
        mixes = []
        for j, h in enumerate((2 * pair, 2 * pair + 1)):
            decay = jnp.exp(log_rows[h : h + 1, :] - log_decay[:, h : h + 1] + bias)
            mix = gram * decay
            mixes.append(mix.astype(BF))
            dmix = cross[j * rows : (j + 1) * rows, :]
            gram_grad = gram_grad + dmix * decay
            flow = dmix * mix
            sent = jnp.where(lane_of == h, jnp.sum(flow, axis=1, keepdims=True), sent)
            received = jnp.where(row_of == h, jnp.sum(flow, axis=0, keepdims=True), received)
        grads = mm(jnp.concatenate(mixes, axis=0), dy)
        inside_grads.append(jnp.where(front, grads[:rows], grads[rows:]))
    dscaled = jnp.concatenate(inside_grads, axis=1) + leave_w * passed
    dkey_in = dkey_in + mm(gram_grad, key_out)
    dkey_out = dkey_out + mm_tn(gram_grad, key_in)
    reduced = jnp.dot(
        split_lanes(
            jnp.concatenate([enter_terms, leave_terms, dscaled * values, jnp.broadcast_to(carry_terms, (8, width))], axis=0), 1
        ),
        reduce_ref[...],
        preferred_element_type=F32,
    )
    after = reduced[:rows] + received.T - sent
    upper = (iota2((rows, rows), 0) <= iota2((rows, rows), 1)).astype(F32)
    strict = (iota2((rows, rows), 0) > iota2((rows, rows), 1)).astype(F32)
    decay_grad = exact_mm(upper, after) + exact_mm(strict, reduced[rows : 2 * rows]) + reduced[3 * rows : 3 * rows + 1]
    dstep = decay_grad * heads_ref[1:2, :] + reduced[2 * rows : 3 * rows]
    draw = dstep * sigmoid(raw)
    grads_ref[:, 2 * width + 2 * states :] = draw.astype(BF)
    hsums_ref[0:1, :] += jnp.sum(draw, axis=0, keepdims=True)
    hsums_ref[1:2, :] += jnp.sum(decay_grad * step, axis=0, keepdims=True) * heads_ref[1:2, :]
    dvalues = dscaled * step_w + dscan * taps_ref[5:6, :]
    dpre = dvalues * (pre_gate * (1.0 + pre * (1.0 - pre_gate)))
    dboth = jnp.concatenate([dkey_in, dkey_out], axis=1)
    dpre_bc = dboth * (bc_gate * (1.0 + pre_bc * (1.0 - bc_gate)))
    for dpre_now, buffer, dbuffer, taps, totals, lanes in (
        (dpre, xbuf, dxbuf, taps_ref, sums_ref, slice(width, 2 * width)),
        (dpre_bc, bcbuf, dbcbuf, staps_ref, ssums_ref, slice(2 * width, 2 * width + 2 * states)),
    ):
        dbuffer[0:rows, :] = dpre_now
        grad = dpre_now * taps[3:4, :]
        totals[3:4, :] += jnp.sum(dpre_now * buffer[8 : 8 + rows, :], axis=0, keepdims=True)
        totals[4:5, :] += jnp.sum(dpre_now, axis=0, keepdims=True)
        for k in range(1, 4):
            grad = grad + dbuffer[k : k + rows, :] * feats[:, 5 + k : 6 + k] * taps[3 - k : 4 - k, :]
            totals[3 - k : 4 - k, :] += jnp.sum(
                dpre_now * buffer[8 - k : 8 - k + rows, :] * feats[:, k : k + 1], axis=0, keepdims=True
            )
        grads_ref[:, lanes] = grad.astype(BF)
        dbuffer[rows : rows + 8, :] = dbuffer[0:8, :]


def expand_matrix(width):
    one = np.arange(LANES)[:, None] == np.arange(width)[None, :] // (LANES // 2)
    return np.concatenate([one, one], axis=0).astype(ml_dtypes.bfloat16)


def spec(block, index):
    return pl.BlockSpec(block, index)


def mamba_forward(feats, doc_row, ssm_in, taps, staps, heads, gain, width, states2):
    total = ssm_in.shape[0]
    rows = CHUNK
    count = total // rows
    block = lambda w, place=0: spec((rows, w), lambda i: (i, place))
    whole = lambda a: spec(a.shape, lambda i: (0,) * a.ndim)
    expand = expand_matrix(width)
    return pl.pallas_call(
        mamba_fwd_kernel,
        grid=(count,),
        in_specs=[
            block(LANES), spec((1, rows), lambda i: (0, i)), block(width, 1), block(states2, 2 * width // states2),
            block(LANES, (2 * width + states2) // LANES), block(width), whole(taps), whole(staps), whole(heads), whole(expand), whole(gain),
        ],
        out_specs=[block(width), block(width), spec((8, LANES), lambda i: (i, 0)), spec((1, states2 // 2, width), lambda i: (i, 0, 0))],
        out_shape=[
            jax.ShapeDtypeStruct((total, width), F32),
            jax.ShapeDtypeStruct((total, width), BF),
            jax.ShapeDtypeStruct((8 * count, LANES), F32),
            jax.ShapeDtypeStruct((count, states2 // 2, width), BF),
        ],
        scratch_shapes=[
            pltpu.VMEM((rows + 8, width), F32), pltpu.VMEM((rows + 8, states2), F32), pltpu.VMEM((states2 // 2, width), F32),
        ],
        compiler_params=pltpu.CompilerParams(vmem_limit_bytes=VMEM_LIMIT),
        cost_estimate=pl.CostEstimate(flops=20 * 10**9, bytes_accessed=total * width * 20, transcendentals=total * width * 4),
        name="mamba_fwd",
    )(feats, doc_row, ssm_in, ssm_in, ssm_in, ssm_in, taps, staps, heads, expand, gain)


def swap_halves(values):
    lane = iota2(values.shape, 1) % (LANES // 2)
    return jnp.where(lane < LANES // 4, pltpu.roll(values, LANES - LANES // 4, 1), pltpu.roll(values, LANES // 4, 1))


def stack_heads(part):
    front = iota2(part.shape, 1) < LANES // 2
    zero = jnp.zeros_like(part)
    return jnp.concatenate([jnp.where(front, part, zero), jnp.where(front, zero, part)], axis=0)


def attention_fwd_kernel(
    groups, tensors, docs_col_ref, docs_ref, q_ref, kv_ref, cos_ref, sin_ref, low_ref, square_ref, out_ref, lse_ref, qrot_ref, keys_ref, values_ref, square_out_ref, *scratch,
):
    total = q_ref.shape[0]
    wide = low_ref.shape[1]
    exchange = TensorSum(tensors, *scratch)
    exchange.begin(square_ref[...])
    pairs = q_ref.shape[1] // LANES
    block = min(QBLOCK, total)
    cos, sin = cos_ref[...], sin_ref[...]
    front = iota2((total, LANES), 1) < LANES // 2
    for g in range(groups):
        lanes = slice(g * LANES, (g + 1) * LANES)
        raw = kv_ref[:, lanes]
        turned = raw * cos + swap_halves(raw) * sin
        keys_ref[:, lanes] = jnp.where(front, turned, pltpu.roll(turned, LANES // 2, 1)).astype(BF)
        values_ref[:, lanes] = jnp.where(front, pltpu.roll(raw, LANES // 2, 1), raw).astype(BF)
    for p in range(pairs):
        lanes = slice(p * LANES, (p + 1) * LANES)
        raw = q_ref[:, lanes]
        qrot_ref[:, lanes] = ((raw * cos + swap_halves(raw) * sin).astype(BF).astype(F32) * (LANES // 2) ** -0.5).astype(BF)
    front = iota2((block, LANES), 1) < LANES // 2
    lane_of = iota2((block, LANES), 1)
    for start in range(0, total, block):
        rows, end = slice(start, start + block), start + block
        allowed = (docs_col_ref[rows, 0:1] == docs_ref[:, :end]) & (
            iota2((block, end), 0) + start >= iota2((block, end), 1)
        )
        bias = jnp.where(allowed, 0.0, MASKED)
        bias = jnp.concatenate([bias, bias], axis=0)
        sums = jnp.zeros((block, LANES), F32)
        for p in range(pairs):
            lanes = slice(p * LANES, (p + 1) * LANES)
            g = p * groups // pairs
            kv = slice(g * LANES, (g + 1) * LANES)
            scores = mm_nt(stack_heads(qrot_ref[rows, lanes]), keys_ref[:end, kv]) + bias
            top = jnp.max(scores, axis=1, keepdims=True)
            raised = jnp.exp(scores - top)
            whole = jnp.sum(raised, axis=1, keepdims=True)
            mixed = mm(raised, values_ref[:end, kv]) / whole
            out_ref[rows, wide + p * LANES : wide + (p + 1) * LANES] = jnp.where(front, mixed[:block], mixed[block:]).astype(BF)
            logs = top + jnp.log(whole)
            sums = jnp.where(lane_of == 2 * p, logs[:block], sums)
            sums = jnp.where(lane_of == 2 * p + 1, logs[block:], sums)
        lse_ref[rows, :] = sums
    square_out_ref[...] = exchange.end()
    for i in range(total // LANES):
        piece = slice(i * LANES, (i + 1) * LANES)
        scale = as_column(gated_scale(square_out_ref[8 * i : 8 * i + 1, :]))
        out_ref[piece, :wide] = (low_ref[piece, :].astype(F32) * scale).astype(BF)


def attention_bwd_block(
    start, groups, docs_col_ref, docs_ref, qrot_ref, keys_ref, values_ref, lse_ref, up_ref, cos_ref, sin_ref, grads_ref, dk_acc, dv_acc,
):
    pairs = qrot_ref.shape[1] // LANES
    block = up_ref.shape[0]
    front = iota2((block, LANES), 1) < LANES // 2
    rows, end = slice(start, start + block), start + block
    allowed = (docs_col_ref[:end, 0:1] == docs_ref[:, rows]) & (
        iota2((end, block), 0) <= iota2((end, block), 1) + start
    )
    bias = jnp.where(allowed, 0.0, MASKED)
    logs = lse_ref[...].T
    cos, sin = cos_ref[rows, :], sin_ref[rows, :]
    for p in range(pairs):
        lanes = slice(p * LANES, (p + 1) * LANES)
        g = p * groups // pairs
        kv = slice(g * LANES, (g + 1) * LANES)
        keys, values = keys_ref[:end, kv], values_ref[:end, kv]
        queries = stack_heads(qrot_ref[rows, lanes])
        ups = stack_heads(up_ref[:, lanes])
        shift = jnp.concatenate([bias - logs[2 * p : 2 * p + 1], bias - logs[2 * p + 1 : 2 * p + 2]], axis=1)
        probs = jnp.exp(mm_nt(keys, queries) + shift)
        grads = mm_nt(values, ups)
        centre = jnp.sum(probs * grads, axis=0, keepdims=True)
        score_grads = (probs * (grads - centre)).astype(BF)
        dk_acc[:end, kv] += mm(score_grads, queries)
        dv_acc[:end, kv] += mm(probs, ups)
        dq = mm_tn(score_grads, keys)
        dq = jnp.where(front, dq[:block], dq[block:]) * (LANES // 2) ** -0.5
        grads_ref[rows, lanes] = (dq * cos - swap_halves(dq) * sin).astype(BF)


def attention_bwd_end(groups, pairs, cos_ref, sin_ref, grads_ref, dk_acc, dv_acc):
    total = dk_acc.shape[0]
    front = iota2((total, LANES), 1) < LANES // 2
    for g in range(groups):
        kv = slice(g * LANES, (g + 1) * LANES)
        dk, dv = dk_acc[:, kv], dv_acc[:, kv]
        dk = dk + pltpu.roll(dk, LANES // 2, 1)
        dk = dk * cos_ref[...] - swap_halves(dk) * sin_ref[...]
        dv = dv + pltpu.roll(dv, LANES // 2, 1)
        out = slice((pairs + g) * LANES, (pairs + g + 1) * LANES)
        grads_ref[:, out] = jnp.where(front, dk, dv).astype(BF)


def attention_forward(groups, tensors, doc_col, doc_row, qkv, cos, sin, query_width, low, squares, collective_id):
    total = qkv.shape[0]
    kv_width = qkv.shape[1] - query_width
    whole = lambda a: spec(a.shape, lambda i: (0,) * a.ndim)
    columns = lambda w, place=0: spec((total, w), lambda i: (0, place))
    return pl.pallas_call(
        functools.partial(attention_fwd_kernel, groups, tensors),
        grid=(1,),
        in_specs=[whole(doc_col), whole(doc_row), columns(query_width), columns(kv_width, query_width // kv_width), whole(cos), whole(sin), whole(low), whole(squares)],
        out_specs=[columns(low.shape[1] + query_width), columns(LANES), columns(query_width), columns(kv_width), columns(kv_width), whole(squares)],
        out_shape=[
            jax.ShapeDtypeStruct((total, low.shape[1] + query_width), BF), jax.ShapeDtypeStruct((total, LANES), F32),
            jax.ShapeDtypeStruct((total, query_width), BF), jax.ShapeDtypeStruct((total, kv_width), BF),
            jax.ShapeDtypeStruct((total, kv_width), BF), jax.ShapeDtypeStruct(squares.shape, F32),
        ],
        scratch_shapes=tensor_sum_scratch(tensors, squares.shape),
        compiler_params=pltpu.CompilerParams(vmem_limit_bytes=VMEM_LIMIT, collective_id=collective_id, has_side_effects=True),
        cost_estimate=pl.CostEstimate(flops=12 * 10**9, bytes_accessed=total * query_width * 10, transcendentals=total * total * 2),
        name="attention_fwd",
    )(doc_col, doc_row, qkv, qkv, cos, sin, low, squares)


def gather_kernel(
    count, tensors, shard_ref, tokens_ref, cotangent_ref, gain_ref, *refs,
):
    tables, (full_ref, all_tokens_ref, all_cotangent_ref, normed_ref, scale_ref, turned_ref) = refs[:8], refs[8:14]
    table_outs, (own_sem, send_sems, recv_sems, core_send, core_recv) = refs[14:20], refs[20:]
    unit, columns = shard_ref.shape
    levels = count // 4
    me = lax.axis_index("fsdp")
    half = columns // 2 // LANES * LANES
    parts = (slice(0, half), slice(half, columns))
    neighbours = (flipped(me, 1), flipped(me, 2))
    far = [flipped(me, 4 * d) for d in range(1, levels)]
    core = lax.axis_index("tensor")
    cores = [flipped(core, k) for k in range(1, tensors)]
    greet([("fsdp", p) for p in neighbours] + [("fsdp", p) for p in far] + [("tensor", p) for p in cores])

    def rows(owner):
        return pl.ds(pl.multiple_of(owner * unit, unit), unit)

    started = []

    def send(source, owner, lanes, slot, place):
        copy = remote(source, full_ref.at[rows(owner), lanes], send_sems.at[slot], recv_sems.at[slot], "fsdp", place)
        copy.start()
        started.append(copy)
        return copy

    def arrival(owner, lanes, slot):
        piece = full_ref.at[rows(owner), lanes]
        return remote(piece, piece, send_sems.at[slot], recv_sems.at[slot], "fsdp", neighbours[0])

    everything = slice(0, columns)
    own = pltpu.make_async_copy(shard_ref, full_ref.at[rows(me), :], own_sem)
    own.start()
    for d in range(1, levels):
        send(shard_ref, me, everything, d, far[d - 1])
    base = levels
    for axis in range(2):
        send(shard_ref, me, everything, base + axis * levels, neighbours[axis])
    cross = base + 2 * levels
    own_rows = tokens_ref.shape[0]
    share = lambda owner: pl.ds(pl.multiple_of(owner * own_rows, own_rows), own_rows)
    exchanges = []
    for k, place in enumerate(cores):
        for j, (source, target) in enumerate(((tokens_ref, all_tokens_ref), (cotangent_ref, all_cotangent_ref))):
            copy = remote(
                source, target.at[share(core), :], core_send.at[2 * k + j], core_recv.at[2 * k + j], "tensor", place
            )
            copy.start()
            exchanges.append(copy)
    all_tokens_ref[share(core), :] = tokens_ref[...]
    all_cotangent_ref[share(core), :] = cotangent_ref[...]
    for copy in exchanges:
        copy.wait()

    def norm(i, carry):
        piece = pl.ds(pl.multiple_of(i * LANES, LANES), LANES)
        values = all_tokens_ref[piece, :].astype(F32)
        scale = lax.rsqrt(jnp.mean(values * values, axis=1, keepdims=True) + EPS)
        scale_ref[piece, :] = scale
        normed = values * scale * gain_ref[...]
        normed_ref[piece, :] = normed.astype(BF)
        turned_ref[:, piece] = normed.T.astype(BF)
        return carry

    lax.fori_loop(0, normed_ref.shape[0] // LANES, norm, 0)
    table_kernel(*tables, *table_outs)

    def pass_on(d):
        for axis in range(2):
            owner = flipped(neighbours[axis], 4 * d)
            arrival(owner, everything, base + axis * levels + d).wait_recv()
            piece = full_ref.at[rows(owner), parts[axis]]
            send(piece, owner, parts[axis], cross + axis * levels + d, neighbours[1 - axis])

    for d in range(1, levels):
        arrival(far[d - 1], everything, d).wait_recv()
        for axis in range(2):
            send(full_ref.at[rows(far[d - 1]), :], far[d - 1], everything, base + axis * levels + d, neighbours[axis])
        pass_on(d - 1)
    pass_on(levels - 1)
    for d in range(levels):
        for axis in range(2):
            owner = flipped(me, 4 * d + 3)
            arrival(owner, parts[axis], cross + axis * levels + d).wait_recv()
    for copy in started:
        copy.wait_send()
    own.wait()


def gather_weights(shard, tokens, cotangent, gain, tables, wide, count, tensors, collective_id):
    unit, columns = shard.shape
    own_rows, hidden = tokens.shape
    total = own_rows * tensors
    slots = 5 * (count // 4)
    vmem, anywhere = pl.BlockSpec(memory_space=pltpu.VMEM), pl.BlockSpec(memory_space=pl.ANY)
    low = jax.ShapeDtypeStruct((total, hidden), BF)
    shape = lambda r, c: jax.ShapeDtypeStruct((r, c), F32)
    return pl.pallas_call(
        functools.partial(gather_kernel, count, tensors),
        in_specs=[anywhere, vmem, vmem, vmem] + [vmem] * len(tables),
        out_specs=[anywhere] + [vmem] * 11,
        out_shape=[jax.ShapeDtypeStruct((count * unit, columns), shard.dtype), low, low, low, jax.ShapeDtypeStruct((total, 1), F32),
            jax.ShapeDtypeStruct((hidden, total), BF), shape(total, LANES), shape(total, LANES), shape(total, LANES), shape(8, wide),
            shape(8, tables[3].shape[1]), shape(8, LANES),
        ],
        scratch_shapes=[
            pltpu.SemaphoreType.DMA, pltpu.SemaphoreType.DMA((slots,)), pltpu.SemaphoreType.DMA((slots,)),
            pltpu.SemaphoreType.DMA((2 * (tensors - 1),)), pltpu.SemaphoreType.DMA((2 * (tensors - 1),)),
        ],
        compiler_params=pltpu.CompilerParams(collective_id=collective_id, has_side_effects=True, vmem_limit_bytes=VMEM_LIMIT),
        cost_estimate=pl.CostEstimate(flops=0, bytes_accessed=2 * count * unit * columns * 2, transcendentals=0),
        name="gather_weights",
    )(shard, tokens, cotangent, gain, *tables)


def backward_kernel(c, *refs):
    r = types.SimpleNamespace(**dict(zip(c.names, refs)))
    now = pl.program_id(0)
    me, core = lax.axis_index("fsdp"), lax.axis_index("tensor")
    levels, unit, blocks, chunks, tiles = c.count // 4, c.unit, c.blocks, c.chunks, c.tiles
    near = (flipped(me, 1), flipped(me, 2))
    far = [None] + [flipped(me, 4 * d) for d in range(1, levels)]
    bits = [1 << k for k in range((c.count - 1).bit_length())]
    cores = [flipped(core, k) for k in range(1, c.tensors)]
    halves = [("tensor", flipped(core, 1 << k)) for k in range((c.tensors - 1).bit_length())]
    stages = [("fsdp", flipped(me, bit)) for bit in bits] + halves
    order = sorted(range(levels), key=lambda d: (d & -d if d else levels, -d))
    pieces = []
    for i, (name, lanes, path, out, out_lanes) in enumerate(c.pieces):
        pieces.append((i, getattr(r, name), lanes, path, getattr(r, out), out_lanes))
    early, late, flat = pieces[: c.early], pieces[c.early : c.flat], pieces[c.flat :]

    def own_copies():
        copies = []
        for i, grad, lanes, path, _, _ in early:
            parts = getattr(r, "own%d" % i)
            for d in order:
                for k, owner in ((d, flipped(near[path], 4 * d)), (levels + d, flipped(me, 4 * d))):
                    copies.append(pltpu.make_async_copy(grad.at[rows(owner), lanes], parts.at[k], r.own_sems.at[i, k]))
        return copies

    def own_part(i, grad, lanes, owner, k):
        if i < c.early:
            return getattr(r, "own%d" % i)[k].astype(F32)
        return grad[spot(i, owner), lanes].astype(F32)

    cross, along, inbound = [], [], []
    for i in range(len(pieces)):
        cross.append(getattr(r, "cross%d" % i))
        along.append((getattr(r, "along_x%d" % i), getattr(r, "along_y%d" % i)))
        inbound.append(getattr(r, "inbound%d" % i))

    def rows(owner):
        return pl.ds(pl.multiple_of(owner * unit, unit), unit)

    def spot(i, owner):
        return rows(owner % 4 if i >= c.flat else owner)

    def link(source, target, i, kind, d, place):
        slot = (i * 4 + kind) * levels + d
        return remote(source, target, r.send_sems.at[slot], r.recv_sems.at[slot], "fsdp", place)

    def begin(group, d):
        for i, grad, lanes, path, _, _ in group:
            link(grad.at[spot(i, flipped(me, 4 * d + 3)), lanes], cross[i].at[d], i, 0, d, near[1 - path]).start()

    def raw(group, d):
        for i, grad, lanes, path, _, _ in group:
            other = 1 - path
            link(grad.at[spot(i, flipped(near[other], 4 * d)), lanes], along[i][other].at[d], i, 1 + other, d, near[other]).start()

    def middle(group, d):
        for i, grad, lanes, path, _, _ in group:
            link(cross[i].at[d], cross[i].at[d], i, 0, d, near[0]).wait_recv()
            own = own_part(i, grad, lanes, flipped(near[path], 4 * d), d)
            cross[i][d] = (own + cross[i][d].astype(F32)).astype(BF)
            link(cross[i].at[d], along[i][path].at[d], i, 1 + path, d, near[path]).start()

    def finish(group, d):
        lowest = d & -d if d else levels
        for i, grad, lanes, path, out, out_lanes in group:
            for axis in range(2):
                link(along[i][axis].at[d], along[i][axis].at[d], i, 1 + axis, d, near[0]).wait_recv()
            own = own_part(i, grad, lanes, flipped(me, 4 * d), levels + d)
            total = own + along[i][0][d].astype(F32) + along[i][1][d].astype(F32)
            bit = 1
            while bit < lowest and i < c.flat:
                slot = d + bit - 1
                link(inbound[i].at[slot], inbound[i].at[slot], i, 3, d + bit, near[0]).wait_recv()
                total = total + inbound[i][slot].astype(F32)
                bit *= 2
            if d:
                along[i][0][d] = total.astype(BF)
                link(along[i][0].at[d], inbound[i].at[d - 1], i, 3, d, far[lowest]).start()
            else:
                out[:, out_lanes] = total

    def quad(d):
        return pl.ds(pl.multiple_of(flipped(me, 4 * d) // 4 * (4 * unit), 4 * unit), 4 * unit)

    def level_own(d):
        return pltpu.make_async_copy(r.grad_level.at[quad(d), :], r.level_sum.at[d // 2], r.level_local.at[d // 2])

    def level_send(source, d):
        place = far[d & -d]
        return remote(source, r.level_in.at[d - 1], r.level_send.at[d - 1], r.level_recv.at[d - 1], "fsdp", place)

    def level_start():
        for d in order:
            if d % 2:
                level_send(r.grad_level.at[quad(d), :], d).start()
            else:
                level_own(d).start()

    def level_pass(d):
        level_own(d).wait()
        total = r.level_sum[d // 2].astype(F32)
        bit, lowest = 1, d & -d if d else levels
        while bit < lowest:
            level_send(r.level_in.at[d + bit - 1], d + bit).wait_recv()
            total = total + r.level_in[d + bit - 1].astype(F32)
            bit *= 2
        if d:
            r.level_sum[d // 2] = total.astype(BF)
            level_send(r.level_sum.at[d // 2], d).start()
        else:
            r.level_done[...] = total.astype(BF)

    weights_copy = pltpu.make_async_copy(r.weights.at[:, 0 : r.held.shape[1]], r.held, r.local_sems.at[0])
    own_rows = r.tokens.shape[0]
    share = lambda owner: pl.ds(pl.multiple_of(owner * own_rows, own_rows), own_rows)
    turned_copy = pltpu.make_async_copy(r.normed_turned, r.turned, r.local_sems.at[2])
    branch_copy = pltpu.make_async_copy(r.branch_low.at[share(core), :], r.branch_own, r.local_sems.at[1])
    inners = TensorSum(c.tensors, r.inner_own, r.inner_in, r.inner_send, r.inner_recv)

    @pl.when(now == 0)
    def _():
        greet([("fsdp", p) for p in near] + [("fsdp", flipped(me, bit)) for bit in bits[2:]] + [("tensor", p) for p in cores])
        level_start()
        for d in order:
            begin(early, d)
        for copy in own_copies():
            copy.start()
        turned_copy.start()
        weights_copy.start()
        branch_copy.start()
        r.dk_acc[...] = jnp.zeros_like(r.dk_acc)
        r.dv_acc[...] = jnp.zeros_like(r.dv_acc)

    block = r.mix_up.shape[0]
    for j in range(blocks):

        @pl.when(now == j)
        def _(j=j):
            for i in range(block // LANES):
                part = slice(i * LANES, (i + 1) * LANES)
                inner = jnp.sum(r.mix_norm[part, :].astype(F32) * r.mix_low[part, :].astype(F32), axis=1, keepdims=True)
                at = 8 * (j * (block // LANES) + i)
                r.inner_rows[at : at + 8, :] = jnp.broadcast_to(inner, (LANES, LANES)).T[0:8, :]
            attention_bwd_block(
                j * block, c.groups, r.feats_all, r.doc_row, r.qrot, r.keys, r.values, r.lse, r.mix_up, r.cos, r.sin, r.qkv_grad,
                r.dk_acc, r.dv_acc,
            )
            if j == blocks - 1:
                inners.begin(r.inner_rows[...], met=True)
                attention_bwd_end(c.groups, r.qrot.shape[1] // LANES, r.cos, r.sin, r.qkv_grad, r.dk_acc, r.dv_acc)

    @pl.when(now == blocks)
    def _():
        r.dxbuf[CHUNK : CHUNK + 8, :] = jnp.zeros((8, r.dxbuf.shape[1]), F32)
        r.dbcbuf[CHUNK : CHUNK + 8, :] = jnp.zeros((8, r.dbcbuf.shape[1]), F32)
        r.dmemory[...] = jnp.zeros_like(r.dmemory)
        r.x_sums[...] = jnp.zeros_like(r.x_sums)
        r.state_sums[...] = jnp.zeros_like(r.state_sums)
        r.head_sums[...] = jnp.zeros_like(r.head_sums)
        r.inner_sum[...] = inners.end()

    @pl.when((now >= blocks) & (now < blocks + chunks))
    def _():
        chunk = chunks - 1 - (now - blocks)
        mamba_bwd_block(
            r.feats, r.square, r.inner_sum, chunk, r.docs, r.x, r.x_before, r.bc, r.bc_before, r.step, r.z, r.scan, r.states,
            r.norm_grad, r.taps, r.staps, r.heads, r.expand, r.reduce, r.gain,
            r.ssm_grad.at[pl.ds(pl.multiple_of(chunk * CHUNK, CHUNK), CHUNK), :], r.x_sums, r.state_sums, r.head_sums,
            r.xbuf, r.bcbuf, r.dxbuf, r.dbcbuf, r.dmemory,
        )

    for k, d in enumerate(order):

        @pl.when(now == blocks + 1 + k)
        def _(d=d):
            if d == order[0]:
                for copy in own_copies():
                    copy.wait()
            middle(early, d)
            raw(early, d)

    base = blocks + chunks
    ssm_wide = r.ssm_grad.shape[1]
    for k, d in enumerate(order):

        @pl.when(now == base + k)
        def _(d=d):
            quad = pl.ds(pl.multiple_of(flipped(me, 4 * d) // 4 * (4 * unit), 4 * unit), 4 * unit)
            if d == order[0]:
                turned_copy.wait()
            turned = r.turned[quad, :]
            r.grad_first[quad, :ssm_wide] = jnp.dot(turned, r.ssm_grad[...], preferred_element_type=F32).astype(BF)
            r.grad_first[quad, ssm_wide:] = jnp.dot(turned, r.qkv_grad[...], preferred_element_type=F32).astype(BF)
            begin(late, d)
            raw(late, d)

    base = base + levels

    @pl.when(now == base)
    def _():
        weights_copy.wait()

    @pl.when((now >= base) & (now < base + tiles))
    def _():
        part = pl.ds(pl.multiple_of((now - base) * c.tile, c.tile), c.tile)
        r.normed_part[part, :] = (
            mm_nt(r.ssm_grad[part, :], r.held[:, :ssm_wide]) + mm_nt(r.qkv_grad[part, :], r.held[:, ssm_wide:])
        ).astype(BF)

    def normed_copies():
        return [
            remote(r.normed_part.at[share(place), :], r.normed_in.at[k], r.core_send.at[k], r.core_recv.at[k], "tensor", place)
            for k, place in enumerate(cores)
        ]

    for k, step in enumerate((base - levels + 1, base + 1)):

        @pl.when(now == step)
        def _(d=order[k]):
            finish(early, d)

    for k, d in enumerate([d for d in order if d % 2 == 0]):

        @pl.when(now == c.level_steps[k])
        def _(d=d):
            level_pass(d)
            if d == 0:
                begin(flat, 0)
                raw(flat, 0)

    settled = []

    def stage_copy(k):
        axis, place = stages[k]
        return remote(r.sums.at[k], r.sums_in.at[k], r.sum_send.at[k], r.sum_recv.at[k], axis, place)

    def next_stage():
        k = len(settled)
        if k < len(stages):
            stage_copy(k).wait()
            r.sums[k + 1] = r.sums[k] + r.sums_in[k]
            settled.append(k)
            if k + 1 < len(stages):
                stage_copy(k + 1).start()

    @pl.when(now == base + tiles)
    def _():
        for copy in normed_copies():
            copy.start()
        for copy in normed_copies():
            copy.wait()
        branch_copy.wait()
        r.gain_sum[...] = jnp.zeros_like(r.gain_sum)
        size = min(CHUNK, own_rows)

        def first_norm_back(i, carry):
            part = pl.ds(pl.multiple_of(i * size, size), size)
            whole = pl.ds(pl.multiple_of(core * own_rows + i * size, size), size)
            grad = r.normed_part[whole, :].astype(F32)
            for k in range(len(cores)):
                grad = grad + r.normed_in[k, part, :].astype(F32)
            scale = r.scale[whole, :]
            shape = r.tokens[part, :].astype(F32) * scale
            weighted = grad * r.input_gain[...]
            inner = jnp.mean(weighted * shape, axis=1, keepdims=True)
            r.input_grad[part, :] = r.branch_own[part, :].astype(F32) + scale * (weighted - shape * inner)
            r.gain_sum[0:1, :] += jnp.sum(grad * shape, axis=0, keepdims=True)
            return carry

        lax.fori_loop(0, own_rows // size, first_norm_back, 0)
        at = 0
        for ref in (r.x_sums, r.head_sums, r.state_sums):
            r.sums[0, :, at : at + ref.shape[1]] = ref[...]
            at += ref.shape[1]
        eighth = r.gain_sum.shape[1] // 8
        for ref, factor in ((r.second_part, 1.0 / c.tensors), (r.gain_sum, 1.0)):
            for k in range(8):
                r.sums[0, k : k + 1, at : at + eighth] = ref[0:1, k * eighth : (k + 1) * eighth] * factor
            at += eighth
        stage_copy(0).start()
        for d in order[2:]:
            finish(early, d)
            next_stage()
        middle(flat, 0)
        for d in order:
            middle(late, d)
        for d in order:
            finish(late, d)
            next_stage()
        finish(flat, 0)
        while len(settled) < len(stages):
            next_stage()
        r.small_out[:, : c.split] = r.sums[len(bits), :, : c.split]
        r.small_out[:, c.split :] = r.sums[len(stages), :, c.split :]
        states2 = c.state_at[1] - c.state_at[0]
        wide_shared = r.shared.shape[2]
        leading = core * (wide_shared - states2) // (c.tensors * LANES)
        r.shared[0, :, :states2] = r.out_first[:, c.state_at[0] : c.state_at[1]]
        for g in range((wide_shared - states2) // LANES):
            value = jnp.zeros((unit, LANES), F32)
            for j in range(c.groups):
                value = jnp.where(leading + j == g, r.out_first[:, c.kv_at + j * LANES : c.kv_at + (j + 1) * LANES], value)
            r.shared[0, :, states2 + g * LANES : states2 + (g + 1) * LANES] = value
        for k, (axis, place) in enumerate(halves):
            copy = remote(r.shared.at[k], r.shared_in.at[k], r.half_send.at[k], r.half_recv.at[k], axis, place)
            copy.start()
            copy.wait()
            r.shared[k + 1] = r.shared[k] + r.shared_in[k]
        r.shared_out[...] = r.shared[len(halves)]
        for d in order[:-1]:
            level_send(r.level_in.at[d - 1], d).wait_send()
        for i in range(len(pieces)):
            for d in range(levels):
                for kind in range(4):
                    if (kind < 3 or d) and (i < c.flat or kind < 3 and d == 0):
                        link(cross[i].at[d], cross[i].at[d], i, kind, d, near[0]).wait_send()


def backward(
    groups, feats, doc_row, qrot, keys, values, lse, mix_grad, mix, cos, sin, squares, ssm_in, scan, states, taps, staps, heads, gain,
    grad_gate_up, grad_down, grad_mix, normed_turned, first, branch_low, tokens, scale, input_gain, second_part, width, states2,
    count, tensors, collective_id,
):
    total, hidden = branch_low.shape
    own_rows = tokens.shape[0]
    unit = hidden // count
    levels = count // 4
    query_wide, kv_wide = qrot.shape[1], keys.shape[1]
    block, tile = min(QBLOCK, total), min(QBLOCK, total)
    blocks, chunks, tiles = total // block, total // CHUNK, total // tile
    ssm_wide, qkv_wide = 2 * width + states2 + LANES, query_wide + kv_wide
    chunk = lambda s: jnp.clip(chunks - 1 - (s - blocks), 0, chunks - 1)
    query = lambda s: jnp.minimum(s, blocks - 1)
    by_chunk = lambda w, place=0: spec((CHUNK, w), lambda s: (chunk(s), place))
    by_query = lambda w, place=0: spec((block, w), lambda s: (query(s), place))
    before = lambda w, place=0: spec((8, w), lambda s: (jnp.maximum(chunk(s) * (CHUNK // 8) - 1, 0), place))
    whole = lambda a: pl.BlockSpec(a.shape, lambda s: (0,) * a.ndim, pipeline_mode=pl.Buffered(1))
    anywhere = pl.BlockSpec(memory_space=pl.ANY)
    vmem = pl.BlockSpec(memory_space=pltpu.VMEM)
    expand = expand_matrix(width)
    reduce = np.concatenate([expand[:LANES].T] * 2, axis=0)
    state_place, step_place = 2 * width // states2, (2 * width + states2) // LANES
    ins = dict(
        feats_all=(feats, whole(feats)), doc_row=(doc_row, whole(doc_row)), qrot=(qrot, whole(qrot)), keys=(keys, whole(keys)),
        values=(values, whole(values)), lse=(lse, by_query(LANES)), mix_up=(mix_grad, by_query(query_wide, width // query_wide)),
        mix_norm=(mix_grad, by_query(width)), mix_low=(mix, by_query(width)), cos=(cos, whole(cos)), sin=(sin, whole(sin)),
        feats=(feats, by_chunk(LANES)), docs=(doc_row, spec((1, CHUNK), lambda s: (0, chunk(s)))),
        square=(squares, spec((8, LANES), lambda s: (chunk(s), 0))), x=(ssm_in, by_chunk(width, 1)),
        x_before=(ssm_in, before(width, 1)), bc=(ssm_in, by_chunk(states2, state_place)),
        bc_before=(ssm_in, before(states2, state_place)), step=(ssm_in, by_chunk(LANES, step_place)),
        z=(ssm_in, by_chunk(width)), scan=(scan, by_chunk(width)),
        states=(states, spec((1, states2 // 2, width), lambda s: (chunk(s), 0, 0))), norm_grad=(mix_grad, by_chunk(width)),
        taps=(taps, whole(taps)), staps=(staps, whole(staps)), heads=(heads, whole(heads)), expand=(expand, whole(expand)),
        reduce=(reduce, whole(reduce)), gain=(gain, whole(gain)), grad_gate_up=(grad_gate_up, anywhere),
        grad_level=(grad_down, anywhere), grad_mix=(grad_mix, anywhere),
        normed_turned=(normed_turned, anywhere), weights=(first, anywhere), branch_low=(branch_low, anywhere),
        tokens=(tokens, whole(tokens)), scale=(scale, whole(scale)), input_gain=(input_gain, whole(input_gain)),
        second_part=(second_part, whole(second_part)),
    )
    small = width + LANES + states2 + 2 * (hidden // 8)
    shared = states2 + KEYVAL_HEADS * LANES
    outs = dict(
        input_grad=(own_rows, hidden), out_gate_up=(unit, grad_gate_up.shape[1]), out_down=(unit, grad_down.shape[1]),
        out_mix=(unit, grad_mix.shape[1]), out_first=(unit, ssm_wide + qkv_wide), small_out=(8, small),
        shared_out=(unit, shared),
    )
    cut = (ssm_wide + qkv_wide) // (2 * LANES) * LANES
    ffn = grad_down.shape[1]
    split_at, most = ffn // (2 * LANES) * LANES, 3 * ffn // (2 * LANES) * LANES
    every = lambda a: slice(0, a)
    pieces = [
        ("grad_gate_up", slice(0, most), 0, "out_gate_up", slice(0, most)),
        ("grad_gate_up", slice(most, 2 * ffn), 1, "out_gate_up", slice(most, 2 * ffn)),
        ("grad_mix", every(grad_mix.shape[1]), 1, "out_mix", every(grad_mix.shape[1])),
        ("grad_first", slice(0, cut), 0, "out_first", slice(0, cut)),
        ("grad_first", slice(cut, ssm_wide + qkv_wide), 1, "out_first", slice(cut, ssm_wide + qkv_wide)),
        ("level_done", slice(0, split_at), 0, "out_down", slice(0, split_at)),
        ("level_done", slice(split_at, ffn), 1, "out_down", slice(split_at, ffn)),
    ]
    steps, stages = (tensors - 1).bit_length(), (count - 1).bit_length() + (tensors - 1).bit_length()
    inner = (total // 16, LANES)
    f32 = lambda *dims: pltpu.VMEM(dims, F32)
    low = lambda *dims: pltpu.VMEM(dims, BF)
    dma = lambda n: pltpu.SemaphoreType.DMA((n,))
    scratch = dict(
        dk_acc=f32(total, kv_wide), dv_acc=f32(total, kv_wide), qkv_grad=low(total, qkv_wide), inner_rows=f32(*inner),
        inner_sum=f32(*inner), inner_own=f32(steps + 1, *inner), inner_in=f32(steps, *inner), inner_send=dma(steps),
        inner_recv=dma(steps), xbuf=f32(CHUNK + 8, width), bcbuf=f32(CHUNK + 8, states2), dxbuf=f32(CHUNK + 8, width),
        dbcbuf=f32(CHUNK + 8, states2), dmemory=f32(states2 // 2, width), ssm_grad=low(total, ssm_wide),
        x_sums=f32(8, width), state_sums=f32(8, states2), head_sums=f32(8, LANES),
        held=low(hidden, ssm_wide + qkv_wide), grad_first=low(hidden, ssm_wide + qkv_wide), branch_own=low(own_rows, hidden),
        normed_part=low(total, hidden), normed_in=low(tensors - 1, own_rows, hidden), gain_sum=f32(8, hidden),
        sums=f32(stages + 1, 8, small), sums_in=f32(stages, 8, small), sum_send=dma(stages), sum_recv=dma(stages),
        shared=f32(steps + 1, unit, shared), shared_in=f32(steps, unit, shared), half_send=dma(steps),
        half_recv=dma(steps), core_send=dma(tensors - 1), core_recv=dma(tensors - 1), local_sems=dma(3), turned=low(hidden, total),
        own_sems=pltpu.SemaphoreType.DMA((3, 2 * levels)),
        level_in=low(levels - 1, 4 * unit, ffn), level_sum=low(levels // 2, 4 * unit, ffn), level_done=low(4 * unit, ffn),
        level_send=dma(levels - 1), level_recv=dma(levels - 1), level_local=dma(levels // 2),
        send_sems=dma(4 * levels * len(pieces)), recv_sems=dma(4 * levels * len(pieces)),
    )
    for i, piece in enumerate(pieces):
        columns = piece[1].stop - piece[1].start
        scratch.update({
            "cross%d" % i: low(levels, unit, columns), "along_x%d" % i: low(levels, unit, columns),
            "along_y%d" % i: low(levels, unit, columns), "inbound%d" % i: low(levels - 1, unit, columns),
        })
        if i < 3:
            scratch["own%d" % i] = low(2 * levels, unit, columns)
    names = list(ins) + list(outs) + list(scratch)
    odd = levels // 2
    level_steps = [blocks + chunks * (k + 1) // odd - (k + 1 < odd) for k in range(odd)]
    c = types.SimpleNamespace(
        names=names, pieces=pieces, early=3, flat=5, level_steps=level_steps, count=count, tensors=tensors, unit=unit, blocks=blocks, chunks=chunks, tiles=tiles, tile=tile,
        groups=groups, split=width + LANES, state_at=(2 * width, 2 * width + states2), kv_at=ssm_wide + query_wide,
    )
    return pl.pallas_call(
        functools.partial(backward_kernel, c),
        grid=(blocks + chunks + levels + tiles + 1,),
        in_specs=[v[1] for v in ins.values()],
        out_specs=[vmem] * len(outs),
        out_shape=[jax.ShapeDtypeStruct(v, F32) for v in outs.values()],
        scratch_shapes=list(scratch.values()),
        compiler_params=pltpu.CompilerParams(collective_id=collective_id, has_side_effects=True, vmem_limit_bytes=VMEM_ALL),
        name="backward",
    )(*(v[0] for v in ins.values()))


def tensor_swap(values):
    return lax.ppermute(values, "tensor", [(0, 1), (1, 0)])


def tensor_pair(values):
    if lax.axis_size("tensor") == 2:
        return values, tensor_swap(values)
    return lax.psum(values.astype(F32), "tensor").astype(values.dtype), jnp.zeros_like(values)


def pad_to(values, size, axis=-1):
    pads = [(0, 0)] * values.ndim
    pads[axis] = (0, size - values.shape[axis])
    return jnp.pad(values, pads) if size > values.shape[axis] else values


def pack_kernel(
    mixer_ref, state_ref, step_ref, query_ref, keyval_ref, proj_ref, attention_ref, gate_up_ref, down_ref,
    first_ref, second_ref,
):
    unit = state_ref.shape[0]
    width, wide = mixer_ref.shape[2], -(-mixer_ref.shape[2] // LANES) * LANES
    same = (iota2((unit, unit), 0) == iota2((unit, unit), 1)).astype(BF)
    place = 0

    def put(out_ref, value, size):
        nonlocal place
        value = value.astype(BF)
        if size > value.shape[1]:
            value = jnp.concatenate([value, jnp.zeros((unit, size - value.shape[1]), BF)], axis=1)
        out_ref[:, place : place + size] = value
        place += size

    put(first_ref, mixer_ref[:, 0, :], wide)
    put(first_ref, mixer_ref[:, 1, :], wide)
    put(first_ref, state_ref[...], state_ref.shape[1])
    put(first_ref, lax.dot_general(same, step_ref[...].astype(BF), (((1,), (1,)), ((), ())), preferred_element_type=F32), LANES)
    query_wide = -(-query_ref.shape[1] // LANES) * LANES
    put(first_ref, query_ref[...], query_wide)
    put(first_ref, keyval_ref[...], keyval_ref.shape[1])
    put(first_ref, proj_ref[...], wide)
    put(first_ref, attention_ref[...], query_wide)
    place = 0
    put(second_ref, gate_up_ref[:, 0, :], gate_up_ref.shape[2])
    put(second_ref, gate_up_ref[:, 1, :], gate_up_ref.shape[2])
    put(second_ref, down_ref[...], down_ref.shape[1])


def pack_weights(mixer, state, step, query, keyval, proj, attention, gate_up, down):
    unit = state.shape[0]
    lanes = lambda size: -(-size // LANES) * LANES
    first = 3 * lanes(mixer.shape[2]) + state.shape[1] + LANES + 2 * lanes(query.shape[1]) + keyval.shape[1]
    second = 2 * gate_up.shape[2] + down.shape[1]
    whole = lambda shape: spec(shape, lambda i: (0,) * len(shape))
    weights = (mixer, state, step, query, keyval, proj, attention, gate_up, down)
    return pl.pallas_call(
        pack_kernel,
        grid=(1,),
        in_specs=[whole(v.shape) for v in weights],
        out_specs=[whole((unit, first)), whole((unit, second))],
        out_shape=[jax.ShapeDtypeStruct((unit, first), BF), jax.ShapeDtypeStruct((unit, second), BF)],
        compiler_params=pltpu.CompilerParams(vmem_limit_bytes=VMEM_WHOLE),
        name="pack_weights",
    )(*weights)


def table_kernel(
    docs_ref, conv_ref, conv_bias_ref, state_conv_ref, state_bias_ref, step_bias_ref, decay_ref, skip_ref,
    feats_ref, cos_ref, sin_ref, taps_ref, state_taps_ref, heads_ref,
):
    total = docs_ref.shape[1]
    docs = docs_ref[...]
    tall = jnp.broadcast_to(docs, (LANES, total)).T
    spot = iota2((1, total), 1)
    begin = jnp.sum((tall[:, 0:1] < docs).astype(F32), axis=0, keepdims=True)
    rows = [docs]
    eight = jnp.broadcast_to(docs, (8, total))
    for k in (1, 2, 3):
        rows.append(jnp.where(spot >= k, (pltpu.roll(eight, k, 1)[0:1] == docs).astype(F32), 0.0))
    blocks = [docs[:, i : i + CHUNK] for i in range(0, total, CHUNK)]
    before = [jnp.full((1, 1), -1.0, F32)] + [v[:, CHUNK - 1 :] for v in blocks[:-1]]
    rows.append(jnp.concatenate([(v == w).astype(F32) for v, w in zip(blocks, before)], axis=1))
    rows.append(jnp.concatenate([(v == v[:, CHUNK - 1 :]).astype(F32) for v in blocks], axis=1))
    for k in (1, 2, 3):
        rows.append(jnp.where(spot < total - k, (pltpu.roll(eight, total - k, 1)[0:1] == docs).astype(F32), 0.0))
    rows.append(spot.astype(F32) - begin)
    rows.append(jnp.zeros((LANES - len(rows), total), F32))
    feats = jnp.concatenate(rows, axis=0).T
    feats_ref[...] = feats
    lane = iota2((1, LANES), 1)
    rates = jnp.exp((lane % (HEAD_SIZE // 2)).astype(F32) * (-2.0 * math.log(THETA) / HEAD_SIZE))
    angles = feats[:, 9:10] * rates
    cos_ref[...] = jnp.cos(angles)
    sin_ref[...] = jnp.sin(angles) * jnp.where(lane % HEAD_SIZE < HEAD_SIZE // 2, -1.0, 1.0)
    width, heads = conv_ref.shape[1], skip_ref.shape[1]
    taps_ref[...] = jnp.zeros_like(taps_ref)
    taps_ref[0:4, :width] = conv_ref[...]
    taps_ref[4:5, :width] = conv_bias_ref[...]
    spread = (iota2((heads, width), 0) == iota2((heads, width), 1) // (width // heads)).astype(F32)
    taps_ref[5:6, :width] = exact_mm(jnp.broadcast_to(skip_ref[...], (8, heads)), spread)[0:1]
    state_taps_ref[...] = jnp.zeros_like(state_taps_ref)
    state_taps_ref[0:4, :] = state_conv_ref[...]
    state_taps_ref[4:5, :] = state_bias_ref[...]
    heads_ref[...] = jnp.zeros_like(heads_ref)
    heads_ref[0:1, :heads] = step_bias_ref[...]
    heads_ref[1:2, :heads] = -jnp.exp(decay_ref[...])


def second_norm_kernel(tokens_ref, part_ref, part_in_ref, gain_ref, middle_ref, second_ref, scale_ref):
    middle = tokens_ref[...].astype(F32) + part_ref[...].astype(F32) + part_in_ref[...].astype(F32)
    scale = lax.rsqrt(jnp.mean(middle * middle, axis=1, keepdims=True) + EPS)
    middle_ref[...] = middle
    scale_ref[...] = scale
    second_ref[...] = (middle * scale * gain_ref[...]).astype(BF)


def by_rows(kernel, name, rows, count, ins, outs, scalars=(), tensors=1, limit=VMEM_LIMIT):
    number = len(scalars)

    def place(shape, kind):
        if kind == "whole":
            return spec(shape, lambda i, *s: (0,) * len(shape))
        if kind == "own":
            own = shape[0] // rows if shape[0] < rows * count else count // tensors
            if shape[0] < rows * count:
                return spec((rows, shape[1]), lambda i, *s: (jnp.clip(i - s[0][0] * own, 0, own - 1), 0))
            return spec((rows, shape[1]), lambda i, *s: (jnp.clip(i, s[0][0] * own, s[0][0] * own + own - 1), 0))
        return spec((rows, shape[1]), lambda i, *s: (i, 0))

    return pl.pallas_call(
        kernel,
        grid_spec=pltpu.PrefetchScalarGridSpec(
            num_scalar_prefetch=number,
            grid=(count,),
            in_specs=[place(v.shape, kind) for v, kind in ins],
            out_specs=[place((r, c), kind) for r, c, _, kind in outs],
        ),
        out_shape=[jax.ShapeDtypeStruct((r, c), dtype) for r, c, dtype, _ in outs],
        compiler_params=pltpu.CompilerParams(vmem_limit_bytes=limit),
        name=name,
    )(*scalars, *(v for v, _ in ins))


def ffn_kernel(second_ref, up_ref, weights_ref, active_ref, grads_ref, out_ref, back_ref):
    ffn = active_ref.shape[1]
    gate_vals = jnp.dot(second_ref[...], weights_ref[:, : 2 * ffn], preferred_element_type=F32)
    active_grad = jnp.dot(up_ref[...], weights_ref[:, 2 * ffn :], preferred_element_type=F32)
    gate, up = gate_vals[:, :ffn], gate_vals[:, ffn:]
    sig = sigmoid(gate)
    silu = gate * sig
    active = (silu * up).astype(BF)
    active_ref[...] = active
    grads_ref[:, :ffn] = (active_grad * up * (sig + silu * (1.0 - sig))).astype(BF)
    grads_ref[:, ffn:] = (active_grad * silu).astype(BF)
    out_ref[...] = mm_nt(active, weights_ref[:, 2 * ffn :]).astype(BF)
    back_ref[...] = mm_nt(grads_ref[...], weights_ref[:, : 2 * ffn]).astype(BF)


def second_back_kernel(
    own_count, core_ref, grad_ref, grad_in_ref, middle_ref, scale_ref, up_ref, gain_ref, part_ref, part_in_ref, low_ref, gain_grad_ref, out_ref
):
    offset = pl.program_id(0) - core_ref[0] * own_count

    @pl.when(pl.program_id(0) == 0)
    def _():
        gain_grad_ref[...] = jnp.zeros_like(gain_grad_ref)

    grad = grad_ref[...].astype(F32) + grad_in_ref[...].astype(F32)
    middle, scale = middle_ref[...], scale_ref[...]
    shape = middle * scale
    weighted = grad * gain_ref[...]
    inner = jnp.mean(weighted * shape, axis=1, keepdims=True)
    low_ref[...] = (up_ref[...].astype(F32) + scale * (weighted - shape * inner)).astype(BF)
    gain_grad_ref[0:1, :] += jnp.sum(grad * shape, axis=0, keepdims=True)

    @pl.when((offset >= 0) & (offset < own_count))
    def _():
        out_ref[...] = (middle + part_ref[...].astype(F32) + part_in_ref[...].astype(F32)).astype(BF)


def finish_kernel(
    sizes, first_ref, mix_ref, shared_ref, small_ref, gate_up_sum_ref, down_sum_ref, input_grad_ref,
    mixer_ref, state_ref, step_ref, conv_ref, conv_bias_ref, state_conv_ref, state_bias_ref, step_bias_ref, decay_ref, skip_ref,
    mixer_gain_ref, proj_ref, query_ref, keyval_ref, attention_ref, gate_up_ref, down_ref, second_gain_ref, input_gain_ref, input_back_ref,
):
    wide, width, states2, heads, query_width, ffn = sizes
    input_back_ref[...] = input_grad_ref[...]
    mixer_ref[:, 0, :] = first_ref[:, :width]
    mixer_ref[:, 1, :] = first_ref[:, wide : wide + width]
    state_ref[...] = shared_ref[:, :states2]
    start = 2 * wide + states2
    step_ref[...] = first_ref[:, start : start + LANES].T[:heads, :]
    start = 2 * wide + states2 + LANES
    query_ref[...] = first_ref[:, start : start + query_width]
    groups = [shared_ref[:, i : i + LANES] for i in range(states2, shared_ref.shape[1], LANES)]
    keyval_ref[:, 0, :] = jnp.concatenate([v[:, :HEAD_SIZE] for v in groups], axis=1)
    keyval_ref[:, 1, :] = jnp.concatenate([v[:, HEAD_SIZE:] for v in groups], axis=1)
    proj_ref[...] = mix_ref[:, :width]
    attention_ref[...] = mix_ref[:, wide : wide + query_width]
    gate_up_ref[:, 0, :] = gate_up_sum_ref[:, :ffn]
    gate_up_ref[:, 1, :] = gate_up_sum_ref[:, ffn:]
    down_ref[...] = down_sum_ref[...]
    conv_ref[...] = small_ref[0:4, :width]
    for out_ref, row in ((conv_bias_ref, 4), (mixer_gain_ref, 6)):
        for k in range(out_ref.shape[0]):
            size = out_ref.shape[1]
            out_ref[k : k + 1, :] = small_ref[row : row + 1, k * size : (k + 1) * size]
    place = iota2((width, heads), 0) // (width // heads)
    gather = (place == iota2((width, heads), 1)).astype(F32)
    skip_ref[...] = exact_mm(jnp.broadcast_to(small_ref[5:6, :width], (8, width)), gather)[0:1]
    step_bias_ref[...] = small_ref[0:1, wide : wide + heads]
    decay_ref[...] = small_ref[1:2, wide : wide + heads]
    base = wide + LANES
    state_conv_ref[...] = small_ref[0:4, base : base + states2]
    state_bias_ref[...] = small_ref[4:5, base : base + states2]
    base += states2
    for out_ref in (second_gain_ref, input_gain_ref):
        out_ref[...] = small_ref[:, base : base + out_ref.shape[1]]
        base += out_ref.shape[1]


def body(
    layer_input, doc_ids, input_gain, mixer_weight, state_weight, step_weight, conv_weight, conv_bias, state_conv,
    state_conv_bias, step_bias, decay_log, skip_gain, mixer_gain, mixer_proj, query_weight, keyval_projection,
    attention_proj, second_gain, gate_up, down_proj, cotangent,
):
    tensor_count = lax.axis_size("tensor")
    tensor_index = lax.axis_index("tensor")
    fsdp_count = lax.axis_size("fsdp")
    own_rows, hidden = layer_input.shape
    unit = state_weight.shape[0]
    seq_count, seq_length = doc_ids.shape
    total = seq_count * seq_length
    heads = step_bias.shape[0]
    width = conv_weight.shape[1]
    wide = -(-width // LANES) * LANES
    query_width = query_weight.shape[1]
    query_wide = -(-query_width // LANES) * LANES
    query_heads = query_width // HEAD_SIZE
    per_group = QUERY_HEADS // KEYVAL_HEADS
    kv_heads = max(1, query_heads // per_group)
    kv_leading = tensor_index * query_heads // per_group
    states2 = state_weight.shape[1]
    ffn = down_proj.shape[0]
    low = lambda v: v.astype(BF)

    own_keyval = lax.dynamic_slice_in_dim(keyval_projection, kv_leading * HEAD_SIZE, kv_heads * HEAD_SIZE, 2)
    own_keyval = own_keyval.reshape(unit, 2, kv_heads, HEAD_SIZE).transpose(0, 2, 1, 3).reshape(unit, 2 * kv_heads * HEAD_SIZE)
    kv_wide = 2 * kv_heads * HEAD_SIZE
    first, rest = pack_weights(
        mixer_weight, state_weight, step_weight.T, query_weight, own_keyval, mixer_proj.T, attention_proj.T, gate_up, down_proj.T
    )
    rest = lax.all_gather(rest, "fsdp", axis=0, tiled=True)
    docs = (doc_ids + jnp.arange(seq_count, dtype=jnp.int32)[:, None] * seq_length).reshape(1, total)
    doc_row = docs.astype(F32)
    tables = (
        doc_row, conv_weight, conv_bias[None], state_conv, state_conv_bias[None], step_bias[None], decay_log[None], skip_gain[None]
    )
    first, tokens, upstream, normed, first_scale, normed_turned, feats, cos, sin, taps, state_taps, head_rows = gather_weights(
        first, layer_input, cotangent, input_gain[None], tables, wide, fsdp_count, tensor_count, 0
    )
    ssm_wide = 2 * wide + states2 + LANES
    cuts = np.cumsum([0, ssm_wide, query_wide + kv_wide, wide + query_wide])
    full_ssm, full_qkv, full_mix = (first[:, cuts[i] : cuts[i + 1]] for i in range(3))
    gain_row = pad_to(mixer_gain[None], wide)
    second_row = second_gain[None]

    ssm_in = plain_dot(normed, full_ssm)
    qkv_in = plain_dot(normed, full_qkv)
    scan, gated_low, squares, states = mamba_forward(feats, doc_row, ssm_in, taps, state_taps, head_rows, gain_row, wide, states2)
    mix, log_sums, query_rot, keys, values, squares = attention_forward(
        kv_heads, tensor_count, feats, doc_row, qkv_in, cos, sin, query_wide, gated_low, squares, 2
    )
    branch = tensor_pair(low(right_dot(mix, full_mix)))
    middle, second, second_scale = by_rows(
        second_norm_kernel, "second_norm", CHUNK, total // CHUNK,
        [(tokens, "rows"), (branch[0], "rows"), (branch[1], "rows"), (second_row, "whole")],
        [(total, hidden, F32, "rows"), (total, hidden, BF, "rows"), (total, 1, F32, "rows")],
    )
    active, gu_grad, ffn_out, second_grad = by_rows(
        ffn_kernel, "ffn", min(FFN_ROWS, total), max(total // FFN_ROWS, 1),
        [(second, "rows"), (upstream, "rows"), (rest, "whole")],
        [(total, ffn, BF, "rows"), (total, 2 * ffn, BF, "rows"), (total, hidden, BF, "rows"), (total, hidden, BF, "rows")],
        limit=VMEM_WHOLE,
    )
    second_grad, ffn_out = tensor_pair(second_grad), tensor_pair(ffn_out)
    grad_gate_up, grad_down = low(left_dot(second, gu_grad)), low(left_dot(upstream, active))
    core = jnp.full((1,), tensor_index, jnp.int32)
    rows = min(CHUNK, own_rows)
    branch_low, second_gain_part, layer_output = by_rows(
        functools.partial(second_back_kernel, own_rows // rows), "second_back", rows, total // rows,
        [
            (second_grad[0], "rows"), (second_grad[1], "rows"), (middle, "rows"), (second_scale, "rows"), (upstream, "rows"),
            (second_row, "whole"), (ffn_out[0], "own"), (ffn_out[1], "own"),
        ],
        [(total, hidden, BF, "rows"), (8, hidden, F32, "whole"), (own_rows, hidden, BF, "own")], (core,), tensor_count,
    )
    mix_grad = low(plain_dot(branch_low, full_mix))
    grad_mix = low(left_dot(branch_low, mix))
    input_back, sum_gate_up, sum_down, sum_mix, sum_first, small, shared = backward(
        kv_heads, feats, doc_row, query_rot, keys, values, log_sums, mix_grad, mix, cos, sin, squares, ssm_in, scan, states, taps,
        state_taps, head_rows, gain_row, grad_gate_up, grad_down, grad_mix, normed_turned, first, branch_low, layer_input, first_scale,
        input_gain[None], second_gain_part, wide, states2, fsdp_count, tensor_count, 1,
    )
    shape = lambda *dims: jax.ShapeDtypeStruct(dims, F32)
    folded = (width // LANES, LANES) if width % LANES == 0 else (1, width)
    parts = (sum_first, sum_mix, shared, small, sum_gate_up, sum_down, input_back)
    done = pl.pallas_call(
        functools.partial(finish_kernel, (wide, width, states2, heads, query_width, ffn)),
        grid=(1,),
        in_specs=[spec(v.shape, lambda i: (0,) * 2) for v in parts],
        out_shape=[
            shape(unit, 2, width), shape(unit, states2), shape(heads, unit), shape(4, width), shape(*folded), shape(4, states2),
            shape(1, states2), shape(1, heads), shape(1, heads), shape(1, heads), shape(*folded), shape(unit, width),
            shape(unit, query_width), shape(unit, 2, KEYVAL_HEADS * HEAD_SIZE), shape(unit, query_width), shape(unit, 2, ffn),
            shape(unit, ffn), shape(8, hidden // 8), shape(8, hidden // 8), shape(own_rows, hidden),
        ],
        compiler_params=pltpu.CompilerParams(vmem_limit_bytes=VMEM_WHOLE),
        name="finish",
    )(*parts)
    (
        mixer_sum, state_sum, step_sum, conv_sum, conv_bias_sum, state_conv_sum, state_bias_sum, step_bias_sum, decay_sum, skip_sum,
        mixer_gain_sum, proj_sum, query_sum, keyval_sum, attention_sum, gate_up_sum, down_sum, second_gain_sum, input_gain_sum, input_grad,
    ) = done
    return (
        layer_output, input_grad, input_gain_sum.reshape(hidden), mixer_sum, state_sum, step_sum.T, conv_sum, conv_bias_sum.reshape(width), state_conv_sum,
        state_bias_sum[0], step_bias_sum[0], decay_sum[0], skip_sum[0], mixer_gain_sum.reshape(width), proj_sum.T, query_sum, keyval_sum,
        attention_sum.T, second_gain_sum.reshape(hidden), gate_up_sum, down_sum.T,
    )


def solution(mesh):
    placed = (
        P(("fsdp", "tensor"), None),
        P("fsdp", None),
        P(),
        P("fsdp", None, "tensor"),
        P("fsdp", None),
        P("fsdp", "tensor"),
        P(None, "tensor"),
        P("tensor"),
        P(),
        P(),
        P("tensor"),
        P("tensor"),
        P("tensor"),
        P("tensor"),
        P("tensor", "fsdp"),
        P("fsdp", "tensor"),
        P("fsdp", None, None),
        P("tensor", "fsdp"),
        P(),
        P("fsdp", None, "tensor"),
        P("tensor", "fsdp"),
        P(("fsdp", "tensor"), None),
    )
    return jax.shard_map(
        body,
        mesh=mesh,
        in_specs=placed,
        out_specs=(
            P(("fsdp", "tensor"), None),
            P(("fsdp", "tensor"), None),
            P(),
            P("fsdp", None, "tensor"),
            P("fsdp", None),
            P("fsdp", "tensor"),
            P(None, "tensor"),
            P("tensor"),
            P(),
            P(),
            P("tensor"),
            P("tensor"),
            P("tensor"),
            P("tensor"),
            P("tensor", "fsdp"),
            P("fsdp", "tensor"),
            P("fsdp", None, None),
            P("tensor", "fsdp"),
            P(),
            P("fsdp", None, "tensor"),
            P("tensor", "fsdp"),
        ),
        check_vma=False,
    )
```

```python
import functools
import math
import types

import jax
import jax.numpy as jnp
import ml_dtypes
import numpy as np
from jax import lax
from jax.experimental import pallas as pl
from jax.experimental.pallas import tpu as pltpu
from jax.sharding import PartitionSpec as P

QUERY_HEADS = 8
KEYVAL_HEADS = 2
HEAD_SIZE = 64
DSSM = 1536
EPS = 1e-05
THETA = 100000000000.0

LANES = 128
CHUNK = 128
FFN_ROWS = 256
QBLOCK = 256
VMEM_LIMIT = 32 * 2**20
VMEM_WHOLE = 60 * 2**20
VMEM_ALL = 63 * 2**20
MASKED = -1e30
BF, F32 = jnp.bfloat16, jnp.float32


def left_dot(left_side, right_side):
    return lax.dot_general(left_side, right_side, (((0,), (0,)), ((), ())), preferred_element_type=F32)


def right_dot(left_side, right_side):
    return lax.dot_general(left_side, right_side, (((1,), (1,)), ((), ())), preferred_element_type=F32)


def plain_dot(left_side, right_side):
    return jnp.dot(left_side, right_side, preferred_element_type=F32)


def mm(a, b):
    return jnp.dot(a.astype(BF), b.astype(BF), preferred_element_type=F32)


def mm_nt(a, b):
    return lax.dot_general(a.astype(BF), b.astype(BF), (((1,), (1,)), ((), ())), preferred_element_type=F32)


def mm_tn(a, b):
    return lax.dot_general(a.astype(BF), b.astype(BF), (((0,), (0,)), ((), ())), preferred_element_type=F32)


def exact_mm(a, b):
    return jnp.dot(a, b, precision=lax.Precision.HIGHEST, preferred_element_type=F32)


def sigmoid(v):
    return 1.0 / (1.0 + jnp.exp(-v))


def softplus(v):
    return jnp.maximum(v, 0.0) + jnp.log1p(jnp.exp(-jnp.abs(v)))


def split_lanes(values, axis):
    high = values.astype(BF)
    low = (values - high.astype(F32)).astype(BF)
    return jnp.concatenate([high, low], axis=axis)


def iota2(shape, axis):
    return lax.broadcasted_iota(jnp.int32, shape, axis)


def flipped(index, mask):
    bit = 1
    while bit <= mask:
        if mask & bit:
            index = index + bit * (1 - 2 * ((index // bit) % 2))
        bit *= 2
    return index


def greet(partners):
    barrier = pltpu.get_barrier_semaphore()
    for axis, place in partners:
        pl.semaphore_signal(barrier, inc=1, device_id={axis: place}, device_id_type=pl.DeviceIdType.MESH)
    pl.semaphore_wait(barrier, len(partners))


def remote(source, target, send, recv, axis, place):
    return pltpu.make_async_remote_copy(
        src_ref=source, dst_ref=target, send_sem=send, recv_sem=recv,
        device_id={axis: place}, device_id_type=pl.DeviceIdType.MESH,
    )


class TensorSum:
    def __init__(self, tensors, own, arrived, send, recv):
        self.core = lax.axis_index("tensor")
        self.places = [flipped(self.core, 1 << k) for k in range((tensors - 1).bit_length())]
        self.refs = own, arrived, send, recv

    def copy(self, k):
        own, arrived, send, recv = self.refs
        return remote(own.at[k], arrived.at[k], send.at[k], recv.at[k], "tensor", self.places[k])

    def begin(self, value, met=False):
        if not met:
            greet([("tensor", place) for place in self.places])
        self.refs[0][0] = value
        self.copy(0).start()

    def end(self):
        own, arrived, _, _ = self.refs
        for k in range(len(self.places)):
            copy = self.copy(k)
            if k:
                copy.start()
            copy.wait()
            own[k + 1] = own[k] + arrived[k]
        return own[len(self.places)]


def tensor_sum_scratch(tensors, shape):
    steps = (tensors - 1).bit_length()
    return [
        pltpu.VMEM((steps + 1,) + shape, F32), pltpu.VMEM((steps,) + shape, F32),
        pltpu.SemaphoreType.DMA((steps,)), pltpu.SemaphoreType.DMA((steps,)),
    ]


def conv_taps(buffer, feats, taps, bias, rows):
    total = buffer[8 : 8 + rows, :] * taps[3:4, :] + bias
    for k in range(1, 4):
        total = total + buffer[8 - k : 8 - k + rows, :] * feats[:, k : k + 1] * taps[3 - k : 4 - k, :]
    return total


def step_parts(step_ref, heads_ref, feats, rows):
    raw = step_ref[...] + heads_ref[0:1, :]
    step = softplus(raw)
    lower = (iota2((rows, rows), 0) >= iota2((rows, rows), 1)).astype(F32)
    log_decay = exact_mm(lower, step * heads_ref[1:2, :])
    last = log_decay[rows - 1 : rows, :]
    enter = jnp.exp(log_decay) * feats[:, 4:5]
    leave = jnp.exp(last - log_decay) * feats[:, 5:6]
    return raw, step, log_decay, enter, leave


def gated_scale(squares):
    return lax.rsqrt(squares / DSSM + EPS)


def as_column(row):
    return jnp.broadcast_to(row, (LANES, row.shape[1])).T[:, 0:1]


def mamba_fwd_kernel(
    feats_ref, docs_ref, x_ref, bc_ref, step_ref, z_ref, taps_ref, staps_ref, heads_ref, expand_ref,
    gain_ref, scan_ref, low_ref, square_ref, states_ref, xbuf, bcbuf, memory,
):
    rows, width = x_ref.shape
    states = bc_ref.shape[1] // 2

    @pl.when(pl.program_id(0) == 0)
    def _():
        xbuf[0:8, :] = jnp.zeros((8, width), F32)
        bcbuf[0:8, :] = jnp.zeros((8, 2 * states), F32)
        memory[...] = jnp.zeros_like(memory)

    feats = feats_ref[...]
    xbuf[8 : 8 + rows, :] = x_ref[...]
    bcbuf[8 : 8 + rows, :] = bc_ref[...]
    pre = conv_taps(xbuf, feats, taps_ref, taps_ref[4:5, :], rows)
    values = pre * sigmoid(pre)
    pre_bc = conv_taps(bcbuf, feats, staps_ref, staps_ref[4:5, :], rows)
    both = pre_bc * sigmoid(pre_bc)
    xbuf[0:8, :] = xbuf[rows : rows + 8, :]
    bcbuf[0:8, :] = bcbuf[rows : rows + 8, :]
    key_in = both[:, :states].astype(BF)
    key_out = both[:, states:].astype(BF)
    _, step, log_decay, enter, leave = step_parts(step_ref, heads_ref, feats, rows)
    expanded = jnp.dot(
        split_lanes(jnp.concatenate([step, enter, leave], axis=0), 1), expand_ref[...], preferred_element_type=F32
    )
    step_w, enter_w, leave_w = expanded[:rows], expanded[rows : 2 * rows], expanded[2 * rows :]
    scaled = values * step_w
    gram = mm_nt(key_out, key_in)
    allowed = (feats[:, 0:1] == docs_ref[...]) & (iota2((rows, rows), 0) >= iota2((rows, rows), 1))
    bias = jnp.where(allowed, 0.0, MASKED)
    log_rows = log_decay.T
    front = iota2((rows, LANES), 1) < LANES // 2
    held = memory[...]
    states_ref[0] = held.astype(BF)
    carried = mm(key_out, held) * enter_w
    fresh = mm_tn(key_in, leave_w * scaled)
    memory[...] = held * enter_w[rows - 1 : rows, :] + fresh
    squares = jnp.zeros((rows, 1), F32)
    for pair in range(width // LANES):
        lanes = slice(pair * LANES, (pair + 1) * LANES)
        mixes = []
        for h in (2 * pair, 2 * pair + 1):
            decay = jnp.exp(log_decay[:, h : h + 1] - log_rows[h : h + 1, :] + bias)
            mixes.append((gram * decay).astype(BF))
        part = scaled[:, lanes]
        stacked = jnp.concatenate([jnp.where(front, part, 0.0), jnp.where(front, 0.0, part)], axis=0)
        inside = mm(jnp.concatenate(mixes, axis=1), stacked)
        scan = inside + carried[:, lanes] + values[:, lanes] * taps_ref[5:6, lanes]
        scan_ref[:, lanes] = scan
        z = z_ref[:, lanes]
        gated = scan * (z * sigmoid(z))
        low_ref[:, lanes] = (gated * gain_ref[:, lanes]).astype(BF)
        squares = squares + jnp.sum(gated * gated, axis=1, keepdims=True)
    square_ref[...] = jnp.broadcast_to(squares, (rows, LANES)).T[0:8, :]


def mamba_bwd_block(
    feats_ref, square_ref, inner_sum, block, docs_ref, x_ref, x_before_ref, bc_ref, bc_before_ref, step_ref, z_ref, scan_ref, states_ref, norm_grad_ref,
    taps_ref, staps_ref, heads_ref, expand_ref, reduce_ref, gain_ref,
    grads_ref, sums_ref, ssums_ref, hsums_ref,
    xbuf, bcbuf, dxbuf, dbcbuf, dmemory,
):
    rows, width = x_ref.shape
    states = bc_ref.shape[1] // 2

    feats = feats_ref[...]
    xbuf[0:8, :] = x_before_ref[...]
    bcbuf[0:8, :] = bc_before_ref[...]
    xbuf[8 : 8 + rows, :] = x_ref[...]
    bcbuf[8 : 8 + rows, :] = bc_ref[...]
    pre = conv_taps(xbuf, feats, taps_ref, taps_ref[4:5, :], rows)
    pre_gate = sigmoid(pre)
    values = pre * pre_gate
    pre_bc = conv_taps(bcbuf, feats, staps_ref, staps_ref[4:5, :], rows)
    bc_gate = sigmoid(pre_bc)
    both = pre_bc * bc_gate
    key_in = both[:, :states].astype(BF)
    key_out = both[:, states:].astype(BF)
    raw, step, log_decay, enter, leave = step_parts(step_ref, heads_ref, feats, rows)
    expanded = jnp.dot(
        split_lanes(jnp.concatenate([step, enter, leave], axis=0), 1), expand_ref[...], preferred_element_type=F32
    )
    step_w, enter_w, leave_w = expanded[:rows], expanded[rows : 2 * rows], expanded[2 * rows :]
    scaled = values * step_w
    z = z_ref[...]
    z_gate = sigmoid(z)
    z_silu = z * z_gate
    scan = scan_ref[...]
    gated = scan * z_silu
    norm_grad = norm_grad_ref[...].astype(F32)
    row_scale = gated_scale(square_ref[0:1, :])
    row_inner = inner_sum[pl.ds(pl.multiple_of(block * 8, 8), 8), :][0:1, :] * row_scale * row_scale / DSSM
    scale, coefficient = as_column(row_scale), as_column(row_inner)
    weighted = norm_grad * scale
    gated_grad = weighted * gain_ref[...] - gated * coefficient
    dscan = gated_grad * z_silu
    grads_ref[:, 0:width] = (gated_grad * scan * (z_gate * (1.0 + z * (1.0 - z_gate)))).astype(BF)
    sums_ref[6:7, :] += jnp.sum(weighted * gated, axis=0, keepdims=True)
    sums_ref[5:6, :] += jnp.sum(dscan * values, axis=0, keepdims=True)
    held = states_ref[0]
    dheld = dmemory[...]
    dheld_low = dheld.astype(BF)
    enter_grad = (dscan * enter_w).astype(BF)
    left = leave_w * scaled
    passed = mm(key_in, dheld_low)
    arrived = mm(key_out, held)
    dkey_out = mm_nt(enter_grad, held)
    dkey_in = mm_nt(left, dheld_low)
    carry = enter_w[rows - 1 : rows, :]
    dmemory[...] = dheld * carry + mm_tn(key_out, enter_grad)
    enter_terms = dscan * enter_w * arrived
    leave_terms = left * passed
    carry_terms = jnp.sum(dheld * held.astype(F32), axis=0, keepdims=True) * carry
    gram = mm_nt(key_in, key_out)
    allowed = (feats[:, 0:1] == docs_ref[...]) & (iota2((rows, rows), 0) <= iota2((rows, rows), 1))
    bias = jnp.where(allowed, 0.0, MASKED)
    log_rows = log_decay.T
    front = iota2((rows, LANES), 1) < LANES // 2
    gram_grad = jnp.zeros((rows, rows), F32)
    lane_of = iota2((rows, LANES), 1)
    row_of = iota2((LANES, rows), 0)
    sent = jnp.zeros((rows, LANES), F32)
    received = jnp.zeros((LANES, rows), F32)
    inside_grads = []
    for pair in range(width // LANES):
        lanes = slice(pair * LANES, (pair + 1) * LANES)
        dy = dscan[:, lanes].astype(BF)
        part = scaled[:, lanes]
        stacked = jnp.concatenate([jnp.where(front, part, 0.0), jnp.where(front, 0.0, part)], axis=0)
        cross = mm_nt(stacked, dy)
        mixes = []
        for j, h in enumerate((2 * pair, 2 * pair + 1)):
            decay = jnp.exp(log_rows[h : h + 1, :] - log_decay[:, h : h + 1] + bias)
            mix = gram * decay
            mixes.append(mix.astype(BF))
            dmix = cross[j * rows : (j + 1) * rows, :]
            gram_grad = gram_grad + dmix * decay
            flow = dmix * mix
            sent = jnp.where(lane_of == h, jnp.sum(flow, axis=1, keepdims=True), sent)
            received = jnp.where(row_of == h, jnp.sum(flow, axis=0, keepdims=True), received)
        grads = mm(jnp.concatenate(mixes, axis=0), dy)
        inside_grads.append(jnp.where(front, grads[:rows], grads[rows:]))
    dscaled = jnp.concatenate(inside_grads, axis=1) + leave_w * passed
    dkey_in = dkey_in + mm(gram_grad, key_out)
    dkey_out = dkey_out + mm_tn(gram_grad, key_in)
    reduced = jnp.dot(
        split_lanes(
            jnp.concatenate([enter_terms, leave_terms, dscaled * values, jnp.broadcast_to(carry_terms, (8, width))], axis=0), 1
        ),
        reduce_ref[...],
        preferred_element_type=F32,
    )
    after = reduced[:rows] + received.T - sent
    upper = (iota2((rows, rows), 0) <= iota2((rows, rows), 1)).astype(F32)
    strict = (iota2((rows, rows), 0) > iota2((rows, rows), 1)).astype(F32)
    decay_grad = exact_mm(upper, after) + exact_mm(strict, reduced[rows : 2 * rows]) + reduced[3 * rows : 3 * rows + 1]
    dstep = decay_grad * heads_ref[1:2, :] + reduced[2 * rows : 3 * rows]
    draw = dstep * sigmoid(raw)
    grads_ref[:, 2 * width + 2 * states :] = draw.astype(BF)
    hsums_ref[0:1, :] += jnp.sum(draw, axis=0, keepdims=True)
    hsums_ref[1:2, :] += jnp.sum(decay_grad * step, axis=0, keepdims=True) * heads_ref[1:2, :]
    dvalues = dscaled * step_w + dscan * taps_ref[5:6, :]
    dpre = dvalues * (pre_gate * (1.0 + pre * (1.0 - pre_gate)))
    dboth = jnp.concatenate([dkey_in, dkey_out], axis=1)
    dpre_bc = dboth * (bc_gate * (1.0 + pre_bc * (1.0 - bc_gate)))
    for dpre_now, buffer, dbuffer, taps, totals, lanes in (
        (dpre, xbuf, dxbuf, taps_ref, sums_ref, slice(width, 2 * width)),
        (dpre_bc, bcbuf, dbcbuf, staps_ref, ssums_ref, slice(2 * width, 2 * width + 2 * states)),
    ):
        dbuffer[0:rows, :] = dpre_now
        grad = dpre_now * taps[3:4, :]
        totals[3:4, :] += jnp.sum(dpre_now * buffer[8 : 8 + rows, :], axis=0, keepdims=True)
        totals[4:5, :] += jnp.sum(dpre_now, axis=0, keepdims=True)
        for k in range(1, 4):
            grad = grad + dbuffer[k : k + rows, :] * feats[:, 5 + k : 6 + k] * taps[3 - k : 4 - k, :]
            totals[3 - k : 4 - k, :] += jnp.sum(
                dpre_now * buffer[8 - k : 8 - k + rows, :] * feats[:, k : k + 1], axis=0, keepdims=True
            )
        grads_ref[:, lanes] = grad.astype(BF)
        dbuffer[rows : rows + 8, :] = dbuffer[0:8, :]


def expand_matrix(width):
    one = np.arange(LANES)[:, None] == np.arange(width)[None, :] // (LANES // 2)
    return np.concatenate([one, one], axis=0).astype(ml_dtypes.bfloat16)


def spec(block, index):
    return pl.BlockSpec(block, index)


def mamba_forward(feats, doc_row, ssm_in, taps, staps, heads, gain, width, states2):
    total = ssm_in.shape[0]
    rows = CHUNK
    count = total // rows
    block = lambda w, place=0: spec((rows, w), lambda i: (i, place))
    whole = lambda a: spec(a.shape, lambda i: (0,) * a.ndim)
    expand = expand_matrix(width)
    return pl.pallas_call(
        mamba_fwd_kernel,
        grid=(count,),
        in_specs=[
            block(LANES), spec((1, rows), lambda i: (0, i)), block(width, 1), block(states2, 2 * width // states2),
            block(LANES, (2 * width + states2) // LANES), block(width), whole(taps), whole(staps), whole(heads), whole(expand), whole(gain),
        ],
        out_specs=[block(width), block(width), spec((8, LANES), lambda i: (i, 0)), spec((1, states2 // 2, width), lambda i: (i, 0, 0))],
        out_shape=[
            jax.ShapeDtypeStruct((total, width), F32),
            jax.ShapeDtypeStruct((total, width), BF),
            jax.ShapeDtypeStruct((8 * count, LANES), F32),
            jax.ShapeDtypeStruct((count, states2 // 2, width), BF),
        ],
        scratch_shapes=[
            pltpu.VMEM((rows + 8, width), F32), pltpu.VMEM((rows + 8, states2), F32), pltpu.VMEM((states2 // 2, width), F32),
        ],
        compiler_params=pltpu.CompilerParams(vmem_limit_bytes=VMEM_LIMIT),
        cost_estimate=pl.CostEstimate(flops=20 * 10**9, bytes_accessed=total * width * 20, transcendentals=total * width * 4),
        name="mamba_fwd",
    )(feats, doc_row, ssm_in, ssm_in, ssm_in, ssm_in, taps, staps, heads, expand, gain)


def swap_halves(values):
    lane = iota2(values.shape, 1) % (LANES // 2)
    return jnp.where(lane < LANES // 4, pltpu.roll(values, LANES - LANES // 4, 1), pltpu.roll(values, LANES // 4, 1))


def stack_heads(part):
    front = iota2(part.shape, 1) < LANES // 2
    zero = jnp.zeros_like(part)
    return jnp.concatenate([jnp.where(front, part, zero), jnp.where(front, zero, part)], axis=0)


def attention_fwd_kernel(
    groups, tensors, docs_col_ref, docs_ref, q_ref, kv_ref, cos_ref, sin_ref, low_ref, square_ref, out_ref, lse_ref, qrot_ref, keys_ref, values_ref, square_out_ref, *scratch,
):
    total = q_ref.shape[0]
    wide = low_ref.shape[1]
    exchange = TensorSum(tensors, *scratch)
    exchange.begin(square_ref[...])
    pairs = q_ref.shape[1] // LANES
    block = min(QBLOCK, total)
    cos, sin = cos_ref[...], sin_ref[...]
    front = iota2((total, LANES), 1) < LANES // 2
    for g in range(groups):
        lanes = slice(g * LANES, (g + 1) * LANES)
        raw = kv_ref[:, lanes]
        turned = raw * cos + swap_halves(raw) * sin
        keys_ref[:, lanes] = jnp.where(front, turned, pltpu.roll(turned, LANES // 2, 1)).astype(BF)
        values_ref[:, lanes] = jnp.where(front, pltpu.roll(raw, LANES // 2, 1), raw).astype(BF)
    for p in range(pairs):
        lanes = slice(p * LANES, (p + 1) * LANES)
        raw = q_ref[:, lanes]
        qrot_ref[:, lanes] = ((raw * cos + swap_halves(raw) * sin).astype(BF).astype(F32) * (LANES // 2) ** -0.5).astype(BF)
    front = iota2((block, LANES), 1) < LANES // 2
    lane_of = iota2((block, LANES), 1)
    for start in range(0, total, block):
        rows, end = slice(start, start + block), start + block
        allowed = (docs_col_ref[rows, 0:1] == docs_ref[:, :end]) & (
            iota2((block, end), 0) + start >= iota2((block, end), 1)
        )
        bias = jnp.where(allowed, 0.0, MASKED)
        bias = jnp.concatenate([bias, bias], axis=0)
        sums = jnp.zeros((block, LANES), F32)
        for p in range(pairs):
            lanes = slice(p * LANES, (p + 1) * LANES)
            g = p * groups // pairs
            kv = slice(g * LANES, (g + 1) * LANES)
            scores = mm_nt(stack_heads(qrot_ref[rows, lanes]), keys_ref[:end, kv]) + bias
            top = jnp.max(scores, axis=1, keepdims=True)
            raised = jnp.exp(scores - top)
            whole = jnp.sum(raised, axis=1, keepdims=True)
            mixed = mm(raised, values_ref[:end, kv]) / whole
            out_ref[rows, wide + p * LANES : wide + (p + 1) * LANES] = jnp.where(front, mixed[:block], mixed[block:]).astype(BF)
            logs = top + jnp.log(whole)
            sums = jnp.where(lane_of == 2 * p, logs[:block], sums)
            sums = jnp.where(lane_of == 2 * p + 1, logs[block:], sums)
        lse_ref[rows, :] = sums
    square_out_ref[...] = exchange.end()
    for i in range(total // LANES):
        piece = slice(i * LANES, (i + 1) * LANES)
        scale = as_column(gated_scale(square_out_ref[8 * i : 8 * i + 1, :]))
        out_ref[piece, :wide] = (low_ref[piece, :].astype(F32) * scale).astype(BF)


def attention_bwd_block(
    start, groups, docs_col_ref, docs_ref, qrot_ref, keys_ref, values_ref, lse_ref, up_ref, cos_ref, sin_ref, grads_ref, dk_acc, dv_acc,
):
    pairs = qrot_ref.shape[1] // LANES
    block = up_ref.shape[0]
    front = iota2((block, LANES), 1) < LANES // 2
    rows, end = slice(start, start + block), start + block
    allowed = (docs_col_ref[:end, 0:1] == docs_ref[:, rows]) & (
        iota2((end, block), 0) <= iota2((end, block), 1) + start
    )
    bias = jnp.where(allowed, 0.0, MASKED)
    logs = lse_ref[...].T
    cos, sin = cos_ref[rows, :], sin_ref[rows, :]
    for p in range(pairs):
        lanes = slice(p * LANES, (p + 1) * LANES)
        g = p * groups // pairs
        kv = slice(g * LANES, (g + 1) * LANES)
        keys, values = keys_ref[:end, kv], values_ref[:end, kv]
        queries = stack_heads(qrot_ref[rows, lanes])
        ups = stack_heads(up_ref[:, lanes])
        shift = jnp.concatenate([bias - logs[2 * p : 2 * p + 1], bias - logs[2 * p + 1 : 2 * p + 2]], axis=1)
        probs = jnp.exp(mm_nt(keys, queries) + shift)
        grads = mm_nt(values, ups)
        centre = jnp.sum(probs * grads, axis=0, keepdims=True)
        score_grads = (probs * (grads - centre)).astype(BF)
        dk_acc[:end, kv] += mm(score_grads, queries)
        dv_acc[:end, kv] += mm(probs, ups)
        dq = mm_tn(score_grads, keys)
        dq = jnp.where(front, dq[:block], dq[block:]) * (LANES // 2) ** -0.5
        grads_ref[rows, lanes] = (dq * cos - swap_halves(dq) * sin).astype(BF)


def attention_bwd_end(groups, pairs, cos_ref, sin_ref, grads_ref, dk_acc, dv_acc):
    total = dk_acc.shape[0]
    front = iota2((total, LANES), 1) < LANES // 2
    for g in range(groups):
        kv = slice(g * LANES, (g + 1) * LANES)
        dk, dv = dk_acc[:, kv], dv_acc[:, kv]
        dk = dk + pltpu.roll(dk, LANES // 2, 1)
        dk = dk * cos_ref[...] - swap_halves(dk) * sin_ref[...]
        dv = dv + pltpu.roll(dv, LANES // 2, 1)
        out = slice((pairs + g) * LANES, (pairs + g + 1) * LANES)
        grads_ref[:, out] = jnp.where(front, dk, dv).astype(BF)


def attention_forward(groups, tensors, doc_col, doc_row, qkv, cos, sin, query_width, low, squares, collective_id):
    total = qkv.shape[0]
    kv_width = qkv.shape[1] - query_width
    whole = lambda a: spec(a.shape, lambda i: (0,) * a.ndim)
    columns = lambda w, place=0: spec((total, w), lambda i: (0, place))
    return pl.pallas_call(
        functools.partial(attention_fwd_kernel, groups, tensors),
        grid=(1,),
        in_specs=[whole(doc_col), whole(doc_row), columns(query_width), columns(kv_width, query_width // kv_width), whole(cos), whole(sin), whole(low), whole(squares)],
        out_specs=[columns(low.shape[1] + query_width), columns(LANES), columns(query_width), columns(kv_width), columns(kv_width), whole(squares)],
        out_shape=[
            jax.ShapeDtypeStruct((total, low.shape[1] + query_width), BF), jax.ShapeDtypeStruct((total, LANES), F32),
            jax.ShapeDtypeStruct((total, query_width), BF), jax.ShapeDtypeStruct((total, kv_width), BF),
            jax.ShapeDtypeStruct((total, kv_width), BF), jax.ShapeDtypeStruct(squares.shape, F32),
        ],
        scratch_shapes=tensor_sum_scratch(tensors, squares.shape),
        compiler_params=pltpu.CompilerParams(vmem_limit_bytes=VMEM_LIMIT, collective_id=collective_id, has_side_effects=True),
        cost_estimate=pl.CostEstimate(flops=12 * 10**9, bytes_accessed=total * query_width * 10, transcendentals=total * total * 2),
        name="attention_fwd",
    )(doc_col, doc_row, qkv, qkv, cos, sin, low, squares)


def gather_kernel(
    count, tensors, shard_ref, tokens_ref, cotangent_ref, gain_ref, *refs,
):
    tables, (full_ref, all_tokens_ref, all_cotangent_ref, normed_ref, scale_ref, turned_ref) = refs[:8], refs[8:14]
    table_outs, (own_sem, send_sems, recv_sems, core_send, core_recv) = refs[14:20], refs[20:]
    unit, columns = shard_ref.shape
    levels = count // 4
    me = lax.axis_index("fsdp")
    main = columns - columns // 5 // LANES * LANES
    half, middle = main // 2 // LANES * LANES, (main + columns) // 2 // LANES * LANES
    parts, flat_parts = (slice(0, half), slice(half, main)), (slice(main, middle), slice(middle, columns))
    neighbours = (flipped(me, 1), flipped(me, 2))
    bits = [1 << k for k in range((levels - 1).bit_length())]
    core = lax.axis_index("tensor")
    cores = [flipped(core, k) for k in range(1, tensors)]
    greet([("fsdp", p) for p in neighbours] + [("fsdp", flipped(me, 4 * bit)) for bit in bits] + [("tensor", p) for p in cores])

    def rows(owner):
        return pl.ds(pl.multiple_of(owner * unit, unit), unit)

    started = []

    def send(source, owner, lanes, slot, place):
        copy = remote(source, full_ref.at[rows(owner), lanes], send_sems.at[slot], recv_sems.at[slot], "fsdp", place)
        copy.start()
        started.append(copy)
        return copy

    def arrival(owner, lanes, slot):
        piece = full_ref.at[rows(owner), lanes]
        return remote(piece, piece, send_sems.at[slot], recv_sems.at[slot], "fsdp", neighbours[0])

    everything, flat = slice(0, main), slice(main, columns)
    own = pltpu.make_async_copy(shard_ref, full_ref.at[rows(me), :], own_sem)
    own.start()
    base = levels
    cross = base + 2 * levels
    level, flat_base = cross + 2 * levels, cross + 3 * levels

    def along_z(d):
        for bit in reversed(bits):
            if d == 0 or bit < (d & -d):
                source = shard_ref.at[:, everything] if d == 0 else full_ref.at[rows(flipped(me, 4 * d)), everything]
                send(source, flipped(me, 4 * d), everything, d + bit, flipped(me, 4 * bit))

    def quad(d):
        return full_ref.at[pl.ds(pl.multiple_of(flipped(me, 4 * d) // 4 * (4 * unit), 4 * unit), 4 * unit), flat]

    def quad_copy(d, bit):
        return remote(quad(d), quad(d), send_sems.at[level + d + bit], recv_sems.at[level + d + bit], "fsdp", flipped(me, 4 * bit))

    def quads_along_z(d):
        if d:
            place = neighbours[0]
            remote(quad(d), quad(d), send_sems.at[level + d], recv_sems.at[level + d], "fsdp", place).wait_recv()
        for bit in reversed(bits):
            if d == 0 or bit < (d & -d):
                copy = quad_copy(d, bit)
                copy.start()
                started.append(copy)

    along_z(0)
    for axis in range(2):
        send(shard_ref.at[:, flat], me, flat, flat_base + axis, neighbours[axis])
    for axis in range(2):
        send(shard_ref.at[:, everything], me, everything, base + axis * levels, neighbours[axis])
    own_rows = tokens_ref.shape[0]
    share = lambda owner: pl.ds(pl.multiple_of(owner * own_rows, own_rows), own_rows)
    exchanges = []
    for k, place in enumerate(cores):
        for j, (source, target) in enumerate(((tokens_ref, all_tokens_ref), (cotangent_ref, all_cotangent_ref))):
            copy = remote(
                source, target.at[share(core), :], core_send.at[2 * k + j], core_recv.at[2 * k + j], "tensor", place
            )
            copy.start()
            exchanges.append(copy)
    all_tokens_ref[share(core), :] = tokens_ref[...]
    all_cotangent_ref[share(core), :] = cotangent_ref[...]
    for copy in exchanges:
        copy.wait()

    def norm(i, carry):
        piece = pl.ds(pl.multiple_of(i * LANES, LANES), LANES)
        values = all_tokens_ref[piece, :].astype(F32)
        scale = lax.rsqrt(jnp.mean(values * values, axis=1, keepdims=True) + EPS)
        scale_ref[piece, :] = scale
        normed = values * scale * gain_ref[...]
        normed_ref[piece, :] = normed.astype(BF)
        turned_ref[:, piece] = normed.T.astype(BF)
        return carry

    lax.fori_loop(0, normed_ref.shape[0] // LANES, norm, 0)
    table_kernel(*tables, *table_outs)

    def pass_on(d):
        for axis in range(2):
            owner = flipped(neighbours[axis], 4 * d)
            arrival(owner, everything, base + axis * levels + d).wait_recv()
            piece = full_ref.at[rows(owner), parts[axis]]
            send(piece, owner, parts[axis], cross + axis * levels + d, neighbours[1 - axis])

    for axis in range(2):
        arrival(neighbours[axis], flat, flat_base + axis).wait_recv()
        piece = full_ref.at[rows(neighbours[axis]), flat_parts[axis]]
        send(piece, neighbours[axis], flat_parts[axis], flat_base + 2 + axis, neighbours[1 - axis])
    order = sorted(range(1, levels), key=lambda d: (-(d & -d), d))
    before = 0
    for d in order:
        owner = flipped(me, 4 * d)
        arrival(owner, everything, d).wait_recv()
        along_z(d)
        for axis in range(2):
            send(full_ref.at[rows(owner), everything], owner, everything, base + axis * levels + d, neighbours[axis])
        pass_on(before)
        before = d
        if d == order[0]:
            for axis in range(2):
                arrival(flipped(me, 3), flat_parts[axis], flat_base + 2 + axis).wait_recv()
            own.wait()
            quads_along_z(0)
    quads_along_z(order[0])
    pass_on(before)
    for d in order[1:]:
        quads_along_z(d)
    for d in range(levels):
        for axis in range(2):
            owner = flipped(me, 4 * d + 3)
            arrival(owner, parts[axis], cross + axis * levels + d).wait_recv()
    for copy in started:
        copy.wait_send()


def gather_weights(shard, tokens, cotangent, gain, tables, wide, count, tensors, collective_id):
    unit, columns = shard.shape
    own_rows, hidden = tokens.shape
    total = own_rows * tensors
    slots = 6 * (count // 4) + 4
    vmem, anywhere = pl.BlockSpec(memory_space=pltpu.VMEM), pl.BlockSpec(memory_space=pl.ANY)
    low = jax.ShapeDtypeStruct((total, hidden), BF)
    shape = lambda r, c: jax.ShapeDtypeStruct((r, c), F32)
    return pl.pallas_call(
        functools.partial(gather_kernel, count, tensors),
        in_specs=[anywhere, vmem, vmem, vmem] + [vmem] * len(tables),
        out_specs=[anywhere] + [vmem] * 11,
        out_shape=[jax.ShapeDtypeStruct((count * unit, columns), shard.dtype), low, low, low, jax.ShapeDtypeStruct((total, 1), F32),
            jax.ShapeDtypeStruct((hidden, total), BF), shape(total, LANES), shape(total, LANES), shape(total, LANES), shape(8, wide),
            shape(8, tables[3].shape[1]), shape(8, LANES),
        ],
        scratch_shapes=[
            pltpu.SemaphoreType.DMA, pltpu.SemaphoreType.DMA((slots,)), pltpu.SemaphoreType.DMA((slots,)),
            pltpu.SemaphoreType.DMA((2 * (tensors - 1),)), pltpu.SemaphoreType.DMA((2 * (tensors - 1),)),
        ],
        compiler_params=pltpu.CompilerParams(collective_id=collective_id, has_side_effects=True, vmem_limit_bytes=VMEM_LIMIT),
        cost_estimate=pl.CostEstimate(flops=0, bytes_accessed=2 * count * unit * columns * 2, transcendentals=0),
        name="gather_weights",
    )(shard, tokens, cotangent, gain, *tables)


def backward_kernel(c, *refs):
    r = types.SimpleNamespace(**dict(zip(c.names, refs)))
    now = pl.program_id(0)
    me, core = lax.axis_index("fsdp"), lax.axis_index("tensor")
    levels, unit, blocks, chunks, tiles = c.count // 4, c.unit, c.blocks, c.chunks, c.tiles
    near = (flipped(me, 1), flipped(me, 2))
    far = [None] + [flipped(me, 4 * d) for d in range(1, levels)]
    bits = [1 << k for k in range((c.count - 1).bit_length())]
    cores = [flipped(core, k) for k in range(1, c.tensors)]
    halves = [("tensor", flipped(core, 1 << k)) for k in range((c.tensors - 1).bit_length())]
    stages = [("fsdp", flipped(me, bit)) for bit in bits] + halves
    order = sorted(range(levels), key=lambda d: (d & -d if d else levels, -d))
    pieces = []
    for i, (name, lanes, path, out, out_lanes) in enumerate(c.pieces):
        pieces.append((i, getattr(r, name), lanes, path, getattr(r, out), out_lanes))
    early, late, flat = pieces[: c.early], pieces[c.early : c.flat], pieces[c.flat :]

    def own_copies():
        copies = []
        for i, grad, lanes, path, _, _ in early:
            parts = getattr(r, "own%d" % i)
            for d in order:
                for k, owner in ((d, flipped(near[path], 4 * d)), (levels + d, flipped(me, 4 * d))):
                    copies.append(pltpu.make_async_copy(grad.at[rows(owner), lanes], parts.at[k], r.own_sems.at[i, k]))
        return copies

    def own_part(i, grad, lanes, owner, k):
        if i < c.early:
            return getattr(r, "own%d" % i)[k].astype(F32)
        return grad[spot(i, owner), lanes].astype(F32)

    cross, along, inbound = [], [], []
    for i in range(len(pieces)):
        cross.append(getattr(r, "cross%d" % i))
        along.append((getattr(r, "along_x%d" % i), getattr(r, "along_y%d" % i)))
        inbound.append(getattr(r, "inbound%d" % i))

    def rows(owner):
        return pl.ds(pl.multiple_of(owner * unit, unit), unit)

    def spot(i, owner):
        return rows(owner % 4 if i >= c.flat else owner)

    def link(source, target, i, kind, d, place):
        slot = (i * 4 + kind) * levels + d
        return remote(source, target, r.send_sems.at[slot], r.recv_sems.at[slot], "fsdp", place)

    def begin(group, d):
        for i, grad, lanes, path, _, _ in group:
            link(grad.at[spot(i, flipped(me, 4 * d + 3)), lanes], cross[i].at[d], i, 0, d, near[1 - path]).start()

    def raw(group, d):
        for i, grad, lanes, path, _, _ in group:
            other = 1 - path
            link(grad.at[spot(i, flipped(near[other], 4 * d)), lanes], along[i][other].at[d], i, 1 + other, d, near[other]).start()

    def middle(group, d):
        for i, grad, lanes, path, _, _ in group:
            link(cross[i].at[d], cross[i].at[d], i, 0, d, near[0]).wait_recv()
            own = own_part(i, grad, lanes, flipped(near[path], 4 * d), d)
            cross[i][d] = (own + cross[i][d].astype(F32)).astype(BF)
            link(cross[i].at[d], along[i][path].at[d], i, 1 + path, d, near[path]).start()

    def finish(group, d):
        lowest = d & -d if d else levels
        for i, grad, lanes, path, out, out_lanes in group:
            for axis in range(2):
                link(along[i][axis].at[d], along[i][axis].at[d], i, 1 + axis, d, near[0]).wait_recv()
            own = own_part(i, grad, lanes, flipped(me, 4 * d), levels + d)
            total = own + along[i][0][d].astype(F32) + along[i][1][d].astype(F32)
            bit = 1
            while bit < lowest and i < c.flat:
                slot = d + bit - 1
                link(inbound[i].at[slot], inbound[i].at[slot], i, 3, d + bit, near[0]).wait_recv()
                total = total + inbound[i][slot].astype(F32)
                bit *= 2
            if d:
                along[i][0][d] = total.astype(BF)
                link(along[i][0].at[d], inbound[i].at[d - 1], i, 3, d, far[lowest]).start()
            else:
                out[:, out_lanes] = total

    def quad(d):
        return pl.ds(pl.multiple_of(flipped(me, 4 * d) // 4 * (4 * unit), 4 * unit), 4 * unit)

    def level_own(d):
        return pltpu.make_async_copy(r.grad_level.at[quad(d), :], r.level_sum.at[d // 2], r.level_local.at[d // 2])

    def level_send(source, d):
        place = far[d & -d]
        return remote(source, r.level_in.at[d - 1], r.level_send.at[d - 1], r.level_recv.at[d - 1], "fsdp", place)

    def level_start():
        for d in order:
            if d % 2:
                level_send(r.grad_level.at[quad(d), :], d).start()
            else:
                level_own(d).start()

    def level_pass(d):
        level_own(d).wait()
        total = r.level_sum[d // 2].astype(F32)
        bit, lowest = 1, d & -d if d else levels
        while bit < lowest:
            level_send(r.level_in.at[d + bit - 1], d + bit).wait_recv()
            total = total + r.level_in[d + bit - 1].astype(F32)
            bit *= 2
        if d:
            r.level_sum[d // 2] = total.astype(BF)
            level_send(r.level_sum.at[d // 2], d).start()
        else:
            r.level_done[...] = total.astype(BF)

    weights_copy = pltpu.make_async_copy(r.weights.at[:, 0 : r.held.shape[1]], r.held, r.local_sems.at[0])
    own_rows = r.tokens.shape[0]
    share = lambda owner: pl.ds(pl.multiple_of(owner * own_rows, own_rows), own_rows)
    turned_copy = pltpu.make_async_copy(r.normed_turned, r.turned, r.local_sems.at[2])
    branch_copy = pltpu.make_async_copy(r.branch_low.at[share(core), :], r.branch_own, r.local_sems.at[1])
    inners = TensorSum(c.tensors, r.inner_own, r.inner_in, r.inner_send, r.inner_recv)

    @pl.when(now == 0)
    def _():
        greet([("fsdp", p) for p in near] + [("fsdp", flipped(me, bit)) for bit in bits[2:]] + [("tensor", p) for p in cores])
        level_start()
        for d in order:
            begin(early, d)
        for copy in own_copies():
            copy.start()
        turned_copy.start()
        weights_copy.start()
        branch_copy.start()
        r.dk_acc[...] = jnp.zeros_like(r.dk_acc)
        r.dv_acc[...] = jnp.zeros_like(r.dv_acc)

    block = r.mix_up.shape[0]
    for j in range(blocks):

        @pl.when(now == j)
        def _(j=j):
            for i in range(block // LANES):
                part = slice(i * LANES, (i + 1) * LANES)
                inner = jnp.sum(r.mix_norm[part, :].astype(F32) * r.mix_low[part, :].astype(F32), axis=1, keepdims=True)
                at = 8 * (j * (block // LANES) + i)
                r.inner_rows[at : at + 8, :] = jnp.broadcast_to(inner, (LANES, LANES)).T[0:8, :]
            attention_bwd_block(
                j * block, c.groups, r.feats_all, r.doc_row, r.qrot, r.keys, r.values, r.lse, r.mix_up, r.cos, r.sin, r.qkv_grad,
                r.dk_acc, r.dv_acc,
            )
            if j == blocks - 1:
                inners.begin(r.inner_rows[...], met=True)
                attention_bwd_end(c.groups, r.qrot.shape[1] // LANES, r.cos, r.sin, r.qkv_grad, r.dk_acc, r.dv_acc)

    @pl.when(now == blocks)
    def _():
        r.dxbuf[CHUNK : CHUNK + 8, :] = jnp.zeros((8, r.dxbuf.shape[1]), F32)
        r.dbcbuf[CHUNK : CHUNK + 8, :] = jnp.zeros((8, r.dbcbuf.shape[1]), F32)
        r.dmemory[...] = jnp.zeros_like(r.dmemory)
        r.x_sums[...] = jnp.zeros_like(r.x_sums)
        r.state_sums[...] = jnp.zeros_like(r.state_sums)
        r.head_sums[...] = jnp.zeros_like(r.head_sums)
        r.inner_sum[...] = inners.end()

    @pl.when((now >= blocks) & (now < blocks + chunks))
    def _():
        chunk = chunks - 1 - (now - blocks)
        mamba_bwd_block(
            r.feats, r.square, r.inner_sum, chunk, r.docs, r.x, r.x_before, r.bc, r.bc_before, r.step, r.z, r.scan, r.states,
            r.norm_grad, r.taps, r.staps, r.heads, r.expand, r.reduce, r.gain,
            r.ssm_grad.at[pl.ds(pl.multiple_of(chunk * CHUNK, CHUNK), CHUNK), :], r.x_sums, r.state_sums, r.head_sums,
            r.xbuf, r.bcbuf, r.dxbuf, r.dbcbuf, r.dmemory,
        )

    for k, d in enumerate(order):

        @pl.when(now == blocks + 1 + k)
        def _(d=d):
            if d == order[0]:
                for copy in own_copies():
                    copy.wait()
            middle(early, d)
            raw(early, d)

    base = blocks + chunks
    ssm_wide = r.ssm_grad.shape[1]
    for k, d in enumerate(order):

        @pl.when(now == base + k)
        def _(d=d):
            quad = pl.ds(pl.multiple_of(flipped(me, 4 * d) // 4 * (4 * unit), 4 * unit), 4 * unit)
            if d == order[0]:
                turned_copy.wait()
            turned = r.turned[quad, :]
            r.grad_first[quad, :ssm_wide] = jnp.dot(turned, r.ssm_grad[...], preferred_element_type=F32).astype(BF)
            r.grad_first[quad, ssm_wide:] = jnp.dot(turned, r.qkv_grad[...], preferred_element_type=F32).astype(BF)
            begin(late, d)
            raw(late, d)

    base = base + levels

    @pl.when(now == base)
    def _():
        weights_copy.wait()

    @pl.when((now >= base) & (now < base + tiles))
    def _():
        part = pl.ds(pl.multiple_of((now - base) * c.tile, c.tile), c.tile)
        r.normed_part[part, :] = (
            mm_nt(r.ssm_grad[part, :], r.held[:, :ssm_wide]) + mm_nt(r.qkv_grad[part, :], r.held[:, ssm_wide:])
        ).astype(BF)

    def normed_copies():
        return [
            remote(r.normed_part.at[share(place), :], r.normed_in.at[k], r.core_send.at[k], r.core_recv.at[k], "tensor", place)
            for k, place in enumerate(cores)
        ]

    for k, step in enumerate((base - levels + 1, base + 1)):

        @pl.when(now == step)
        def _(d=order[k]):
            finish(early, d)

    for k, d in enumerate([d for d in order if d % 2 == 0]):

        @pl.when(now == c.level_steps[k])
        def _(d=d):
            level_pass(d)
            if d == 0:
                begin(flat, 0)
                raw(flat, 0)

    settled = []

    def stage_copy(k):
        axis, place = stages[k]
        return remote(r.sums.at[k], r.sums_in.at[k], r.sum_send.at[k], r.sum_recv.at[k], axis, place)

    def next_stage():
        k = len(settled)
        if k < len(stages):
            stage_copy(k).wait()
            r.sums[k + 1] = r.sums[k] + r.sums_in[k]
            settled.append(k)
            if k + 1 < len(stages):
                stage_copy(k + 1).start()

    @pl.when(now == base + tiles)
    def _():
        for copy in normed_copies():
            copy.start()
        for copy in normed_copies():
            copy.wait()
        branch_copy.wait()
        r.gain_sum[...] = jnp.zeros_like(r.gain_sum)
        size = min(CHUNK, own_rows)

        def first_norm_back(i, carry):
            part = pl.ds(pl.multiple_of(i * size, size), size)
            whole = pl.ds(pl.multiple_of(core * own_rows + i * size, size), size)
            grad = r.normed_part[whole, :].astype(F32)
            for k in range(len(cores)):
                grad = grad + r.normed_in[k, part, :].astype(F32)
            scale = r.scale[whole, :]
            shape = r.tokens[part, :].astype(F32) * scale
            weighted = grad * r.input_gain[...]
            inner = jnp.mean(weighted * shape, axis=1, keepdims=True)
            r.input_grad[part, :] = r.branch_own[part, :].astype(F32) + scale * (weighted - shape * inner)
            r.gain_sum[0:1, :] += jnp.sum(grad * shape, axis=0, keepdims=True)
            return carry

        lax.fori_loop(0, own_rows // size, first_norm_back, 0)
        at = 0
        for ref in (r.x_sums, r.head_sums, r.state_sums):
            r.sums[0, :, at : at + ref.shape[1]] = ref[...]
            at += ref.shape[1]
        eighth = r.gain_sum.shape[1] // 8
        for ref, factor in ((r.second_part, 1.0 / c.tensors), (r.gain_sum, 1.0)):
            for k in range(8):
                r.sums[0, k : k + 1, at : at + eighth] = ref[0:1, k * eighth : (k + 1) * eighth] * factor
            at += eighth
        stage_copy(0).start()
        for d in order[2:]:
            finish(early, d)
            next_stage()
        middle(flat, 0)
        for d in order:
            middle(late, d)
        for d in order:
            finish(late, d)
            next_stage()
        finish(flat, 0)
        while len(settled) < len(stages):
            next_stage()
        r.small_out[:, : c.split] = r.sums[len(bits), :, : c.split]
        r.small_out[:, c.split :] = r.sums[len(stages), :, c.split :]
        states2 = c.state_at[1] - c.state_at[0]
        wide_shared = r.shared.shape[2]
        leading = core * (wide_shared - states2) // (c.tensors * LANES)
        r.shared[0, :, :states2] = r.out_first[:, c.state_at[0] : c.state_at[1]]
        for g in range((wide_shared - states2) // LANES):
            value = jnp.zeros((unit, LANES), F32)
            for j in range(c.groups):
                value = jnp.where(leading + j == g, r.out_first[:, c.kv_at + j * LANES : c.kv_at + (j + 1) * LANES], value)
            r.shared[0, :, states2 + g * LANES : states2 + (g + 1) * LANES] = value
        for k, (axis, place) in enumerate(halves):
            copy = remote(r.shared.at[k], r.shared_in.at[k], r.half_send.at[k], r.half_recv.at[k], axis, place)
            copy.start()
            copy.wait()
            r.shared[k + 1] = r.shared[k] + r.shared_in[k]
        r.shared_out[...] = r.shared[len(halves)]
        for d in order[:-1]:
            level_send(r.level_in.at[d - 1], d).wait_send()
        for i in range(len(pieces)):
            for d in range(levels):
                for kind in range(4):
                    if (kind < 3 or d) and (i < c.flat or kind < 3 and d == 0):
                        link(cross[i].at[d], cross[i].at[d], i, kind, d, near[0]).wait_send()


def backward(
    groups, feats, doc_row, qrot, keys, values, lse, mix_grad, mix, cos, sin, squares, ssm_in, scan, states, taps, staps, heads, gain,
    grad_gate_up, grad_down, grad_mix, normed_turned, first, branch_low, tokens, scale, input_gain, second_part, width, states2,
    count, tensors, collective_id,
):
    total, hidden = branch_low.shape
    own_rows = tokens.shape[0]
    unit = hidden // count
    levels = count // 4
    query_wide, kv_wide = qrot.shape[1], keys.shape[1]
    block, tile = min(QBLOCK, total), min(QBLOCK, total)
    blocks, chunks, tiles = total // block, total // CHUNK, total // tile
    ssm_wide, qkv_wide = 2 * width + states2 + LANES, query_wide + kv_wide
    chunk = lambda s: jnp.clip(chunks - 1 - (s - blocks), 0, chunks - 1)
    query = lambda s: jnp.minimum(s, blocks - 1)
    by_chunk = lambda w, place=0: spec((CHUNK, w), lambda s: (chunk(s), place))
    by_query = lambda w, place=0: spec((block, w), lambda s: (query(s), place))
    before = lambda w, place=0: spec((8, w), lambda s: (jnp.maximum(chunk(s) * (CHUNK // 8) - 1, 0), place))
    whole = lambda a: pl.BlockSpec(a.shape, lambda s: (0,) * a.ndim, pipeline_mode=pl.Buffered(1))
    anywhere = pl.BlockSpec(memory_space=pl.ANY)
    vmem = pl.BlockSpec(memory_space=pltpu.VMEM)
    expand = expand_matrix(width)
    reduce = np.concatenate([expand[:LANES].T] * 2, axis=0)
    state_place, step_place = 2 * width // states2, (2 * width + states2) // LANES
    ins = dict(
        feats_all=(feats, whole(feats)), doc_row=(doc_row, whole(doc_row)), qrot=(qrot, whole(qrot)), keys=(keys, whole(keys)),
        values=(values, whole(values)), lse=(lse, by_query(LANES)), mix_up=(mix_grad, by_query(query_wide, width // query_wide)),
        mix_norm=(mix_grad, by_query(width)), mix_low=(mix, by_query(width)), cos=(cos, whole(cos)), sin=(sin, whole(sin)),
        feats=(feats, by_chunk(LANES)), docs=(doc_row, spec((1, CHUNK), lambda s: (0, chunk(s)))),
        square=(squares, spec((8, LANES), lambda s: (chunk(s), 0))), x=(ssm_in, by_chunk(width, 1)),
        x_before=(ssm_in, before(width, 1)), bc=(ssm_in, by_chunk(states2, state_place)),
        bc_before=(ssm_in, before(states2, state_place)), step=(ssm_in, by_chunk(LANES, step_place)),
        z=(ssm_in, by_chunk(width)), scan=(scan, by_chunk(width)),
        states=(states, spec((1, states2 // 2, width), lambda s: (chunk(s), 0, 0))), norm_grad=(mix_grad, by_chunk(width)),
        taps=(taps, whole(taps)), staps=(staps, whole(staps)), heads=(heads, whole(heads)), expand=(expand, whole(expand)),
        reduce=(reduce, whole(reduce)), gain=(gain, whole(gain)), grad_gate_up=(grad_gate_up, anywhere),
        grad_level=(grad_down, anywhere), grad_mix=(grad_mix, anywhere),
        normed_turned=(normed_turned, anywhere), weights=(first, anywhere), branch_low=(branch_low, anywhere),
        tokens=(tokens, whole(tokens)), scale=(scale, whole(scale)), input_gain=(input_gain, whole(input_gain)),
        second_part=(second_part, whole(second_part)),
    )
    small = width + LANES + states2 + 2 * (hidden // 8)
    shared = states2 + KEYVAL_HEADS * LANES
    outs = dict(
        input_grad=(own_rows, hidden), out_gate_up=(unit, grad_gate_up.shape[1]), out_down=(unit, grad_down.shape[1]),
        out_mix=(unit, grad_mix.shape[1]), out_first=(unit, ssm_wide + qkv_wide), small_out=(8, small),
        shared_out=(unit, shared),
    )
    cut = (ssm_wide + qkv_wide) // (2 * LANES) * LANES
    ffn = grad_down.shape[1]
    split_at, most = ffn // (2 * LANES) * LANES, 3 * ffn // (2 * LANES) * LANES
    every = lambda a: slice(0, a)
    pieces = [
        ("grad_gate_up", slice(0, most), 0, "out_gate_up", slice(0, most)),
        ("grad_gate_up", slice(most, 2 * ffn), 1, "out_gate_up", slice(most, 2 * ffn)),
        ("grad_mix", every(grad_mix.shape[1]), 1, "out_mix", every(grad_mix.shape[1])),
        ("grad_first", slice(0, cut), 0, "out_first", slice(0, cut)),
        ("grad_first", slice(cut, ssm_wide + qkv_wide), 1, "out_first", slice(cut, ssm_wide + qkv_wide)),
        ("level_done", slice(0, split_at), 0, "out_down", slice(0, split_at)),
        ("level_done", slice(split_at, ffn), 1, "out_down", slice(split_at, ffn)),
    ]
    steps, stages = (tensors - 1).bit_length(), (count - 1).bit_length() + (tensors - 1).bit_length()
    inner = (total // 16, LANES)
    f32 = lambda *dims: pltpu.VMEM(dims, F32)
    low = lambda *dims: pltpu.VMEM(dims, BF)
    dma = lambda n: pltpu.SemaphoreType.DMA((n,))
    scratch = dict(
        dk_acc=f32(total, kv_wide), dv_acc=f32(total, kv_wide), qkv_grad=low(total, qkv_wide), inner_rows=f32(*inner),
        inner_sum=f32(*inner), inner_own=f32(steps + 1, *inner), inner_in=f32(steps, *inner), inner_send=dma(steps),
        inner_recv=dma(steps), xbuf=f32(CHUNK + 8, width), bcbuf=f32(CHUNK + 8, states2), dxbuf=f32(CHUNK + 8, width),
        dbcbuf=f32(CHUNK + 8, states2), dmemory=f32(states2 // 2, width), ssm_grad=low(total, ssm_wide),
        x_sums=f32(8, width), state_sums=f32(8, states2), head_sums=f32(8, LANES),
        held=low(hidden, ssm_wide + qkv_wide), grad_first=low(hidden, ssm_wide + qkv_wide), branch_own=low(own_rows, hidden),
        normed_part=low(total, hidden), normed_in=low(tensors - 1, own_rows, hidden), gain_sum=f32(8, hidden),
        sums=f32(stages + 1, 8, small), sums_in=f32(stages, 8, small), sum_send=dma(stages), sum_recv=dma(stages),
        shared=f32(steps + 1, unit, shared), shared_in=f32(steps, unit, shared), half_send=dma(steps),
        half_recv=dma(steps), core_send=dma(tensors - 1), core_recv=dma(tensors - 1), local_sems=dma(3), turned=low(hidden, total),
        own_sems=pltpu.SemaphoreType.DMA((3, 2 * levels)),
        level_in=low(levels - 1, 4 * unit, ffn), level_sum=low(levels // 2, 4 * unit, ffn), level_done=low(4 * unit, ffn),
        level_send=dma(levels - 1), level_recv=dma(levels - 1), level_local=dma(levels // 2),
        send_sems=dma(4 * levels * len(pieces)), recv_sems=dma(4 * levels * len(pieces)),
    )
    for i, piece in enumerate(pieces):
        columns = piece[1].stop - piece[1].start
        scratch.update({
            "cross%d" % i: low(levels, unit, columns), "along_x%d" % i: low(levels, unit, columns),
            "along_y%d" % i: low(levels, unit, columns), "inbound%d" % i: low(levels - 1, unit, columns),
        })
        if i < 3:
            scratch["own%d" % i] = low(2 * levels, unit, columns)
    names = list(ins) + list(outs) + list(scratch)
    odd = levels // 2
    level_steps = [blocks + chunks * (k + 1) // odd - (k + 1 < odd) for k in range(odd)]
    c = types.SimpleNamespace(
        names=names, pieces=pieces, early=3, flat=5, level_steps=level_steps, count=count, tensors=tensors, unit=unit, blocks=blocks, chunks=chunks, tiles=tiles, tile=tile,
        groups=groups, split=width + LANES, state_at=(2 * width, 2 * width + states2), kv_at=ssm_wide + query_wide,
    )
    return pl.pallas_call(
        functools.partial(backward_kernel, c),
        grid=(blocks + chunks + levels + tiles + 1,),
        in_specs=[v[1] for v in ins.values()],
        out_specs=[vmem] * len(outs),
        out_shape=[jax.ShapeDtypeStruct(v, F32) for v in outs.values()],
        scratch_shapes=list(scratch.values()),
        compiler_params=pltpu.CompilerParams(collective_id=collective_id, has_side_effects=True, vmem_limit_bytes=VMEM_ALL),
        name="backward",
    )(*(v[0] for v in ins.values()))


def tensor_swap(values):
    return lax.ppermute(values, "tensor", [(0, 1), (1, 0)])


def tensor_pair(values):
    if lax.axis_size("tensor") == 2:
        return values, tensor_swap(values)
    return lax.psum(values.astype(F32), "tensor").astype(values.dtype), jnp.zeros_like(values)


def pad_to(values, size, axis=-1):
    pads = [(0, 0)] * values.ndim
    pads[axis] = (0, size - values.shape[axis])
    return jnp.pad(values, pads) if size > values.shape[axis] else values


def pack_kernel(
    mixer_ref, state_ref, step_ref, query_ref, keyval_ref, proj_ref, attention_ref, gate_up_ref, down_ref,
    first_ref, second_ref,
):
    unit = state_ref.shape[0]
    width, wide = mixer_ref.shape[2], -(-mixer_ref.shape[2] // LANES) * LANES
    same = (iota2((unit, unit), 0) == iota2((unit, unit), 1)).astype(BF)
    place = 0

    def put(out_ref, value, size):
        nonlocal place
        value = value.astype(BF)
        if size > value.shape[1]:
            value = jnp.concatenate([value, jnp.zeros((unit, size - value.shape[1]), BF)], axis=1)
        out_ref[:, place : place + size] = value
        place += size

    put(first_ref, mixer_ref[:, 0, :], wide)
    put(first_ref, mixer_ref[:, 1, :], wide)
    put(first_ref, state_ref[...], state_ref.shape[1])
    put(first_ref, lax.dot_general(same, step_ref[...].astype(BF), (((1,), (1,)), ((), ())), preferred_element_type=F32), LANES)
    query_wide = -(-query_ref.shape[1] // LANES) * LANES
    put(first_ref, query_ref[...], query_wide)
    put(first_ref, keyval_ref[...], keyval_ref.shape[1])
    put(first_ref, proj_ref[...], wide)
    put(first_ref, attention_ref[...], query_wide)
    place = 0
    put(second_ref, gate_up_ref[:, 0, :], gate_up_ref.shape[2])
    put(second_ref, gate_up_ref[:, 1, :], gate_up_ref.shape[2])
    put(second_ref, down_ref[...], down_ref.shape[1])


def pack_weights(mixer, state, step, query, keyval, proj, attention, gate_up, down):
    unit = state.shape[0]
    lanes = lambda size: -(-size // LANES) * LANES
    first = 3 * lanes(mixer.shape[2]) + state.shape[1] + LANES + 2 * lanes(query.shape[1]) + keyval.shape[1]
    second = 2 * gate_up.shape[2] + down.shape[1]
    whole = lambda shape: spec(shape, lambda i: (0,) * len(shape))
    weights = (mixer, state, step, query, keyval, proj, attention, gate_up, down)
    return pl.pallas_call(
        pack_kernel,
        grid=(1,),
        in_specs=[whole(v.shape) for v in weights],
        out_specs=[whole((unit, first)), whole((unit, second))],
        out_shape=[jax.ShapeDtypeStruct((unit, first), BF), jax.ShapeDtypeStruct((unit, second), BF)],
        compiler_params=pltpu.CompilerParams(vmem_limit_bytes=VMEM_WHOLE),
        name="pack_weights",
    )(*weights)


def table_kernel(
    docs_ref, conv_ref, conv_bias_ref, state_conv_ref, state_bias_ref, step_bias_ref, decay_ref, skip_ref,
    feats_ref, cos_ref, sin_ref, taps_ref, state_taps_ref, heads_ref,
):
    total = docs_ref.shape[1]
    docs = docs_ref[...]
    tall = jnp.broadcast_to(docs, (LANES, total)).T
    spot = iota2((1, total), 1)
    begin = jnp.sum((tall[:, 0:1] < docs).astype(F32), axis=0, keepdims=True)
    rows = [docs]
    eight = jnp.broadcast_to(docs, (8, total))
    for k in (1, 2, 3):
        rows.append(jnp.where(spot >= k, (pltpu.roll(eight, k, 1)[0:1] == docs).astype(F32), 0.0))
    blocks = [docs[:, i : i + CHUNK] for i in range(0, total, CHUNK)]
    before = [jnp.full((1, 1), -1.0, F32)] + [v[:, CHUNK - 1 :] for v in blocks[:-1]]
    rows.append(jnp.concatenate([(v == w).astype(F32) for v, w in zip(blocks, before)], axis=1))
    rows.append(jnp.concatenate([(v == v[:, CHUNK - 1 :]).astype(F32) for v in blocks], axis=1))
    for k in (1, 2, 3):
        rows.append(jnp.where(spot < total - k, (pltpu.roll(eight, total - k, 1)[0:1] == docs).astype(F32), 0.0))
    rows.append(spot.astype(F32) - begin)
    rows.append(jnp.zeros((LANES - len(rows), total), F32))
    feats = jnp.concatenate(rows, axis=0).T
    feats_ref[...] = feats
    lane = iota2((1, LANES), 1)
    rates = jnp.exp((lane % (HEAD_SIZE // 2)).astype(F32) * (-2.0 * math.log(THETA) / HEAD_SIZE))
    angles = feats[:, 9:10] * rates
    cos_ref[...] = jnp.cos(angles)
    sin_ref[...] = jnp.sin(angles) * jnp.where(lane % HEAD_SIZE < HEAD_SIZE // 2, -1.0, 1.0)
    width, heads = conv_ref.shape[1], skip_ref.shape[1]
    taps_ref[...] = jnp.zeros_like(taps_ref)
    taps_ref[0:4, :width] = conv_ref[...]
    taps_ref[4:5, :width] = conv_bias_ref[...]
    spread = (iota2((heads, width), 0) == iota2((heads, width), 1) // (width // heads)).astype(F32)
    taps_ref[5:6, :width] = exact_mm(jnp.broadcast_to(skip_ref[...], (8, heads)), spread)[0:1]
    state_taps_ref[...] = jnp.zeros_like(state_taps_ref)
    state_taps_ref[0:4, :] = state_conv_ref[...]
    state_taps_ref[4:5, :] = state_bias_ref[...]
    heads_ref[...] = jnp.zeros_like(heads_ref)
    heads_ref[0:1, :heads] = step_bias_ref[...]
    heads_ref[1:2, :heads] = -jnp.exp(decay_ref[...])


def second_norm_kernel(tokens_ref, part_ref, part_in_ref, gain_ref, middle_ref, second_ref, scale_ref):
    middle = tokens_ref[...].astype(F32) + part_ref[...].astype(F32) + part_in_ref[...].astype(F32)
    scale = lax.rsqrt(jnp.mean(middle * middle, axis=1, keepdims=True) + EPS)
    middle_ref[...] = middle
    scale_ref[...] = scale
    second_ref[...] = (middle * scale * gain_ref[...]).astype(BF)


def by_rows(kernel, name, rows, count, ins, outs, scalars=(), tensors=1, limit=VMEM_LIMIT):
    number = len(scalars)

    def place(shape, kind):
        if kind == "whole":
            return spec(shape, lambda i, *s: (0,) * len(shape))
        if kind == "own":
            own = shape[0] // rows if shape[0] < rows * count else count // tensors
            if shape[0] < rows * count:
                return spec((rows, shape[1]), lambda i, *s: (jnp.clip(i - s[0][0] * own, 0, own - 1), 0))
            return spec((rows, shape[1]), lambda i, *s: (jnp.clip(i, s[0][0] * own, s[0][0] * own + own - 1), 0))
        return spec((rows, shape[1]), lambda i, *s: (i, 0))

    return pl.pallas_call(
        kernel,
        grid_spec=pltpu.PrefetchScalarGridSpec(
            num_scalar_prefetch=number,
            grid=(count,),
            in_specs=[place(v.shape, kind) for v, kind in ins],
            out_specs=[place((r, c), kind) for r, c, _, kind in outs],
        ),
        out_shape=[jax.ShapeDtypeStruct((r, c), dtype) for r, c, dtype, _ in outs],
        compiler_params=pltpu.CompilerParams(vmem_limit_bytes=limit),
        name=name,
    )(*scalars, *(v for v, _ in ins))


def ffn_kernel(second_ref, up_ref, weights_ref, active_ref, grads_ref, out_ref, back_ref):
    ffn = active_ref.shape[1]
    gate_vals = jnp.dot(second_ref[...], weights_ref[:, : 2 * ffn], preferred_element_type=F32)
    active_grad = jnp.dot(up_ref[...], weights_ref[:, 2 * ffn :], preferred_element_type=F32)
    gate, up = gate_vals[:, :ffn], gate_vals[:, ffn:]
    sig = sigmoid(gate)
    silu = gate * sig
    active = (silu * up).astype(BF)
    active_ref[...] = active
    grads_ref[:, :ffn] = (active_grad * up * (sig + silu * (1.0 - sig))).astype(BF)
    grads_ref[:, ffn:] = (active_grad * silu).astype(BF)
    out_ref[...] = mm_nt(active, weights_ref[:, 2 * ffn :]).astype(BF)
    back_ref[...] = mm_nt(grads_ref[...], weights_ref[:, : 2 * ffn]).astype(BF)


def second_back_kernel(
    own_count, core_ref, grad_ref, grad_in_ref, middle_ref, scale_ref, up_ref, gain_ref, part_ref, part_in_ref, low_ref, gain_grad_ref, out_ref
):
    offset = pl.program_id(0) - core_ref[0] * own_count

    @pl.when(pl.program_id(0) == 0)
    def _():
        gain_grad_ref[...] = jnp.zeros_like(gain_grad_ref)

    grad = grad_ref[...].astype(F32) + grad_in_ref[...].astype(F32)
    middle, scale = middle_ref[...], scale_ref[...]
    shape = middle * scale
    weighted = grad * gain_ref[...]
    inner = jnp.mean(weighted * shape, axis=1, keepdims=True)
    low_ref[...] = (up_ref[...].astype(F32) + scale * (weighted - shape * inner)).astype(BF)
    gain_grad_ref[0:1, :] += jnp.sum(grad * shape, axis=0, keepdims=True)

    @pl.when((offset >= 0) & (offset < own_count))
    def _():
        out_ref[...] = (middle + part_ref[...].astype(F32) + part_in_ref[...].astype(F32)).astype(BF)


def finish_kernel(
    sizes, first_ref, mix_ref, shared_ref, small_ref, gate_up_sum_ref, down_sum_ref, input_grad_ref,
    mixer_ref, state_ref, step_ref, conv_ref, conv_bias_ref, state_conv_ref, state_bias_ref, step_bias_ref, decay_ref, skip_ref,
    mixer_gain_ref, proj_ref, query_ref, keyval_ref, attention_ref, gate_up_ref, down_ref, second_gain_ref, input_gain_ref, input_back_ref,
):
    wide, width, states2, heads, query_width, ffn = sizes
    input_back_ref[...] = input_grad_ref[...]
    mixer_ref[:, 0, :] = first_ref[:, :width]
    mixer_ref[:, 1, :] = first_ref[:, wide : wide + width]
    state_ref[...] = shared_ref[:, :states2]
    start = 2 * wide + states2
    step_ref[...] = first_ref[:, start : start + LANES].T[:heads, :]
    start = 2 * wide + states2 + LANES
    query_ref[...] = first_ref[:, start : start + query_width]
    groups = [shared_ref[:, i : i + LANES] for i in range(states2, shared_ref.shape[1], LANES)]
    keyval_ref[:, 0, :] = jnp.concatenate([v[:, :HEAD_SIZE] for v in groups], axis=1)
    keyval_ref[:, 1, :] = jnp.concatenate([v[:, HEAD_SIZE:] for v in groups], axis=1)
    proj_ref[...] = mix_ref[:, :width]
    attention_ref[...] = mix_ref[:, wide : wide + query_width]
    gate_up_ref[:, 0, :] = gate_up_sum_ref[:, :ffn]
    gate_up_ref[:, 1, :] = gate_up_sum_ref[:, ffn:]
    down_ref[...] = down_sum_ref[...]
    conv_ref[...] = small_ref[0:4, :width]
    for out_ref, row in ((conv_bias_ref, 4), (mixer_gain_ref, 6)):
        for k in range(out_ref.shape[0]):
            size = out_ref.shape[1]
            out_ref[k : k + 1, :] = small_ref[row : row + 1, k * size : (k + 1) * size]
    place = iota2((width, heads), 0) // (width // heads)
    gather = (place == iota2((width, heads), 1)).astype(F32)
    skip_ref[...] = exact_mm(jnp.broadcast_to(small_ref[5:6, :width], (8, width)), gather)[0:1]
    step_bias_ref[...] = small_ref[0:1, wide : wide + heads]
    decay_ref[...] = small_ref[1:2, wide : wide + heads]
    base = wide + LANES
    state_conv_ref[...] = small_ref[0:4, base : base + states2]
    state_bias_ref[...] = small_ref[4:5, base : base + states2]
    base += states2
    for out_ref in (second_gain_ref, input_gain_ref):
        out_ref[...] = small_ref[:, base : base + out_ref.shape[1]]
        base += out_ref.shape[1]


def body(
    layer_input, doc_ids, input_gain, mixer_weight, state_weight, step_weight, conv_weight, conv_bias, state_conv,
    state_conv_bias, step_bias, decay_log, skip_gain, mixer_gain, mixer_proj, query_weight, keyval_projection,
    attention_proj, second_gain, gate_up, down_proj, cotangent,
):
    tensor_count = lax.axis_size("tensor")
    tensor_index = lax.axis_index("tensor")
    fsdp_count = lax.axis_size("fsdp")
    own_rows, hidden = layer_input.shape
    unit = state_weight.shape[0]
    seq_count, seq_length = doc_ids.shape
    total = seq_count * seq_length
    heads = step_bias.shape[0]
    width = conv_weight.shape[1]
    wide = -(-width // LANES) * LANES
    query_width = query_weight.shape[1]
    query_wide = -(-query_width // LANES) * LANES
    query_heads = query_width // HEAD_SIZE
    per_group = QUERY_HEADS // KEYVAL_HEADS
    kv_heads = max(1, query_heads // per_group)
    kv_leading = tensor_index * query_heads // per_group
    states2 = state_weight.shape[1]
    ffn = down_proj.shape[0]
    low = lambda v: v.astype(BF)

    own_keyval = lax.dynamic_slice_in_dim(keyval_projection, kv_leading * HEAD_SIZE, kv_heads * HEAD_SIZE, 2)
    own_keyval = own_keyval.reshape(unit, 2, kv_heads, HEAD_SIZE).transpose(0, 2, 1, 3).reshape(unit, 2 * kv_heads * HEAD_SIZE)
    kv_wide = 2 * kv_heads * HEAD_SIZE
    first, rest = pack_weights(
        mixer_weight, state_weight, step_weight.T, query_weight, own_keyval, mixer_proj.T, attention_proj.T, gate_up, down_proj.T
    )
    rest = lax.all_gather(rest, "fsdp", axis=0, tiled=True)
    docs = (doc_ids + jnp.arange(seq_count, dtype=jnp.int32)[:, None] * seq_length).reshape(1, total)
    doc_row = docs.astype(F32)
    tables = (
        doc_row, conv_weight, conv_bias[None], state_conv, state_conv_bias[None], step_bias[None], decay_log[None], skip_gain[None]
    )
    first, tokens, upstream, normed, first_scale, normed_turned, feats, cos, sin, taps, state_taps, head_rows = gather_weights(
        first, layer_input, cotangent, input_gain[None], tables, wide, fsdp_count, tensor_count, 0
    )
    ssm_wide = 2 * wide + states2 + LANES
    cuts = np.cumsum([0, ssm_wide, query_wide + kv_wide, wide + query_wide])
    full_ssm, full_qkv, full_mix = (first[:, cuts[i] : cuts[i + 1]] for i in range(3))
    gain_row = pad_to(mixer_gain[None], wide)
    second_row = second_gain[None]

    ssm_in = plain_dot(normed, full_ssm)
    qkv_in = plain_dot(normed, full_qkv)
    scan, gated_low, squares, states = mamba_forward(feats, doc_row, ssm_in, taps, state_taps, head_rows, gain_row, wide, states2)
    mix, log_sums, query_rot, keys, values, squares = attention_forward(
        kv_heads, tensor_count, feats, doc_row, qkv_in, cos, sin, query_wide, gated_low, squares, 2
    )
    branch = tensor_pair(low(right_dot(mix, full_mix)))
    middle, second, second_scale = by_rows(
        second_norm_kernel, "second_norm", CHUNK, total // CHUNK,
        [(tokens, "rows"), (branch[0], "rows"), (branch[1], "rows"), (second_row, "whole")],
        [(total, hidden, F32, "rows"), (total, hidden, BF, "rows"), (total, 1, F32, "rows")],
    )
    active, gu_grad, ffn_out, second_grad = by_rows(
        ffn_kernel, "ffn", min(FFN_ROWS, total), max(total // FFN_ROWS, 1),
        [(second, "rows"), (upstream, "rows"), (rest, "whole")],
        [(total, ffn, BF, "rows"), (total, 2 * ffn, BF, "rows"), (total, hidden, BF, "rows"), (total, hidden, BF, "rows")],
        limit=VMEM_WHOLE,
    )
    second_grad, ffn_out = tensor_pair(second_grad), tensor_pair(ffn_out)
    grad_gate_up, grad_down = low(left_dot(second, gu_grad)), low(left_dot(upstream, active))
    core = jnp.full((1,), tensor_index, jnp.int32)
    rows = min(CHUNK, own_rows)
    branch_low, second_gain_part, layer_output = by_rows(
        functools.partial(second_back_kernel, own_rows // rows), "second_back", rows, total // rows,
        [
            (second_grad[0], "rows"), (second_grad[1], "rows"), (middle, "rows"), (second_scale, "rows"), (upstream, "rows"),
            (second_row, "whole"), (ffn_out[0], "own"), (ffn_out[1], "own"),
        ],
        [(total, hidden, BF, "rows"), (8, hidden, F32, "whole"), (own_rows, hidden, BF, "own")], (core,), tensor_count,
    )
    mix_grad = low(plain_dot(branch_low, full_mix))
    grad_mix = low(left_dot(branch_low, mix))
    input_back, sum_gate_up, sum_down, sum_mix, sum_first, small, shared = backward(
        kv_heads, feats, doc_row, query_rot, keys, values, log_sums, mix_grad, mix, cos, sin, squares, ssm_in, scan, states, taps,
        state_taps, head_rows, gain_row, grad_gate_up, grad_down, grad_mix, normed_turned, first, branch_low, layer_input, first_scale,
        input_gain[None], second_gain_part, wide, states2, fsdp_count, tensor_count, 1,
    )
    shape = lambda *dims: jax.ShapeDtypeStruct(dims, F32)
    folded = (width // LANES, LANES) if width % LANES == 0 else (1, width)
    parts = (sum_first, sum_mix, shared, small, sum_gate_up, sum_down, input_back)
    done = pl.pallas_call(
        functools.partial(finish_kernel, (wide, width, states2, heads, query_width, ffn)),
        grid=(1,),
        in_specs=[spec(v.shape, lambda i: (0,) * 2) for v in parts],
        out_shape=[
            shape(unit, 2, width), shape(unit, states2), shape(heads, unit), shape(4, width), shape(*folded), shape(4, states2),
            shape(1, states2), shape(1, heads), shape(1, heads), shape(1, heads), shape(*folded), shape(unit, width),
            shape(unit, query_width), shape(unit, 2, KEYVAL_HEADS * HEAD_SIZE), shape(unit, query_width), shape(unit, 2, ffn),
            shape(unit, ffn), shape(8, hidden // 8), shape(8, hidden // 8), shape(own_rows, hidden),
        ],
        compiler_params=pltpu.CompilerParams(vmem_limit_bytes=VMEM_WHOLE),
        name="finish",
    )(*parts)
    (
        mixer_sum, state_sum, step_sum, conv_sum, conv_bias_sum, state_conv_sum, state_bias_sum, step_bias_sum, decay_sum, skip_sum,
        mixer_gain_sum, proj_sum, query_sum, keyval_sum, attention_sum, gate_up_sum, down_sum, second_gain_sum, input_gain_sum, input_grad,
    ) = done
    return (
        layer_output, input_grad, input_gain_sum.reshape(hidden), mixer_sum, state_sum, step_sum.T, conv_sum, conv_bias_sum.reshape(width), state_conv_sum,
        state_bias_sum[0], step_bias_sum[0], decay_sum[0], skip_sum[0], mixer_gain_sum.reshape(width), proj_sum.T, query_sum, keyval_sum,
        attention_sum.T, second_gain_sum.reshape(hidden), gate_up_sum, down_sum.T,
    )


def solution(mesh):
    placed = (
        P(("fsdp", "tensor"), None),
        P("fsdp", None),
        P(),
        P("fsdp", None, "tensor"),
        P("fsdp", None),
        P("fsdp", "tensor"),
        P(None, "tensor"),
        P("tensor"),
        P(),
        P(),
        P("tensor"),
        P("tensor"),
        P("tensor"),
        P("tensor"),
        P("tensor", "fsdp"),
        P("fsdp", "tensor"),
        P("fsdp", None, None),
        P("tensor", "fsdp"),
        P(),
        P("fsdp", None, "tensor"),
        P("tensor", "fsdp"),
        P(("fsdp", "tensor"), None),
    )
    return jax.shard_map(
        body,
        mesh=mesh,
        in_specs=placed,
        out_specs=(
            P(("fsdp", "tensor"), None),
            P(("fsdp", "tensor"), None),
            P(),
            P("fsdp", None, "tensor"),
            P("fsdp", None),
            P("fsdp", "tensor"),
            P(None, "tensor"),
            P("tensor"),
            P(),
            P(),
            P("tensor"),
            P("tensor"),
            P("tensor"),
            P("tensor"),
            P("tensor", "fsdp"),
            P("fsdp", "tensor"),
            P("fsdp", None, None),
            P("tensor", "fsdp"),
            P(),
            P("fsdp", None, "tensor"),
            P("tensor", "fsdp"),
        ),
        check_vma=False,
    )
```

```python
import functools
import math
import types

import jax
import jax.numpy as jnp
import ml_dtypes
import numpy as np
from jax import lax
from jax.experimental import pallas as pl
from jax.experimental.pallas import tpu as pltpu
from jax.sharding import PartitionSpec as P

QUERY_HEADS = 8
KEYVAL_HEADS = 2
HEAD_SIZE = 64
DSSM = 1536
EPS = 1e-05
THETA = 100000000000.0

LANES = 128
CHUNK = 128
FFN_ROWS = 256
QBLOCK = 256
VMEM_LIMIT = 32 * 2**20
VMEM_WHOLE = 60 * 2**20
VMEM_ALL = 63 * 2**20
MASKED = -1e30
BF, F32 = jnp.bfloat16, jnp.float32


def left_dot(left_side, right_side):
    return lax.dot_general(left_side, right_side, (((0,), (0,)), ((), ())), preferred_element_type=F32)


def right_dot(left_side, right_side):
    return lax.dot_general(left_side, right_side, (((1,), (1,)), ((), ())), preferred_element_type=F32)


def plain_dot(left_side, right_side):
    return jnp.dot(left_side, right_side, preferred_element_type=F32)


def mm(a, b):
    return jnp.dot(a.astype(BF), b.astype(BF), preferred_element_type=F32)


def mm_nt(a, b):
    return lax.dot_general(a.astype(BF), b.astype(BF), (((1,), (1,)), ((), ())), preferred_element_type=F32)


def mm_tn(a, b):
    return lax.dot_general(a.astype(BF), b.astype(BF), (((0,), (0,)), ((), ())), preferred_element_type=F32)


def exact_mm(a, b):
    return jnp.dot(a, b, precision=lax.Precision.HIGHEST, preferred_element_type=F32)


def sigmoid(v):
    return 1.0 / (1.0 + jnp.exp(-v))


def softplus(v):
    return jnp.maximum(v, 0.0) + jnp.log1p(jnp.exp(-jnp.abs(v)))


def split_lanes(values, axis):
    high = values.astype(BF)
    low = (values - high.astype(F32)).astype(BF)
    return jnp.concatenate([high, low], axis=axis)


def iota2(shape, axis):
    return lax.broadcasted_iota(jnp.int32, shape, axis)


def flipped(index, mask):
    bit = 1
    while bit <= mask:
        if mask & bit:
            index = index + bit * (1 - 2 * ((index // bit) % 2))
        bit *= 2
    return index


def greet(partners):
    barrier = pltpu.get_barrier_semaphore()
    for axis, place in partners:
        pl.semaphore_signal(barrier, inc=1, device_id={axis: place}, device_id_type=pl.DeviceIdType.MESH)
    pl.semaphore_wait(barrier, len(partners))


def remote(source, target, send, recv, axis, place):
    return pltpu.make_async_remote_copy(
        src_ref=source, dst_ref=target, send_sem=send, recv_sem=recv,
        device_id={axis: place}, device_id_type=pl.DeviceIdType.MESH,
    )


class TensorSum:
    def __init__(self, tensors, own, arrived, send, recv):
        self.core = lax.axis_index("tensor")
        self.places = [flipped(self.core, 1 << k) for k in range((tensors - 1).bit_length())]
        self.refs = own, arrived, send, recv

    def copy(self, k):
        own, arrived, send, recv = self.refs
        return remote(own.at[k], arrived.at[k], send.at[k], recv.at[k], "tensor", self.places[k])

    def begin(self, value, met=False):
        if not met:
            greet([("tensor", place) for place in self.places])
        self.refs[0][0] = value
        self.copy(0).start()

    def end(self):
        own, arrived, _, _ = self.refs
        for k in range(len(self.places)):
            copy = self.copy(k)
            if k:
                copy.start()
            copy.wait()
            own[k + 1] = own[k] + arrived[k]
        return own[len(self.places)]


def tensor_sum_scratch(tensors, shape):
    steps = (tensors - 1).bit_length()
    return [
        pltpu.VMEM((steps + 1,) + shape, F32), pltpu.VMEM((steps,) + shape, F32),
        pltpu.SemaphoreType.DMA((steps,)), pltpu.SemaphoreType.DMA((steps,)),
    ]


def conv_taps(buffer, feats, taps, bias, rows):
    total = buffer[8 : 8 + rows, :] * taps[3:4, :] + bias
    for k in range(1, 4):
        total = total + buffer[8 - k : 8 - k + rows, :] * feats[:, k : k + 1] * taps[3 - k : 4 - k, :]
    return total


def step_parts(step_ref, heads_ref, feats, rows):
    raw = step_ref[...] + heads_ref[0:1, :]
    step = softplus(raw)
    lower = (iota2((rows, rows), 0) >= iota2((rows, rows), 1)).astype(F32)
    log_decay = exact_mm(lower, step * heads_ref[1:2, :])
    last = log_decay[rows - 1 : rows, :]
    enter = jnp.exp(log_decay) * feats[:, 4:5]
    leave = jnp.exp(last - log_decay) * feats[:, 5:6]
    return raw, step, log_decay, enter, leave


def gated_scale(squares):
    return lax.rsqrt(squares / DSSM + EPS)


def as_column(row):
    return jnp.broadcast_to(row, (LANES, row.shape[1])).T[:, 0:1]


def mamba_fwd_kernel(
    feats_ref, docs_ref, x_ref, bc_ref, step_ref, z_ref, taps_ref, staps_ref, heads_ref, expand_ref,
    gain_ref, scan_ref, low_ref, square_ref, states_ref, xbuf, bcbuf, memory,
):
    rows, width = x_ref.shape
    states = bc_ref.shape[1] // 2

    @pl.when(pl.program_id(0) == 0)
    def _():
        xbuf[0:8, :] = jnp.zeros((8, width), F32)
        bcbuf[0:8, :] = jnp.zeros((8, 2 * states), F32)
        memory[...] = jnp.zeros_like(memory)

    feats = feats_ref[...]
    xbuf[8 : 8 + rows, :] = x_ref[...]
    bcbuf[8 : 8 + rows, :] = bc_ref[...]
    pre = conv_taps(xbuf, feats, taps_ref, taps_ref[4:5, :], rows)
    values = pre * sigmoid(pre)
    pre_bc = conv_taps(bcbuf, feats, staps_ref, staps_ref[4:5, :], rows)
    both = pre_bc * sigmoid(pre_bc)
    xbuf[0:8, :] = xbuf[rows : rows + 8, :]
    bcbuf[0:8, :] = bcbuf[rows : rows + 8, :]
    key_in = both[:, :states].astype(BF)
    key_out = both[:, states:].astype(BF)
    _, step, log_decay, enter, leave = step_parts(step_ref, heads_ref, feats, rows)
    expanded = jnp.dot(
        split_lanes(jnp.concatenate([step, enter, leave], axis=0), 1), expand_ref[...], preferred_element_type=F32
    )
    step_w, enter_w, leave_w = expanded[:rows], expanded[rows : 2 * rows], expanded[2 * rows :]
    scaled = values * step_w
    gram = mm_nt(key_out, key_in)
    allowed = (feats[:, 0:1] == docs_ref[...]) & (iota2((rows, rows), 0) >= iota2((rows, rows), 1))
    bias = jnp.where(allowed, 0.0, MASKED)
    log_rows = log_decay.T
    front = iota2((rows, LANES), 1) < LANES // 2
    held = memory[...]
    states_ref[0] = held.astype(BF)
    carried = mm(key_out, held) * enter_w
    fresh = mm_tn(key_in, leave_w * scaled)
    memory[...] = held * enter_w[rows - 1 : rows, :] + fresh
    squares = jnp.zeros((rows, 1), F32)
    for pair in range(width // LANES):
        lanes = slice(pair * LANES, (pair + 1) * LANES)
        mixes = []
        for h in (2 * pair, 2 * pair + 1):
            decay = jnp.exp(log_decay[:, h : h + 1] - log_rows[h : h + 1, :] + bias)
            mixes.append((gram * decay).astype(BF))
        part = scaled[:, lanes]
        stacked = jnp.concatenate([jnp.where(front, part, 0.0), jnp.where(front, 0.0, part)], axis=0)
        inside = mm(jnp.concatenate(mixes, axis=1), stacked)
        scan = inside + carried[:, lanes] + values[:, lanes] * taps_ref[5:6, lanes]
        scan_ref[:, lanes] = scan
        z = z_ref[:, lanes]
        gated = scan * (z * sigmoid(z))
        low_ref[:, lanes] = (gated * gain_ref[:, lanes]).astype(BF)
        squares = squares + jnp.sum(gated * gated, axis=1, keepdims=True)
    square_ref[...] = jnp.broadcast_to(squares, (rows, LANES)).T[0:8, :]


def mamba_bwd_block(
    feats_ref, square_ref, inner_sum, block, docs_ref, x_ref, x_before_ref, bc_ref, bc_before_ref, step_ref, z_ref, scan_ref, states_ref, norm_grad_ref,
    taps_ref, staps_ref, heads_ref, expand_ref, reduce_ref, gain_ref,
    grads_ref, sums_ref, ssums_ref, hsums_ref,
    xbuf, bcbuf, dxbuf, dbcbuf, dmemory,
):
    rows, width = x_ref.shape
    states = bc_ref.shape[1] // 2

    feats = feats_ref[...]
    xbuf[0:8, :] = x_before_ref[...]
    bcbuf[0:8, :] = bc_before_ref[...]
    xbuf[8 : 8 + rows, :] = x_ref[...]
    bcbuf[8 : 8 + rows, :] = bc_ref[...]
    pre = conv_taps(xbuf, feats, taps_ref, taps_ref[4:5, :], rows)
    pre_gate = sigmoid(pre)
    values = pre * pre_gate
    pre_bc = conv_taps(bcbuf, feats, staps_ref, staps_ref[4:5, :], rows)
    bc_gate = sigmoid(pre_bc)
    both = pre_bc * bc_gate
    key_in = both[:, :states].astype(BF)
    key_out = both[:, states:].astype(BF)
    raw, step, log_decay, enter, leave = step_parts(step_ref, heads_ref, feats, rows)
    expanded = jnp.dot(
        split_lanes(jnp.concatenate([step, enter, leave], axis=0), 1), expand_ref[...], preferred_element_type=F32
    )
    step_w, enter_w, leave_w = expanded[:rows], expanded[rows : 2 * rows], expanded[2 * rows :]
    scaled = values * step_w
    z = z_ref[...]
    z_gate = sigmoid(z)
    z_silu = z * z_gate
    scan = scan_ref[...]
    gated = scan * z_silu
    norm_grad = norm_grad_ref[...].astype(F32)
    row_scale = gated_scale(square_ref[0:1, :])
    row_inner = inner_sum[pl.ds(pl.multiple_of(block * 8, 8), 8), :][0:1, :] * row_scale * row_scale / DSSM
    scale, coefficient = as_column(row_scale), as_column(row_inner)
    weighted = norm_grad * scale
    gated_grad = weighted * gain_ref[...] - gated * coefficient
    dscan = gated_grad * z_silu
    grads_ref[:, 0:width] = (gated_grad * scan * (z_gate * (1.0 + z * (1.0 - z_gate)))).astype(BF)
    sums_ref[6:7, :] += jnp.sum(weighted * gated, axis=0, keepdims=True)
    sums_ref[5:6, :] += jnp.sum(dscan * values, axis=0, keepdims=True)
    held = states_ref[0]
    dheld = dmemory[...]
    dheld_low = dheld.astype(BF)
    enter_grad = (dscan * enter_w).astype(BF)
    left = leave_w * scaled
    passed = mm(key_in, dheld_low)
    arrived = mm(key_out, held)
    dkey_out = mm_nt(enter_grad, held)
    dkey_in = mm_nt(left, dheld_low)
    carry = enter_w[rows - 1 : rows, :]
    dmemory[...] = dheld * carry + mm_tn(key_out, enter_grad)
    enter_terms = dscan * enter_w * arrived
    leave_terms = left * passed
    carry_terms = jnp.sum(dheld * held.astype(F32), axis=0, keepdims=True) * carry
    gram = mm_nt(key_in, key_out)
    allowed = (feats[:, 0:1] == docs_ref[...]) & (iota2((rows, rows), 0) <= iota2((rows, rows), 1))
    bias = jnp.where(allowed, 0.0, MASKED)
    log_rows = log_decay.T
    front = iota2((rows, LANES), 1) < LANES // 2
    gram_grad = jnp.zeros((rows, rows), F32)
    lane_of = iota2((rows, LANES), 1)
    row_of = iota2((LANES, rows), 0)
    sent = jnp.zeros((rows, LANES), F32)
    received = jnp.zeros((LANES, rows), F32)
    inside_grads = []
    for pair in range(width // LANES):
        lanes = slice(pair * LANES, (pair + 1) * LANES)
        dy = dscan[:, lanes].astype(BF)
        part = scaled[:, lanes]
        stacked = jnp.concatenate([jnp.where(front, part, 0.0), jnp.where(front, 0.0, part)], axis=0)
        cross = mm_nt(stacked, dy)
        mixes = []
        for j, h in enumerate((2 * pair, 2 * pair + 1)):
            decay = jnp.exp(log_rows[h : h + 1, :] - log_decay[:, h : h + 1] + bias)
            mix = gram * decay
            mixes.append(mix.astype(BF))
            dmix = cross[j * rows : (j + 1) * rows, :]
            gram_grad = gram_grad + dmix * decay
            flow = dmix * mix
            sent = jnp.where(lane_of == h, jnp.sum(flow, axis=1, keepdims=True), sent)
            received = jnp.where(row_of == h, jnp.sum(flow, axis=0, keepdims=True), received)
        grads = mm(jnp.concatenate(mixes, axis=0), dy)
        inside_grads.append(jnp.where(front, grads[:rows], grads[rows:]))
    dscaled = jnp.concatenate(inside_grads, axis=1) + leave_w * passed
    dkey_in = dkey_in + mm(gram_grad, key_out)
    dkey_out = dkey_out + mm_tn(gram_grad, key_in)
    reduced = jnp.dot(
        split_lanes(
            jnp.concatenate([enter_terms, leave_terms, dscaled * values, jnp.broadcast_to(carry_terms, (8, width))], axis=0), 1
        ),
        reduce_ref[...],
        preferred_element_type=F32,
    )
    after = reduced[:rows] + received.T - sent
    upper = (iota2((rows, rows), 0) <= iota2((rows, rows), 1)).astype(F32)
    strict = (iota2((rows, rows), 0) > iota2((rows, rows), 1)).astype(F32)
    decay_grad = exact_mm(upper, after) + exact_mm(strict, reduced[rows : 2 * rows]) + reduced[3 * rows : 3 * rows + 1]
    dstep = decay_grad * heads_ref[1:2, :] + reduced[2 * rows : 3 * rows]
    draw = dstep * sigmoid(raw)
    grads_ref[:, 2 * width + 2 * states :] = draw.astype(BF)
    hsums_ref[0:1, :] += jnp.sum(draw, axis=0, keepdims=True)
    hsums_ref[1:2, :] += jnp.sum(decay_grad * step, axis=0, keepdims=True) * heads_ref[1:2, :]
    dvalues = dscaled * step_w + dscan * taps_ref[5:6, :]
    dpre = dvalues * (pre_gate * (1.0 + pre * (1.0 - pre_gate)))
    dboth = jnp.concatenate([dkey_in, dkey_out], axis=1)
    dpre_bc = dboth * (bc_gate * (1.0 + pre_bc * (1.0 - bc_gate)))
    for dpre_now, buffer, dbuffer, taps, totals, lanes in (
        (dpre, xbuf, dxbuf, taps_ref, sums_ref, slice(width, 2 * width)),
        (dpre_bc, bcbuf, dbcbuf, staps_ref, ssums_ref, slice(2 * width, 2 * width + 2 * states)),
    ):
        dbuffer[0:rows, :] = dpre_now
        grad = dpre_now * taps[3:4, :]
        totals[3:4, :] += jnp.sum(dpre_now * buffer[8 : 8 + rows, :], axis=0, keepdims=True)
        totals[4:5, :] += jnp.sum(dpre_now, axis=0, keepdims=True)
        for k in range(1, 4):
            grad = grad + dbuffer[k : k + rows, :] * feats[:, 5 + k : 6 + k] * taps[3 - k : 4 - k, :]
            totals[3 - k : 4 - k, :] += jnp.sum(
                dpre_now * buffer[8 - k : 8 - k + rows, :] * feats[:, k : k + 1], axis=0, keepdims=True
            )
        grads_ref[:, lanes] = grad.astype(BF)
        dbuffer[rows : rows + 8, :] = dbuffer[0:8, :]


def expand_matrix(width):
    one = np.arange(LANES)[:, None] == np.arange(width)[None, :] // (LANES // 2)
    return np.concatenate([one, one], axis=0).astype(ml_dtypes.bfloat16)


def spec(block, index):
    return pl.BlockSpec(block, index)


def mamba_forward(feats, doc_row, ssm_in, taps, staps, heads, gain, width, states2):
    total = ssm_in.shape[0]
    rows = CHUNK
    count = total // rows
    block = lambda w, place=0: spec((rows, w), lambda i: (i, place))
    whole = lambda a: spec(a.shape, lambda i: (0,) * a.ndim)
    expand = expand_matrix(width)
    return pl.pallas_call(
        mamba_fwd_kernel,
        grid=(count,),
        in_specs=[
            block(LANES), spec((1, rows), lambda i: (0, i)), block(width, 1), block(states2, 2 * width // states2),
            block(LANES, (2 * width + states2) // LANES), block(width), whole(taps), whole(staps), whole(heads), whole(expand), whole(gain),
        ],
        out_specs=[block(width), block(width), spec((8, LANES), lambda i: (i, 0)), spec((1, states2 // 2, width), lambda i: (i, 0, 0))],
        out_shape=[
            jax.ShapeDtypeStruct((total, width), F32),
            jax.ShapeDtypeStruct((total, width), BF),
            jax.ShapeDtypeStruct((8 * count, LANES), F32),
            jax.ShapeDtypeStruct((count, states2 // 2, width), BF),
        ],
        scratch_shapes=[
            pltpu.VMEM((rows + 8, width), F32), pltpu.VMEM((rows + 8, states2), F32), pltpu.VMEM((states2 // 2, width), F32),
        ],
        compiler_params=pltpu.CompilerParams(vmem_limit_bytes=VMEM_LIMIT),
        cost_estimate=pl.CostEstimate(flops=20 * 10**9, bytes_accessed=total * width * 20, transcendentals=total * width * 4),
        name="mamba_fwd",
    )(feats, doc_row, ssm_in, ssm_in, ssm_in, ssm_in, taps, staps, heads, expand, gain)


def swap_halves(values):
    lane = iota2(values.shape, 1) % (LANES // 2)
    return jnp.where(lane < LANES // 4, pltpu.roll(values, LANES - LANES // 4, 1), pltpu.roll(values, LANES // 4, 1))


def stack_heads(part):
    front = iota2(part.shape, 1) < LANES // 2
    zero = jnp.zeros_like(part)
    return jnp.concatenate([jnp.where(front, part, zero), jnp.where(front, zero, part)], axis=0)


def attention_fwd_kernel(
    groups, tensors, docs_col_ref, docs_ref, q_ref, kv_ref, cos_ref, sin_ref, low_ref, square_ref, out_ref, lse_ref, qrot_ref, keys_ref, values_ref, square_out_ref, *scratch,
):
    total = q_ref.shape[0]
    wide = low_ref.shape[1]
    exchange = TensorSum(tensors, *scratch)
    exchange.begin(square_ref[...])
    pairs = q_ref.shape[1] // LANES
    block = min(QBLOCK, total)
    cos, sin = cos_ref[...], sin_ref[...]
    front = iota2((total, LANES), 1) < LANES // 2
    for g in range(groups):
        lanes = slice(g * LANES, (g + 1) * LANES)
        raw = kv_ref[:, lanes]
        turned = raw * cos + swap_halves(raw) * sin
        keys_ref[:, lanes] = jnp.where(front, turned, pltpu.roll(turned, LANES // 2, 1)).astype(BF)
        values_ref[:, lanes] = jnp.where(front, pltpu.roll(raw, LANES // 2, 1), raw).astype(BF)
    for p in range(pairs):
        lanes = slice(p * LANES, (p + 1) * LANES)
        raw = q_ref[:, lanes]
        qrot_ref[:, lanes] = ((raw * cos + swap_halves(raw) * sin).astype(BF).astype(F32) * (LANES // 2) ** -0.5).astype(BF)
    front = iota2((block, LANES), 1) < LANES // 2
    lane_of = iota2((block, LANES), 1)
    for start in range(0, total, block):
        rows, end = slice(start, start + block), start + block
        allowed = (docs_col_ref[rows, 0:1] == docs_ref[:, :end]) & (
            iota2((block, end), 0) + start >= iota2((block, end), 1)
        )
        bias = jnp.where(allowed, 0.0, MASKED)
        bias = jnp.concatenate([bias, bias], axis=0)
        sums = jnp.zeros((block, LANES), F32)
        for p in range(pairs):
            lanes = slice(p * LANES, (p + 1) * LANES)
            g = p * groups // pairs
            kv = slice(g * LANES, (g + 1) * LANES)
            scores = mm_nt(stack_heads(qrot_ref[rows, lanes]), keys_ref[:end, kv]) + bias
            top = jnp.max(scores, axis=1, keepdims=True)
            raised = jnp.exp(scores - top)
            whole = jnp.sum(raised, axis=1, keepdims=True)
            mixed = mm(raised, values_ref[:end, kv]) / whole
            out_ref[rows, wide + p * LANES : wide + (p + 1) * LANES] = jnp.where(front, mixed[:block], mixed[block:]).astype(BF)
            logs = top + jnp.log(whole)
            sums = jnp.where(lane_of == 2 * p, logs[:block], sums)
            sums = jnp.where(lane_of == 2 * p + 1, logs[block:], sums)
        lse_ref[rows, :] = sums
    square_out_ref[...] = exchange.end()
    for i in range(total // LANES):
        piece = slice(i * LANES, (i + 1) * LANES)
        scale = as_column(gated_scale(square_out_ref[8 * i : 8 * i + 1, :]))
        out_ref[piece, :wide] = (low_ref[piece, :].astype(F32) * scale).astype(BF)


def attention_bwd_block(
    start, groups, docs_col_ref, docs_ref, qrot_ref, keys_ref, values_ref, lse_ref, up_ref, cos_ref, sin_ref, grads_ref, dk_acc, dv_acc,
):
    pairs = qrot_ref.shape[1] // LANES
    block = up_ref.shape[0]
    front = iota2((block, LANES), 1) < LANES // 2
    rows, end = slice(start, start + block), start + block
    allowed = (docs_col_ref[:end, 0:1] == docs_ref[:, rows]) & (
        iota2((end, block), 0) <= iota2((end, block), 1) + start
    )
    bias = jnp.where(allowed, 0.0, MASKED)
    logs = lse_ref[...].T
    cos, sin = cos_ref[rows, :], sin_ref[rows, :]
    for p in range(pairs):
        lanes = slice(p * LANES, (p + 1) * LANES)
        g = p * groups // pairs
        kv = slice(g * LANES, (g + 1) * LANES)
        keys, values = keys_ref[:end, kv], values_ref[:end, kv]
        queries = stack_heads(qrot_ref[rows, lanes])
        ups = stack_heads(up_ref[:, lanes])
        shift = jnp.concatenate([bias - logs[2 * p : 2 * p + 1], bias - logs[2 * p + 1 : 2 * p + 2]], axis=1)
        probs = jnp.exp(mm_nt(keys, queries) + shift)
        grads = mm_nt(values, ups)
        centre = jnp.sum(probs * grads, axis=0, keepdims=True)
        score_grads = (probs * (grads - centre)).astype(BF)
        dk_acc[:end, kv] += mm(score_grads, queries)
        dv_acc[:end, kv] += mm(probs, ups)
        dq = mm_tn(score_grads, keys)
        dq = jnp.where(front, dq[:block], dq[block:]) * (LANES // 2) ** -0.5
        grads_ref[rows, lanes] = (dq * cos - swap_halves(dq) * sin).astype(BF)


def attention_bwd_end(groups, pairs, cos_ref, sin_ref, grads_ref, dk_acc, dv_acc):
    total = dk_acc.shape[0]
    front = iota2((total, LANES), 1) < LANES // 2
    for g in range(groups):
        kv = slice(g * LANES, (g + 1) * LANES)
        dk, dv = dk_acc[:, kv], dv_acc[:, kv]
        dk = dk + pltpu.roll(dk, LANES // 2, 1)
        dk = dk * cos_ref[...] - swap_halves(dk) * sin_ref[...]
        dv = dv + pltpu.roll(dv, LANES // 2, 1)
        out = slice((pairs + g) * LANES, (pairs + g + 1) * LANES)
        grads_ref[:, out] = jnp.where(front, dk, dv).astype(BF)


def attention_forward(groups, tensors, doc_col, doc_row, qkv, cos, sin, query_width, low, squares, collective_id):
    total = qkv.shape[0]
    kv_width = qkv.shape[1] - query_width
    whole = lambda a: spec(a.shape, lambda i: (0,) * a.ndim)
    columns = lambda w, place=0: spec((total, w), lambda i: (0, place))
    return pl.pallas_call(
        functools.partial(attention_fwd_kernel, groups, tensors),
        grid=(1,),
        in_specs=[whole(doc_col), whole(doc_row), columns(query_width), columns(kv_width, query_width // kv_width), whole(cos), whole(sin), whole(low), whole(squares)],
        out_specs=[columns(low.shape[1] + query_width), columns(LANES), columns(query_width), columns(kv_width), columns(kv_width), whole(squares)],
        out_shape=[
            jax.ShapeDtypeStruct((total, low.shape[1] + query_width), BF), jax.ShapeDtypeStruct((total, LANES), F32),
            jax.ShapeDtypeStruct((total, query_width), BF), jax.ShapeDtypeStruct((total, kv_width), BF),
            jax.ShapeDtypeStruct((total, kv_width), BF), jax.ShapeDtypeStruct(squares.shape, F32),
        ],
        scratch_shapes=tensor_sum_scratch(tensors, squares.shape),
        compiler_params=pltpu.CompilerParams(vmem_limit_bytes=VMEM_LIMIT, collective_id=collective_id, has_side_effects=True),
        cost_estimate=pl.CostEstimate(flops=12 * 10**9, bytes_accessed=total * query_width * 10, transcendentals=total * total * 2),
        name="attention_fwd",
    )(doc_col, doc_row, qkv, qkv, cos, sin, low, squares)


def gather_kernel(
    count, tensors, shard_ref, tokens_ref, cotangent_ref, gain_ref, *refs,
):
    tables, (full_ref, all_tokens_ref, all_cotangent_ref, normed_ref, scale_ref, turned_ref) = refs[:8], refs[8:14]
    table_outs, (own_sem, send_sems, recv_sems, core_send, core_recv) = refs[14:20], refs[20:]
    unit, columns = shard_ref.shape
    levels = count // 4
    me = lax.axis_index("fsdp")
    main = columns - columns // 5 // LANES * LANES
    half, middle = main // 2 // LANES * LANES, (main + columns) // 2 // LANES * LANES
    parts, flat_parts = (slice(0, half), slice(half, main)), (slice(main, middle), slice(middle, columns))
    neighbours = (flipped(me, 1), flipped(me, 2))
    bits = [1 << k for k in range((levels - 1).bit_length())]
    core = lax.axis_index("tensor")
    cores = [flipped(core, k) for k in range(1, tensors)]
    greet([("fsdp", p) for p in neighbours] + [("fsdp", flipped(me, 4 * bit)) for bit in bits] + [("tensor", p) for p in cores])

    def rows(owner):
        return pl.ds(pl.multiple_of(owner * unit, unit), unit)

    started = []

    def send(source, owner, lanes, slot, place):
        copy = remote(source, full_ref.at[rows(owner), lanes], send_sems.at[slot], recv_sems.at[slot], "fsdp", place)
        copy.start()
        started.append(copy)
        return copy

    def arrival(owner, lanes, slot):
        piece = full_ref.at[rows(owner), lanes]
        return remote(piece, piece, send_sems.at[slot], recv_sems.at[slot], "fsdp", neighbours[0])

    everything, flat = slice(0, main), slice(main, columns)
    own = pltpu.make_async_copy(shard_ref, full_ref.at[rows(me), :], own_sem)
    own.start()
    base = levels
    cross = base + 2 * levels
    level, flat_base = cross + 2 * levels, cross + 3 * levels

    def along_z(d):
        for bit in reversed(bits):
            if d == 0 or bit < (d & -d):
                source = shard_ref.at[:, everything] if d == 0 else full_ref.at[rows(flipped(me, 4 * d)), everything]
                send(source, flipped(me, 4 * d), everything, d + bit, flipped(me, 4 * bit))

    def quad(d):
        return full_ref.at[pl.ds(pl.multiple_of(flipped(me, 4 * d) // 4 * (4 * unit), 4 * unit), 4 * unit), flat]

    def quad_copy(d, bit):
        return remote(quad(d), quad(d), send_sems.at[level + d + bit], recv_sems.at[level + d + bit], "fsdp", flipped(me, 4 * bit))

    def quads_along_z(d):
        if d:
            place = neighbours[0]
            remote(quad(d), quad(d), send_sems.at[level + d], recv_sems.at[level + d], "fsdp", place).wait_recv()
        for bit in reversed(bits):
            if d == 0 or bit < (d & -d):
                copy = quad_copy(d, bit)
                copy.start()
                started.append(copy)

    along_z(0)
    for axis in range(2):
        send(shard_ref.at[:, flat], me, flat, flat_base + axis, neighbours[axis])
    for axis in range(2):
        send(shard_ref.at[:, everything], me, everything, base + axis * levels, neighbours[axis])
    own_rows = tokens_ref.shape[0]
    share = lambda owner: pl.ds(pl.multiple_of(owner * own_rows, own_rows), own_rows)
    exchanges = []
    for k, place in enumerate(cores):
        for j, (source, target) in enumerate(((tokens_ref, all_tokens_ref), (cotangent_ref, all_cotangent_ref))):
            copy = remote(
                source, target.at[share(core), :], core_send.at[2 * k + j], core_recv.at[2 * k + j], "tensor", place
            )
            copy.start()
            exchanges.append(copy)
    all_tokens_ref[share(core), :] = tokens_ref[...]
    all_cotangent_ref[share(core), :] = cotangent_ref[...]
    for copy in exchanges:
        copy.wait()

    def norm(i, carry):
        piece = pl.ds(pl.multiple_of(i * LANES, LANES), LANES)
        values = all_tokens_ref[piece, :].astype(F32)
        scale = lax.rsqrt(jnp.mean(values * values, axis=1, keepdims=True) + EPS)
        scale_ref[piece, :] = scale
        normed = values * scale * gain_ref[...]
        normed_ref[piece, :] = normed.astype(BF)
        turned_ref[:, piece] = normed.T.astype(BF)
        return carry

    lax.fori_loop(0, normed_ref.shape[0] // LANES, norm, 0)

    def pass_on(d):
        for axis in range(2):
            owner = flipped(neighbours[axis], 4 * d)
            arrival(owner, everything, base + axis * levels + d).wait_recv()
            piece = full_ref.at[rows(owner), parts[axis]]
            send(piece, owner, parts[axis], cross + axis * levels + d, neighbours[1 - axis])

    for axis in range(2):
        arrival(neighbours[axis], flat, flat_base + axis).wait_recv()
        piece = full_ref.at[rows(neighbours[axis]), flat_parts[axis]]
        send(piece, neighbours[axis], flat_parts[axis], flat_base + 2 + axis, neighbours[1 - axis])
    order = sorted(range(1, levels), key=lambda d: (-(d & -d), d))
    before = 0
    for d in order:
        owner = flipped(me, 4 * d)
        arrival(owner, everything, d).wait_recv()
        along_z(d)
        for axis in range(2):
            send(full_ref.at[rows(owner), everything], owner, everything, base + axis * levels + d, neighbours[axis])
        pass_on(before)
        before = d
        if d == order[0]:
            for axis in range(2):
                arrival(flipped(me, 3), flat_parts[axis], flat_base + 2 + axis).wait_recv()
            own.wait()
            quads_along_z(0)
            table_kernel(*tables, *table_outs)
    quads_along_z(order[0])
    pass_on(before)
    for d in order[1:]:
        quads_along_z(d)
    for d in range(levels):
        for axis in range(2):
            owner = flipped(me, 4 * d + 3)
            arrival(owner, parts[axis], cross + axis * levels + d).wait_recv()
    for copy in started:
        copy.wait_send()


def gather_weights(shard, tokens, cotangent, gain, tables, wide, count, tensors, collective_id):
    unit, columns = shard.shape
    own_rows, hidden = tokens.shape
    total = own_rows * tensors
    slots = 6 * (count // 4) + 4
    vmem, anywhere = pl.BlockSpec(memory_space=pltpu.VMEM), pl.BlockSpec(memory_space=pl.ANY)
    low = jax.ShapeDtypeStruct((total, hidden), BF)
    shape = lambda r, c: jax.ShapeDtypeStruct((r, c), F32)
    return pl.pallas_call(
        functools.partial(gather_kernel, count, tensors),
        in_specs=[anywhere, vmem, vmem, vmem] + [vmem] * len(tables),
        out_specs=[anywhere] + [vmem] * 11,
        out_shape=[jax.ShapeDtypeStruct((count * unit, columns), shard.dtype), low, low, low, jax.ShapeDtypeStruct((total, 1), F32),
            jax.ShapeDtypeStruct((hidden, total), BF), shape(total, LANES), shape(total, LANES), shape(total, LANES), shape(8, wide),
            shape(8, tables[3].shape[1]), shape(8, LANES),
        ],
        scratch_shapes=[
            pltpu.SemaphoreType.DMA, pltpu.SemaphoreType.DMA((slots,)), pltpu.SemaphoreType.DMA((slots,)),
            pltpu.SemaphoreType.DMA((2 * (tensors - 1),)), pltpu.SemaphoreType.DMA((2 * (tensors - 1),)),
        ],
        compiler_params=pltpu.CompilerParams(collective_id=collective_id, has_side_effects=True, vmem_limit_bytes=VMEM_LIMIT),
        cost_estimate=pl.CostEstimate(flops=0, bytes_accessed=2 * count * unit * columns * 2, transcendentals=0),
        name="gather_weights",
    )(shard, tokens, cotangent, gain, *tables)


def backward_kernel(c, *refs):
    r = types.SimpleNamespace(**dict(zip(c.names, refs)))
    now = pl.program_id(0)
    me, core = lax.axis_index("fsdp"), lax.axis_index("tensor")
    levels, unit, blocks, chunks, tiles = c.count // 4, c.unit, c.blocks, c.chunks, c.tiles
    near = (flipped(me, 1), flipped(me, 2))
    far = [None] + [flipped(me, 4 * d) for d in range(1, levels)]
    bits = [1 << k for k in range((c.count - 1).bit_length())]
    cores = [flipped(core, k) for k in range(1, c.tensors)]
    halves = [("tensor", flipped(core, 1 << k)) for k in range((c.tensors - 1).bit_length())]
    stages = [("fsdp", flipped(me, bit)) for bit in bits] + halves
    order = sorted(range(levels), key=lambda d: (d & -d if d else levels, -d))
    pieces = []
    for i, (name, lanes, path, out, out_lanes) in enumerate(c.pieces):
        pieces.append((i, getattr(r, name), lanes, path, getattr(r, out), out_lanes))
    early, late, flat = pieces[: c.early], pieces[c.early : c.flat], pieces[c.flat :]

    def own_copies():
        copies = []
        for i, grad, lanes, path, _, _ in early:
            parts = getattr(r, "own%d" % i)
            for d in order:
                for k, owner in ((d, flipped(near[path], 4 * d)), (levels + d, flipped(me, 4 * d))):
                    copies.append(pltpu.make_async_copy(grad.at[rows(owner), lanes], parts.at[k], r.own_sems.at[i, k]))
        return copies

    def own_part(i, grad, lanes, owner, k):
        if i < c.early:
            return getattr(r, "own%d" % i)[k].astype(F32)
        return grad[spot(i, owner), lanes].astype(F32)

    cross, along, inbound = [], [], []
    for i in range(len(pieces)):
        cross.append(getattr(r, "cross%d" % i))
        along.append((getattr(r, "along_x%d" % i), getattr(r, "along_y%d" % i)))
        inbound.append(getattr(r, "inbound%d" % i))

    def rows(owner):
        return pl.ds(pl.multiple_of(owner * unit, unit), unit)

    def spot(i, owner):
        return rows(owner % 4 if i >= c.flat else owner)

    def link(source, target, i, kind, d, place):
        slot = (i * 4 + kind) * levels + d
        return remote(source, target, r.send_sems.at[slot], r.recv_sems.at[slot], "fsdp", place)

    def begin(group, d):
        for i, grad, lanes, path, _, _ in group:
            link(grad.at[spot(i, flipped(me, 4 * d + 3)), lanes], cross[i].at[d], i, 0, d, near[1 - path]).start()

    def raw(group, d):
        for i, grad, lanes, path, _, _ in group:
            other = 1 - path
            link(grad.at[spot(i, flipped(near[other], 4 * d)), lanes], along[i][other].at[d], i, 1 + other, d, near[other]).start()

    def middle(group, d):
        for i, grad, lanes, path, _, _ in group:
            link(cross[i].at[d], cross[i].at[d], i, 0, d, near[0]).wait_recv()
            own = own_part(i, grad, lanes, flipped(near[path], 4 * d), d)
            cross[i][d] = (own + cross[i][d].astype(F32)).astype(BF)
            link(cross[i].at[d], along[i][path].at[d], i, 1 + path, d, near[path]).start()

    def finish(group, d):
        lowest = d & -d if d else levels
        for i, grad, lanes, path, out, out_lanes in group:
            for axis in range(2):
                link(along[i][axis].at[d], along[i][axis].at[d], i, 1 + axis, d, near[0]).wait_recv()
            own = own_part(i, grad, lanes, flipped(me, 4 * d), levels + d)
            total = own + along[i][0][d].astype(F32) + along[i][1][d].astype(F32)
            bit = 1
            while bit < lowest and i < c.flat:
                slot = d + bit - 1
                link(inbound[i].at[slot], inbound[i].at[slot], i, 3, d + bit, near[0]).wait_recv()
                total = total + inbound[i][slot].astype(F32)
                bit *= 2
            if d:
                along[i][0][d] = total.astype(BF)
                link(along[i][0].at[d], inbound[i].at[d - 1], i, 3, d, far[lowest]).start()
            else:
                out[:, out_lanes] = total

    def quad(d):
        return pl.ds(pl.multiple_of(flipped(me, 4 * d) // 4 * (4 * unit), 4 * unit), 4 * unit)

    def level_own(d):
        return pltpu.make_async_copy(r.grad_level.at[quad(d), :], r.level_sum.at[d // 2], r.level_local.at[d // 2])

    def level_send(source, d):
        place = far[d & -d]
        return remote(source, r.level_in.at[d - 1], r.level_send.at[d - 1], r.level_recv.at[d - 1], "fsdp", place)

    def level_start():
        for d in order:
            if d % 2:
                level_send(r.grad_level.at[quad(d), :], d).start()
            else:
                level_own(d).start()

    def level_pass(d):
        level_own(d).wait()
        total = r.level_sum[d // 2].astype(F32)
        bit, lowest = 1, d & -d if d else levels
        while bit < lowest:
            level_send(r.level_in.at[d + bit - 1], d + bit).wait_recv()
            total = total + r.level_in[d + bit - 1].astype(F32)
            bit *= 2
        if d:
            r.level_sum[d // 2] = total.astype(BF)
            level_send(r.level_sum.at[d // 2], d).start()
        else:
            r.level_done[...] = total.astype(BF)

    weights_copy = pltpu.make_async_copy(r.weights.at[:, 0 : r.held.shape[1]], r.held, r.local_sems.at[0])
    own_rows = r.tokens.shape[0]
    share = lambda owner: pl.ds(pl.multiple_of(owner * own_rows, own_rows), own_rows)
    turned_copy = pltpu.make_async_copy(r.normed_turned, r.turned, r.local_sems.at[2])
    branch_copy = pltpu.make_async_copy(r.branch_low.at[share(core), :], r.branch_own, r.local_sems.at[1])
    inners = TensorSum(c.tensors, r.inner_own, r.inner_in, r.inner_send, r.inner_recv)

    @pl.when(now == 0)
    def _():
        greet([("fsdp", p) for p in near] + [("fsdp", flipped(me, bit)) for bit in bits[2:]] + [("tensor", p) for p in cores])
        level_start()
        for d in order:
            begin(early, d)
        for copy in own_copies():
            copy.start()
        turned_copy.start()
        weights_copy.start()
        branch_copy.start()
        r.dk_acc[...] = jnp.zeros_like(r.dk_acc)
        r.dv_acc[...] = jnp.zeros_like(r.dv_acc)

    block = r.mix_up.shape[0]
    for j in range(blocks):

        @pl.when(now == j)
        def _(j=j):
            for i in range(block // LANES):
                part = slice(i * LANES, (i + 1) * LANES)
                inner = jnp.sum(r.mix_norm[part, :].astype(F32) * r.mix_low[part, :].astype(F32), axis=1, keepdims=True)
                at = 8 * (j * (block // LANES) + i)
                r.inner_rows[at : at + 8, :] = jnp.broadcast_to(inner, (LANES, LANES)).T[0:8, :]
            attention_bwd_block(
                j * block, c.groups, r.feats_all, r.doc_row, r.qrot, r.keys, r.values, r.lse, r.mix_up, r.cos, r.sin, r.qkv_grad,
                r.dk_acc, r.dv_acc,
            )
            if j == blocks - 1:
                inners.begin(r.inner_rows[...], met=True)
                attention_bwd_end(c.groups, r.qrot.shape[1] // LANES, r.cos, r.sin, r.qkv_grad, r.dk_acc, r.dv_acc)

    @pl.when(now == blocks)
    def _():
        r.dxbuf[CHUNK : CHUNK + 8, :] = jnp.zeros((8, r.dxbuf.shape[1]), F32)
        r.dbcbuf[CHUNK : CHUNK + 8, :] = jnp.zeros((8, r.dbcbuf.shape[1]), F32)
        r.dmemory[...] = jnp.zeros_like(r.dmemory)
        r.x_sums[...] = jnp.zeros_like(r.x_sums)
        r.state_sums[...] = jnp.zeros_like(r.state_sums)
        r.head_sums[...] = jnp.zeros_like(r.head_sums)
        r.inner_sum[...] = inners.end()

    @pl.when((now >= blocks) & (now < blocks + chunks))
    def _():
        chunk = chunks - 1 - (now - blocks)
        mamba_bwd_block(
            r.feats, r.square, r.inner_sum, chunk, r.docs, r.x, r.x_before, r.bc, r.bc_before, r.step, r.z, r.scan, r.states,
            r.norm_grad, r.taps, r.staps, r.heads, r.expand, r.reduce, r.gain,
            r.ssm_grad.at[pl.ds(pl.multiple_of(chunk * CHUNK, CHUNK), CHUNK), :], r.x_sums, r.state_sums, r.head_sums,
            r.xbuf, r.bcbuf, r.dxbuf, r.dbcbuf, r.dmemory,
        )

    for k, d in enumerate(order):

        @pl.when(now == blocks + 1 + k)
        def _(d=d):
            if d == order[0]:
                for copy in own_copies():
                    copy.wait()
            middle(early, d)
            raw(early, d)

    base = blocks + chunks
    ssm_wide = r.ssm_grad.shape[1]
    for k, d in enumerate(order):

        @pl.when(now == base + k)
        def _(d=d):
            quad = pl.ds(pl.multiple_of(flipped(me, 4 * d) // 4 * (4 * unit), 4 * unit), 4 * unit)
            if d == order[0]:
                turned_copy.wait()
            turned = r.turned[quad, :]
            r.grad_first[quad, :ssm_wide] = jnp.dot(turned, r.ssm_grad[...], preferred_element_type=F32).astype(BF)
            r.grad_first[quad, ssm_wide:] = jnp.dot(turned, r.qkv_grad[...], preferred_element_type=F32).astype(BF)
            begin(late, d)
            raw(late, d)

    base = base + levels

    @pl.when(now == base)
    def _():
        weights_copy.wait()

    @pl.when((now >= base) & (now < base + tiles))
    def _():
        part = pl.ds(pl.multiple_of((now - base) * c.tile, c.tile), c.tile)
        r.normed_part[part, :] = (
            mm_nt(r.ssm_grad[part, :], r.held[:, :ssm_wide]) + mm_nt(r.qkv_grad[part, :], r.held[:, ssm_wide:])
        ).astype(BF)

    def normed_copies():
        return [
            remote(r.normed_part.at[share(place), :], r.normed_in.at[k], r.core_send.at[k], r.core_recv.at[k], "tensor", place)
            for k, place in enumerate(cores)
        ]

    for k, step in enumerate((base - levels + 1, base + 1)):

        @pl.when(now == step)
        def _(d=order[k]):
            finish(early, d)

    for k, d in enumerate([d for d in order if d % 2 == 0]):

        @pl.when(now == c.level_steps[k])
        def _(d=d):
            level_pass(d)
            if d == 0:
                begin(flat, 0)
                raw(flat, 0)

    settled = []

    def stage_copy(k):
        axis, place = stages[k]
        return remote(r.sums.at[k], r.sums_in.at[k], r.sum_send.at[k], r.sum_recv.at[k], axis, place)

    def next_stage():
        k = len(settled)
        if k < len(stages):
            stage_copy(k).wait()
            r.sums[k + 1] = r.sums[k] + r.sums_in[k]
            settled.append(k)
            if k + 1 < len(stages):
                stage_copy(k + 1).start()

    @pl.when(now == base + tiles)
    def _():
        for copy in normed_copies():
            copy.start()
        for copy in normed_copies():
            copy.wait()
        branch_copy.wait()
        r.gain_sum[...] = jnp.zeros_like(r.gain_sum)
        size = min(CHUNK, own_rows)

        def first_norm_back(i, carry):
            part = pl.ds(pl.multiple_of(i * size, size), size)
            whole = pl.ds(pl.multiple_of(core * own_rows + i * size, size), size)
            grad = r.normed_part[whole, :].astype(F32)
            for k in range(len(cores)):
                grad = grad + r.normed_in[k, part, :].astype(F32)
            scale = r.scale[whole, :]
            shape = r.tokens[part, :].astype(F32) * scale
            weighted = grad * r.input_gain[...]
            inner = jnp.mean(weighted * shape, axis=1, keepdims=True)
            r.input_grad[part, :] = r.branch_own[part, :].astype(F32) + scale * (weighted - shape * inner)
            r.gain_sum[0:1, :] += jnp.sum(grad * shape, axis=0, keepdims=True)
            return carry

        lax.fori_loop(0, own_rows // size, first_norm_back, 0)
        at = 0
        for ref in (r.x_sums, r.head_sums, r.state_sums):
            r.sums[0, :, at : at + ref.shape[1]] = ref[...]
            at += ref.shape[1]
        eighth = r.gain_sum.shape[1] // 8
        for ref, factor in ((r.second_part, 1.0 / c.tensors), (r.gain_sum, 1.0)):
            for k in range(8):
                r.sums[0, k : k + 1, at : at + eighth] = ref[0:1, k * eighth : (k + 1) * eighth] * factor
            at += eighth
        stage_copy(0).start()
        for d in order[2:]:
            finish(early, d)
            next_stage()
        middle(flat, 0)
        for d in order:
            middle(late, d)
        for d in order:
            finish(late, d)
            next_stage()
        finish(flat, 0)
        while len(settled) < len(stages):
            next_stage()
        r.small_out[:, : c.split] = r.sums[len(bits), :, : c.split]
        r.small_out[:, c.split :] = r.sums[len(stages), :, c.split :]
        states2 = c.state_at[1] - c.state_at[0]
        wide_shared = r.shared.shape[2]
        leading = core * (wide_shared - states2) // (c.tensors * LANES)
        r.shared[0, :, :states2] = r.out_first[:, c.state_at[0] : c.state_at[1]]
        for g in range((wide_shared - states2) // LANES):
            value = jnp.zeros((unit, LANES), F32)
            for j in range(c.groups):
                value = jnp.where(leading + j == g, r.out_first[:, c.kv_at + j * LANES : c.kv_at + (j + 1) * LANES], value)
            r.shared[0, :, states2 + g * LANES : states2 + (g + 1) * LANES] = value
        for k, (axis, place) in enumerate(halves):
            copy = remote(r.shared.at[k], r.shared_in.at[k], r.half_send.at[k], r.half_recv.at[k], axis, place)
            copy.start()
            copy.wait()
            r.shared[k + 1] = r.shared[k] + r.shared_in[k]
        r.shared_out[...] = r.shared[len(halves)]
        for d in order[:-1]:
            level_send(r.level_in.at[d - 1], d).wait_send()
        for i in range(len(pieces)):
            for d in range(levels):
                for kind in range(4):
                    if (kind < 3 or d) and (i < c.flat or kind < 3 and d == 0):
                        link(cross[i].at[d], cross[i].at[d], i, kind, d, near[0]).wait_send()


def backward(
    groups, feats, doc_row, qrot, keys, values, lse, mix_grad, mix, cos, sin, squares, ssm_in, scan, states, taps, staps, heads, gain,
    grad_gate_up, grad_down, grad_mix, normed_turned, first, branch_low, tokens, scale, input_gain, second_part, width, states2,
    count, tensors, collective_id,
):
    total, hidden = branch_low.shape
    own_rows = tokens.shape[0]
    unit = hidden // count
    levels = count // 4
    query_wide, kv_wide = qrot.shape[1], keys.shape[1]
    block, tile = min(QBLOCK, total), min(QBLOCK, total)
    blocks, chunks, tiles = total // block, total // CHUNK, total // tile
    ssm_wide, qkv_wide = 2 * width + states2 + LANES, query_wide + kv_wide
    chunk = lambda s: jnp.clip(chunks - 1 - (s - blocks), 0, chunks - 1)
    query = lambda s: jnp.minimum(s, blocks - 1)
    by_chunk = lambda w, place=0: spec((CHUNK, w), lambda s: (chunk(s), place))
    by_query = lambda w, place=0: spec((block, w), lambda s: (query(s), place))
    before = lambda w, place=0: spec((8, w), lambda s: (jnp.maximum(chunk(s) * (CHUNK // 8) - 1, 0), place))
    whole = lambda a: pl.BlockSpec(a.shape, lambda s: (0,) * a.ndim, pipeline_mode=pl.Buffered(1))
    anywhere = pl.BlockSpec(memory_space=pl.ANY)
    vmem = pl.BlockSpec(memory_space=pltpu.VMEM)
    expand = expand_matrix(width)
    reduce = np.concatenate([expand[:LANES].T] * 2, axis=0)
    state_place, step_place = 2 * width // states2, (2 * width + states2) // LANES
    ins = dict(
        feats_all=(feats, whole(feats)), doc_row=(doc_row, whole(doc_row)), qrot=(qrot, whole(qrot)), keys=(keys, whole(keys)),
        values=(values, whole(values)), lse=(lse, by_query(LANES)), mix_up=(mix_grad, by_query(query_wide, width // query_wide)),
        mix_norm=(mix_grad, by_query(width)), mix_low=(mix, by_query(width)), cos=(cos, whole(cos)), sin=(sin, whole(sin)),
        feats=(feats, by_chunk(LANES)), docs=(doc_row, spec((1, CHUNK), lambda s: (0, chunk(s)))),
        square=(squares, spec((8, LANES), lambda s: (chunk(s), 0))), x=(ssm_in, by_chunk(width, 1)),
        x_before=(ssm_in, before(width, 1)), bc=(ssm_in, by_chunk(states2, state_place)),
        bc_before=(ssm_in, before(states2, state_place)), step=(ssm_in, by_chunk(LANES, step_place)),
        z=(ssm_in, by_chunk(width)), scan=(scan, by_chunk(width)),
        states=(states, spec((1, states2 // 2, width), lambda s: (chunk(s), 0, 0))), norm_grad=(mix_grad, by_chunk(width)),
        taps=(taps, whole(taps)), staps=(staps, whole(staps)), heads=(heads, whole(heads)), expand=(expand, whole(expand)),
        reduce=(reduce, whole(reduce)), gain=(gain, whole(gain)), grad_gate_up=(grad_gate_up, anywhere),
        grad_level=(grad_down, anywhere), grad_mix=(grad_mix, anywhere),
        normed_turned=(normed_turned, anywhere), weights=(first, anywhere), branch_low=(branch_low, anywhere),
        tokens=(tokens, whole(tokens)), scale=(scale, whole(scale)), input_gain=(input_gain, whole(input_gain)),
        second_part=(second_part, whole(second_part)),
    )
    small = width + LANES + states2 + 2 * (hidden // 8)
    shared = states2 + KEYVAL_HEADS * LANES
    outs = dict(
        input_grad=(own_rows, hidden), out_gate_up=(unit, grad_gate_up.shape[1]), out_down=(unit, grad_down.shape[1]),
        out_mix=(unit, grad_mix.shape[1]), out_first=(unit, ssm_wide + qkv_wide), small_out=(8, small),
        shared_out=(unit, shared),
    )
    cut = (ssm_wide + qkv_wide) // (2 * LANES) * LANES
    ffn = grad_down.shape[1]
    split_at, most = ffn // (2 * LANES) * LANES, 3 * ffn // (2 * LANES) * LANES
    every = lambda a: slice(0, a)
    pieces = [
        ("grad_gate_up", slice(0, most), 0, "out_gate_up", slice(0, most)),
        ("grad_gate_up", slice(most, 2 * ffn), 1, "out_gate_up", slice(most, 2 * ffn)),
        ("grad_mix", every(grad_mix.shape[1]), 1, "out_mix", every(grad_mix.shape[1])),
        ("grad_first", slice(0, cut), 0, "out_first", slice(0, cut)),
        ("grad_first", slice(cut, ssm_wide + qkv_wide), 1, "out_first", slice(cut, ssm_wide + qkv_wide)),
        ("level_done", slice(0, split_at), 0, "out_down", slice(0, split_at)),
        ("level_done", slice(split_at, ffn), 1, "out_down", slice(split_at, ffn)),
    ]
    steps, stages = (tensors - 1).bit_length(), (count - 1).bit_length() + (tensors - 1).bit_length()
    inner = (total // 16, LANES)
    f32 = lambda *dims: pltpu.VMEM(dims, F32)
    low = lambda *dims: pltpu.VMEM(dims, BF)
    dma = lambda n: pltpu.SemaphoreType.DMA((n,))
    scratch = dict(
        dk_acc=f32(total, kv_wide), dv_acc=f32(total, kv_wide), qkv_grad=low(total, qkv_wide), inner_rows=f32(*inner),
        inner_sum=f32(*inner), inner_own=f32(steps + 1, *inner), inner_in=f32(steps, *inner), inner_send=dma(steps),
        inner_recv=dma(steps), xbuf=f32(CHUNK + 8, width), bcbuf=f32(CHUNK + 8, states2), dxbuf=f32(CHUNK + 8, width),
        dbcbuf=f32(CHUNK + 8, states2), dmemory=f32(states2 // 2, width), ssm_grad=low(total, ssm_wide),
        x_sums=f32(8, width), state_sums=f32(8, states2), head_sums=f32(8, LANES),
        held=low(hidden, ssm_wide + qkv_wide), grad_first=low(hidden, ssm_wide + qkv_wide), branch_own=low(own_rows, hidden),
        normed_part=low(total, hidden), normed_in=low(tensors - 1, own_rows, hidden), gain_sum=f32(8, hidden),
        sums=f32(stages + 1, 8, small), sums_in=f32(stages, 8, small), sum_send=dma(stages), sum_recv=dma(stages),
        shared=f32(steps + 1, unit, shared), shared_in=f32(steps, unit, shared), half_send=dma(steps),
        half_recv=dma(steps), core_send=dma(tensors - 1), core_recv=dma(tensors - 1), local_sems=dma(3), turned=low(hidden, total),
        own_sems=pltpu.SemaphoreType.DMA((3, 2 * levels)),
        level_in=low(levels - 1, 4 * unit, ffn), level_sum=low(levels // 2, 4 * unit, ffn), level_done=low(4 * unit, ffn),
        level_send=dma(levels - 1), level_recv=dma(levels - 1), level_local=dma(levels // 2),
        send_sems=dma(4 * levels * len(pieces)), recv_sems=dma(4 * levels * len(pieces)),
    )
    for i, piece in enumerate(pieces):
        columns = piece[1].stop - piece[1].start
        scratch.update({
            "cross%d" % i: low(levels, unit, columns), "along_x%d" % i: low(levels, unit, columns),
            "along_y%d" % i: low(levels, unit, columns), "inbound%d" % i: low(levels - 1, unit, columns),
        })
        if i < 3:
            scratch["own%d" % i] = low(2 * levels, unit, columns)
    names = list(ins) + list(outs) + list(scratch)
    odd = levels // 2
    level_steps = [blocks + chunks * (k + 1) // odd - (k + 1 < odd) for k in range(odd)]
    c = types.SimpleNamespace(
        names=names, pieces=pieces, early=3, flat=5, level_steps=level_steps, count=count, tensors=tensors, unit=unit, blocks=blocks, chunks=chunks, tiles=tiles, tile=tile,
        groups=groups, split=width + LANES, state_at=(2 * width, 2 * width + states2), kv_at=ssm_wide + query_wide,
    )
    return pl.pallas_call(
        functools.partial(backward_kernel, c),
        grid=(blocks + chunks + levels + tiles + 1,),
        in_specs=[v[1] for v in ins.values()],
        out_specs=[vmem] * len(outs),
        out_shape=[jax.ShapeDtypeStruct(v, F32) for v in outs.values()],
        scratch_shapes=list(scratch.values()),
        compiler_params=pltpu.CompilerParams(collective_id=collective_id, has_side_effects=True, vmem_limit_bytes=VMEM_ALL),
        name="backward",
    )(*(v[0] for v in ins.values()))


def tensor_swap(values):
    return lax.ppermute(values, "tensor", [(0, 1), (1, 0)])


def tensor_pair(values):
    if lax.axis_size("tensor") == 2:
        return values, tensor_swap(values)
    return lax.psum(values.astype(F32), "tensor").astype(values.dtype), jnp.zeros_like(values)


def pad_to(values, size, axis=-1):
    pads = [(0, 0)] * values.ndim
    pads[axis] = (0, size - values.shape[axis])
    return jnp.pad(values, pads) if size > values.shape[axis] else values


def pack_kernel(
    mixer_ref, state_ref, step_ref, query_ref, keyval_ref, proj_ref, attention_ref, first_ref,
):
    unit = state_ref.shape[0]
    width, wide = mixer_ref.shape[2], -(-mixer_ref.shape[2] // LANES) * LANES
    same = (iota2((unit, unit), 0) == iota2((unit, unit), 1)).astype(BF)
    place = 0

    def put(out_ref, value, size):
        nonlocal place
        value = value.astype(BF)
        if size > value.shape[1]:
            value = jnp.concatenate([value, jnp.zeros((unit, size - value.shape[1]), BF)], axis=1)
        out_ref[:, place : place + size] = value
        place += size

    put(first_ref, mixer_ref[:, 0, :], wide)
    put(first_ref, mixer_ref[:, 1, :], wide)
    put(first_ref, state_ref[...], state_ref.shape[1])
    put(first_ref, lax.dot_general(same, step_ref[...].astype(BF), (((1,), (1,)), ((), ())), preferred_element_type=F32), LANES)
    query_wide = -(-query_ref.shape[1] // LANES) * LANES
    put(first_ref, query_ref[...], query_wide)
    put(first_ref, keyval_ref[...], keyval_ref.shape[1])
    put(first_ref, proj_ref[...], wide)
    put(first_ref, attention_ref[...], query_wide)


def pack_rest_kernel(gate_up_ref, down_ref, out_ref):
    ffn = gate_up_ref.shape[2]
    out_ref[:, :ffn] = gate_up_ref[:, 0, :].astype(BF)
    out_ref[:, ffn : 2 * ffn] = gate_up_ref[:, 1, :].astype(BF)
    out_ref[:, 2 * ffn :] = down_ref[...].astype(BF)


def pack_weights(kernel, columns, name, weights):
    unit = weights[0].shape[0]
    whole = lambda shape: spec(shape, lambda i: (0,) * len(shape))
    return pl.pallas_call(
        kernel,
        grid=(1,),
        in_specs=[whole(v.shape) for v in weights],
        out_specs=whole((unit, columns)),
        out_shape=jax.ShapeDtypeStruct((unit, columns), BF),
        compiler_params=pltpu.CompilerParams(vmem_limit_bytes=VMEM_WHOLE),
        name=name,
    )(*weights)


def table_kernel(
    docs_ref, conv_ref, conv_bias_ref, state_conv_ref, state_bias_ref, step_bias_ref, decay_ref, skip_ref,
    feats_ref, cos_ref, sin_ref, taps_ref, state_taps_ref, heads_ref,
):
    total = docs_ref.shape[1]
    docs = docs_ref[...]
    tall = jnp.broadcast_to(docs, (LANES, total)).T
    spot = iota2((1, total), 1)
    begin = jnp.sum((tall[:, 0:1] < docs).astype(F32), axis=0, keepdims=True)
    rows = [docs]
    eight = jnp.broadcast_to(docs, (8, total))
    for k in (1, 2, 3):
        rows.append(jnp.where(spot >= k, (pltpu.roll(eight, k, 1)[0:1] == docs).astype(F32), 0.0))
    blocks = [docs[:, i : i + CHUNK] for i in range(0, total, CHUNK)]
    before = [jnp.full((1, 1), -1.0, F32)] + [v[:, CHUNK - 1 :] for v in blocks[:-1]]
    rows.append(jnp.concatenate([(v == w).astype(F32) for v, w in zip(blocks, before)], axis=1))
    rows.append(jnp.concatenate([(v == v[:, CHUNK - 1 :]).astype(F32) for v in blocks], axis=1))
    for k in (1, 2, 3):
        rows.append(jnp.where(spot < total - k, (pltpu.roll(eight, total - k, 1)[0:1] == docs).astype(F32), 0.0))
    rows.append(spot.astype(F32) - begin)
    rows.append(jnp.zeros((LANES - len(rows), total), F32))
    feats = jnp.concatenate(rows, axis=0).T
    feats_ref[...] = feats
    lane = iota2((1, LANES), 1)
    rates = jnp.exp((lane % (HEAD_SIZE // 2)).astype(F32) * (-2.0 * math.log(THETA) / HEAD_SIZE))
    angles = feats[:, 9:10] * rates
    cos_ref[...] = jnp.cos(angles)
    sin_ref[...] = jnp.sin(angles) * jnp.where(lane % HEAD_SIZE < HEAD_SIZE // 2, -1.0, 1.0)
    width, heads = conv_ref.shape[1], skip_ref.shape[1]
    taps_ref[...] = jnp.zeros_like(taps_ref)
    taps_ref[0:4, :width] = conv_ref[...]
    taps_ref[4:5, :width] = conv_bias_ref[...]
    spread = (iota2((heads, width), 0) == iota2((heads, width), 1) // (width // heads)).astype(F32)
    taps_ref[5:6, :width] = exact_mm(jnp.broadcast_to(skip_ref[...], (8, heads)), spread)[0:1]
    state_taps_ref[...] = jnp.zeros_like(state_taps_ref)
    state_taps_ref[0:4, :] = state_conv_ref[...]
    state_taps_ref[4:5, :] = state_bias_ref[...]
    heads_ref[...] = jnp.zeros_like(heads_ref)
    heads_ref[0:1, :heads] = step_bias_ref[...]
    heads_ref[1:2, :heads] = -jnp.exp(decay_ref[...])


def second_norm_kernel(tokens_ref, part_ref, part_in_ref, gain_ref, middle_ref, second_ref, scale_ref):
    middle = tokens_ref[...].astype(F32) + part_ref[...].astype(F32) + part_in_ref[...].astype(F32)
    scale = lax.rsqrt(jnp.mean(middle * middle, axis=1, keepdims=True) + EPS)
    middle_ref[...] = middle
    scale_ref[...] = scale
    second_ref[...] = (middle * scale * gain_ref[...]).astype(BF)


def by_rows(kernel, name, rows, count, ins, outs, scalars=(), tensors=1, limit=VMEM_LIMIT):
    number = len(scalars)

    def place(shape, kind):
        if kind == "whole":
            return spec(shape, lambda i, *s: (0,) * len(shape))
        if kind == "own":
            own = shape[0] // rows if shape[0] < rows * count else count // tensors
            if shape[0] < rows * count:
                return spec((rows, shape[1]), lambda i, *s: (jnp.clip(i - s[0][0] * own, 0, own - 1), 0))
            return spec((rows, shape[1]), lambda i, *s: (jnp.clip(i, s[0][0] * own, s[0][0] * own + own - 1), 0))
        return spec((rows, shape[1]), lambda i, *s: (i, 0))

    return pl.pallas_call(
        kernel,
        grid_spec=pltpu.PrefetchScalarGridSpec(
            num_scalar_prefetch=number,
            grid=(count,),
            in_specs=[place(v.shape, kind) for v, kind in ins],
            out_specs=[place((r, c), kind) for r, c, _, kind in outs],
        ),
        out_shape=[jax.ShapeDtypeStruct((r, c), dtype) for r, c, dtype, _ in outs],
        compiler_params=pltpu.CompilerParams(vmem_limit_bytes=limit),
        name=name,
    )(*scalars, *(v for v, _ in ins))


def ffn_kernel(second_ref, up_ref, weights_ref, active_ref, grads_ref, out_ref, back_ref):
    ffn = active_ref.shape[1]
    gate_vals = jnp.dot(second_ref[...], weights_ref[:, : 2 * ffn], preferred_element_type=F32)
    active_grad = jnp.dot(up_ref[...], weights_ref[:, 2 * ffn :], preferred_element_type=F32)
    gate, up = gate_vals[:, :ffn], gate_vals[:, ffn:]
    sig = sigmoid(gate)
    silu = gate * sig
    active = (silu * up).astype(BF)
    active_ref[...] = active
    grads_ref[:, :ffn] = (active_grad * up * (sig + silu * (1.0 - sig))).astype(BF)
    grads_ref[:, ffn:] = (active_grad * silu).astype(BF)
    out_ref[...] = mm_nt(active, weights_ref[:, 2 * ffn :]).astype(BF)
    back_ref[...] = mm_nt(grads_ref[...], weights_ref[:, : 2 * ffn]).astype(BF)


def second_back_kernel(
    own_count, core_ref, grad_ref, grad_in_ref, middle_ref, scale_ref, up_ref, gain_ref, part_ref, part_in_ref, low_ref, gain_grad_ref, out_ref
):
    offset = pl.program_id(0) - core_ref[0] * own_count

    @pl.when(pl.program_id(0) == 0)
    def _():
        gain_grad_ref[...] = jnp.zeros_like(gain_grad_ref)

    grad = grad_ref[...].astype(F32) + grad_in_ref[...].astype(F32)
    middle, scale = middle_ref[...], scale_ref[...]
    shape = middle * scale
    weighted = grad * gain_ref[...]
    inner = jnp.mean(weighted * shape, axis=1, keepdims=True)
    low_ref[...] = (up_ref[...].astype(F32) + scale * (weighted - shape * inner)).astype(BF)
    gain_grad_ref[0:1, :] += jnp.sum(grad * shape, axis=0, keepdims=True)

    @pl.when((offset >= 0) & (offset < own_count))
    def _():
        out_ref[...] = (middle + part_ref[...].astype(F32) + part_in_ref[...].astype(F32)).astype(BF)


def finish_kernel(
    sizes, first_ref, mix_ref, shared_ref, small_ref, gate_up_sum_ref, down_sum_ref, input_grad_ref,
    mixer_ref, state_ref, step_ref, conv_ref, conv_bias_ref, state_conv_ref, state_bias_ref, step_bias_ref, decay_ref, skip_ref,
    mixer_gain_ref, proj_ref, query_ref, keyval_ref, attention_ref, gate_up_ref, down_ref, second_gain_ref, input_gain_ref, input_back_ref,
):
    wide, width, states2, heads, query_width, ffn = sizes
    input_back_ref[...] = input_grad_ref[...]
    mixer_ref[:, 0, :] = first_ref[:, :width]
    mixer_ref[:, 1, :] = first_ref[:, wide : wide + width]
    state_ref[...] = shared_ref[:, :states2]
    start = 2 * wide + states2
    step_ref[...] = first_ref[:, start : start + LANES].T[:heads, :]
    start = 2 * wide + states2 + LANES
    query_ref[...] = first_ref[:, start : start + query_width]
    groups = [shared_ref[:, i : i + LANES] for i in range(states2, shared_ref.shape[1], LANES)]
    keyval_ref[:, 0, :] = jnp.concatenate([v[:, :HEAD_SIZE] for v in groups], axis=1)
    keyval_ref[:, 1, :] = jnp.concatenate([v[:, HEAD_SIZE:] for v in groups], axis=1)
    proj_ref[...] = mix_ref[:, :width]
    attention_ref[...] = mix_ref[:, wide : wide + query_width]
    gate_up_ref[:, 0, :] = gate_up_sum_ref[:, :ffn]
    gate_up_ref[:, 1, :] = gate_up_sum_ref[:, ffn:]
    down_ref[...] = down_sum_ref[...]
    conv_ref[...] = small_ref[0:4, :width]
    for out_ref, row in ((conv_bias_ref, 4), (mixer_gain_ref, 6)):
        for k in range(out_ref.shape[0]):
            size = out_ref.shape[1]
            out_ref[k : k + 1, :] = small_ref[row : row + 1, k * size : (k + 1) * size]
    place = iota2((width, heads), 0) // (width // heads)
    gather = (place == iota2((width, heads), 1)).astype(F32)
    skip_ref[...] = exact_mm(jnp.broadcast_to(small_ref[5:6, :width], (8, width)), gather)[0:1]
    step_bias_ref[...] = small_ref[0:1, wide : wide + heads]
    decay_ref[...] = small_ref[1:2, wide : wide + heads]
    base = wide + LANES
    state_conv_ref[...] = small_ref[0:4, base : base + states2]
    state_bias_ref[...] = small_ref[4:5, base : base + states2]
    base += states2
    for out_ref in (second_gain_ref, input_gain_ref):
        out_ref[...] = small_ref[:, base : base + out_ref.shape[1]]
        base += out_ref.shape[1]


def body(
    layer_input, doc_ids, input_gain, mixer_weight, state_weight, step_weight, conv_weight, conv_bias, state_conv,
    state_conv_bias, step_bias, decay_log, skip_gain, mixer_gain, mixer_proj, query_weight, keyval_projection,
    attention_proj, second_gain, gate_up, down_proj, cotangent,
):
    tensor_count = lax.axis_size("tensor")
    tensor_index = lax.axis_index("tensor")
    fsdp_count = lax.axis_size("fsdp")
    own_rows, hidden = layer_input.shape
    unit = state_weight.shape[0]
    seq_count, seq_length = doc_ids.shape
    total = seq_count * seq_length
    heads = step_bias.shape[0]
    width = conv_weight.shape[1]
    wide = -(-width // LANES) * LANES
    query_width = query_weight.shape[1]
    query_wide = -(-query_width // LANES) * LANES
    query_heads = query_width // HEAD_SIZE
    per_group = QUERY_HEADS // KEYVAL_HEADS
    kv_heads = max(1, query_heads // per_group)
    kv_leading = tensor_index * query_heads // per_group
    states2 = state_weight.shape[1]
    ffn = down_proj.shape[0]
    low = lambda v: v.astype(BF)

    own_keyval = lax.dynamic_slice_in_dim(keyval_projection, kv_leading * HEAD_SIZE, kv_heads * HEAD_SIZE, 2)
    own_keyval = own_keyval.reshape(unit, 2, kv_heads, HEAD_SIZE).transpose(0, 2, 1, 3).reshape(unit, 2 * kv_heads * HEAD_SIZE)
    kv_wide = 2 * kv_heads * HEAD_SIZE
    rest = pack_weights(pack_rest_kernel, 3 * ffn, "pack_rest", (gate_up, down_proj.T))
    rest = lax.all_gather(rest, "fsdp", axis=0, tiled=True)
    first = pack_weights(
        pack_kernel, 3 * wide + states2 + LANES + 2 * query_wide + kv_wide, "pack_first",
        (mixer_weight, state_weight, step_weight.T, query_weight, own_keyval, mixer_proj.T, attention_proj.T),
    )
    docs = (doc_ids + jnp.arange(seq_count, dtype=jnp.int32)[:, None] * seq_length).reshape(1, total)
    doc_row = docs.astype(F32)
    tables = (
        doc_row, conv_weight, conv_bias[None], state_conv, state_conv_bias[None], step_bias[None], decay_log[None], skip_gain[None]
    )
    first, tokens, upstream, normed, first_scale, normed_turned, feats, cos, sin, taps, state_taps, head_rows = gather_weights(
        first, layer_input, cotangent, input_gain[None], tables, wide, fsdp_count, tensor_count, 0
    )
    ssm_wide = 2 * wide + states2 + LANES
    cuts = np.cumsum([0, ssm_wide, query_wide + kv_wide, wide + query_wide])
    full_ssm, full_qkv, full_mix = (first[:, cuts[i] : cuts[i + 1]] for i in range(3))
    gain_row = pad_to(mixer_gain[None], wide)
    second_row = second_gain[None]

    ssm_in = plain_dot(normed, full_ssm)
    qkv_in = plain_dot(normed, full_qkv)
    scan, gated_low, squares, states = mamba_forward(feats, doc_row, ssm_in, taps, state_taps, head_rows, gain_row, wide, states2)
    mix, log_sums, query_rot, keys, values, squares = attention_forward(
        kv_heads, tensor_count, feats, doc_row, qkv_in, cos, sin, query_wide, gated_low, squares, 2
    )
    branch = tensor_pair(low(right_dot(mix, full_mix)))
    middle, second, second_scale = by_rows(
        second_norm_kernel, "second_norm", CHUNK, total // CHUNK,
        [(tokens, "rows"), (branch[0], "rows"), (branch[1], "rows"), (second_row, "whole")],
        [(total, hidden, F32, "rows"), (total, hidden, BF, "rows"), (total, 1, F32, "rows")],
    )
    active, gu_grad, ffn_out, second_grad = by_rows(
        ffn_kernel, "ffn", min(FFN_ROWS, total), max(total // FFN_ROWS, 1),
        [(second, "rows"), (upstream, "rows"), (rest, "whole")],
        [(total, ffn, BF, "rows"), (total, 2 * ffn, BF, "rows"), (total, hidden, BF, "rows"), (total, hidden, BF, "rows")],
        limit=VMEM_WHOLE,
    )
    second_grad, ffn_out = tensor_pair(second_grad), tensor_pair(ffn_out)
    grad_gate_up, grad_down = low(left_dot(second, gu_grad)), low(left_dot(upstream, active))
    core = jnp.full((1,), tensor_index, jnp.int32)
    rows = min(CHUNK, own_rows)
    branch_low, second_gain_part, layer_output = by_rows(
        functools.partial(second_back_kernel, own_rows // rows), "second_back", rows, total // rows,
        [
            (second_grad[0], "rows"), (second_grad[1], "rows"), (middle, "rows"), (second_scale, "rows"), (upstream, "rows"),
            (second_row, "whole"), (ffn_out[0], "own"), (ffn_out[1], "own"),
        ],
        [(total, hidden, BF, "rows"), (8, hidden, F32, "whole"), (own_rows, hidden, BF, "own")], (core,), tensor_count,
    )
    mix_grad = low(plain_dot(branch_low, full_mix))
    grad_mix = low(left_dot(branch_low, mix))
    input_back, sum_gate_up, sum_down, sum_mix, sum_first, small, shared = backward(
        kv_heads, feats, doc_row, query_rot, keys, values, log_sums, mix_grad, mix, cos, sin, squares, ssm_in, scan, states, taps,
        state_taps, head_rows, gain_row, grad_gate_up, grad_down, grad_mix, normed_turned, first, branch_low, layer_input, first_scale,
        input_gain[None], second_gain_part, wide, states2, fsdp_count, tensor_count, 1,
    )
    shape = lambda *dims: jax.ShapeDtypeStruct(dims, F32)
    folded = (width // LANES, LANES) if width % LANES == 0 else (1, width)
    parts = (sum_first, sum_mix, shared, small, sum_gate_up, sum_down, input_back)
    done = pl.pallas_call(
        functools.partial(finish_kernel, (wide, width, states2, heads, query_width, ffn)),
        grid=(1,),
        in_specs=[spec(v.shape, lambda i: (0,) * 2) for v in parts],
        out_shape=[
            shape(unit, 2, width), shape(unit, states2), shape(heads, unit), shape(4, width), shape(*folded), shape(4, states2),
            shape(1, states2), shape(1, heads), shape(1, heads), shape(1, heads), shape(*folded), shape(unit, width),
            shape(unit, query_width), shape(unit, 2, KEYVAL_HEADS * HEAD_SIZE), shape(unit, query_width), shape(unit, 2, ffn),
            shape(unit, ffn), shape(8, hidden // 8), shape(8, hidden // 8), shape(own_rows, hidden),
        ],
        compiler_params=pltpu.CompilerParams(vmem_limit_bytes=VMEM_WHOLE),
        name="finish",
    )(*parts)
    (
        mixer_sum, state_sum, step_sum, conv_sum, conv_bias_sum, state_conv_sum, state_bias_sum, step_bias_sum, decay_sum, skip_sum,
        mixer_gain_sum, proj_sum, query_sum, keyval_sum, attention_sum, gate_up_sum, down_sum, second_gain_sum, input_gain_sum, input_grad,
    ) = done
    return (
        layer_output, input_grad, input_gain_sum.reshape(hidden), mixer_sum, state_sum, step_sum.T, conv_sum, conv_bias_sum.reshape(width), state_conv_sum,
        state_bias_sum[0], step_bias_sum[0], decay_sum[0], skip_sum[0], mixer_gain_sum.reshape(width), proj_sum.T, query_sum, keyval_sum,
        attention_sum.T, second_gain_sum.reshape(hidden), gate_up_sum, down_sum.T,
    )


def solution(mesh):
    placed = (
        P(("fsdp", "tensor"), None),
        P("fsdp", None),
        P(),
        P("fsdp", None, "tensor"),
        P("fsdp", None),
        P("fsdp", "tensor"),
        P(None, "tensor"),
        P("tensor"),
        P(),
        P(),
        P("tensor"),
        P("tensor"),
        P("tensor"),
        P("tensor"),
        P("tensor", "fsdp"),
        P("fsdp", "tensor"),
        P("fsdp", None, None),
        P("tensor", "fsdp"),
        P(),
        P("fsdp", None, "tensor"),
        P("tensor", "fsdp"),
        P(("fsdp", "tensor"), None),
    )
    return jax.shard_map(
        body,
        mesh=mesh,
        in_specs=placed,
        out_specs=(
            P(("fsdp", "tensor"), None),
            P(("fsdp", "tensor"), None),
            P(),
            P("fsdp", None, "tensor"),
            P("fsdp", None),
            P("fsdp", "tensor"),
            P(None, "tensor"),
            P("tensor"),
            P(),
            P(),
            P("tensor"),
            P("tensor"),
            P("tensor"),
            P("tensor"),
            P("tensor", "fsdp"),
            P("fsdp", "tensor"),
            P("fsdp", None, None),
            P("tensor", "fsdp"),
            P(),
            P("fsdp", None, "tensor"),
            P("tensor", "fsdp"),
        ),
        check_vma=False,
    )
```
